32 devices in a mesh: dp: 8 (over z, y), tensor: 4 (over x, core).
Axes of the slice: x: 2, y: 2, z: 4, core: 2. Of those that a mesh axis runs over, the one named last changes fastest.
Arguments:
- tokens: bfloat16 [8192, 2048], P('dp'), may hold values from -6 to 6
- segments: int32 [8192], P('dp'), may hold values from 0 to 7, as said below
- pad_mask: int32 [8192], P('dp'), may hold values from 0 to 1, as said below
- w_query: bfloat16 [2048, 2048], P(None, 'tensor'), may hold values from -0.125 to 0.125
- w_key: bfloat16 [2048, 2048], P(None, 'tensor'), may hold values from -0.125 to 0.125
- w_value: bfloat16 [2048, 2048], P(None, 'tensor'), may hold values from -0.125 to 0.125
- w_out: bfloat16 [2048, 2048], P('tensor'), may hold values from -0.125 to 0.125
- gain_query: bfloat16 [16, 128], P('tensor'), may hold values from 0.25 to 1.75
- gain_key: bfloat16 [16, 128], P('tensor'), may hold values from 0.25 to 1.75
- gain_attn: bfloat16 [2048], replicated, may hold values from 0.25 to 1.75
- w_gate: bfloat16 [2048, 8192], P(None, 'tensor'), may hold values from -0.125 to 0.125
- w_up: bfloat16 [2048, 8192], P(None, 'tensor'), may hold values from -0.125 to 0.125
- w_down: bfloat16 [8192, 2048], P('tensor'), may hold values from -0.0625 to 0.0625
- gain_mlp: bfloat16 [2048], replicated, may hold values from 0.25 to 1.75
- cotangent: bfloat16 [8192, 2048], P('dp'), may hold values from -6 to 6
Outputs:
- output: bfloat16 [8192, 2048], P('dp')
- grad_tokens: bfloat16 [8192, 2048], P('dp')
- grad_query: float32 [2048, 2048], P('dp', 'tensor')
- grad_key: float32 [2048, 2048], P('dp', 'tensor')
- grad_value: float32 [2048, 2048], P('dp', 'tensor')
- grad_out: float32 [2048, 2048], P('tensor', 'dp')
- grad_gain_query: float32 [16, 128], P('tensor', 'dp')
- grad_gain_key: float32 [16, 128], P('tensor', 'dp')
- grad_gain_attn: float32 [2048], P('dp')
- grad_gate: float32 [2048, 8192], P('dp', 'tensor')
- grad_up: float32 [2048, 8192], P('dp', 'tensor')
- grad_down: float32 [8192, 2048], P('tensor', 'dp')
- grad_gain_mlp: float32 [2048], P('dp')
The draws below stay inside these ranges and needn't reach their ends.
Inputs may be any that keep to these rules, and one draw needn't show every extreme that they name: `segments`: within each packed sequence of 1024 rows the numbers start at 0, never fall, and end at 7; a document is a run of one number. `pad_mask`: in each packed sequence of 1024 rows the ones come first, then 1 to 256 pad slots.
All inputs are finite; a program needn't handle non-finite values.
Results may differ from the reference program's by a relative error of at most 0.017.
Values sent between devices are 32-bit elements; how exact they have to be, the bound alone decides.
A program may use at most 320 MiB of HBM per device.

```python
import jax
import jax.numpy as jnp
from jax import lax

D = 2048
HEADS = 16
HEAD = 128
FF = 8192
LENGTH = 1024
CUTS = 7
TOKENS = 8192


def draw_segments(key, part):
    key = jax.random.fold_in(key, 11)
    seq_count = TOKENS // LENGTH
    cut_picks = jax.random.randint(key, (seq_count, CUTS), 1, LENGTH)
    cut_at = 1 + cut_picks * cut_picks // LENGTH
    position = jnp.arange(LENGTH)
    seg_ids = jnp.sum((cut_at[:, None, :] <= position[None, :, None]).astype(jnp.int32), axis=-1)
    return seg_ids.reshape(-1).astype(jnp.int32)


def draw_pad_mask(key, part):
    key = jax.random.fold_in(key, 23)
    seq_count = TOKENS // LENGTH
    pad_tail = jax.random.randint(key, (seq_count, 1), 1, LENGTH // 4 + 1)
    position = jnp.arange(LENGTH)
    return (position[None, :] < LENGTH - pad_tail).astype(jnp.int32).reshape(-1)


def level_of(stream_key, shape, pieces, smallest, top_value):
    gain, own = 1.0, jax.random.fold_in(stream_key, 6)
    for axis_at, parts in pieces:
        draws = jnp.exp(jax.random.uniform(jax.random.fold_in(own, axis_at), (parts,), jnp.float32, smallest / len(pieces), top_value / len(pieces)))
        gain = gain * jnp.repeat(draws, shape[axis_at] // parts).reshape([-1 if axis == axis_at else 1 for axis in range(len(shape))])
    return gain


def gaussian(key, extent, scale, most, cuts=(), kind=jnp.bfloat16):
    array = scale * jax.random.normal(key, extent, jnp.float32)
    if cuts:
        array = array * level_of(key, extent, cuts, -0.22, 0.18)
    return jnp.clip(array, -most, most).astype(kind)


def setup_inputs(seed: int = 0) -> dict:
    splits = jax.random.split(jax.random.key(seed), 16)
    return {
        "tokens": gaussian(splits[0], (TOKENS, D), 1.0, 6.0, ((0, 8),)),
        "segments": draw_segments(jax.random.fold_in(splits[15], 71), 0),
        "pad_mask": draw_pad_mask(jax.random.fold_in(splits[15], 71), 0),
        "w_query": gaussian(splits[3], (D, D), D ** -0.5, 0.125, ((1, 4),)),
        "w_key": gaussian(splits[4], (D, D), D ** -0.5, 0.125, ((1, 4),)),
        "w_value": gaussian(splits[5], (D, D), D ** -0.5, 0.125, ((1, 4),)),
        "w_out": gaussian(splits[6], (D, D), D ** -0.5, 0.125, ((0, 4),)),
        "gain_query": jnp.clip(1.0 + 0.15 * jax.random.normal(splits[7], (HEADS, HEAD), jnp.float32), 0.25, 1.75).astype(jnp.bfloat16),
        "gain_key": jnp.clip(1.0 + 0.15 * jax.random.normal(splits[8], (HEADS, HEAD), jnp.float32), 0.25, 1.75).astype(jnp.bfloat16),
        "gain_attn": jnp.clip(1.0 + 0.15 * jax.random.normal(splits[9], (D,), jnp.float32), 0.25, 1.75).astype(jnp.bfloat16),
        "w_gate": gaussian(splits[10], (D, FF), D ** -0.5, 0.125, ((1, 4),)),
        "w_up": gaussian(splits[11], (D, FF), D ** -0.5, 0.125, ((1, 4),)),
        "w_down": gaussian(splits[12], (FF, D), FF ** -0.5, 0.0625, ((0, 4),)),
        "gain_mlp": jnp.clip(1.0 + 0.15 * jax.random.normal(splits[13], (D,), jnp.float32), 0.25, 1.75).astype(jnp.bfloat16),
        "cotangent": gaussian(splits[14], (TOKENS, D), 1.0, 6.0, ((0, 8),)),
    }


EPSILON = 1e-06
NEG_FILL = -1e+30
ROPE_BASE = 500000.0

@jax.custom_vjp
def low(v):
    return lax.optimization_barrier(v.astype(jnp.bfloat16)).astype(jnp.float32)

@jax.custom_vjp
def low_back(v):
    return v

def low_keep(v):
    return (low(v), None)

def low_pass(kept, grad):
    return (grad,)

def back_keep(v):
    return (v, None)

def back_low(kept, grad):
    return (low(grad),)
low.defvjp(low_keep, low_pass)
low_back.defvjp(back_keep, back_low)

def project(left, right):
    return jnp.dot(left, right, precision=lax.Precision.HIGHEST)

def rms_scale(values):
    return lax.rsqrt(lax.optimization_barrier(jnp.mean(values * values, axis=1, keepdims=True)) + EPSILON)

def rope_tables():
    half_size = HEAD // 2
    freq_row = ROPE_BASE ** (-(jnp.arange(half_size, dtype=jnp.float32) * 2.0) / HEAD)
    angle = jnp.arange(LENGTH, dtype=jnp.float32)[:, None] * freq_row[None, :]
    return (jnp.cos(angle), jnp.sin(angle))

def rotate(values, cosine, sine_part):
    row_count, col_count = values.shape
    half_size = HEAD // 2
    split = values.reshape(row_count // LENGTH, LENGTH, col_count // HEAD, 2, half_size)
    first = split[:, :, :, 0]
    second = split[:, :, :, 1]
    cos_b = cosine[None, :, None, :]
    sin_b = sine_part[None, :, None, :]
    turned = jnp.stack((first * cos_b - second * sin_b, second * cos_b + first * sin_b), axis=3)
    return turned.reshape(row_count, col_count)

def layer(tokens, segment_ids, live_rows, w_query, w_key, w_value, w_out, gain_query, gain_key, gain_attn, w_gate, w_up, w_down, gain_mlp):
    seq_length = tokens.shape[0]
    cosine, sine_part = rope_tables()
    query_raw = low_back(project(tokens, w_query))
    key_raw = low_back(project(tokens, w_key))
    value_rows = low(low_back(project(tokens, w_value)))
    query_norm = low(rotate(query_raw * rms_scale(query_raw) * gain_query.reshape(-1), cosine, sine_part))
    key_norm = low(rotate(key_raw * rms_scale(key_raw) * gain_key.reshape(-1), cosine, sine_part))
    query_heads = query_norm.reshape(seq_length, HEADS, HEAD)
    key_heads = key_norm.reshape(seq_length, HEADS, HEAD)
    value_heads = value_rows.reshape(seq_length, HEADS, HEAD)
    scores = jnp.einsum('ihd,jhd->hij', query_heads, key_heads, precision=lax.Precision.HIGHEST)
    scores = low_back(scores * HEAD ** (-0.5))
    position = jnp.arange(seq_length)
    causal = position[None, :] <= position[:, None]
    same_doc = segment_ids[:, None] == segment_ids[None, :]
    kept_key = (live_rows[None, :] > 0) | (position[None, :] == position[:, None])
    allowed = causal & same_doc & kept_key
    scores = jnp.where(allowed[None], scores, NEG_FILL)
    attn_prob = low(jax.nn.softmax(scores, axis=-1))
    mixed = jnp.einsum('hij,jhd->ihd', attn_prob, value_heads, precision=lax.Precision.HIGHEST)
    mixed = low(low_back(mixed.reshape(seq_length, -1)))
    branch = low_back(project(mixed, w_out))
    hidden_in = tokens + branch * rms_scale(branch) * gain_attn
    hidden_low = low(hidden_in)
    gate_rows = low_back(project(hidden_low, w_gate))
    up_rows = low_back(project(hidden_low, w_up))
    inner_rows = low(jax.nn.silu(gate_rows) * up_rows)
    down_rows = low_back(project(inner_rows, w_down))
    return hidden_in + down_rows * rms_scale(down_rows) * gain_mlp

def reference(tokens, segments, pad_mask, w_query, w_key, w_value, w_out, gain_query, gain_key, gain_attn, w_gate, w_up, w_down, gain_mlp, cotangent):
    weights = tuple((weight.astype(jnp.float32) for weight in (w_query, w_key, w_value, w_out, gain_query, gain_key, gain_attn, w_gate, w_up, w_down, gain_mlp)))
    seq_count = TOKENS // LENGTH
    seq_items = (tokens.astype(jnp.float32).reshape(seq_count, LENGTH, D), segments.reshape(seq_count, LENGTH), pad_mask.reshape(seq_count, LENGTH), cotangent.astype(jnp.float32).reshape(seq_count, LENGTH, D))

    def seq_step(grad_totals, seq_item):
        seq_tokens, seq_segments, seq_live, seq_cot = seq_item

        def forward(tokens_in, *params):
            return layer(tokens_in, seq_segments, seq_live, *params)
        result, pullback = jax.vjp(forward, seq_tokens, *weights)
        grads = pullback(seq_cot * seq_live.astype(jnp.float32)[:, None])
        new_totals = tuple((total + grad_part for total, grad_part in zip(grad_totals, grads[1:])))
        return (new_totals, (result.astype(jnp.bfloat16), grads[0].astype(jnp.bfloat16)))
    start_totals = tuple((jnp.zeros(weight.shape, jnp.float32) for weight in weights))
    final, (results, token_grads) = lax.scan(seq_step, start_totals, seq_items)
    return (results.reshape(TOKENS, D), token_grads.reshape(TOKENS, D), final[0], final[1], final[2], final[3], final[4], final[5], final[6], final[7], final[8], final[9], final[10])
```

```python
import functools

import jax
import jax.numpy as jnp
from jax import lax
from jax.experimental import pallas as pl
from jax.experimental.pallas import tpu as pltpu
from jax.sharding import PartitionSpec as P

HEAD = 128
LENGTH = 1024
EPSILON = 1e-06
NEG_FILL = -1e30
ROPE_BASE = 500000.0
ROW_CHUNKS = 4
F32 = jnp.float32
BF16 = jnp.bfloat16


COLS = 512

def dp_kernel(dp_size, groups, *refs):
    n = len(groups)
    at_refs = refs[:n]
    b_refs = refs[n:2 * n]
    out_ref = refs[2 * n]
    (ysend, yrecv, zsend, zrecv, stage, ys_sem, yr_sem, zs_sem, zr_sem, out_sem,
     y_credit, up_credit, down_credit) = refs[2 * n + 1:]
    line = dp_size // 2
    block = at_refs[0].shape[0] // dp_size
    dp_at = lax.axis_index("dp")
    z, y = dp_at // 2, dp_at % 2
    total = sum(groups)
    partner = dp_at + 1 - 2 * y
    below, above = dp_at - 2, dp_at + 2
    has_below, has_above = z > 0, z < line - 1

    def dev(i):
        return {"dp": i}

    barrier = pltpu.get_barrier_semaphore()
    pl.semaphore_signal(barrier, inc=1, device_id=dev(partner), device_id_type=pl.DeviceIdType.MESH)

    @pl.when(has_below)
    def _():
        pl.semaphore_signal(barrier, inc=1, device_id=dev(below), device_id_type=pl.DeviceIdType.MESH)

    @pl.when(has_above)
    def _():
        pl.semaphore_signal(barrier, inc=1, device_id=dev(above), device_id_type=pl.DeviceIdType.MESH)

    pl.semaphore_wait(barrier, 1 + has_below.astype(jnp.int32) + has_above.astype(jnp.int32))

    def y_copy(p, b):
        return pltpu.make_async_remote_copy(
            src_ref=ysend.at[p, b], dst_ref=yrecv.at[p, b], send_sem=ys_sem.at[p, b],
            recv_sem=yr_sem.at[p, b], device_id=dev(partner), device_id_type=pl.DeviceIdType.MESH)

    def z_copy(p, b, slot, target):
        return pltpu.make_async_remote_copy(
            src_ref=zsend.at[p, b], dst_ref=zrecv.at[p, slot], send_sem=zs_sem.at[p, b],
            recv_sem=zr_sem.at[p, slot], device_id=dev(target), device_id_type=pl.DeviceIdType.MESH)

    def walk(fn, own):
        def body(i, carry):
            @pl.when(z <= i)
            def _():
                fn(z + line - 1 - i, True)

            @pl.when(z >= line - 1 - i)
            def _():
                fn(z - (line - 1 - i), False)
            return carry
        lax.fori_loop(0, line - 1, body, 0)
        own(z)

    def product(at_ref, b_ref, rows_at, col):
        return jnp.dot(
            at_ref[pl.ds(pl.multiple_of(rows_at * block, block), block), :],
            b_ref[:, pl.ds(pl.multiple_of(col * COLS, COLS), COLS)],
            preferred_element_type=F32)

    def send_stage(k, p, at_ref, b_ref, col):
        @pl.when(k >= 2)
        def _():
            for b in range(line):
                y_copy(p, b).wait_send()
            pl.semaphore_wait(y_credit, 1)

        def one(b, up=None):
            ysend[p, b] = product(at_ref, b_ref, 2 * b + 1 - y, col)
            y_copy(p, b).start()
        walk(one, one)

    def sum_stage(k, p, at_ref, b_ref, col):
        @pl.when(k >= 2)
        def _():
            for b in range(line):
                @pl.when(z != b)
                def _():
                    z_copy(p, b, b, below).wait_send()

            @pl.when(has_above)
            def _():
                pl.semaphore_wait(up_credit, 1)

            @pl.when(has_below)
            def _():
                pl.semaphore_wait(down_credit, 1)

        def mine(b):
            part = product(at_ref, b_ref, 2 * b + y, col)
            y_copy(p, b).wait_recv()
            return part + yrecv[p, b]

        def one(b, up):
            has_before, target = (has_below, above) if up else (has_above, below)
            zsend[p, b] = mine(b)

            @pl.when(has_before)
            def _():
                z_copy(p, b, b, target).wait_recv()
                zsend[p, b] += zrecv[p, b]
            if up:
                z_copy(p, b, b, target).start()
            else:
                @pl.when(b == z - 1)
                def _():
                    z_copy(p, b, line, target).start()

                @pl.when(b != z - 1)
                def _():
                    z_copy(p, b, b, target).start()

        def own(b):
            @pl.when(k >= 1)
            def _():
                pltpu.make_async_copy(stage, out_ref.at[k - 1], out_sem).wait()
            stage[...] = mine(b)

            @pl.when(has_below)
            def _():
                z_copy(p, b, b, below).wait_recv()
                stage[...] += zrecv[p, b]

            @pl.when(has_above)
            def _():
                z_copy(p, b, line, below).wait_recv()
                stage[...] += zrecv[p, line]
            pltpu.make_async_copy(stage, out_ref.at[k], out_sem).start()
        walk(one, own)

        @pl.when(k < total - 2)
        def _():
            pl.semaphore_signal(y_credit, inc=1, device_id=dev(partner), device_id_type=pl.DeviceIdType.MESH)

            @pl.when(has_below)
            def _():
                pl.semaphore_signal(up_credit, inc=1, device_id=dev(below), device_id_type=pl.DeviceIdType.MESH)

            @pl.when(has_above)
            def _():
                pl.semaphore_signal(down_credit, inc=1, device_id=dev(above), device_id_type=pl.DeviceIdType.MESH)

    send_stage(0, 0, at_refs[0], b_refs[0], 0)
    k0 = 0
    for g, count in enumerate(groups):
        at_ref, b_ref = at_refs[g], b_refs[g]

        def body(i, carry):
            k = k0 + i
            send_stage(k + 1, lax.rem(k + 1, 2), at_ref, b_ref, i + 1)
            sum_stage(k, lax.rem(k, 2), at_ref, b_ref, i)
            return carry
        lax.fori_loop(0, count - 1, body, 0)
        k = k0 + count - 1
        if g + 1 < n:
            send_stage(k + 1, (k + 1) % 2, at_refs[g + 1], b_refs[g + 1], 0)
        sum_stage(k, k % 2, at_ref, b_ref, count - 1)
        k0 += count
    pltpu.make_async_copy(stage, out_ref.at[total - 1], out_sem).wait()
    for p in range(2):
        for b in range(line):
            y_copy(p, b).wait_send()

            @pl.when(z != b)
            def _():
                z_copy(p, b, b, below).wait_send()

def dp_reduce(dp_size, pairs, collective_id=0):
    line = dp_size // 2
    depth = pairs[0][0].shape[0]
    block = depth // dp_size
    groups = [right.shape[1] // COLS for _, right in pairs]
    total = sum(groups)
    slot = (block, COLS)
    DMA = pltpu.SemaphoreType.DMA
    return pl.pallas_call(
        functools.partial(dp_kernel, dp_size, groups),
        out_shape=jax.ShapeDtypeStruct((total,) + slot, F32),
        in_specs=[pl.BlockSpec(memory_space=pltpu.VMEM)] * (2 * len(pairs)),
        out_specs=pl.BlockSpec(memory_space=pl.ANY),
        scratch_shapes=[
            pltpu.VMEM((2, line) + slot, F32),
            pltpu.VMEM((2, line) + slot, F32),
            pltpu.VMEM((2, line) + slot, F32),
            pltpu.VMEM((2, line + 1) + slot, F32),
            pltpu.VMEM(slot, F32),
            DMA((2, line)), DMA((2, line)), DMA((2, line)), DMA((2, line + 1)), DMA,
            pltpu.SemaphoreType.REGULAR, pltpu.SemaphoreType.REGULAR, pltpu.SemaphoreType.REGULAR,
        ],
        compiler_params=pltpu.CompilerParams(
            collective_id=collective_id, has_side_effects=True, vmem_limit_bytes=60 * 1024 * 1024),
    )(*[left for left, _ in pairs], *[right for _, right in pairs])


def times(left, right):
    return jnp.dot(left, right, preferred_element_type=F32)


def outer_sum(left, right):
    return lax.dot_general(left, right, (((0,), (0,)), ((), ())), preferred_element_type=F32)


def back_product(left, right):
    return lax.dot_general(left, right, (((1,), (1,)), ((), ())), preferred_element_type=F32)


def rope_tables():
    half_size = HEAD // 2
    freq_row = ROPE_BASE ** (-(jnp.arange(half_size, dtype=F32) * 2.0) / HEAD)
    angle = jnp.arange(LENGTH, dtype=F32)[:, None] * freq_row[None, :]
    return (jnp.cos(angle), jnp.sin(angle))


def rotate(values, cosine, sine_part, direction):
    row_count, col_count = values.shape
    half_size = HEAD // 2
    split = values.reshape(row_count // LENGTH, LENGTH, col_count // HEAD, 2, half_size)
    first = split[:, :, :, 0]
    second = split[:, :, :, 1]
    cos_b = cosine[None, :, None, :]
    sin_b = direction * sine_part[None, :, None, :]
    turned = jnp.stack((first * cos_b - second * sin_b, second * cos_b + first * sin_b), axis=3)
    return turned.reshape(row_count, col_count)


def visible_keys(begin_at, block_rows, segment_ids, live_rows):
    seq_length = segment_ids.shape[0]
    key_index = jnp.arange(seq_length)
    query_index = begin_at + jnp.arange(block_rows)
    query_segs = segment_ids[begin_at : begin_at + block_rows]
    same_doc = query_segs[:, None] == segment_ids[None, :]
    causal = key_index[None, :] <= query_index[:, None]
    kept_key = (live_rows[None, :] > 0) | (key_index[None, :] == query_index[:, None])
    return same_doc & causal & kept_key


def block_scores(query_seq, key_heads, begin_at, block_rows, segment_ids, live_rows):
    local_heads = key_heads.shape[1]
    query_heads = query_seq[begin_at : begin_at + block_rows].reshape(block_rows, local_heads, HEAD)
    scores = jnp.einsum(
        "ihd,jhd->hij", query_heads, key_heads, preferred_element_type=F32
    ) * HEAD ** (-0.5)
    allowed = visible_keys(begin_at, block_rows, segment_ids, live_rows)
    return (query_heads, jnp.where(allowed[None], scores, NEG_FILL))


def attend_forward(query_seq, key_seq, value_seq, segment_ids, live_rows):
    seq_length = query_seq.shape[0]
    local_heads = query_seq.shape[1] // HEAD
    block_rows = min(512, seq_length)
    key_heads = key_seq.reshape(seq_length, local_heads, HEAD)
    value_heads = value_seq.reshape(seq_length, local_heads, HEAD)
    mixed_parts = []
    lse_parts = []
    for begin_at in range(0, seq_length, block_rows):
        query_heads, scores = block_scores(
            query_seq, key_heads, begin_at, block_rows, segment_ids, live_rows
        )
        row_max = jnp.max(scores, axis=-1, keepdims=True)
        exp_scores = jnp.exp(scores - row_max)
        row_total = jnp.sum(exp_scores, axis=-1, keepdims=True)
        attn_prob = (exp_scores / row_total).astype(BF16)
        mixed_block = jnp.einsum(
            "hij,jhd->ihd", attn_prob, value_heads, preferred_element_type=F32
        )
        mixed_parts.append(mixed_block.reshape(block_rows, -1).astype(BF16))
        lse_parts.append((row_max + jnp.log(row_total))[..., 0])
    return (jnp.concatenate(mixed_parts, 0), jnp.concatenate(lse_parts, 1))


def attend_backward(query_seq, key_seq, value_seq, grad_seq, log_totals, segment_ids, live_rows):
    seq_length = query_seq.shape[0]
    local_heads = query_seq.shape[1] // HEAD
    block_rows = min(512, seq_length)
    score_scale = HEAD ** (-0.5)
    key_heads = key_seq.reshape(seq_length, local_heads, HEAD)
    value_heads = value_seq.reshape(seq_length, local_heads, HEAD)
    key_total = jnp.zeros((seq_length, local_heads, HEAD), F32)
    value_total = jnp.zeros((seq_length, local_heads, HEAD), F32)
    query_parts = []
    for begin_at in range(0, seq_length, block_rows):
        query_heads, scores = block_scores(
            query_seq, key_heads, begin_at, block_rows, segment_ids, live_rows
        )
        attn_float = jnp.exp(scores - log_totals[:, begin_at : begin_at + block_rows, None])
        attn_prob = attn_float.astype(BF16)
        grad_heads = grad_seq[begin_at : begin_at + block_rows].reshape(
            block_rows, local_heads, HEAD
        )
        grad_prob = jnp.einsum(
            "ihd,jhd->hij", grad_heads, value_heads, preferred_element_type=F32
        )
        row_dot = jnp.sum(attn_float * grad_prob, axis=-1, keepdims=True)
        grad_scores = (attn_float * (grad_prob - row_dot)).astype(BF16)
        query_block = (
            jnp.einsum("hij,jhd->ihd", grad_scores, key_heads, preferred_element_type=F32)
            * score_scale
        )
        query_parts.append(query_block.reshape(block_rows, -1))
        key_total = (
            key_total
            + jnp.einsum("hij,ihd->jhd", grad_scores, query_heads, preferred_element_type=F32)
            * score_scale
        )
        value_total = value_total + jnp.einsum(
            "hij,ihd->jhd", attn_prob, grad_heads, preferred_element_type=F32
        )
    return (
        jnp.concatenate(query_parts, 0),
        key_total.reshape(seq_length, -1),
        value_total.reshape(seq_length, -1).astype(BF16),
    )


def norm_back(grad_rows, values, inv_rms, gain_row, model_width):
    scaled = grad_rows * gain_row
    inner_dot = jnp.sum(scaled * values, axis=1, keepdims=True)
    return inv_rms * scaled - values * inv_rms**3 * inner_dot / model_width


def make_shards(dp_size, tensor_size):
    core_pairs = [(i, i ^ 1) for i in range(tensor_size)]
    tensor_bits = [1 << b for b in range(1, tensor_size.bit_length() - 1)]

    def to_core(values):
        return lax.ppermute(values, "tensor", core_pairs)

    def from_core(values):
        return to_core(values * 0.5) * 2.0

    def wide_sum(values):
        for bit in tensor_bits:
            values = values + lax.ppermute(
                values, "tensor", [(i, i ^ bit) for i in range(tensor_size)]
            )
        return values

    def own_rows_sum(own_part, other_part):
        return wide_sum(own_part + to_core(other_part))

    def shards(
        tokens,
        segments,
        pad_mask,
        w_query,
        w_key,
        w_value,
        w_out,
        gain_query,
        gain_key,
        gain_attn,
        w_gate,
        w_up,
        w_down,
        gain_mlp,
        cotangent,
    ):
        row_count, model_width = tokens.shape
        half_rows = row_count // 2
        chunk = half_rows // ROW_CHUNKS
        block = model_width // dp_size
        core_at = lax.axis_index("tensor") % 2
        cosine, sine_part = rope_tables()

        def split_rows(values):
            own = lax.dynamic_slice_in_dim(values, core_at * half_rows, half_rows, 0)
            other = lax.dynamic_slice_in_dim(values, (1 - core_at) * half_rows, half_rows, 0)
            return own, other

        def join_rows(own, other):
            return jnp.where(
                core_at == 0,
                jnp.concatenate((own, other), 0),
                jnp.concatenate((other, own), 0),
            )

        def cut(values):
            return [values[k * chunk : (k + 1) * chunk] for k in range(ROW_CHUNKS)]

        query_raw = times(tokens, w_query)
        key_raw = times(tokens, w_key)
        value_rows = times(tokens, w_value).astype(BF16)
        squares = jnp.stack(
            (jnp.sum(query_raw * query_raw, axis=1), jnp.sum(key_raw * key_raw, axis=1))
        )
        squares = wide_sum(squares + to_core(squares))
        query_inv = lax.rsqrt(squares[0] / model_width + EPSILON)[:, None]
        key_inv = lax.rsqrt(squares[1] / model_width + EPSILON)[:, None]
        query_gain = gain_query.reshape(-1).astype(F32)
        key_gain = gain_key.reshape(-1).astype(F32)
        query_norm = rotate(query_raw * query_inv * query_gain, cosine, sine_part, 1.0).astype(BF16)
        key_norm = rotate(key_raw * key_inv * key_gain, cosine, sine_part, 1.0).astype(BF16)
        mixed, log_totals = attend_forward(query_norm, key_norm, value_rows, segments, pad_mask)
        mixed_own, mixed_other = split_rows(mixed)
        mixed_rows = jnp.concatenate((mixed_own, mixed_other), 0)
        tokens_own, tokens_other = split_rows(tokens)
        cot_own, _ = split_rows(cotangent)
        live_own, _ = split_rows(pad_mask.astype(F32)[:, None])
        attn_gain = gain_attn.astype(F32)
        mlp_gain = gain_mlp.astype(F32)
        seed = cot_own.astype(F32) * live_own

        branch, branch_inv, hidden_in = [], [], []
        low_own, low_other = [], []
        gates, ups, sigs, inners = {}, {}, {}, {}
        down, down_inv = [], []
        for part, other, tok, tok_other in zip(
            cut(mixed_own), cut(mixed_other), cut(tokens_own), cut(tokens_other)
        ):
            total = own_rows_sum(times(part, w_out), times(other, w_out))
            inv = lax.rsqrt(jnp.mean(total * total, axis=1, keepdims=True) + EPSILON)
            step = total * inv * attn_gain
            branch.append(total)
            branch_inv.append(inv)
            hidden = tok.astype(F32) + step
            hidden_in.append(hidden)
            low_own.append(hidden.astype(BF16))
            low_other.append((tok_other.astype(F32) + to_core(step)).astype(BF16))
        for at in range(ROW_CHUNKS):
            parts = []
            for side, low in ((0, low_own[at]), (1, low_other[at])):
                gate = times(low, w_gate)
                up = times(low, w_up)
                sig = jax.nn.sigmoid(gate)
                inner = (gate * sig * up).astype(BF16)
                gates[side, at], ups[side, at], inners[side, at] = gate, up, inner
                parts.append(times(inner, w_down))
            total = own_rows_sum(*parts)
            down.append(total)
            down_inv.append(lax.rsqrt(jnp.mean(total * total, axis=1, keepdims=True) + EPSILON))

        seeds = cut(seed)
        gain_mlp_part = 0.0
        gdr_own, gdr_other, out_own = [], [], []
        for at in range(ROW_CHUNKS):
            gain_mlp_part = gain_mlp_part + jnp.sum(seeds[at] * down[at] * down_inv[at], axis=0)
            grad = norm_back(seeds[at], down[at], down_inv[at], mlp_gain, model_width)
            gdr_own.append(grad.astype(BF16))
            gdr_other.append(from_core(grad).astype(BF16))
            out_own.append(hidden_in[at] + down[at] * down_inv[at] * mlp_gain)
        out_own = jnp.concatenate(out_own, 0)
        out_other = from_core(out_own)
        output = join_rows(out_own.astype(BF16), out_other.astype(BF16))

        def all_rows(own, other):
            return jnp.concatenate(list(own) + list(other), 0)

        def all_sides(parts):
            return jnp.concatenate(
                [parts[side, at] for side in range(2) for at in range(ROW_CHUNKS)], 0
            )

        grad_down_rows = all_rows(gdr_own, gdr_other)
        inner_rows = all_sides(inners)
        gate_rows = all_sides(gates)
        up_rows = all_sides(ups)
        hidden_low = all_rows(low_own, low_other)
        grad_inner = back_product(grad_down_rows, w_down)
        gate_sig = jax.nn.sigmoid(gate_rows)
        grad_gate_rows = (
            grad_inner * up_rows * gate_sig * (1.0 + gate_rows * (1.0 - gate_sig))
        ).astype(BF16)
        grad_up_rows = (grad_inner * gate_rows * gate_sig).astype(BF16)
        gain_attn_part = 0.0
        gb_own, gb_other, grad_hidden = [], [], []
        for at in range(ROW_CHUNKS):
            parts = []
            for first in (0, half_rows):
                rows = slice(first + at * chunk, first + (at + 1) * chunk)
                parts.append(
                    back_product(grad_gate_rows[rows], w_gate)
                    + back_product(grad_up_rows[rows], w_up)
                )
            total = seeds[at] + own_rows_sum(*parts)
            grad_hidden.append(total)
            gain_attn_part = gain_attn_part + jnp.sum(total * branch[at] * branch_inv[at], axis=0)
            grad = norm_back(total, branch[at], branch_inv[at], attn_gain, model_width)
            gb_own.append(grad.astype(BF16))
            gb_other.append(from_core(grad).astype(BF16))
        grad_branch = all_rows(gb_own, gb_other)
        grad_mixed = back_product(grad_branch, w_out).astype(BF16)
        grad_mixed = join_rows(grad_mixed[:half_rows], grad_mixed[half_rows:])
        grad_query_rot, grad_key_rot, grad_value_rows = attend_backward(
            query_norm, key_norm, value_rows, grad_mixed, log_totals, segments, pad_mask
        )
        grad_query_norm = rotate(grad_query_rot, cosine, sine_part, -1.0)
        grad_key_norm = rotate(grad_key_rot, cosine, sine_part, -1.0)
        gain_query_part = jnp.sum(grad_query_norm * query_raw * query_inv, axis=0)
        gain_key_part = jnp.sum(grad_key_norm * key_raw * key_inv, axis=0)
        query_scaled = grad_query_norm * query_gain
        key_scaled = grad_key_norm * key_gain
        dots = jnp.stack(
            (jnp.sum(query_scaled * query_raw, axis=1), jnp.sum(key_scaled * key_raw, axis=1))
        )
        dots = wide_sum(dots + to_core(dots))
        grad_query_raw = (
            query_inv * query_scaled - query_raw * query_inv**3 * dots[0][:, None] / model_width
        ).astype(BF16)
        grad_key_raw = (
            key_inv * key_scaled - key_raw * key_inv**3 * dots[1][:, None] / model_width
        ).astype(BF16)
        grad_rows = jnp.concatenate((grad_query_raw, grad_key_raw, grad_value_rows), 1)
        w_all = jnp.concatenate((w_query, w_key, w_value), 1)
        rows_own, rows_other = split_rows(grad_rows)
        token_own = []
        for at, (part, other) in enumerate(zip(cut(rows_own), cut(rows_other))):
            token_own.append(
                grad_hidden[at]
                + own_rows_sum(back_product(part, w_all), back_product(other, w_all))
            )
        token_own = jnp.concatenate(token_own, 0)
        token_other = from_core(token_own)
        grad_tokens = join_rows(token_own.astype(BF16), token_other.astype(BF16))

        summed = dp_reduce(
            dp_size,
            [
                (grad_down_rows.T, inner_rows),
                (hidden_low.T, jnp.concatenate((grad_gate_rows, grad_up_rows), 1)),
                (grad_branch.T, mixed_rows),
                (tokens.T, grad_rows),
            ],
        )

        def side_by_side(first, count):
            return jnp.concatenate([summed[first + i] for i in range(count)], 1)

        hidden_chunks, head_chunks = w_gate.shape[1] // COLS, w_query.shape[1] // COLS
        starts = [0, hidden_chunks, 2 * hidden_chunks, 3 * hidden_chunks]
        grad_down, grad_gate, grad_up = (side_by_side(at, hidden_chunks) for at in starts[:3])
        grad_out, grad_query, grad_key, grad_value = (
            side_by_side(starts[3] + i * head_chunks, head_chunks) for i in range(4)
        )

        wide_gains = jnp.concatenate((gain_mlp_part, gain_attn_part))
        wide_gains = wide_gains + to_core(wide_gains)

        def by_block(values):
            heads = values.shape[0]
            return values.reshape(heads, dp_size, -1).transpose(1, 0, 2).reshape(dp_size, -1)

        gains = jnp.concatenate(
            (
                by_block(wide_gains[None, :model_width]),
                by_block(wide_gains[None, model_width:]),
                by_block(gain_query_part.reshape(gain_query.shape)),
                by_block(gain_key_part.reshape(gain_key.shape)),
            ),
            1,
        )
        gains = lax.psum_scatter(gains, "dp", scatter_dimension=0, tiled=True)[0]
        heads, head_block = gain_query.shape[0], HEAD // dp_size
        grad_gain_mlp = gains[:block]
        grad_gain_attn = gains[block : 2 * block]
        head_part = gains[2 * block :].reshape(2, heads, head_block)
        return (
            output,
            grad_tokens,
            grad_query,
            grad_key,
            grad_value,
            grad_out.T,
            head_part[0],
            head_part[1],
            grad_gain_attn,
            grad_gate,
            grad_up,
            grad_down.T,
            grad_gain_mlp,
        )

    return shards


def solution(mesh):
    in_specs = (
        P("dp", None),
        P("dp"),
        P("dp"),
        P(None, "tensor"),
        P(None, "tensor"),
        P(None, "tensor"),
        P("tensor", None),
        P("tensor", None),
        P("tensor", None),
        P(),
        P(None, "tensor"),
        P(None, "tensor"),
        P("tensor", None),
        P(),
        P("dp", None),
    )
    out_specs = (
        P("dp", None),
        P("dp", None),
        P("dp", "tensor"),
        P("dp", "tensor"),
        P("dp", "tensor"),
        P("tensor", "dp"),
        P("tensor", "dp"),
        P("tensor", "dp"),
        P("dp"),
        P("dp", "tensor"),
        P("dp", "tensor"),
        P("tensor", "dp"),
        P("dp"),
    )
    shards = make_shards(mesh.shape["dp"], mesh.shape["tensor"])
    return jax.shard_map(shards, mesh=mesh, in_specs=in_specs, out_specs=out_specs, check_vma=False)
```

```python
import functools

import jax
import jax.numpy as jnp
from jax import lax
from jax.experimental import pallas as pl
from jax.experimental.pallas import tpu as pltpu
from jax.sharding import PartitionSpec as P

HEAD = 128
LENGTH = 1024
EPSILON = 1e-06
NEG_FILL = -1e30
ROPE_BASE = 500000.0
ROW_CHUNKS = 4
F32 = jnp.float32
BF16 = jnp.bfloat16


COLS = 256
SPAN = 6
Y_SLOTS = 3
B_SLOTS = 5
HBM_NAMES = (
    "gdrt", "hlt", "tokens", "inner", "mixed", "gdr", "gate", "up", "branch", "seed",
    "query", "key", "value", "query_raw", "key_raw",
    "w_out", "w_gate", "w_up", "w_down", "w_query", "w_key", "w_value",
)
TILE = 512
VMEM_LIMIT = 63 * 1024 * 1024
MESH = pl.DeviceIdType.MESH

def column_sum(values):
    return jnp.sum(values, axis=0, keepdims=True)


def mean_inverse(values):
    return lax.rsqrt(jnp.mean(values * values, axis=1, keepdims=True) + EPSILON)


def tensor_peers():
    at = lax.axis_index("tensor")
    core = lax.rem(at, 2)
    return core, at + 1 - 2 * core, lax.rem(at + 2, 4)


def greet(*peers):
    barrier = pltpu.get_barrier_semaphore()
    for peer in peers:
        pl.semaphore_signal(barrier, inc=1, device_id=peer, device_id_type=MESH)
    pl.semaphore_wait(barrier, len(peers))


def forward_kernel(
    mixed, w_out, attn_gain, mlp_gain, tok_hbm, seed_hbm, wg_hbm, wu_hbm, wd_hbm,
    gate_out, up_out, inner_out, hlt_out, gdr_out, gdrt_out, branch_out, out_out, gain_out,
    wg, wu, wd, cs, crecv, xs, xr, xr2, ag, gate_buf, up_buf, inner_buf, low_buf, hlt_buf,
    out_buf, tok, seed,
    w_sem, t_sem, s_sem, cs_sem, cr_sem, xs_sem, xr_sem, as_sem, ar_sem, cs2_sem, cr2_sem, xs2_sem, xr2_sem,
    gs_sem, gr_sem, os_sem, or_sem, g_sem, h_sem, b_sem, d_sem, o_sem,
):
    core, sibling, across = tensor_peers()
    chunk = xs.shape[1]
    half = chunk * ROW_CHUNKS
    tiles = wg.shape[1] // TILE
    wide_tiles = wd.shape[1] // TILE
    loads = [
        pltpu.make_async_copy(src, dst, w_sem.at[i])
        for i, (src, dst) in enumerate(((wg_hbm, wg), (wu_hbm, wu), (wd_hbm, wd)))
    ]
    for load in loads:
        load.start()

    def row_load(c, src, dst, sem):
        return pltpu.make_async_copy(
            src.at[pl.ds(c * chunk, chunk)], dst.at[c % 2], sem.at[c % 2])

    for c in range(2):
        row_load(c, tok_hbm, tok, t_sem).start()
        row_load(c, seed_hbm, seed, s_sem).start()
    greet({"tensor": sibling}, {"tensor": across})

    def remote(src, dst, send_sem, recv_sem, peer):
        return pltpu.make_async_remote_copy(
            src_ref=src, dst_ref=dst, send_sem=send_sem, recv_sem=recv_sem,
            device_id={"tensor": peer}, device_id_type=MESH)

    def core_copy(c):
        return remote(cs.at[c % 2], crecv.at[c], cs_sem.at[c], cr_sem.at[c], sibling)

    def x_copy(c):
        return remote(xs.at[c], xr.at[c], xs_sem.at[c], xr_sem.at[c], across)

    def hidden_copy(c):
        return remote(xr.at[c], ag.at[c % 2], as_sem.at[c], ar_sem.at[c], sibling)

    def core2_copy(c):
        return remote(cs.at[c % 2], crecv.at[c], cs2_sem.at[c], cr2_sem.at[c], sibling)

    def x2_copy(c):
        return remote(xs.at[c], xr2.at[c], xs2_sem.at[c], xr2_sem.at[c], across)

    def grad_copy(c):
        return remote(xr2.at[c], ag.at[c % 2], gs_sem.at[c], gr_sem.at[c], sibling)

    def out_copy(c):
        return remote(xr.at[c], crecv.at[c], os_sem.at[c], or_sem.at[c], sibling)

    def rows(first):
        return pl.ds(first, chunk)

    def side_copies(buf, dst, sem, c):
        return [
            pltpu.make_async_copy(
                buf.at[pl.ds(s * chunk, chunk)], dst.at[rows(s * half + c * chunk)], sem.at[s])
            for s in range(2)
        ]

    def turned_copies(buf, dst, sem, c):
        return [
            pltpu.make_async_copy(
                buf.at[:, pl.ds(s * chunk, chunk)], dst.at[:, rows(s * half + c * chunk)], sem.at[s])
            for s in range(2)
        ]

    for c in range(ROW_CHUNKS):
        if c >= 2:
            core_copy(c - 2).wait_send()
        cs[c % 2] = jnp.dot(mixed[rows(half + c * chunk), :], w_out[...], preferred_element_type=F32)
        core_copy(c).start()
        xs[c] = jnp.dot(mixed[rows(c * chunk), :], w_out[...], preferred_element_type=F32)
        if c >= 1:
            core_copy(c - 1).wait_recv()
            xs[c - 1] += crecv[c - 1]
            x_copy(c - 1).start()
    last = ROW_CHUNKS - 1
    core_copy(last).wait_recv()
    xs[last] += crecv[last]
    x_copy(last).start()
    core_copy(last - 1).wait_send()
    core_copy(last).wait_send()

    def feed(c):
        x_copy(c).wait()
        total = xs[c] + xr[c]
        xs[c] = total
        branch_copy = pltpu.make_async_copy(xs.at[c], branch_out.at[rows(c * chunk)], b_sem)
        branch_copy.start()
        row_load(c, tok_hbm, tok, t_sem).wait()
        hidden = tok[c % 2].astype(F32) + total * mean_inverse(total) * attn_gain[...]
        if c + 2 < ROW_CHUNKS:
            row_load(c + 2, tok_hbm, tok, t_sem).start()
        xr[c] = hidden
        hidden_copy(c).start()
        low_buf[0:chunk, :] = hidden.astype(BF16)
        if c >= 1:
            for copy in turned_copies(hlt_buf, hlt_out, h_sem, c - 1):
                copy.wait()
            for buf, dst, i in ((gate_buf, gate_out, 0), (up_buf, up_out, 1), (inner_buf, inner_out, 2)):
                for copy in side_copies(buf, dst, g_sem.at[i], c - 1):
                    copy.wait()
        hlt_buf[:, 0:chunk] = hidden.astype(BF16).T
        hidden_copy(c).wait_recv()
        low_buf[chunk : 2 * chunk, :] = ag[c % 2].astype(BF16)
        hlt_buf[:, chunk : 2 * chunk] = ag[c % 2].astype(BF16).T
        for copy in turned_copies(hlt_buf, hlt_out, h_sem, c):
            copy.start()
        if c == 0:
            loads[0].wait()
            loads[1].wait()

        def tile(n, carry):
            at = pl.ds(pl.multiple_of(n * TILE, TILE), TILE)
            gate = jnp.dot(low_buf[...], wg[:, at], preferred_element_type=F32)
            up = jnp.dot(low_buf[...], wu[:, at], preferred_element_type=F32)
            gate_buf[:, at] = gate
            up_buf[:, at] = up
            inner_buf[:, at] = (gate * jax.nn.sigmoid(gate) * up).astype(BF16)
            return carry
        lax.fori_loop(0, tiles, tile, 0)
        for buf, dst, i in ((gate_buf, gate_out, 0), (up_buf, up_out, 1), (inner_buf, inner_out, 2)):
            for copy in side_copies(buf, dst, g_sem.at[i], c):
                copy.start()
        if c == 0:
            loads[2].wait()
        if c >= 2:
            core2_copy(c - 2).wait_send()
        branch_copy.wait()

        def down_tile(n, carry):
            at = pl.ds(pl.multiple_of(n * TILE, TILE), TILE)
            part = jnp.dot(inner_buf[...], wd[:, at], preferred_element_type=F32)
            xs[c, :, at] = part[0:chunk]
            cs[c % 2, :, at] = part[chunk : 2 * chunk]
            return carry
        lax.fori_loop(0, wide_tiles, down_tile, 0)
        core2_copy(c).start()
        core2_copy(c).wait_recv()
        xs[c] += crecv[c]
        x2_copy(c).start()

    def finish(c, gain_total):
        x2_copy(c).wait()
        down = xs[c] + xr2[c]
        inv = mean_inverse(down)
        row_load(c, seed_hbm, seed, s_sem).wait()
        seed_rows = seed[c % 2].astype(F32)
        if c + 2 < ROW_CHUNKS:
            row_load(c + 2, seed_hbm, seed, s_sem).start()
        normed = down * inv
        gain_total = gain_total + column_sum(seed_rows * normed)
        scaled = seed_rows * mlp_gain[...]
        dot = jnp.sum(scaled * down, axis=1, keepdims=True)
        grad = inv * scaled - down * (inv * inv * inv * dot / down.shape[1])
        hidden_copy(c).wait_send()
        xr2[c] = grad
        grad_copy(c).start()
        xr[c] = xr[c] + normed * mlp_gain[...]
        if c == 0:
            for copy in turned_copies(hlt_buf, hlt_out, h_sem, last):
                copy.wait()
        if c >= 1:
            for copy in turned_copies(hlt_buf, gdrt_out, d_sem.at[0], c - 1):
                copy.wait()
            for copy in side_copies(low_buf, gdr_out, d_sem.at[1], c - 1):
                copy.wait()
        low_buf[0:chunk, :] = grad.astype(BF16)
        hlt_buf[:, 0:chunk] = grad.astype(BF16).T
        grad_copy(c).wait_recv()
        out_copy(c).start()
        low_buf[chunk : 2 * chunk, :] = ag[c % 2].astype(BF16)
        hlt_buf[:, chunk : 2 * chunk] = ag[c % 2].astype(BF16).T
        for copy in turned_copies(hlt_buf, gdrt_out, d_sem.at[0], c):
            copy.start()
        for copy in side_copies(low_buf, gdr_out, d_sem.at[1], c):
            copy.start()
        return gain_total

    def out_copies(c):
        return [
            pltpu.make_async_copy(
                out_buf.at[pl.ds(s * chunk, chunk)],
                out_out.at[pl.ds(pl.multiple_of(at * half + c * chunk, chunk), chunk)], o_sem.at[s])
            for s, at in ((0, core), (1, 1 - core))
        ]

    def place(c):
        if c >= 1:
            for copy in out_copies(c - 1):
                copy.wait()
        out_buf[0:chunk, :] = xr[c].astype(BF16)
        out_copy(c).wait_recv()
        out_buf[chunk : 2 * chunk, :] = crecv[c].astype(BF16)
        for copy in out_copies(c):
            copy.start()

    for c in range(ROW_CHUNKS):
        feed(c)
    gain_total = jnp.zeros(mlp_gain.shape, F32)
    for c in range(ROW_CHUNKS):
        gain_total = finish(c, gain_total)
        if c >= 1:
            place(c - 1)
    place(last)
    gain_out[...] = gain_total
    for buf, dst, i in ((gate_buf, gate_out, 0), (up_buf, up_out, 1), (inner_buf, inner_out, 2)):
        for copy in side_copies(buf, dst, g_sem.at[i], last):
            copy.wait()
    for copy in turned_copies(hlt_buf, gdrt_out, d_sem.at[0], last):
        copy.wait()
    for copy in side_copies(low_buf, gdr_out, d_sem.at[1], last):
        copy.wait()
    for copy in out_copies(last):
        copy.wait()
    core2_copy(last - 1).wait_send()
    core2_copy(last).wait_send()
    for c in range(ROW_CHUNKS):
        grad_copy(c).wait_send()
        out_copy(c).wait_send()


def forward_layer(mixed, w_out, attn_gain, mlp_gain, tok, seed, w_gate, w_up, w_down):
    row_count, width = mixed.shape[0], w_out.shape[1]
    hidden = w_gate.shape[1]
    chunk = row_count // 2 // ROW_CHUNKS
    DMA = pltpu.SemaphoreType.DMA
    vmem, any_space = pl.BlockSpec(memory_space=pltpu.VMEM), pl.BlockSpec(memory_space=pl.ANY)

    def shape(*dims, kind=F32):
        return jax.ShapeDtypeStruct(dims, kind)

    per_chunk = DMA((ROW_CHUNKS,))
    return pl.pallas_call(
        forward_kernel,
        out_shape=(
            shape(row_count, hidden),
            shape(row_count, hidden),
            shape(row_count, hidden, kind=BF16),
            shape(width, row_count, kind=BF16),
            shape(row_count, width, kind=BF16),
            shape(width, row_count, kind=BF16),
            shape(row_count // 2, width),
            shape(row_count, width, kind=BF16),
            shape(1, width),
        ),
        in_specs=[vmem] * 4 + [any_space] * 5,
        out_specs=(any_space,) * 8 + (vmem,),
        scratch_shapes=[
            pltpu.VMEM(w_gate.shape, BF16),
            pltpu.VMEM(w_up.shape, BF16),
            pltpu.VMEM(w_down.shape, BF16),
            pltpu.VMEM((2, chunk, width), F32),
            pltpu.VMEM((ROW_CHUNKS, chunk, width), F32),
            pltpu.VMEM((ROW_CHUNKS, chunk, width), F32),
            pltpu.VMEM((ROW_CHUNKS, chunk, width), F32),
            pltpu.VMEM((ROW_CHUNKS, chunk, width), F32),
            pltpu.VMEM((2, chunk, width), F32),
            pltpu.VMEM((2 * chunk, hidden), F32),
            pltpu.VMEM((2 * chunk, hidden), F32),
            pltpu.VMEM((2 * chunk, hidden), BF16),
            pltpu.VMEM((2 * chunk, width), BF16),
            pltpu.VMEM((width, 2 * chunk), BF16),
            pltpu.VMEM((2 * chunk, width), BF16),
            pltpu.VMEM((2, chunk, width), BF16),
            pltpu.VMEM((2, chunk, width), BF16),
            DMA((3,)),
            DMA((2,)),
            DMA((2,)),
        ]
        + [per_chunk] * 14
        + [DMA((3, 2)), DMA((2,)), DMA, DMA((2, 2)), DMA((2,))],
        compiler_params=pltpu.CompilerParams(
            collective_id=1, has_side_effects=True, vmem_limit_bytes=VMEM_LIMIT),
    )(mixed, w_out, attn_gain, mlp_gain, tok, seed, w_gate, w_up, w_down)


def backward_kernel(
    dp_size, counts,
    gdrt_hbm, hlt_hbm, tok_hbm, inner_hbm, mixed_hbm, gdr_hbm, gate_hbm, up_hbm, branch_hbm, seed_hbm,
    query_hbm, key_hbm, value_hbm, query_raw_hbm, key_raw_hbm,
    w_out_hbm, wg_hbm, wu_hbm, wd_hbm, wq_hbm, wk_hbm, wv_hbm,
    query_inv, key_inv, log_totals, seg_col, seg_row, live_col, cosine, sine,
    query_gain, key_gain, attn_gain, gain_mlp_part,
    turned_out, straight_out, token_out, gains_out,
    ggr_hbm, gur_hbm, gbt_hbm, gh_hbm, gqkv_hbm,
    at, bbuf, ysend, yrecv, zsend, zrecv, stage, stage_t, cs, crecv, xs, xr, ag, dots, dots_in,
    vec, vec_in,
    at_sem, b_sem, ys_sem, yr_sem, zs_sem, zr_sem, out_sem,
    cs_sem, cr_sem, xs_sem, xr_sem, as_sem, ar_sem, cs2_sem, cr2_sem, xs2_sem, xr2_sem, as2_sem,
    ar2_sem, ds_sem, dr_sem, vs_sem, vr_sem, w_sem,
    y_credit, up_credit, down_credit,
):
    n_down, n_hidden, n_heads, n_out = counts
    first_heads = n_down + n_hidden
    first_out = first_heads + n_heads
    total = first_out + n_out
    line = dp_size // 2
    width = at.shape[1]
    block = width // dp_size
    chunk = xs.shape[1]
    half = chunk * ROW_CHUNKS
    full = 2 * half
    head_cols = query_hbm.shape[1]
    passes = total + total // SPAN
    dp_at = lax.axis_index("dp")
    z, y = dp_at // 2, dp_at % 2
    partner = dp_at + 1 - 2 * y
    below, above = dp_at - 2, dp_at + 2
    has_below, has_above = z > 0, z < line - 1
    core, sibling, across = tensor_peers()
    steps = [1 << s for s in range(dp_size.bit_length() - 1)]
    vec_peers = [dp_at + bit * (1 - 2 * ((dp_at // bit) % 2)) for bit in steps]

    def at_dp(i):
        return {"dp": i}

    def at_tensor(i):
        return {"tensor": i}

    barrier = pltpu.get_barrier_semaphore()

    def greet_one(peer):
        pl.semaphore_signal(barrier, inc=1, device_id=peer, device_id_type=MESH)

    other_z = z - 1 + 2 * lax.rem(z, 2)
    has_other = (other_z >= 0) & (other_z < line)
    for peer in vec_peers:
        greet_one(at_dp(peer))
    greet_one(at_tensor(sibling))
    greet_one(at_tensor(across))

    @pl.when(has_other)
    def _():
        greet_one(at_dp(2 * other_z + y))
    pl.semaphore_wait(barrier, len(steps) + 2 + has_other.astype(jnp.int32))

    def remote(src, dst, send_sem, recv_sem, peer):
        return pltpu.make_async_remote_copy(
            src_ref=src, dst_ref=dst, send_sem=send_sem, recv_sem=recv_sem,
            device_id=peer, device_id_type=MESH)

    def y_copy(p, b):
        return remote(ysend.at[p, b], yrecv.at[p, b], ys_sem.at[p, b], yr_sem.at[p, b], at_dp(partner))

    def z_copy(p, b, slot, target):
        return remote(zsend.at[p, b], zrecv.at[p, slot], zs_sem.at[p, b], zr_sem.at[p, slot], at_dp(target))

    def group_of(k):
        return (
            (k >= n_down).astype(jnp.int32)
            + (k >= first_heads).astype(jnp.int32)
            + (k >= first_out).astype(jnp.int32))

    def product(k, rows_at):
        return jnp.dot(
            at[lax.rem(group_of(k), 2), pl.ds(pl.multiple_of(rows_at * block, block), block), :],
            bbuf[lax.rem(k, B_SLOTS)], preferred_element_type=F32)

    def at_load(i):
        src = (gdrt_hbm, hlt_hbm, None, gbt_hbm)[i]
        return pltpu.make_async_copy(src, at.at[i % 2], at_sem.at[i % 2])

    def b_load(k, act):
        def columns(src, at_chunk):
            act(pltpu.make_async_copy(
                src.at[:, pl.ds(pl.multiple_of(at_chunk * COLS, COLS), COLS)],
                bbuf.at[lax.rem(k, B_SLOTS)], b_sem.at[lax.rem(k, B_SLOTS)]))
        per = n_hidden // 2

        @pl.when(k < n_down)
        def _():
            columns(inner_hbm, k)

        @pl.when((k >= n_down) & (k < n_down + per))
        def _():
            columns(ggr_hbm, k - n_down)

        @pl.when((k >= n_down + per) & (k < first_heads))
        def _():
            columns(gur_hbm, k - n_down - per)

        @pl.when((k >= first_heads) & (k < first_out))
        def _():
            columns(gqkv_hbm, k - first_heads)

        @pl.when((k >= first_out) & (k < total))
        def _():
            columns(mixed_hbm, k - first_out)

    def line_first(k):
        return lax.rem(k, SPAN) == SPAN - 1

    def walk(fn):
        def body(i, carry):
            @pl.when(z <= i)
            def _():
                fn(z + line - 1 - i, True)

            @pl.when(z >= line - 1 - i)
            def _():
                fn(z - (line - 1 - i), False)
            return carry
        lax.fori_loop(0, line - 1, body, 0)

    def pair_send(k):
        p = lax.rem(k, Y_SLOTS)

        @pl.when(k >= Y_SLOTS)
        def _():
            pl.semaphore_wait(y_credit, 1)
        b_load(k, lambda copy: copy.wait())

        @pl.when(jnp.logical_not(line_first(k)))
        def _():
            def one(b, up=None):
                ysend[p, b] = product(k, 2 * b + 1 - y)
                y_copy(p, b).start()
            walk(one)
            one(z)

    def line_send(q, k, source):
        p = lax.rem(q, 2)

        @pl.when(q >= 2)
        def _():
            @pl.when(has_above)
            def _():
                pl.semaphore_wait(up_credit, 1)

            @pl.when(has_below)
            def _():
                pl.semaphore_wait(down_credit, 1)

        def one(b, up):
            has_before, target = (has_below, above) if up else (has_above, below)
            zsend[p, b] = source(b)

            @pl.when(has_before)
            def _():
                z_copy(p, b, b, target).wait_recv()
                zsend[p, b] += zrecv[p, b]
            if up:
                z_copy(p, b, b, target).start()
            else:
                @pl.when(b == z - 1)
                def _():
                    z_copy(p, b, line, target).start()

                @pl.when(b != z - 1)
                def _():
                    z_copy(p, b, b, target).start()
        walk(one)

    def line_own(q, dst):
        p = lax.rem(q, 2)

        @pl.when(has_below)
        def _():
            z_copy(p, z, z, below).wait_recv()
            dst[...] += zrecv[p, z]

        @pl.when(has_above)
        def _():
            z_copy(p, z, line, below).wait_recv()
            dst[...] += zrecv[p, line]

        def drain(b, up):
            z_copy(p, b, b, below).wait_send()
        walk(drain)

        @pl.when(q < passes - 2)
        def _():
            @pl.when(has_below)
            def _():
                pl.semaphore_signal(up_credit, inc=1, device_id=at_dp(below), device_id_type=MESH)

            @pl.when(has_above)
            def _():
                pl.semaphore_signal(down_credit, inc=1, device_id=at_dp(above), device_id_type=MESH)

    def is_turned(k):
        return (k < n_down) | (k >= first_out)

    def out_act(k, act):
        @pl.when(is_turned(k))
        def _():
            first = jnp.where(k < n_down, k, k - first_out + n_down) * COLS
            act(pltpu.make_async_copy(
                stage_t, turned_out.at[pl.ds(pl.multiple_of(first, COLS), COLS)], out_sem))

        @pl.when(jnp.logical_not(is_turned(k)))
        def _():
            cols = pl.ds(pl.multiple_of((k - n_down) * COLS, COLS), COLS)
            act(pltpu.make_async_copy(stage, straight_out.at[:, cols], out_sem))

    def finish_chunk(k, q):
        p = lax.rem(k, Y_SLOTS)

        @pl.when(k >= 1)
        def _():
            out_act(k - 1, lambda copy: copy.wait())
        stage[...] = product(k, 2 * z + y)
        y_copy(p, z).wait_recv()
        stage[...] += yrecv[p, z]
        line_own(q, stage)

        @pl.when(is_turned(k))
        def _():
            stage_t[...] = stage[...].T
        out_act(k, lambda copy: copy.start())

        @pl.when(line_first(k))
        def _():
            y_copy(p, z).wait_send()

        @pl.when(jnp.logical_not(line_first(k)))
        def _():
            for b in range(line):
                y_copy(p, b).wait_send()

        @pl.when(k < total - Y_SLOTS)
        def _():
            pl.semaphore_signal(y_credit, inc=1, device_id=at_dp(partner), device_id_type=MESH)

    def tick(k):
        p = lax.rem(k, Y_SLOTS)
        q = k + k // SPAN
        is_line_first = line_first(k)

        @pl.when(jnp.logical_not(is_line_first))
        def _():
            def mine(b):
                part = product(k, 2 * b + y)
                y_copy(p, b).wait_recv()
                return part + yrecv[p, b]
            line_send(q, k, mine)

        @pl.when(is_line_first)
        def _():
            line_send(q, k, lambda b: product(k, 2 * b + 1 - y))

        @pl.when(k >= 1)
        def _():
            finish_chunk(k - 1, q - 1)

        @pl.when(is_line_first)
        def _():
            line_send(q + 1, k, lambda b: product(k, 2 * b + y))
            ysend[p, z] = product(k, 2 * z + 1 - y)
            line_own(q, ysend.at[p, z])
            y_copy(p, z).start()

        @pl.when(k + 2 < total)
        def _():
            pair_send(k + 2)

        @pl.when(k + 3 < total)
        def _():
            b_load(k + 3, lambda copy: copy.start())

    def fetch(*pairs):
        copies = [pltpu.make_async_copy(src, dst, w_sem.at[i]) for i, (src, dst) in enumerate(pairs)]
        for copy in copies:
            copy.start()
        for copy in copies:
            copy.wait()

    def side(hbm, s, c):
        return hbm.at[pl.ds(s * half + c * chunk, chunk)]

    def core_copy(c, again):
        ss, rs = (cs2_sem, cr2_sem) if again else (cs_sem, cr_sem)
        return remote(cs.at[c % 2], crecv.at[c], ss.at[c], rs.at[c], at_tensor(sibling))

    def x_copy(c, again):
        ss, rs = (xs2_sem, xr2_sem) if again else (xs_sem, xr_sem)
        return remote(xs.at[c], xr.at[c], ss.at[c], rs.at[c], at_tensor(across))

    def to_sibling(c, again):
        ss, rs = (as2_sem, ar2_sem) if again else (as_sem, ar_sem)
        return remote(xr.at[c], ag.at[c % 2], ss.at[c], rs.at[c], at_tensor(sibling))

    def send_partial(c, again):
        core_copy(c, again).start()
        core_copy(c, again).wait_recv()
        xs[c] += crecv[c]
        x_copy(c, again).start()
        core_copy(c, again).wait_send()

    def feed_back():
        def scoped(wd, grads, gates, ups, ggr, gur):
            fetch((wd_hbm, wd))
            for c in range(2 * ROW_CHUNKS):
                rows = pl.ds(c * chunk, chunk)
                fetch((gdr_hbm.at[rows], grads), (gate_hbm.at[rows], gates), (up_hbm.at[rows], ups))

                def tile(n, carry):
                    cols = pl.ds(pl.multiple_of(n * TILE, TILE), 512)
                    grad = lax.dot_general(
                        grads[...], wd[cols, :], (((1,), (1,)), ((), ())), preferred_element_type=F32)
                    gate, up = gates[:, cols], ups[:, cols]
                    sig = jax.nn.sigmoid(gate)
                    ggr[:, cols] = (grad * up * sig * (1.0 + gate * (1.0 - sig))).astype(BF16)
                    gur[:, cols] = (grad * gate * sig).astype(BF16)
                    return carry
                lax.fori_loop(0, wd.shape[0] // TILE, tile, 0)
                fetch((ggr, ggr_hbm.at[rows]), (gur, gur_hbm.at[rows]))
        hidden = wd_hbm.shape[0]
        pl.run_scoped(
            scoped, pltpu.VMEM(wd_hbm.shape, BF16), pltpu.VMEM((chunk, width), BF16),
            pltpu.VMEM((chunk, hidden), F32), pltpu.VMEM((chunk, hidden), F32),
            pltpu.VMEM((chunk, hidden), BF16), pltpu.VMEM((chunk, hidden), BF16))

    def hidden_partial():
        def scoped(wg, wu, ggr, gur):
            fetch((wg_hbm, wg), (wu_hbm, wu))
            for c in range(ROW_CHUNKS):
                for s in range(2):
                    fetch((side(ggr_hbm, s, c), ggr), (side(gur_hbm, s, c), gur))

                    def tile(n, carry):
                        rows = pl.ds(pl.multiple_of(n * TILE, TILE), 512)
                        part = lax.dot_general(
                            ggr[...], wg[rows, :], (((1,), (1,)), ((), ())), preferred_element_type=F32)
                        part = part + lax.dot_general(
                            gur[...], wu[rows, :], (((1,), (1,)), ((), ())), preferred_element_type=F32)
                        if s == 0:
                            xs[c, :, rows] = part
                        else:
                            cs[c % 2, :, rows] = part
                        return carry
                    lax.fori_loop(0, width // TILE, tile, 0)
                send_partial(c, False)
        hidden = wg_hbm.shape[1]
        pl.run_scoped(
            scoped, pltpu.VMEM(wg_hbm.shape, BF16), pltpu.VMEM(wu_hbm.shape, BF16),
            pltpu.VMEM((chunk, hidden), BF16), pltpu.VMEM((chunk, hidden), BF16))

    def branch_back(c):
        def scoped(branch, seed, low, turned):
            rows = pl.ds(c * chunk, chunk)
            fetch((branch_hbm.at[rows], branch), (seed_hbm.at[rows], seed))
            x_copy(c, False).wait()
            grad_hidden = xs[c] + xr[c] + seed[...].astype(F32)
            xs[c] = grad_hidden
            values = branch[...]
            inv = mean_inverse(values)
            vec[1:2, :] += column_sum(grad_hidden * values * inv)
            scaled = grad_hidden * attn_gain[...]
            dot = jnp.sum(scaled * values, axis=1, keepdims=True)
            grad = inv * scaled - values * (inv * inv * inv * dot / width)
            xr[c] = grad
            to_sibling(c, False).start()
            low[0:chunk, :] = grad.astype(BF16)
            turned[:, 0:chunk] = grad.astype(BF16).T
            fetch((xs.at[c], gh_hbm.at[rows]))
            to_sibling(c, False).wait_recv()
            low[chunk : 2 * chunk, :] = ag[c % 2].astype(BF16)
            turned[:, chunk : 2 * chunk] = ag[c % 2].astype(BF16).T
            fetch(
                (turned.at[:, pl.ds(0, chunk)], gbt_hbm.at[:, rows]),
                (turned.at[:, pl.ds(chunk, chunk)], gbt_hbm.at[:, pl.ds(half + c * chunk, chunk)]),
                (low.at[pl.ds(0, chunk)], gb_at(0, c)),
                (low.at[pl.ds(chunk, chunk)], gb_at(1, c)))
            to_sibling(c, False).wait_send()

        def gb_at(s, c):
            first = jnp.where(core == s, 0, half) + c * chunk
            return token_out.at[pl.ds(pl.multiple_of(first, chunk), chunk)]
        pl.run_scoped(
            scoped, pltpu.VMEM((chunk, width), F32), pltpu.VMEM((chunk, width), BF16),
            pltpu.VMEM((2 * chunk, width), BF16), pltpu.VMEM((width, 2 * chunk), BF16))

    def attention_back():
        heads = head_cols // HEAD
        q_rows = min(256, full)
        scale = HEAD ** (-0.5)

        def scoped(query, key, value, mixed_grad, dq, dk, dv, raw):
            def products(w_out, rows_buf):
                fetch((w_out_hbm, w_out), (query_hbm, query), (key_hbm, key), (value_hbm, value))
                for c in range(full // q_rows):
                    rows = pl.ds(c * q_rows, q_rows)
                    fetch((token_out.at[rows], rows_buf))
                    mixed_grad[rows, :] = lax.dot_general(
                        rows_buf[...], w_out[...], (((1,), (1,)), ((), ())),
                        preferred_element_type=F32).astype(BF16)
            pl.run_scoped(
                products, pltpu.VMEM(w_out_hbm.shape, BF16), pltpu.VMEM((q_rows, width), BF16))

            def head(h, carry):
                cols = pl.ds(pl.multiple_of(h * HEAD, HEAD), HEAD)
                dk[:, cols] = jnp.zeros((full, HEAD), F32)
                dv[...] = jnp.zeros((full, HEAD), F32)
                for i in range(full // q_rows):
                    rows, keys = slice(i * q_rows, (i + 1) * q_rows), (i + 1) * q_rows
                    q_block, grad_block = query[rows, cols], mixed_grad[rows, cols]
                    key_block, value_block = key[0:keys, cols], value[0:keys, cols]
                    nt = (((1,), (1,)), ((), ()))
                    scores = lax.dot_general(key_block, q_block, nt, preferred_element_type=F32) * scale
                    key_at = lax.broadcasted_iota(jnp.int32, (keys, q_rows), 0)
                    query_at = lax.broadcasted_iota(jnp.int32, (keys, q_rows), 1) + i * q_rows
                    allowed = (
                        (seg_col[0:keys, :] == seg_row[:, rows])
                        & (key_at <= query_at)
                        & ((live_col[0:keys, :] > 0) | (key_at == query_at)))
                    scores = jnp.where(allowed, scores, NEG_FILL)
                    prob = jnp.exp(scores - log_totals[pl.ds(h, 1), rows])
                    grad_prob = lax.dot_general(value_block, grad_block, nt, preferred_element_type=F32)
                    row_dot = jnp.sum(prob * grad_prob, axis=0, keepdims=True)
                    grad_scores = (prob * (grad_prob - row_dot)).astype(BF16)
                    dq[rows, cols] = lax.dot_general(
                        grad_scores, key_block, (((0,), (0,)), ((), ())), preferred_element_type=F32) * scale
                    dk[0:keys, cols] += jnp.dot(grad_scores, q_block, preferred_element_type=F32) * scale
                    dv[0:keys, :] += jnp.dot(prob.astype(BF16), grad_block, preferred_element_type=F32)
                mixed_grad[:, cols] = dv[...].astype(BF16)
                return carry
            lax.fori_loop(0, heads, head, 0)
            fetch((mixed_grad, gqkv_hbm.at[:, pl.ds(2 * head_cols, head_cols)]))

            lanes = lax.broadcasted_iota(jnp.int32, (q_rows, HEAD), 1)
            vec[2:3, :] = jnp.zeros((1, width), F32)
            for which, (grads, raw_hbm, inv, gain) in enumerate((
                (dq, query_raw_hbm, query_inv, query_gain), (dk, key_raw_hbm, key_inv, key_gain))):
                fetch((raw_hbm, raw))

                def back(i, carry):
                    rows = pl.ds(pl.multiple_of(i * q_rows, q_rows), q_rows)
                    dot = jnp.zeros((q_rows, 1), F32)
                    for h in range(heads):
                        cols = slice(h * HEAD, (h + 1) * HEAD)
                        grad = grads[rows, cols]
                        grad = grad * cosine[rows, :] + pltpu.roll(grad, HEAD // 2, 1) * sine[rows, :]
                        raw_rows = raw[rows, cols]
                        gain_cols = slice(which * head_cols + h * HEAD, which * head_cols + (h + 1) * HEAD)
                        vec[2:3, gain_cols] += column_sum(grad * raw_rows * inv[rows, :])
                        scaled = grad * gain[:, cols]
                        grads[rows, cols] = scaled
                        dot = dot + jnp.sum(scaled * raw_rows, axis=1, keepdims=True)
                    if which == 0:
                        dots[rows, :] = jnp.broadcast_to(dot, (q_rows, HEAD))
                    else:
                        dots[rows, :] = jnp.where(lanes == 0, dots[rows, :], dot)
                    return carry
                lax.fori_loop(0, full // q_rows, back, 0)
            for i, peer in enumerate((sibling, across)):
                copy = remote(dots, dots_in.at[i], ds_sem.at[i], dr_sem.at[i], at_tensor(peer))
                copy.start()
                copy.wait()
                dots[...] += dots_in[i]
            for which, (grads, raw_hbm, inv) in enumerate((
                (dq, query_raw_hbm, query_inv), (dk, key_raw_hbm, key_inv))):
                fetch((raw_hbm, raw))
                for i in range(full // q_rows):
                    rows = slice(i * q_rows, (i + 1) * q_rows)
                    inv_rows = inv[rows, :]
                    dot = dots[rows, which : which + 1]
                    mixed_grad[rows, :] = (
                        inv_rows * grads[rows, :]
                        - raw[rows, :] * (inv_rows * inv_rows * inv_rows * dot / width)
                    ).astype(BF16)
                fetch((mixed_grad, gqkv_hbm.at[:, pl.ds(which * head_cols, head_cols)]))
        rows_of = (full, head_cols)
        pl.run_scoped(
            scoped, pltpu.VMEM(rows_of, BF16), pltpu.VMEM(rows_of, BF16), pltpu.VMEM(rows_of, BF16),
            pltpu.VMEM(rows_of, BF16), pltpu.VMEM(rows_of, F32), pltpu.VMEM(rows_of, F32),
            pltpu.VMEM((full, HEAD), F32), pltpu.VMEM(rows_of, F32))

    def gains_sum():
        copy = remote(vec, vec_in.at[0], vs_sem.at[0], vr_sem.at[0], at_tensor(sibling))
        copy.start()
        copy.wait()
        vec[0:2, :] += vec_in[0, 0:2, :]
        for i, peer in enumerate(vec_peers):
            copy = remote(vec, vec_in.at[i + 1], vs_sem.at[i + 1], vr_sem.at[i + 1], at_dp(peer))
            copy.start()
            copy.wait()
            vec[...] += vec_in[i + 1]

    def turn_tokens():
        def scoped(rows_buf):
            for i in range(full // 256):
                rows = pl.ds(i * 256, 256)
                fetch((tok_hbm.at[rows], rows_buf))
                at[0, :, rows] = rows_buf[...].T
        pl.run_scoped(scoped, pltpu.VMEM((256, width), BF16))

    def input_partial():
        def scoped(weights, grads):
            fetch(*[(w, weights.at[i]) for i, w in enumerate((wq_hbm, wk_hbm, wv_hbm))], (gqkv_hbm, grads))
            for c in range(ROW_CHUNKS):
                for s in range(2):
                    first = jnp.where(core == s, 0, half) + c * chunk
                    rows = pl.ds(pl.multiple_of(first, chunk), chunk)

                    def tile(n, carry):
                        cols = pl.ds(pl.multiple_of(n * TILE, TILE), 512)
                        part = jnp.zeros((chunk, TILE), F32)
                        for i in range(3):
                            part = part + lax.dot_general(
                                grads[rows, i * head_cols : (i + 1) * head_cols], weights[i, cols, :],
                                (((1,), (1,)), ((), ())), preferred_element_type=F32)
                        if s == 0:
                            xs[c, :, cols] = part
                        else:
                            cs[c % 2, :, cols] = part
                        return carry
                    lax.fori_loop(0, width // TILE, tile, 0)
                send_partial(c, True)
        pl.run_scoped(
            scoped, pltpu.VMEM((3,) + wq_hbm.shape, BF16), pltpu.VMEM((full, 3 * head_cols), BF16))

    def token_grads(c):
        def scoped(grad_hidden, low):
            fetch((gh_hbm.at[pl.ds(c * chunk, chunk)], grad_hidden))
            x_copy(c, True).wait()
            total_rows = xs[c] + xr[c] + grad_hidden[...]
            xr[c] = total_rows
            to_sibling(c, True).start()
            low[0] = total_rows.astype(BF16)
            to_sibling(c, True).wait_recv()
            low[1] = ag[c % 2].astype(BF16)
            copies = []
            for s in range(2):
                first = jnp.where(core == s, 0, half) + c * chunk
                copies.append((low.at[s], token_out.at[pl.ds(pl.multiple_of(first, chunk), chunk)]))
            fetch(*copies)
            to_sibling(c, True).wait_send()
        pl.run_scoped(scoped, pltpu.VMEM((chunk, width), F32), pltpu.VMEM((2, chunk, width), BF16))

    vec[...] = jnp.zeros(vec.shape, F32)
    vec[0:1, :] = gain_mlp_part[...]
    at_load(0).start()
    at_load(1).start()
    for k in range(3):
        b_load(jnp.int32(k), lambda copy: copy.start())
    at_load(0).wait()
    pair_send(jnp.int32(0))
    pair_send(jnp.int32(1))
    feed_back()
    at_load(1).wait()

    work = {0: hidden_partial, 8: attention_back, 9: turn_tokens, 10: input_partial, 11: gains_sum}
    for c in range(ROW_CHUNKS):
        work[3 + c] = functools.partial(branch_back, c)
        work[13 + c] = functools.partial(token_grads, c)

    def body(k, carry):
        tick(k)
        for when, fn in work.items():
            @pl.when(k == when)
            def _(fn=fn):
                fn()

        @pl.when(k == first_heads + 1)
        def _():
            at_load(3).start()

        @pl.when(k == first_heads + 2)
        def _():
            at_load(3).wait()
        return carry
    lax.fori_loop(0, total, body, 0)
    finish_chunk(jnp.int32(total - 1), jnp.int32(passes - 1))
    out_act(jnp.int32(total - 1), lambda copy: copy.wait())
    gains_out[...] = vec[...]


def backward_layer(dp_size, hbm, vmem_args):
    names = dict(zip(HBM_NAMES, hbm, strict=True))
    width, row_count = names["gdrt"].shape
    hidden, head_cols = names["inner"].shape[1], names["query"].shape[1]
    line, block = dp_size // 2, width // dp_size
    chunk = row_count // 2 // ROW_CHUNKS
    counts = (hidden // COLS, 2 * hidden // COLS, 3 * head_cols // COLS, head_cols // COLS)
    DMA, REG = pltpu.SemaphoreType.DMA, pltpu.SemaphoreType.REGULAR
    vmem, any_space = pl.BlockSpec(memory_space=pltpu.VMEM), pl.BlockSpec(memory_space=pl.ANY)

    def shape(*dims, kind=F32):
        return jax.ShapeDtypeStruct(dims, kind)

    slot = (block, COLS)
    per_chunk = DMA((ROW_CHUNKS,))
    steps = dp_size.bit_length() - 1
    results = pl.pallas_call(
        functools.partial(backward_kernel, dp_size, counts),
        out_shape=(
            shape((counts[0] + counts[3]) * COLS, block),
            shape(block, (counts[1] + counts[2]) * COLS),
            shape(row_count, width, kind=BF16),
            shape(8, width),
            shape(row_count, hidden, kind=BF16),
            shape(row_count, hidden, kind=BF16),
            shape(width, row_count, kind=BF16),
            shape(row_count // 2, width),
            shape(row_count, 3 * head_cols, kind=BF16),
        ),
        in_specs=[any_space] * len(hbm) + [vmem] * len(vmem_args),
        out_specs=(any_space,) * 3 + (vmem,) + (any_space,) * 5,
        scratch_shapes=[
            pltpu.VMEM((2, width, row_count), BF16),
            pltpu.VMEM((B_SLOTS, row_count, COLS), BF16),
            pltpu.VMEM((Y_SLOTS, line) + slot, F32),
            pltpu.VMEM((Y_SLOTS, line) + slot, F32),
            pltpu.VMEM((2, line) + slot, F32),
            pltpu.VMEM((2, line + 1) + slot, F32),
            pltpu.VMEM(slot, F32),
            pltpu.VMEM((COLS, block), F32),
            pltpu.VMEM((2, chunk, width), F32),
            pltpu.VMEM((ROW_CHUNKS, chunk, width), F32),
            pltpu.VMEM((ROW_CHUNKS, chunk, width), F32),
            pltpu.VMEM((ROW_CHUNKS, chunk, width), F32),
            pltpu.VMEM((2, chunk, width), F32),
            pltpu.VMEM((row_count, HEAD), F32),
            pltpu.VMEM((2, row_count, HEAD), F32),
            pltpu.VMEM((8, width), F32),
            pltpu.VMEM((steps + 1, 8, width), F32),
            DMA((2,)),
            DMA((B_SLOTS,)),
            DMA((Y_SLOTS, line)),
            DMA((Y_SLOTS, line)),
            DMA((2, line)),
            DMA((2, line + 1)),
            DMA,
        ]
        + [per_chunk] * 12
        + [DMA((2,)), DMA((2,)), DMA((steps + 1,)), DMA((steps + 1,)), DMA((4,)), REG, REG, REG],
        compiler_params=pltpu.CompilerParams(
            collective_id=2, has_side_effects=True, vmem_limit_bytes=VMEM_LIMIT),
    )(*hbm, *vmem_args)
    return results[:4]


def times(left, right):
    return jnp.dot(left, right, preferred_element_type=F32)


def rope_tables():
    half_size = HEAD // 2
    freq_row = ROPE_BASE ** (-(jnp.arange(half_size, dtype=F32) * 2.0) / HEAD)
    angle = jnp.arange(LENGTH, dtype=F32)[:, None] * freq_row[None, :]
    return (jnp.cos(angle), jnp.sin(angle))


def rotate(values, cosine, sine_part, direction):
    row_count, col_count = values.shape
    half_size = HEAD // 2
    split = values.reshape(row_count // LENGTH, LENGTH, col_count // HEAD, 2, half_size)
    first = split[:, :, :, 0]
    second = split[:, :, :, 1]
    cos_b = cosine[None, :, None, :]
    sin_b = direction * sine_part[None, :, None, :]
    turned = jnp.stack((first * cos_b - second * sin_b, second * cos_b + first * sin_b), axis=3)
    return turned.reshape(row_count, col_count)


def visible_keys(begin_at, block_rows, segment_ids, live_rows):
    seq_length = segment_ids.shape[0]
    key_index = jnp.arange(seq_length)
    query_index = begin_at + jnp.arange(block_rows)
    query_segs = segment_ids[begin_at : begin_at + block_rows]
    same_doc = query_segs[:, None] == segment_ids[None, :]
    causal = key_index[None, :] <= query_index[:, None]
    kept_key = (live_rows[None, :] > 0) | (key_index[None, :] == query_index[:, None])
    return same_doc & causal & kept_key


def block_scores(query_seq, key_heads, begin_at, block_rows, segment_ids, live_rows):
    local_heads = key_heads.shape[1]
    query_heads = query_seq[begin_at : begin_at + block_rows].reshape(block_rows, local_heads, HEAD)
    scores = jnp.einsum(
        "ihd,jhd->hij", query_heads, key_heads, preferred_element_type=F32
    ) * HEAD ** (-0.5)
    allowed = visible_keys(begin_at, block_rows, segment_ids, live_rows)
    return (query_heads, jnp.where(allowed[None], scores, NEG_FILL))


def attend_forward(query_seq, key_seq, value_seq, segment_ids, live_rows):
    seq_length = query_seq.shape[0]
    local_heads = query_seq.shape[1] // HEAD
    block_rows = min(512, seq_length)
    key_heads = key_seq.reshape(seq_length, local_heads, HEAD)
    value_heads = value_seq.reshape(seq_length, local_heads, HEAD)
    mixed_parts = []
    lse_parts = []
    for begin_at in range(0, seq_length, block_rows):
        query_heads, scores = block_scores(
            query_seq, key_heads, begin_at, block_rows, segment_ids, live_rows
        )
        row_max = jnp.max(scores, axis=-1, keepdims=True)
        exp_scores = jnp.exp(scores - row_max)
        row_total = jnp.sum(exp_scores, axis=-1, keepdims=True)
        attn_prob = (exp_scores / row_total).astype(BF16)
        mixed_block = jnp.einsum(
            "hij,jhd->ihd", attn_prob, value_heads, preferred_element_type=F32
        )
        mixed_parts.append(mixed_block.reshape(block_rows, -1).astype(BF16))
        lse_parts.append((row_max + jnp.log(row_total))[..., 0])
    return (jnp.concatenate(mixed_parts, 0), jnp.concatenate(lse_parts, 1))


def make_shards(dp_size, tensor_size):
    core_pairs = [(i, i ^ 1) for i in range(tensor_size)]
    tensor_bits = [1 << b for b in range(1, tensor_size.bit_length() - 1)]

    def to_core(values):
        return lax.ppermute(values, "tensor", core_pairs)

    def wide_sum(values):
        for bit in tensor_bits:
            values = values + lax.ppermute(
                values, "tensor", [(i, i ^ bit) for i in range(tensor_size)]
            )
        return values

    def shards(
        tokens,
        segments,
        pad_mask,
        w_query,
        w_key,
        w_value,
        w_out,
        gain_query,
        gain_key,
        gain_attn,
        w_gate,
        w_up,
        w_down,
        gain_mlp,
        cotangent,
    ):
        row_count, model_width = tokens.shape
        half_rows = row_count // 2
        block = model_width // dp_size
        core_at = lax.axis_index("tensor") % 2
        cosine, sine_part = rope_tables()

        def split_rows(values):
            own = lax.dynamic_slice_in_dim(values, core_at * half_rows, half_rows, 0)
            other = lax.dynamic_slice_in_dim(values, (1 - core_at) * half_rows, half_rows, 0)
            return own, other

        query_raw = times(tokens, w_query)
        key_raw = times(tokens, w_key)
        value_rows = times(tokens, w_value).astype(BF16)
        squares = jnp.stack(
            (jnp.sum(query_raw * query_raw, axis=1), jnp.sum(key_raw * key_raw, axis=1))
        )
        squares = wide_sum(squares + to_core(squares))
        query_inv = lax.rsqrt(squares[0] / model_width + EPSILON)[:, None]
        key_inv = lax.rsqrt(squares[1] / model_width + EPSILON)[:, None]
        query_gain = gain_query.reshape(-1).astype(F32)
        key_gain = gain_key.reshape(-1).astype(F32)
        query_norm = rotate(query_raw * query_inv * query_gain, cosine, sine_part, 1.0).astype(BF16)
        key_norm = rotate(key_raw * key_inv * key_gain, cosine, sine_part, 1.0).astype(BF16)
        mixed, log_totals = attend_forward(query_norm, key_norm, value_rows, segments, pad_mask)
        mixed_own, mixed_other = split_rows(mixed)
        mixed_rows = jnp.concatenate((mixed_own, mixed_other), 0)
        tokens_own, tokens_other = split_rows(tokens)
        cot_own, _ = split_rows(cotangent)
        live_own, _ = split_rows(pad_mask[:, None])
        attn_gain = gain_attn.astype(F32)
        mlp_gain = gain_mlp.astype(F32)
        seed = jnp.where(live_own > 0, cot_own, jnp.zeros_like(cot_own))

        (
            gate_rows,
            up_rows,
            inner_rows,
            hidden_turned,
            grad_down_rows,
            grad_down_turned,
            branch_rows,
            output,
            gain_mlp_part,
        ) = forward_layer(
            mixed_rows,
            w_out,
            attn_gain[None, :],
            mlp_gain[None, :],
            tokens_own,
            seed,
            w_gate,
            w_up,
            w_down,
        )
        turned, straight, grad_tokens, gains = backward_layer(
            dp_size,
            (
                grad_down_turned, hidden_turned, tokens, inner_rows, mixed_rows, grad_down_rows,
                gate_rows, up_rows, branch_rows, seed,
                query_norm, key_norm, value_rows, query_raw, key_raw,
                w_out, w_gate, w_up, w_down, w_query, w_key, w_value,
            ),
            (
                query_inv, key_inv, log_totals, segments[:, None], segments[None, :],
                pad_mask[:, None], jnp.concatenate((cosine, cosine), 1),
                jnp.concatenate((sine_part, -sine_part), 1),
                query_gain[None, :], key_gain[None, :], attn_gain[None, :], gain_mlp_part,
            ),
        )
        hidden, head_cols = w_gate.shape[1], w_query.shape[1]
        grad_gate, grad_up = straight[:, :hidden], straight[:, hidden : 2 * hidden]
        grad_query, grad_key, grad_value = (
            straight[:, 2 * hidden + i * head_cols : 2 * hidden + (i + 1) * head_cols]
            for i in range(3)
        )
        dp_at = lax.axis_index("dp")
        wide = lax.dynamic_slice_in_dim(gains[:2], dp_at * block, block, 1)
        head_gains = gains[2, : 2 * head_cols].reshape(2 * gain_query.shape[0], HEAD)
        head_gains = lax.dynamic_slice_in_dim(head_gains, dp_at * (HEAD // dp_size), HEAD // dp_size, 1)
        return (
            output,
            grad_tokens,
            grad_query,
            grad_key,
            grad_value,
            turned[hidden:],
            head_gains[: gain_query.shape[0]],
            head_gains[gain_query.shape[0] :],
            wide[1],
            grad_gate,
            grad_up,
            turned[:hidden],
            wide[0],
        )

    return shards


def solution(mesh):
    in_specs = (
        P("dp", None),
        P("dp"),
        P("dp"),
        P(None, "tensor"),
        P(None, "tensor"),
        P(None, "tensor"),
        P("tensor", None),
        P("tensor", None),
        P("tensor", None),
        P(),
        P(None, "tensor"),
        P(None, "tensor"),
        P("tensor", None),
        P(),
        P("dp", None),
    )
    out_specs = (
        P("dp", None),
        P("dp", None),
        P("dp", "tensor"),
        P("dp", "tensor"),
        P("dp", "tensor"),
        P("tensor", "dp"),
        P("tensor", "dp"),
        P("tensor", "dp"),
        P("dp"),
        P("dp", "tensor"),
        P("dp", "tensor"),
        P("tensor", "dp"),
        P("dp"),
    )
    shards = make_shards(mesh.shape["dp"], mesh.shape["tensor"])
    return jax.shard_map(shards, mesh=mesh, in_specs=in_specs, out_specs=out_specs, check_vma=False)
```

```python
import functools

import jax
import jax.numpy as jnp
from jax import lax
from jax.experimental import pallas as pl
from jax.experimental.pallas import tpu as pltpu
from jax.sharding import PartitionSpec as P

HEAD = 128
LENGTH = 1024
EPSILON = 1e-06
NEG_FILL = -1e30
ROPE_BASE = 500000.0
ROW_CHUNKS = 4
F32 = jnp.float32
BF16 = jnp.bfloat16


COLS = 256
SPAN = 6
Y_SLOTS = 3
B_SLOTS = 5
FEED_TICK = 3
HIDDEN_TICK = 7
BRANCH_TICK = 12
INPUT_TICK = 21
TOKEN_TICK = 26
HBM_NAMES = (
    "gdrt", "hlt", "tokens", "inner", "mixed", "gdr", "gate", "up", "branch", "seed",
    "query", "key", "value", "query_raw", "key_raw",
    "w_out", "w_gate", "w_up", "w_down", "w_query", "w_key", "w_value",
)
TILE = 512
VMEM_LIMIT = 63 * 1024 * 1024
MESH = pl.DeviceIdType.MESH

def column_sum(values):
    return jnp.sum(values, axis=0, keepdims=True)


def mean_inverse(values):
    return lax.rsqrt(jnp.mean(values * values, axis=1, keepdims=True) + EPSILON)


def tensor_peers():
    at = lax.axis_index("tensor")
    core = lax.rem(at, 2)
    return core, at + 1 - 2 * core, lax.rem(at + 2, 4)


def greet(*peers):
    barrier = pltpu.get_barrier_semaphore()
    for peer in peers:
        pl.semaphore_signal(barrier, inc=1, device_id=peer, device_id_type=MESH)
    pl.semaphore_wait(barrier, len(peers))


def forward_kernel(
    mixed, w_out, attn_gain, mlp_gain, tok_hbm, seed_hbm, wg_hbm, wu_hbm, wd_hbm,
    gate_out, up_out, inner_out, hlt_out, gdr_out, gdrt_out, branch_out, out_out, gain_out,
    wg, wu, wd, cs, crecv, xs, xr, xr2, ag, gate_buf, up_buf, inner_buf, low_buf, hlt_buf,
    out_buf, tok, seed,
    w_sem, t_sem, s_sem, cs_sem, cr_sem, xs_sem, xr_sem, as_sem, ar_sem, cs2_sem, cr2_sem, xs2_sem, xr2_sem,
    gs_sem, gr_sem, os_sem, or_sem, g_sem, h_sem, b_sem, d_sem, o_sem,
):
    core, sibling, across = tensor_peers()
    chunk = xs.shape[1]
    half = chunk * ROW_CHUNKS
    tiles = wg.shape[1] // TILE
    wide_tiles = wd.shape[1] // TILE
    loads = [
        pltpu.make_async_copy(src, dst, w_sem.at[i])
        for i, (src, dst) in enumerate(((wg_hbm, wg), (wu_hbm, wu), (wd_hbm, wd)))
    ]
    for load in loads:
        load.start()

    def row_load(c, src, dst, sem):
        return pltpu.make_async_copy(
            src.at[pl.ds(c * chunk, chunk)], dst.at[c % 2], sem.at[c % 2])

    for c in range(2):
        row_load(c, tok_hbm, tok, t_sem).start()
        row_load(c, seed_hbm, seed, s_sem).start()
    greet({"tensor": sibling}, {"tensor": across})

    def remote(src, dst, send_sem, recv_sem, peer):
        return pltpu.make_async_remote_copy(
            src_ref=src, dst_ref=dst, send_sem=send_sem, recv_sem=recv_sem,
            device_id={"tensor": peer}, device_id_type=MESH)

    def core_copy(c):
        return remote(cs.at[c % 2], crecv.at[c], cs_sem.at[c], cr_sem.at[c], sibling)

    def x_copy(c):
        return remote(xs.at[c], xr.at[c], xs_sem.at[c], xr_sem.at[c], across)

    def hidden_copy(c):
        return remote(xr.at[c], ag.at[c % 2], as_sem.at[c], ar_sem.at[c], sibling)

    def core2_copy(c):
        return remote(cs.at[c % 2], crecv.at[c], cs2_sem.at[c], cr2_sem.at[c], sibling)

    def x2_copy(c):
        return remote(xs.at[c], xr2.at[c], xs2_sem.at[c], xr2_sem.at[c], across)

    def grad_copy(c):
        return remote(xr2.at[c], ag.at[c % 2], gs_sem.at[c], gr_sem.at[c], sibling)

    def out_copy(c):
        return remote(xr.at[c], crecv.at[c], os_sem.at[c], or_sem.at[c], sibling)

    def rows(first):
        return pl.ds(first, chunk)

    def side_copies(buf, dst, sem, c):
        return [
            pltpu.make_async_copy(
                buf.at[pl.ds(s * chunk, chunk)], dst.at[rows(s * half + c * chunk)], sem.at[s])
            for s in range(2)
        ]

    def turned_copies(buf, dst, sem, c):
        return [
            pltpu.make_async_copy(
                buf.at[:, pl.ds(s * chunk, chunk)], dst.at[:, rows(s * half + c * chunk)], sem.at[s])
            for s in range(2)
        ]

    for c in range(ROW_CHUNKS):
        if c >= 2:
            core_copy(c - 2).wait_send()
        cs[c % 2] = jnp.dot(mixed[rows(half + c * chunk), :], w_out[...], preferred_element_type=F32)
        core_copy(c).start()
        xs[c] = jnp.dot(mixed[rows(c * chunk), :], w_out[...], preferred_element_type=F32)
        if c >= 1:
            core_copy(c - 1).wait_recv()
            xs[c - 1] += crecv[c - 1]
            x_copy(c - 1).start()
    last = ROW_CHUNKS - 1
    core_copy(last).wait_recv()
    xs[last] += crecv[last]
    x_copy(last).start()
    core_copy(last - 1).wait_send()
    core_copy(last).wait_send()

    def feed(c):
        x_copy(c).wait()
        total = xs[c] + xr[c]
        xs[c] = total
        branch_copy = pltpu.make_async_copy(xs.at[c], branch_out.at[rows(c * chunk)], b_sem)
        branch_copy.start()
        row_load(c, tok_hbm, tok, t_sem).wait()
        hidden = tok[c % 2].astype(F32) + total * mean_inverse(total) * attn_gain[...]
        if c + 2 < ROW_CHUNKS:
            row_load(c + 2, tok_hbm, tok, t_sem).start()
        xr[c] = hidden
        hidden_copy(c).start()
        low_buf[0:chunk, :] = hidden.astype(BF16)
        if c >= 1:
            for copy in turned_copies(hlt_buf, hlt_out, h_sem, c - 1):
                copy.wait()
            for buf, dst, i in ((gate_buf, gate_out, 0), (up_buf, up_out, 1), (inner_buf, inner_out, 2)):
                for copy in side_copies(buf, dst, g_sem.at[i], c - 1):
                    copy.wait()
        hlt_buf[:, 0:chunk] = hidden.astype(BF16).T
        hidden_copy(c).wait_recv()
        low_buf[chunk : 2 * chunk, :] = ag[c % 2].astype(BF16)
        hlt_buf[:, chunk : 2 * chunk] = ag[c % 2].astype(BF16).T
        for copy in turned_copies(hlt_buf, hlt_out, h_sem, c):
            copy.start()
        if c == 0:
            loads[0].wait()
            loads[1].wait()

        def tile(n, carry):
            at = pl.ds(pl.multiple_of(n * TILE, TILE), TILE)
            gate = jnp.dot(low_buf[...], wg[:, at], preferred_element_type=F32)
            up = jnp.dot(low_buf[...], wu[:, at], preferred_element_type=F32)
            gate_buf[:, at] = gate
            up_buf[:, at] = up
            inner_buf[:, at] = (gate * jax.nn.sigmoid(gate) * up).astype(BF16)
            return carry
        lax.fori_loop(0, tiles, tile, 0)
        for buf, dst, i in ((gate_buf, gate_out, 0), (up_buf, up_out, 1), (inner_buf, inner_out, 2)):
            for copy in side_copies(buf, dst, g_sem.at[i], c):
                copy.start()
        if c == 0:
            loads[2].wait()
        if c >= 2:
            core2_copy(c - 2).wait_send()
        branch_copy.wait()

        def down_tile(n, carry):
            at = pl.ds(pl.multiple_of(n * TILE, TILE), TILE)
            part = jnp.dot(inner_buf[...], wd[:, at], preferred_element_type=F32)
            xs[c, :, at] = part[0:chunk]
            cs[c % 2, :, at] = part[chunk : 2 * chunk]
            return carry
        lax.fori_loop(0, wide_tiles, down_tile, 0)
        core2_copy(c).start()
        core2_copy(c).wait_recv()
        xs[c] += crecv[c]
        x2_copy(c).start()

    def finish(c, gain_total):
        x2_copy(c).wait()
        down = xs[c] + xr2[c]
        inv = mean_inverse(down)
        row_load(c, seed_hbm, seed, s_sem).wait()
        seed_rows = seed[c % 2].astype(F32)
        if c + 2 < ROW_CHUNKS:
            row_load(c + 2, seed_hbm, seed, s_sem).start()
        normed = down * inv
        gain_total = gain_total + column_sum(seed_rows * normed)
        scaled = seed_rows * mlp_gain[...]
        dot = jnp.sum(scaled * down, axis=1, keepdims=True)
        grad = inv * scaled - down * (inv * inv * inv * dot / down.shape[1])
        hidden_copy(c).wait_send()
        xr2[c] = grad
        grad_copy(c).start()
        xr[c] = xr[c] + normed * mlp_gain[...]
        if c == 0:
            for copy in turned_copies(hlt_buf, hlt_out, h_sem, last):
                copy.wait()
        if c >= 1:
            for copy in turned_copies(hlt_buf, gdrt_out, d_sem.at[0], c - 1):
                copy.wait()
            for copy in side_copies(low_buf, gdr_out, d_sem.at[1], c - 1):
                copy.wait()
        low_buf[0:chunk, :] = grad.astype(BF16)
        hlt_buf[:, 0:chunk] = grad.astype(BF16).T
        grad_copy(c).wait_recv()
        out_copy(c).start()
        low_buf[chunk : 2 * chunk, :] = ag[c % 2].astype(BF16)
        hlt_buf[:, chunk : 2 * chunk] = ag[c % 2].astype(BF16).T
        for copy in turned_copies(hlt_buf, gdrt_out, d_sem.at[0], c):
            copy.start()
        for copy in side_copies(low_buf, gdr_out, d_sem.at[1], c):
            copy.start()
        return gain_total

    def out_copies(c):
        return [
            pltpu.make_async_copy(
                out_buf.at[pl.ds(s * chunk, chunk)],
                out_out.at[pl.ds(pl.multiple_of(at * half + c * chunk, chunk), chunk)], o_sem.at[s])
            for s, at in ((0, core), (1, 1 - core))
        ]

    def place(c):
        if c >= 1:
            for copy in out_copies(c - 1):
                copy.wait()
        out_buf[0:chunk, :] = xr[c].astype(BF16)
        out_copy(c).wait_recv()
        out_buf[chunk : 2 * chunk, :] = crecv[c].astype(BF16)
        for copy in out_copies(c):
            copy.start()

    for c in range(ROW_CHUNKS):
        feed(c)
    gain_total = jnp.zeros(mlp_gain.shape, F32)
    for c in range(ROW_CHUNKS):
        gain_total = finish(c, gain_total)
        if c >= 1:
            place(c - 1)
    place(last)
    gain_out[...] = gain_total
    for buf, dst, i in ((gate_buf, gate_out, 0), (up_buf, up_out, 1), (inner_buf, inner_out, 2)):
        for copy in side_copies(buf, dst, g_sem.at[i], last):
            copy.wait()
    for copy in turned_copies(hlt_buf, gdrt_out, d_sem.at[0], last):
        copy.wait()
    for copy in side_copies(low_buf, gdr_out, d_sem.at[1], last):
        copy.wait()
    for copy in out_copies(last):
        copy.wait()
    core2_copy(last - 1).wait_send()
    core2_copy(last).wait_send()
    for c in range(ROW_CHUNKS):
        grad_copy(c).wait_send()
        out_copy(c).wait_send()


def forward_layer(mixed, w_out, attn_gain, mlp_gain, tok, seed, w_gate, w_up, w_down):
    row_count, width = mixed.shape[0], w_out.shape[1]
    hidden = w_gate.shape[1]
    chunk = row_count // 2 // ROW_CHUNKS
    DMA = pltpu.SemaphoreType.DMA
    vmem, any_space = pl.BlockSpec(memory_space=pltpu.VMEM), pl.BlockSpec(memory_space=pl.ANY)

    def shape(*dims, kind=F32):
        return jax.ShapeDtypeStruct(dims, kind)

    per_chunk = DMA((ROW_CHUNKS,))
    return pl.pallas_call(
        forward_kernel,
        out_shape=(
            shape(row_count, hidden),
            shape(row_count, hidden),
            shape(row_count, hidden, kind=BF16),
            shape(width, row_count, kind=BF16),
            shape(row_count, width, kind=BF16),
            shape(width, row_count, kind=BF16),
            shape(row_count // 2, width),
            shape(row_count, width, kind=BF16),
            shape(1, width),
        ),
        in_specs=[vmem] * 4 + [any_space] * 5,
        out_specs=(any_space,) * 8 + (vmem,),
        scratch_shapes=[
            pltpu.VMEM(w_gate.shape, BF16),
            pltpu.VMEM(w_up.shape, BF16),
            pltpu.VMEM(w_down.shape, BF16),
            pltpu.VMEM((2, chunk, width), F32),
            pltpu.VMEM((ROW_CHUNKS, chunk, width), F32),
            pltpu.VMEM((ROW_CHUNKS, chunk, width), F32),
            pltpu.VMEM((ROW_CHUNKS, chunk, width), F32),
            pltpu.VMEM((ROW_CHUNKS, chunk, width), F32),
            pltpu.VMEM((2, chunk, width), F32),
            pltpu.VMEM((2 * chunk, hidden), F32),
            pltpu.VMEM((2 * chunk, hidden), F32),
            pltpu.VMEM((2 * chunk, hidden), BF16),
            pltpu.VMEM((2 * chunk, width), BF16),
            pltpu.VMEM((width, 2 * chunk), BF16),
            pltpu.VMEM((2 * chunk, width), BF16),
            pltpu.VMEM((2, chunk, width), BF16),
            pltpu.VMEM((2, chunk, width), BF16),
            DMA((3,)),
            DMA((2,)),
            DMA((2,)),
        ]
        + [per_chunk] * 14
        + [DMA((3, 2)), DMA((2,)), DMA, DMA((2, 2)), DMA((2,))],
        compiler_params=pltpu.CompilerParams(
            collective_id=1, has_side_effects=True, vmem_limit_bytes=VMEM_LIMIT),
    )(mixed, w_out, attn_gain, mlp_gain, tok, seed, w_gate, w_up, w_down)


def backward_kernel(
    dp_size, counts,
    gdrt_hbm, hlt_hbm, tok_hbm, inner_hbm, mixed_hbm, gdr_hbm, gate_hbm, up_hbm, branch_hbm, seed_hbm,
    query_hbm, key_hbm, value_hbm, query_raw_hbm, key_raw_hbm,
    w_out_hbm, wg_hbm, wu_hbm, wd_hbm, wq_hbm, wk_hbm, wv_hbm,
    query_inv, key_inv, log_totals, seg_col, seg_row, live_col, cosine, sine,
    query_gain, key_gain, attn_gain, gain_mlp_part,
    turned_out, straight_out, token_out, gains_out,
    ggr_hbm, gur_hbm, gbt_hbm, gh_hbm, gqkv_hbm,
    at, bbuf, ysend, yrecv, zsend, zrecv, stage, stage_t, cs, crecv, xs, xr, ag, dots, dots_in,
    vec, vec_in,
    at_sem, b_sem, ys_sem, yr_sem, zs_sem, zr_sem, out_sem,
    cs_sem, cr_sem, xs_sem, xr_sem, as_sem, ar_sem, cs2_sem, cr2_sem, xs2_sem, xr2_sem, as2_sem,
    ar2_sem, ds_sem, dr_sem, vs_sem, vr_sem, w_sem, pre_sem, st_sem, gh_sem, tok_sem,
    y_credit, up_credit, down_credit,
):
    n_down, n_hidden, n_heads, n_out = counts
    first_heads = n_down + n_hidden
    first_out = first_heads + n_heads
    total = first_out + n_out
    line = dp_size // 2
    width = at.shape[1]
    block = width // dp_size
    chunk = xs.shape[1]
    half = chunk * ROW_CHUNKS
    full = 2 * half
    head_cols = query_hbm.shape[1]
    passes = total + total // SPAN
    dp_at = lax.axis_index("dp")
    z, y = dp_at // 2, dp_at % 2
    partner = dp_at + 1 - 2 * y
    below, above = dp_at - 2, dp_at + 2
    has_below, has_above = z > 0, z < line - 1
    core, sibling, across = tensor_peers()
    steps = [1 << s for s in range(dp_size.bit_length() - 1)]
    vec_peers = [dp_at + bit * (1 - 2 * ((dp_at // bit) % 2)) for bit in steps]

    def at_dp(i):
        return {"dp": i}

    def at_tensor(i):
        return {"tensor": i}

    barrier = pltpu.get_barrier_semaphore()

    def greet_one(peer):
        pl.semaphore_signal(barrier, inc=1, device_id=peer, device_id_type=MESH)

    other_z = z - 1 + 2 * lax.rem(z, 2)
    has_other = (other_z >= 0) & (other_z < line)
    for peer in vec_peers:
        greet_one(at_dp(peer))
    greet_one(at_tensor(sibling))
    greet_one(at_tensor(across))

    @pl.when(has_other)
    def _():
        greet_one(at_dp(2 * other_z + y))
    pl.semaphore_wait(barrier, len(steps) + 2 + has_other.astype(jnp.int32))

    def remote(src, dst, send_sem, recv_sem, peer):
        return pltpu.make_async_remote_copy(
            src_ref=src, dst_ref=dst, send_sem=send_sem, recv_sem=recv_sem,
            device_id=peer, device_id_type=MESH)

    def y_copy(p, b):
        return remote(ysend.at[p, b], yrecv.at[p, b], ys_sem.at[p, b], yr_sem.at[p, b], at_dp(partner))

    def z_copy(p, b, slot, target):
        return remote(zsend.at[p, b], zrecv.at[p, slot], zs_sem.at[p, b], zr_sem.at[p, slot], at_dp(target))

    def group_of(k):
        return (
            (k >= n_down).astype(jnp.int32)
            + (k >= first_heads).astype(jnp.int32)
            + (k >= first_out).astype(jnp.int32))

    def product(k, rows_at):
        return jnp.dot(
            at[lax.rem(group_of(k), 2), pl.ds(pl.multiple_of(rows_at * block, block), block), :],
            bbuf[lax.rem(k, B_SLOTS)], preferred_element_type=F32)

    def at_load(i):
        src = (gdrt_hbm, hlt_hbm, None, gbt_hbm)[i]
        return pltpu.make_async_copy(src, at.at[i % 2], at_sem.at[i % 2])

    def b_load(k, act):
        def columns(src, at_chunk):
            act(pltpu.make_async_copy(
                src.at[:, pl.ds(pl.multiple_of(at_chunk * COLS, COLS), COLS)],
                bbuf.at[lax.rem(k, B_SLOTS)], b_sem.at[lax.rem(k, B_SLOTS)]))
        per = n_hidden // 2

        @pl.when(k < n_down)
        def _():
            columns(inner_hbm, k)

        @pl.when((k >= n_down) & (k < n_down + per))
        def _():
            columns(ggr_hbm, k - n_down)

        @pl.when((k >= n_down + per) & (k < first_heads))
        def _():
            columns(gur_hbm, k - n_down - per)

        @pl.when((k >= first_heads) & (k < first_out))
        def _():
            columns(gqkv_hbm, k - first_heads)

        @pl.when((k >= first_out) & (k < total))
        def _():
            columns(mixed_hbm, k - first_out)

    def line_first(k):
        return lax.rem(k, SPAN) == SPAN - 1

    def walk(fn):
        def body(i, carry):
            @pl.when(z <= i)
            def _():
                fn(z + line - 1 - i, True)

            @pl.when(z >= line - 1 - i)
            def _():
                fn(z - (line - 1 - i), False)
            return carry
        lax.fori_loop(0, line - 1, body, 0)

    def pair_send(k):
        p = lax.rem(k, Y_SLOTS)

        @pl.when(k >= Y_SLOTS)
        def _():
            pl.semaphore_wait(y_credit, 1)
        b_load(k, lambda copy: copy.wait())

        @pl.when(jnp.logical_not(line_first(k)))
        def _():
            def one(b, up=None):
                ysend[p, b] = product(k, 2 * b + 1 - y)
                y_copy(p, b).start()
            walk(one)
            one(z)

    def line_send(q, k, source):
        p = lax.rem(q, 2)

        @pl.when(q >= 2)
        def _():
            @pl.when(has_above)
            def _():
                pl.semaphore_wait(up_credit, 1)

            @pl.when(has_below)
            def _():
                pl.semaphore_wait(down_credit, 1)

        def one(b, up):
            has_before, target = (has_below, above) if up else (has_above, below)
            zsend[p, b] = source(b)

            @pl.when(has_before)
            def _():
                z_copy(p, b, b, target).wait_recv()
                zsend[p, b] += zrecv[p, b]
            if up:
                z_copy(p, b, b, target).start()
            else:
                @pl.when(b == z - 1)
                def _():
                    z_copy(p, b, line, target).start()

                @pl.when(b != z - 1)
                def _():
                    z_copy(p, b, b, target).start()
        walk(one)

    def line_own(q, dst):
        p = lax.rem(q, 2)

        @pl.when(has_below)
        def _():
            z_copy(p, z, z, below).wait_recv()
            dst[...] += zrecv[p, z]

        @pl.when(has_above)
        def _():
            z_copy(p, z, line, below).wait_recv()
            dst[...] += zrecv[p, line]

        def drain(b, up):
            z_copy(p, b, b, below).wait_send()
        walk(drain)

        @pl.when(q < passes - 2)
        def _():
            @pl.when(has_below)
            def _():
                pl.semaphore_signal(up_credit, inc=1, device_id=at_dp(below), device_id_type=MESH)

            @pl.when(has_above)
            def _():
                pl.semaphore_signal(down_credit, inc=1, device_id=at_dp(above), device_id_type=MESH)

    def is_turned(k):
        return (k < n_down) | (k >= first_out)

    def out_act(k, act):
        @pl.when(is_turned(k))
        def _():
            first = jnp.where(k < n_down, k, k - first_out + n_down) * COLS
            act(pltpu.make_async_copy(
                stage_t, turned_out.at[pl.ds(pl.multiple_of(first, COLS), COLS)], out_sem))

        @pl.when(jnp.logical_not(is_turned(k)))
        def _():
            cols = pl.ds(pl.multiple_of((k - n_down) * COLS, COLS), COLS)
            act(pltpu.make_async_copy(stage, straight_out.at[:, cols], out_sem))

    def finish_chunk(k, q):
        p = lax.rem(k, Y_SLOTS)

        @pl.when(k >= 1)
        def _():
            out_act(k - 1, lambda copy: copy.wait())
        stage[...] = product(k, 2 * z + y)
        y_copy(p, z).wait_recv()
        stage[...] += yrecv[p, z]
        line_own(q, stage)

        @pl.when(is_turned(k))
        def _():
            stage_t[...] = stage[...].T
        out_act(k, lambda copy: copy.start())

        @pl.when(line_first(k))
        def _():
            y_copy(p, z).wait_send()

        @pl.when(jnp.logical_not(line_first(k)))
        def _():
            for b in range(line):
                y_copy(p, b).wait_send()

        @pl.when(k < total - Y_SLOTS)
        def _():
            pl.semaphore_signal(y_credit, inc=1, device_id=at_dp(partner), device_id_type=MESH)

    def tick(k):
        p = lax.rem(k, Y_SLOTS)
        q = k + k // SPAN
        is_line_first = line_first(k)

        @pl.when(jnp.logical_not(is_line_first))
        def _():
            def mine(b):
                part = product(k, 2 * b + y)
                y_copy(p, b).wait_recv()
                return part + yrecv[p, b]
            line_send(q, k, mine)

        @pl.when(is_line_first)
        def _():
            line_send(q, k, lambda b: product(k, 2 * b + 1 - y))

        @pl.when(k >= 1)
        def _():
            finish_chunk(k - 1, q - 1)

        @pl.when(is_line_first)
        def _():
            line_send(q + 1, k, lambda b: product(k, 2 * b + y))
            ysend[p, z] = product(k, 2 * z + 1 - y)
            line_own(q, ysend.at[p, z])
            y_copy(p, z).start()

        @pl.when(k + 2 < total)
        def _():
            pair_send(k + 2)

        @pl.when(k + 3 < total)
        def _():
            b_load(k + 3, lambda copy: copy.start())

    nt = (((1,), (1,)), ((), ()))

    def copies_of(sem, *pairs):
        return [pltpu.make_async_copy(src, dst, sem.at[i]) for i, (src, dst) in enumerate(pairs)]

    def start(copies):
        for copy in copies:
            copy.start()

    def finish(copies):
        for copy in copies:
            copy.wait()

    def run_ticks(first, last, work):
        def body(k, carry):
            tick(k)
            for when, fn in work.items():
                low, high = when if isinstance(when, tuple) else (when, when + 1)

                @pl.when((k >= low) & (k < high))
                def _(fn=fn, low=low):
                    if isinstance(fn, list):
                        for one in fn:
                            one()
                    elif low + 1 == high:
                        fn()
                    else:
                        fn(k - low)
            return carry
        lax.fori_loop(first, last, body, 0)

    def part(fn, *args):
        return functools.partial(fn, *args)

    def side_rows(s, c):
        return pl.ds(s * half + c * chunk, chunk)

    def both_sides(hbm, buf, c, out=False):
        pairs = [(hbm.at[side_rows(s, c)], buf.at[pl.ds(s * chunk, chunk)]) for s in range(2)]
        return [(b, a) for a, b in pairs] if out else pairs

    def sequence_rows(s, c):
        return pl.ds(pl.multiple_of(jnp.where(core == s, 0, half) + c * chunk, chunk), chunk)

    def core_copy(c, again):
        ss, rs = (cs2_sem, cr2_sem) if again else (cs_sem, cr_sem)
        return remote(cs.at[c % 2], crecv.at[c], ss.at[c], rs.at[c], at_tensor(sibling))

    def x_copy(c, again):
        ss, rs = (xs2_sem, xr2_sem) if again else (xs_sem, xr_sem)
        return remote(xs.at[c], xr.at[c], ss.at[c], rs.at[c], at_tensor(across))

    def to_sibling(c, again):
        ss, rs = (as2_sem, ar2_sem) if again else (as_sem, ar_sem)
        return remote(xr.at[c], ag.at[c % 2], ss.at[c], rs.at[c], at_tensor(sibling))

    def pass_on(c, again):
        core_copy(c, again).wait_recv()
        xs[c] += crecv[c]
        x_copy(c, again).start()
        core_copy(c, again).wait_send()

    hidden = wd_hbm.shape[0]

    def feed_phase(wd, grads, gates, ups, ggr, gur):
        def loads(c):
            return copies_of(
                pre_sem, *both_sides(gdr_hbm, grads, c), *both_sides(gate_hbm, gates, c),
                *both_sides(up_hbm, ups, c))

        def stores(c):
            return copies_of(
                st_sem, *both_sides(ggr_hbm, ggr, c, True), *both_sides(gur_hbm, gur, c, True))

        def piece(c):
            finish(loads(c))
            if c >= 1:
                finish(stores(c - 1))

            def tile(n, carry):
                cols = pl.ds(pl.multiple_of(n * TILE, TILE), TILE)
                grad = lax.dot_general(grads[...], wd[cols, :], nt, preferred_element_type=F32)
                gate = gates[:, cols]
                sig = jax.nn.sigmoid(gate)
                act = gate * sig
                ggr[:, cols] = (grad * ups[:, cols] * (sig + act * (1.0 - sig))).astype(BF16)
                gur[:, cols] = (grad * act).astype(BF16)
                return carry
            lax.fori_loop(0, hidden // TILE, tile, 0)
            start(stores(c))
            if c + 1 < ROW_CHUNKS:
                start(loads(c + 1))

        load_weight = copies_of(w_sem, (wd_hbm, wd))
        start(load_weight)
        start(loads(0))
        at_load(0).wait()
        pair_send(jnp.int32(0))
        pair_send(jnp.int32(1))
        finish(load_weight)
        piece(0)
        run_ticks(0, FEED_TICK, {c - 1: part(piece, c) for c in range(1, ROW_CHUNKS)})
        finish(stores(ROW_CHUNKS - 1))

    def hidden_phase(weights, ggr, gur):
        load_weights = copies_of(w_sem, (wg_hbm, weights.at[0]), (wu_hbm, weights.at[1]))

        def loads(c):
            return copies_of(pre_sem, *both_sides(ggr_hbm, ggr, c), *both_sides(gur_hbm, gur, c))

        def piece(c):
            if c == 0:
                finish(load_weights)
            else:
                pass_on(c - 1, False)
            finish(loads(c))

            def tile(n, carry):
                rows = pl.ds(pl.multiple_of(n * TILE, TILE), TILE)
                total_part = lax.dot_general(ggr[...], weights[0, rows, :], nt, preferred_element_type=F32)
                total_part = total_part + lax.dot_general(
                    gur[...], weights[1, rows, :], nt, preferred_element_type=F32)
                xs[c, :, rows] = total_part[0:chunk]
                cs[c % 2, :, rows] = total_part[chunk : 2 * chunk]
                return carry
            lax.fori_loop(0, width // TILE, tile, 0)
            core_copy(c, False).start()
            if c + 1 < ROW_CHUNKS:
                start(loads(c + 1))

        start(load_weights)
        start(loads(0))
        run_ticks(
            FEED_TICK, HIDDEN_TICK, {FEED_TICK + c: part(piece, c) for c in range(ROW_CHUNKS)})

    def branch_phase(branch, seed, low, turned, w_out, mixed_grad, token_rows):
        load_weight = copies_of(w_sem, (w_out_hbm, w_out))
        token_piece = full // ROW_CHUNKS

        def loads(c):
            rows = pl.ds(c * chunk, chunk)
            return copies_of(pre_sem, (branch_hbm.at[rows], branch), (seed_hbm.at[rows], seed))

        def stores(c):
            i = c % 2
            return copies_of(
                st_sem.at[pl.ds(4 * i, 4)],
                (turned.at[i, :, pl.ds(0, chunk)], gbt_hbm.at[:, side_rows(0, c)]),
                (turned.at[i, :, pl.ds(chunk, chunk)], gbt_hbm.at[:, side_rows(1, c)]),
                *[(
                    mixed_grad.at[i, pl.ds(s * chunk, chunk)],
                    gqkv_hbm.at[sequence_rows(s, c), pl.ds(2 * head_cols, head_cols)],
                ) for s in range(2)])

        def hidden_store(c):
            return copies_of(gh_sem, (xs.at[c], gh_hbm.at[pl.ds(c * chunk, chunk)]))

        def token_load(c):
            return copies_of(tok_sem, (tok_hbm.at[pl.ds(c * token_piece, token_piece)], token_rows))

        def first(c):
            i = c % 2
            finish(loads(c))
            x_copy(c, False).wait()
            grad_hidden = xs[c] + xr[c] + seed[...].astype(F32)
            xs[c] = grad_hidden
            start(hidden_store(c))
            values = branch[...]
            inv = mean_inverse(values)
            vec[1:2, :] += column_sum(grad_hidden * values * inv)
            scaled = grad_hidden * attn_gain[...]
            dot = jnp.sum(scaled * values, axis=1, keepdims=True)
            grad = inv * scaled - values * (inv * inv * inv * dot / width)
            xr[c] = grad
            to_sibling(c, False).start()
            if c >= 2:
                finish(stores(c - 2))
            low[i, 0:chunk, :] = grad.astype(BF16)
            turned[i, :, 0:chunk] = grad.astype(BF16).T
            if c + 1 < ROW_CHUNKS:
                start(loads(c + 1))

        def second(c):
            i = c % 2
            to_sibling(c, False).wait_recv()
            if c == 0:
                finish(load_weight)
            other = ag[i].astype(BF16)
            low[i, chunk : 2 * chunk, :] = other
            turned[i, :, chunk : 2 * chunk] = other.T
            mixed_grad[i] = lax.dot_general(
                low[i], w_out[...], nt, preferred_element_type=F32).astype(BF16)
            start(stores(c))
            finish(hidden_store(c))
            to_sibling(c, False).wait_send()

        def turn(c):
            finish(token_load(c))
            at[0, :, pl.ds(c * token_piece, token_piece)] = token_rows[...].T
            if c + 1 < ROW_CHUNKS:
                start(token_load(c + 1))

        start(load_weight)
        start(loads(0))
        start(token_load(0))
        work = {HIDDEN_TICK + c: [] for c in range(ROW_CHUNKS + 1)}
        work[HIDDEN_TICK].append(part(pass_on, ROW_CHUNKS - 1, False))
        for c in range(ROW_CHUNKS):
            work[HIDDEN_TICK + c].append(part(first, c))
            work[HIDDEN_TICK + c + 1].append(part(second, c))
        work[HIDDEN_TICK + 3] += [part(turn, 0)]
        work[HIDDEN_TICK + 4] += [part(turn, c) for c in range(1, ROW_CHUNKS)]
        run_ticks(HIDDEN_TICK, BRANCH_TICK, work)
        for c in range(ROW_CHUNKS - 2, ROW_CHUNKS):
            finish(stores(c))

    def attention_phase(query, key, value, mixed_grad, dq, dk, dv, raw, bias):
        heads = head_cols // HEAD
        q_rows = min(256, full)
        scale = HEAD ** (-0.5)
        value_cols = pl.ds(2 * head_cols, head_cols)
        loads = copies_of(
            pre_sem, (query_hbm, query), (key_hbm, key), (value_hbm, value),
            (gqkv_hbm.at[:, value_cols], mixed_grad))

        def masks():
            for i in range(full // q_rows):
                rows, keys = slice(i * q_rows, (i + 1) * q_rows), (i + 1) * q_rows
                key_at = lax.broadcasted_iota(jnp.int32, (keys, q_rows), 0)
                query_at = lax.broadcasted_iota(jnp.int32, (keys, q_rows), 1) + i * q_rows
                allowed = (
                    (seg_col[0:keys, :] == seg_row[:, rows])
                    & (key_at <= query_at)
                    & ((live_col[0:keys, :] > 0) | (key_at == query_at)))
                bias[0:keys, rows] = jnp.where(allowed, 0.0, NEG_FILL)
            finish(loads)

        def head(h):
            cols = pl.ds(pl.multiple_of(h * HEAD, HEAD), HEAD)
            dk[:, cols] = jnp.zeros((full, HEAD), F32)
            dv[...] = jnp.zeros((full, HEAD), F32)
            for i in range(full // q_rows):
                rows, keys = slice(i * q_rows, (i + 1) * q_rows), (i + 1) * q_rows
                q_block, grad_block = query[rows, cols], mixed_grad[rows, cols]
                key_block, value_block = key[0:keys, cols], value[0:keys, cols]
                scores = lax.dot_general(key_block, q_block, nt, preferred_element_type=F32) * scale
                prob = jnp.exp(scores + bias[0:keys, rows] - log_totals[pl.ds(h, 1), rows])
                grad_prob = lax.dot_general(value_block, grad_block, nt, preferred_element_type=F32)
                row_dot = jnp.sum(prob * grad_prob, axis=0, keepdims=True)
                grad_scores = (prob * (grad_prob - row_dot)).astype(BF16)
                dq[rows, cols] = lax.dot_general(
                    grad_scores, key_block, (((0,), (0,)), ((), ())), preferred_element_type=F32) * scale
                dk[0:keys, cols] += jnp.dot(grad_scores, q_block, preferred_element_type=F32) * scale
                dv[0:keys, :] += jnp.dot(prob.astype(BF16), grad_block, preferred_element_type=F32)
            mixed_grad[:, cols] = dv[...].astype(BF16)

        store_value = copies_of(st_sem, (mixed_grad, gqkv_hbm.at[:, value_cols]))
        sides = ((dq, query_raw_hbm, query_inv, query_gain), (dk, key_raw_hbm, key_inv, key_gain))

        def load_raw(which):
            return copies_of(pre_sem, (sides[which][1], raw))

        def back(which):
            grads, _, inv, gain = sides[which]
            finish(load_raw(which))
            lanes = lax.broadcasted_iota(jnp.int32, (q_rows, HEAD), 1)

            def block_back(i, carry):
                rows = pl.ds(pl.multiple_of(i * q_rows, q_rows), q_rows)
                dot = jnp.zeros((q_rows, 1), F32)
                for h in range(heads):
                    cols = slice(h * HEAD, (h + 1) * HEAD)
                    grad = grads[rows, cols]
                    grad = grad * cosine[rows, :] + pltpu.roll(grad, HEAD // 2, 1) * sine[rows, :]
                    raw_rows = raw[rows, cols]
                    gain_cols = slice(which * head_cols + h * HEAD, which * head_cols + (h + 1) * HEAD)
                    vec[2:3, gain_cols] += column_sum(grad * raw_rows * inv[rows, :])
                    scaled = grad * gain[:, cols]
                    grads[rows, cols] = scaled
                    dot = dot + jnp.sum(scaled * raw_rows, axis=1, keepdims=True)
                if which == 0:
                    dots[rows, :] = jnp.broadcast_to(dot, (q_rows, HEAD))
                else:
                    dots[rows, :] = jnp.where(lanes == 0, dots[rows, :], dot)
                return carry
            lax.fori_loop(0, full // q_rows, block_back, 0)

        def dots_copy(i):
            return remote(
                dots, dots_in.at[i], ds_sem.at[i], dr_sem.at[i], at_tensor((sibling, across)[i]))

        def dots_add(i):
            dots_copy(i).wait()
            dots[...] += dots_in[i]

        def combine(which):
            grads, _, inv, _ = sides[which]
            for i in range(full // q_rows):
                rows = slice(i * q_rows, (i + 1) * q_rows)
                inv_rows = inv[rows, :]
                dot = dots[rows, which : which + 1]
                mixed_grad[rows, :] = (
                    inv_rows * grads[rows, :]
                    - raw[rows, :] * (inv_rows * inv_rows * inv_rows * dot / width)
                ).astype(BF16)

        def store_grads(which):
            return copies_of(
                st_sem, (mixed_grad, gqkv_hbm.at[:, pl.ds(which * head_cols, head_cols)]))

        def after_heads():
            start(store_value)
            start(load_raw(0))

        def back_query():
            back(0)
            start(load_raw(1))

        def back_key():
            back(1)
            dots_copy(0).start()
            finish(store_value)

        def first_sum():
            dots_add(0)
            dots_copy(1).start()

        def second_sum():
            dots_add(1)
            combine(1)
            start(store_grads(1))
            start(load_raw(0))

        def last_part():
            finish(store_grads(1))
            finish(load_raw(0))
            combine(0)
            start(store_grads(0))

        start(loads)
        t = BRANCH_TICK
        run_ticks(t, INPUT_TICK, {
            t: masks,
            (t + 1, t + 1 + heads): head,
            t + heads: after_heads,
            t + heads + 1: back_query,
            t + heads + 2: back_key,
            t + heads + 3: first_sum,
            t + heads + 4: [second_sum, last_part],
        })
        finish(store_grads(0))

    def input_phase(weights, grads, grad_hidden, low):
        loads = copies_of(
            w_sem, *[(w, weights.at[i]) for i, w in enumerate((wq_hbm, wk_hbm, wv_hbm))],
            (gqkv_hbm, grads))

        def piece(c):
            if c == 0:
                finish(loads)
            else:
                pass_on(c - 1, True)
            for s in range(2):
                rows = sequence_rows(s, c)

                def tile(n, carry):
                    cols = pl.ds(pl.multiple_of(n * TILE, TILE), TILE)
                    total_part = jnp.zeros((chunk, TILE), F32)
                    for i in range(3):
                        total_part = total_part + lax.dot_general(
                            grads[rows, i * head_cols : (i + 1) * head_cols], weights[i, cols, :],
                            nt, preferred_element_type=F32)
                    if s == 0:
                        xs[c, :, cols] = total_part
                    else:
                        cs[c % 2, :, cols] = total_part
                    return carry
                lax.fori_loop(0, width // TILE, tile, 0)
            core_copy(c, True).start()

        def hidden_load(c):
            return copies_of(gh_sem, (gh_hbm.at[pl.ds(c * chunk, chunk)], grad_hidden))

        def stores(c):
            return copies_of(
                st_sem, *[(low.at[s], token_out.at[sequence_rows(s, c)]) for s in range(2)])

        def first(c):
            finish(hidden_load(c))
            x_copy(c, True).wait()
            xr[c] = xs[c] + xr[c] + grad_hidden[...]
            to_sibling(c, True).start()
            if c + 1 < ROW_CHUNKS:
                start(hidden_load(c + 1))

        def second(c):
            if c >= 1:
                finish(stores(c - 1))
            low[0] = xr[c].astype(BF16)
            to_sibling(c, True).wait_recv()
            low[1] = ag[c % 2].astype(BF16)
            start(stores(c))
            to_sibling(c, True).wait_send()

        vec_peer_ids = [at_tensor(sibling)] + [at_dp(peer) for peer in vec_peers]

        def vec_copy(i):
            return remote(vec, vec_in.at[i], vs_sem.at[i], vr_sem.at[i], vec_peer_ids[i])

        def vec_step(i):
            if i >= 1:
                vec_copy(i - 1).wait()
                if i == 1:
                    vec[0:2, :] += vec_in[0, 0:2, :]
                else:
                    vec[...] += vec_in[i - 1]
            if i < len(vec_peer_ids):
                vec_copy(i).start()

        start(loads)
        start(hidden_load(0))
        work = {k: [] for k in range(INPUT_TICK, total)}
        for c in range(ROW_CHUNKS):
            work[INPUT_TICK + c].append(part(piece, c))
            work[TOKEN_TICK + c].append(part(first, c))
            work[TOKEN_TICK + c + 1].append(part(second, c))
        work[INPUT_TICK + ROW_CHUNKS].append(part(pass_on, ROW_CHUNKS - 1, True))
        for i in range(len(vec_peer_ids) + 1):
            work[INPUT_TICK + 2 + i].append(part(vec_step, i))
        work[first_heads + 1].append(lambda: at_load(3).start())
        work[first_heads + 2].append(lambda: at_load(3).wait())
        run_ticks(INPUT_TICK, total, {k: fns for k, fns in work.items() if fns})
        finish(stores(ROW_CHUNKS - 1))

    vec[...] = jnp.zeros(vec.shape, F32)
    vec[0:1, :] = gain_mlp_part[...]
    at_load(0).start()
    at_load(1).start()
    for k in range(3):
        b_load(jnp.int32(k), lambda copy: copy.start())
    both = 2 * chunk
    rows_of = (full, head_cols)
    pl.run_scoped(
        feed_phase, pltpu.VMEM(wd_hbm.shape, BF16), pltpu.VMEM((both, width), BF16),
        pltpu.VMEM((both, hidden), F32), pltpu.VMEM((both, hidden), F32),
        pltpu.VMEM((both, hidden), BF16), pltpu.VMEM((both, hidden), BF16))
    at_load(1).wait()
    pl.run_scoped(
        hidden_phase, pltpu.VMEM((2,) + wg_hbm.shape, BF16), pltpu.VMEM((both, hidden), BF16),
        pltpu.VMEM((both, hidden), BF16))
    pl.run_scoped(
        branch_phase, pltpu.VMEM((chunk, width), F32), pltpu.VMEM((chunk, width), BF16),
        pltpu.VMEM((2, both, width), BF16), pltpu.VMEM((2, width, both), BF16),
        pltpu.VMEM(w_out_hbm.shape, BF16), pltpu.VMEM((2, both, head_cols), BF16),
        pltpu.VMEM((full // ROW_CHUNKS, width), BF16))
    pl.run_scoped(
        attention_phase, pltpu.VMEM(rows_of, BF16), pltpu.VMEM(rows_of, BF16), pltpu.VMEM(rows_of, BF16),
        pltpu.VMEM(rows_of, BF16), pltpu.VMEM(rows_of, F32), pltpu.VMEM(rows_of, F32),
        pltpu.VMEM((full, HEAD), F32), pltpu.VMEM(rows_of, F32), pltpu.VMEM((full, full), F32))
    pl.run_scoped(
        input_phase, pltpu.VMEM((3,) + wq_hbm.shape, BF16), pltpu.VMEM((full, 3 * head_cols), BF16),
        pltpu.VMEM((chunk, width), F32), pltpu.VMEM((2, chunk, width), BF16))
    finish_chunk(jnp.int32(total - 1), jnp.int32(passes - 1))
    out_act(jnp.int32(total - 1), lambda copy: copy.wait())
    gains_out[...] = vec[...]


def backward_layer(dp_size, hbm, vmem_args):
    names = dict(zip(HBM_NAMES, hbm, strict=True))
    width, row_count = names["gdrt"].shape
    hidden, head_cols = names["inner"].shape[1], names["query"].shape[1]
    line, block = dp_size // 2, width // dp_size
    chunk = row_count // 2 // ROW_CHUNKS
    counts = (hidden // COLS, 2 * hidden // COLS, 3 * head_cols // COLS, head_cols // COLS)
    DMA, REG = pltpu.SemaphoreType.DMA, pltpu.SemaphoreType.REGULAR
    vmem, any_space = pl.BlockSpec(memory_space=pltpu.VMEM), pl.BlockSpec(memory_space=pl.ANY)

    def shape(*dims, kind=F32):
        return jax.ShapeDtypeStruct(dims, kind)

    slot = (block, COLS)
    per_chunk = DMA((ROW_CHUNKS,))
    steps = dp_size.bit_length() - 1
    results = pl.pallas_call(
        functools.partial(backward_kernel, dp_size, counts),
        out_shape=(
            shape((counts[0] + counts[3]) * COLS, block),
            shape(block, (counts[1] + counts[2]) * COLS),
            shape(row_count, width, kind=BF16),
            shape(8, width),
            shape(row_count, hidden, kind=BF16),
            shape(row_count, hidden, kind=BF16),
            shape(width, row_count, kind=BF16),
            shape(row_count // 2, width),
            shape(row_count, 3 * head_cols, kind=BF16),
        ),
        in_specs=[any_space] * len(hbm) + [vmem] * len(vmem_args),
        out_specs=(any_space,) * 3 + (vmem,) + (any_space,) * 5,
        scratch_shapes=[
            pltpu.VMEM((2, width, row_count), BF16),
            pltpu.VMEM((B_SLOTS, row_count, COLS), BF16),
            pltpu.VMEM((Y_SLOTS, line) + slot, F32),
            pltpu.VMEM((Y_SLOTS, line) + slot, F32),
            pltpu.VMEM((2, line) + slot, F32),
            pltpu.VMEM((2, line + 1) + slot, F32),
            pltpu.VMEM(slot, F32),
            pltpu.VMEM((COLS, block), F32),
            pltpu.VMEM((2, chunk, width), F32),
            pltpu.VMEM((ROW_CHUNKS, chunk, width), F32),
            pltpu.VMEM((ROW_CHUNKS, chunk, width), F32),
            pltpu.VMEM((ROW_CHUNKS, chunk, width), F32),
            pltpu.VMEM((2, chunk, width), F32),
            pltpu.VMEM((row_count, HEAD), F32),
            pltpu.VMEM((2, row_count, HEAD), F32),
            pltpu.VMEM((8, width), F32),
            pltpu.VMEM((steps + 1, 8, width), F32),
            DMA((2,)),
            DMA((B_SLOTS,)),
            DMA((Y_SLOTS, line)),
            DMA((Y_SLOTS, line)),
            DMA((2, line)),
            DMA((2, line + 1)),
            DMA,
        ]
        + [per_chunk] * 12
        + [DMA((2,)), DMA((2,)), DMA((steps + 1,)), DMA((steps + 1,)), DMA((4,)), DMA((6,)), DMA((8,)), DMA((1,)), DMA((1,)),
           REG, REG, REG],
        compiler_params=pltpu.CompilerParams(
            collective_id=2, has_side_effects=True, vmem_limit_bytes=VMEM_LIMIT),
    )(*hbm, *vmem_args)
    return results[:4]


def times(left, right):
    return jnp.dot(left, right, preferred_element_type=F32)


def rope_tables():
    half_size = HEAD // 2
    freq_row = ROPE_BASE ** (-(jnp.arange(half_size, dtype=F32) * 2.0) / HEAD)
    angle = jnp.arange(LENGTH, dtype=F32)[:, None] * freq_row[None, :]
    return (jnp.cos(angle), jnp.sin(angle))


def rotate(values, cosine, sine_part, direction):
    row_count, col_count = values.shape
    half_size = HEAD // 2
    split = values.reshape(row_count // LENGTH, LENGTH, col_count // HEAD, 2, half_size)
    first = split[:, :, :, 0]
    second = split[:, :, :, 1]
    cos_b = cosine[None, :, None, :]
    sin_b = direction * sine_part[None, :, None, :]
    turned = jnp.stack((first * cos_b - second * sin_b, second * cos_b + first * sin_b), axis=3)
    return turned.reshape(row_count, col_count)


def visible_keys(begin_at, block_rows, segment_ids, live_rows):
    seq_length = segment_ids.shape[0]
    key_index = jnp.arange(seq_length)
    query_index = begin_at + jnp.arange(block_rows)
    query_segs = segment_ids[begin_at : begin_at + block_rows]
    same_doc = query_segs[:, None] == segment_ids[None, :]
    causal = key_index[None, :] <= query_index[:, None]
    kept_key = (live_rows[None, :] > 0) | (key_index[None, :] == query_index[:, None])
    return same_doc & causal & kept_key


def block_scores(query_seq, key_heads, begin_at, block_rows, segment_ids, live_rows):
    local_heads = key_heads.shape[1]
    query_heads = query_seq[begin_at : begin_at + block_rows].reshape(block_rows, local_heads, HEAD)
    scores = jnp.einsum(
        "ihd,jhd->hij", query_heads, key_heads, preferred_element_type=F32
    ) * HEAD ** (-0.5)
    allowed = visible_keys(begin_at, block_rows, segment_ids, live_rows)
    return (query_heads, jnp.where(allowed[None], scores, NEG_FILL))


def attend_forward(query_seq, key_seq, value_seq, segment_ids, live_rows):
    seq_length = query_seq.shape[0]
    local_heads = query_seq.shape[1] // HEAD
    block_rows = min(512, seq_length)
    key_heads = key_seq.reshape(seq_length, local_heads, HEAD)
    value_heads = value_seq.reshape(seq_length, local_heads, HEAD)
    mixed_parts = []
    lse_parts = []
    for begin_at in range(0, seq_length, block_rows):
        query_heads, scores = block_scores(
            query_seq, key_heads, begin_at, block_rows, segment_ids, live_rows
        )
        row_max = jnp.max(scores, axis=-1, keepdims=True)
        exp_scores = jnp.exp(scores - row_max)
        row_total = jnp.sum(exp_scores, axis=-1, keepdims=True)
        attn_prob = (exp_scores / row_total).astype(BF16)
        mixed_block = jnp.einsum(
            "hij,jhd->ihd", attn_prob, value_heads, preferred_element_type=F32
        )
        mixed_parts.append(mixed_block.reshape(block_rows, -1).astype(BF16))
        lse_parts.append((row_max + jnp.log(row_total))[..., 0])
    return (jnp.concatenate(mixed_parts, 0), jnp.concatenate(lse_parts, 1))


def make_shards(dp_size, tensor_size):
    core_pairs = [(i, i ^ 1) for i in range(tensor_size)]
    tensor_bits = [1 << b for b in range(1, tensor_size.bit_length() - 1)]

    def to_core(values):
        return lax.ppermute(values, "tensor", core_pairs)

    def wide_sum(values):
        for bit in tensor_bits:
            values = values + lax.ppermute(
                values, "tensor", [(i, i ^ bit) for i in range(tensor_size)]
            )
        return values

    def shards(
        tokens,
        segments,
        pad_mask,
        w_query,
        w_key,
        w_value,
        w_out,
        gain_query,
        gain_key,
        gain_attn,
        w_gate,
        w_up,
        w_down,
        gain_mlp,
        cotangent,
    ):
        row_count, model_width = tokens.shape
        half_rows = row_count // 2
        block = model_width // dp_size
        core_at = lax.axis_index("tensor") % 2
        cosine, sine_part = rope_tables()

        def split_rows(values):
            own = lax.dynamic_slice_in_dim(values, core_at * half_rows, half_rows, 0)
            other = lax.dynamic_slice_in_dim(values, (1 - core_at) * half_rows, half_rows, 0)
            return own, other

        query_raw = times(tokens, w_query)
        key_raw = times(tokens, w_key)
        value_rows = times(tokens, w_value).astype(BF16)
        squares = jnp.stack(
            (jnp.sum(query_raw * query_raw, axis=1), jnp.sum(key_raw * key_raw, axis=1))
        )
        squares = wide_sum(squares + to_core(squares))
        query_inv = lax.rsqrt(squares[0] / model_width + EPSILON)[:, None]
        key_inv = lax.rsqrt(squares[1] / model_width + EPSILON)[:, None]
        query_gain = gain_query.reshape(-1).astype(F32)
        key_gain = gain_key.reshape(-1).astype(F32)
        query_norm = rotate(query_raw * query_inv * query_gain, cosine, sine_part, 1.0).astype(BF16)
        key_norm = rotate(key_raw * key_inv * key_gain, cosine, sine_part, 1.0).astype(BF16)
        mixed, log_totals = attend_forward(query_norm, key_norm, value_rows, segments, pad_mask)
        mixed_own, mixed_other = split_rows(mixed)
        mixed_rows = jnp.concatenate((mixed_own, mixed_other), 0)
        tokens_own, tokens_other = split_rows(tokens)
        cot_own, _ = split_rows(cotangent)
        live_own, _ = split_rows(pad_mask[:, None])
        attn_gain = gain_attn.astype(F32)
        mlp_gain = gain_mlp.astype(F32)
        seed = jnp.where(live_own > 0, cot_own, jnp.zeros_like(cot_own))

        (
            gate_rows,
            up_rows,
            inner_rows,
            hidden_turned,
            grad_down_rows,
            grad_down_turned,
            branch_rows,
            output,
            gain_mlp_part,
        ) = forward_layer(
            mixed_rows,
            w_out,
            attn_gain[None, :],
            mlp_gain[None, :],
            tokens_own,
            seed,
            w_gate,
            w_up,
            w_down,
        )
        turned, straight, grad_tokens, gains = backward_layer(
            dp_size,
            (
                grad_down_turned, hidden_turned, tokens, inner_rows, mixed_rows, grad_down_rows,
                gate_rows, up_rows, branch_rows, seed,
                query_norm, key_norm, value_rows, query_raw, key_raw,
                w_out, w_gate, w_up, w_down, w_query, w_key, w_value,
            ),
            (
                query_inv, key_inv, log_totals, segments[:, None], segments[None, :],
                pad_mask[:, None], jnp.concatenate((cosine, cosine), 1),
                jnp.concatenate((sine_part, -sine_part), 1),
                query_gain[None, :], key_gain[None, :], attn_gain[None, :], gain_mlp_part,
            ),
        )
        hidden, head_cols = w_gate.shape[1], w_query.shape[1]
        grad_gate, grad_up = straight[:, :hidden], straight[:, hidden : 2 * hidden]
        grad_query, grad_key, grad_value = (
            straight[:, 2 * hidden + i * head_cols : 2 * hidden + (i + 1) * head_cols]
            for i in range(3)
        )
        dp_at = lax.axis_index("dp")
        wide = lax.dynamic_slice_in_dim(gains[:2], dp_at * block, block, 1)
        head_gains = gains[2, : 2 * head_cols].reshape(2 * gain_query.shape[0], HEAD)
        head_gains = lax.dynamic_slice_in_dim(head_gains, dp_at * (HEAD // dp_size), HEAD // dp_size, 1)
        return (
            output,
            grad_tokens,
            grad_query,
            grad_key,
            grad_value,
            turned[hidden:],
            head_gains[: gain_query.shape[0]],
            head_gains[gain_query.shape[0] :],
            wide[1],
            grad_gate,
            grad_up,
            turned[:hidden],
            wide[0],
        )

    return shards


def solution(mesh):
    in_specs = (
        P("dp", None),
        P("dp"),
        P("dp"),
        P(None, "tensor"),
        P(None, "tensor"),
        P(None, "tensor"),
        P("tensor", None),
        P("tensor", None),
        P("tensor", None),
        P(),
        P(None, "tensor"),
        P(None, "tensor"),
        P("tensor", None),
        P(),
        P("dp", None),
    )
    out_specs = (
        P("dp", None),
        P("dp", None),
        P("dp", "tensor"),
        P("dp", "tensor"),
        P("dp", "tensor"),
        P("tensor", "dp"),
        P("tensor", "dp"),
        P("tensor", "dp"),
        P("dp"),
        P("dp", "tensor"),
        P("dp", "tensor"),
        P("tensor", "dp"),
        P("dp"),
    )
    shards = make_shards(mesh.shape["dp"], mesh.shape["tensor"])
    return jax.shard_map(shards, mesh=mesh, in_specs=in_specs, out_specs=out_specs, check_vma=False)
```

```python
import functools

import jax
import jax.numpy as jnp
from jax import lax
from jax.experimental import pallas as pl
from jax.experimental.pallas import tpu as pltpu
from jax.sharding import PartitionSpec as P

HEAD = 128
LENGTH = 1024
EPSILON = 1e-06
NEG_FILL = -1e30
ROPE_BASE = 500000.0
ROW_CHUNKS = 4
F32 = jnp.float32
BF16 = jnp.bfloat16


COLS = 256
SPAN = 6
Y_SLOTS = 3
B_SLOTS = 5
FEED_TICK = 3
HIDDEN_TICK = 7
BRANCH_TICK = 12
INPUT_TICK = 21
TOKEN_TICK = 26
HBM_NAMES = (
    "gdrt", "hlt", "tokens", "inner", "mixed", "gdr", "gate", "up", "branch", "cotangent",
    "query", "key", "value", "query_raw", "key_raw",
    "w_out", "w_gate", "w_up", "w_down", "w_query", "w_key", "w_value",
)
TILE = 512
VMEM_LIMIT = 63 * 1024 * 1024
MESH = pl.DeviceIdType.MESH

def column_sum(values):
    return jnp.sum(values, axis=0, keepdims=True)


def mean_inverse(values):
    return lax.rsqrt(jnp.mean(values * values, axis=1, keepdims=True) + EPSILON)


def tensor_peers():
    at = lax.axis_index("tensor")
    core = lax.rem(at, 2)
    return core, at + 1 - 2 * core, lax.rem(at + 2, 4)


def greet(*peers):
    barrier = pltpu.get_barrier_semaphore()
    for peer in peers:
        pl.semaphore_signal(barrier, inc=1, device_id=peer, device_id_type=MESH)
    pl.semaphore_wait(barrier, len(peers))


def forward_kernel(
    tok_hbm, cot_hbm, wq_hbm, wk_hbm, wv_hbm, wo_hbm, wg_hbm, wu_hbm, wd_hbm, cos_hbm, sin_hbm,
    seg_live, seg_row, query_gain, key_gain, attn_gain, mlp_gain,
    gate_out, up_out, inner_out, hlt_out, gdr_out, gdrt_out, branch_out, out_out,
    query_out, key_out, value_out, query_raw_out, key_raw_out, mixed_out,
    gain_out, inverse_out, log_out,
    wg, wu, cs, crecv, xs, xr, xr2, ag, squares, squares_in,
    w_sem, t_sem, s_sem, a_sem, r_sem, m_sem, sq_s_sem, sq_r_sem, sx_s_sem, sx_r_sem,
    cs_sem, cr_sem, xs_sem, xr_sem, as_sem, ar_sem, cs2_sem, cr2_sem, xs2_sem, xr2_sem,
    gs_sem, gr_sem, os_sem, or_sem, g_sem, h_sem, b_sem, d_sem, o_sem,
):
    core, sibling, across = tensor_peers()
    chunk = xs.shape[1]
    half = chunk * ROW_CHUNKS
    full = 2 * half
    both = 2 * chunk
    width, hidden = xs.shape[2], wg.shape[1]
    head_cols = wq_hbm.shape[1]
    heads = head_cols // HEAD
    tiles = hidden // TILE
    wide_tiles = width // TILE
    last = ROW_CHUNKS - 1
    nt = (((1,), (1,)), ((), ()))

    def start(copies):
        for copy in copies:
            copy.start()

    def finish(copies):
        for copy in copies:
            copy.wait()

    def own_rows(s, c):
        return pl.ds(pl.multiple_of(c * both + jnp.where(core == s, 0, chunk), chunk), chunk)

    def row_load(c, src, dst, sem):
        return pltpu.make_async_copy(src.at[own_rows(0, c)], dst.at[c % 2], sem.at[c % 2])

    wide_loads = [
        pltpu.make_async_copy(src, dst, w_sem.at[i])
        for i, (src, dst) in enumerate(((wg_hbm, wg), (wu_hbm, wu)))
    ]

    def remote(src, dst, send_sem, recv_sem, peer):
        return pltpu.make_async_remote_copy(
            src_ref=src, dst_ref=dst, send_sem=send_sem, recv_sem=recv_sem,
            device_id={"tensor": peer}, device_id_type=MESH)

    def core_copy(c):
        return remote(cs.at[c % 2], crecv.at[c], cs_sem.at[c], cr_sem.at[c], sibling)

    def x_copy(c):
        return remote(xs.at[c], xr.at[c], xs_sem.at[c], xr_sem.at[c], across)

    def hidden_copy(c):
        return remote(xr.at[c], ag.at[c % 2], as_sem.at[c], ar_sem.at[c], sibling)

    def core2_copy(c):
        return remote(cs.at[c % 2], crecv.at[c], cs2_sem.at[c], cr2_sem.at[c], sibling)

    def x2_copy(c):
        return remote(xs.at[c], xr2.at[c], xs2_sem.at[c], xr2_sem.at[c], across)

    def grad_copy(c):
        return remote(xr2.at[c], ag.at[c % 2], gs_sem.at[c], gr_sem.at[c], sibling)

    def out_copy(c):
        return remote(xr.at[c], crecv.at[c], os_sem.at[c], or_sem.at[c], sibling)

    def rows(first):
        return pl.ds(first, chunk)

    def side_copies(buf, dst, sem, c):
        return [
            pltpu.make_async_copy(
                buf.at[pl.ds(s * chunk, chunk)], dst.at[rows(s * half + c * chunk)], sem.at[s])
            for s in range(2)
        ]

    def turned_copies(buf, dst, sem, c):
        return [
            pltpu.make_async_copy(
                buf.at[:, pl.ds(s * chunk, chunk)], dst.at[:, rows(s * half + c * chunk)], sem.at[s])
            for s in range(2)
        ]

    def square_copy(c):
        return remote(
            squares.at[c], squares_in.at[0, c], sq_s_sem.at[c], sq_r_sem.at[c], sibling)

    def square_x_copy(c):
        return remote(
            squares.at[c], squares_in.at[1, c], sx_s_sem.at[c], sx_r_sem.at[c], across)

    def square_pass_on(c):
        square_copy(c).wait()
        squares[c] += squares_in[0, c]
        square_x_copy(c).start()

    def projections(weights, tok, query_raw, key_raw, value, value_turned):
        def tok_load(c):
            return pltpu.make_async_copy(
                tok_hbm.at[pl.ds(c * both, both)], tok.at[c % 2], t_sem.at[c % 2])

        loads = [
            pltpu.make_async_copy(w, weights.at[i], a_sem.at[i])
            for i, w in enumerate((wq_hbm, wk_hbm, wv_hbm))
        ]
        tok_load(0).start()
        start(loads)
        tok_load(1).start()
        greet({"tensor": sibling}, {"tensor": across})
        lanes = lax.broadcasted_iota(jnp.int32, (both, HEAD), 1)
        for c in range(ROW_CHUNKS):
            at = slice(c * both, (c + 1) * both)
            tok_load(c).wait()
            if c == 0:
                loads[0].wait()
            query_raw[at, :] = jnp.dot(tok[c % 2], weights[0], preferred_element_type=F32)
            if c == 0:
                loads[1].wait()
            key_raw[at, :] = jnp.dot(tok[c % 2], weights[1], preferred_element_type=F32)
            query_square = jnp.sum(query_raw[at, :] * query_raw[at, :], axis=1, keepdims=True)
            key_square = jnp.sum(key_raw[at, :] * key_raw[at, :], axis=1, keepdims=True)
            squares[c] = jnp.where(lanes == 0, query_square, key_square)
            square_copy(c).start()
            if c == 0:
                loads[2].wait()
                start(wide_loads)
            value[at, :] = jnp.dot(tok[c % 2], weights[2], preferred_element_type=F32).astype(BF16)
            value_turned[:, at] = value[at, :].T
            if c + 2 < ROW_CHUNKS:
                tok_load(c + 2).start()
            if c >= 1:
                square_pass_on(c - 1)
        square_pass_on(last)

    def attend(c, query_raw, key_raw, query, key, value_turned, cosine, sine, w_out, mixed, bias):
        first, keys = c * both, (c + 1) * both
        at = slice(first, keys)
        square_x_copy(c).wait()
        squares[c] += squares_in[1, c]
        inverse = lax.rsqrt(squares[c] / width + EPSILON)
        inverse_out[at, :] = inverse
        for raw, gain, lane, dst in (
            (query_raw, query_gain, 0, query), (key_raw, key_gain, 1, key)):
            gains = gain[...].astype(F32)
            for h in range(heads):
                cols = slice(h * HEAD, (h + 1) * HEAD)
                normed = raw[at, cols] * inverse[:, lane : lane + 1] * gains[h : h + 1, :]
                turned = normed * cosine[at, :] + pltpu.roll(normed, HEAD // 2, 1) * sine[at, :]
                dst[at, cols] = turned.astype(BF16)
        key_at = lax.broadcasted_iota(jnp.int32, (keys, both), 0)
        query_at = lax.broadcasted_iota(jnp.int32, (keys, both), 1) + first
        allowed = (
            (seg_live[0:keys, 0:1] == seg_row[:, at])
            & (key_at <= query_at)
            & ((seg_live[0:keys, 1:2] > 0) | (key_at == query_at)))
        bias[0:keys, :] = jnp.where(allowed, 0.0, NEG_FILL)

        def head(h, carry):
            cols = pl.ds(pl.multiple_of(h * HEAD, HEAD), HEAD)
            scores = lax.dot_general(
                key[0:keys, cols], query[at, cols], nt, preferred_element_type=F32) * HEAD ** (-0.5)
            scores = scores + bias[0:keys, :]
            top = jnp.max(scores, axis=0, keepdims=True)
            powers = jnp.exp(scores - top)
            total = jnp.sum(powers, axis=0, keepdims=True)
            prob = (powers / total).astype(BF16)
            log_out[pl.ds(h, 1), at] = top + jnp.log(total)
            turned = jnp.dot(value_turned[cols, 0:keys], prob, preferred_element_type=F32)
            mixed[c % 2, :, cols] = turned.T.astype(BF16)
            return carry
        lax.fori_loop(0, heads, head, 0)

        def mixed_rows(s):
            return pl.ds(pl.multiple_of(jnp.where(core == s, 0, chunk), chunk), chunk)
        if c >= 2:
            core_copy(c - 2).wait_send()
        cs[c % 2] = jnp.dot(mixed[c % 2, mixed_rows(1), :], w_out[...], preferred_element_type=F32)
        core_copy(c).start()
        xs[c] = jnp.dot(mixed[c % 2, mixed_rows(0), :], w_out[...], preferred_element_type=F32)
        start(mixed_copies(c, mixed))
        if c >= 1:
            pass_on(c - 1)

    def mixed_copies(c, mixed):
        return [
            pltpu.make_async_copy(
                mixed.at[c % 2, pl.ds(pl.multiple_of(jnp.where(core == s, 0, chunk), chunk), chunk)],
                mixed_out.at[rows(s * half + c * chunk)], m_sem.at[c % 2, s])
            for s in range(2)
        ]

    def pass_on(c):
        core_copy(c).wait_recv()
        xs[c] += crecv[c]
        x_copy(c).start()

    def attention(query_raw, key_raw, query, key, value, value_turned, cosine, sine, w_out):
        tables = [
            pltpu.make_async_copy(src, dst, r_sem.at[i])
            for i, (src, dst) in enumerate(((cos_hbm, cosine), (sin_hbm, sine), (wo_hbm, w_out)))
        ]
        start(tables)
        pl.run_scoped(
            functools.partial(
                projections, query_raw=query_raw, key_raw=key_raw, value=value,
                value_turned=value_turned),
            pltpu.VMEM((3,) + wq_hbm.shape, BF16), pltpu.VMEM((2, both, width), BF16))
        finish(tables)
        results = [
            pltpu.make_async_copy(src, dst, a_sem.at[i])
            for i, (src, dst) in enumerate((
                (value, value_out), (query_raw, query_raw_out), (key_raw, key_raw_out),
                (query, query_out), (key, key_out)))
        ]
        start(results[:3])

        def chunks(mixed, bias):
            for c in range(ROW_CHUNKS):
                if c >= 2:
                    finish(mixed_copies(c - 2, mixed))
                attend(
                    c, query_raw, key_raw, query, key, value_turned, cosine, sine, w_out, mixed, bias)
            start(results[3:])
            pass_on(last)
            for c in range(last - 1, ROW_CHUNKS):
                core_copy(c).wait_send()
                finish(mixed_copies(c, mixed))
            finish(results)
        pl.run_scoped(
            chunks, pltpu.VMEM((2, both, head_cols), BF16), pltpu.VMEM((full, both), F32))

    rows_of = (full, head_cols)
    pl.run_scoped(
        attention, pltpu.VMEM(rows_of, F32), pltpu.VMEM(rows_of, F32), pltpu.VMEM(rows_of, BF16),
        pltpu.VMEM(rows_of, BF16), pltpu.VMEM(rows_of, BF16), pltpu.VMEM((head_cols, full), BF16),
        pltpu.VMEM((full, HEAD), F32), pltpu.VMEM((full, HEAD), F32), pltpu.VMEM(wo_hbm.shape, BF16))
    pl.run_scoped(
        functools.partial(
            feed_forward, core, chunk, own_rows, row_load, rows, side_copies, turned_copies,
            (x_copy, hidden_copy, core2_copy, x2_copy, grad_copy, out_copy), wide_loads, seg_live,
            (tok_hbm, cot_hbm, wd_hbm, attn_gain, mlp_gain, wg, wu),
            (gate_out, up_out, inner_out, hlt_out, gdr_out, gdrt_out, branch_out, out_out, gain_out),
            (cs, crecv, xs, xr, xr2, ag),
            (w_sem, t_sem, s_sem, g_sem, h_sem, b_sem, d_sem, o_sem)),
        pltpu.VMEM(wd_hbm.shape, BF16), pltpu.VMEM((both, hidden), F32), pltpu.VMEM((both, hidden), F32),
        pltpu.VMEM((both, hidden), BF16), pltpu.VMEM((both, width), BF16), pltpu.VMEM((width, both), BF16),
        pltpu.VMEM((both, width), BF16), pltpu.VMEM((2, chunk, width), BF16),
        pltpu.VMEM((2, chunk, width), BF16))


def feed_forward(
    core, chunk, own_rows, row_load, rows, side_copies, turned_copies, remote_copies, wide_loads, seg_live,
    operands, results, buffers, sems,
    wd, gate_buf, up_buf, inner_buf, low_buf, hlt_buf, out_buf, tok, seed,
):
    x_copy, hidden_copy, core2_copy, x2_copy, grad_copy, out_copy = remote_copies
    tok_hbm, cot_hbm, wd_hbm, attn_gain, mlp_gain, wg, wu = operands
    gate_out, up_out, inner_out, hlt_out, gdr_out, gdrt_out, branch_out, out_out, gain_out = results
    cs, crecv, xs, xr, xr2, ag = buffers
    w_sem, t_sem, s_sem, g_sem, h_sem, b_sem, d_sem, o_sem = sems
    last = ROW_CHUNKS - 1
    tiles, wide_tiles = wg.shape[1] // TILE, wd.shape[1] // TILE
    loads = wide_loads + [pltpu.make_async_copy(wd_hbm, wd, w_sem.at[2])]
    loads[2].start()
    for c in range(2):
        row_load(c, tok_hbm, tok, t_sem).start()
        row_load(c, cot_hbm, seed, s_sem).start()

    def feed(c):
        x_copy(c).wait()
        total = xs[c] + xr[c]
        xs[c] = total
        branch_copy = pltpu.make_async_copy(xs.at[c], branch_out.at[rows(c * chunk)], b_sem)
        branch_copy.start()
        row_load(c, tok_hbm, tok, t_sem).wait()
        hidden = tok[c % 2].astype(F32) + total * mean_inverse(total) * attn_gain[...]
        if c + 2 < ROW_CHUNKS:
            row_load(c + 2, tok_hbm, tok, t_sem).start()
        xr[c] = hidden
        hidden_copy(c).start()
        low_buf[0:chunk, :] = hidden.astype(BF16)
        if c >= 1:
            for copy in turned_copies(hlt_buf, hlt_out, h_sem, c - 1):
                copy.wait()
            for buf, dst, i in ((gate_buf, gate_out, 0), (up_buf, up_out, 1), (inner_buf, inner_out, 2)):
                for copy in side_copies(buf, dst, g_sem.at[i], c - 1):
                    copy.wait()
        hlt_buf[:, 0:chunk] = hidden.astype(BF16).T
        hidden_copy(c).wait_recv()
        low_buf[chunk : 2 * chunk, :] = ag[c % 2].astype(BF16)
        hlt_buf[:, chunk : 2 * chunk] = ag[c % 2].astype(BF16).T
        for copy in turned_copies(hlt_buf, hlt_out, h_sem, c):
            copy.start()
        if c == 0:
            loads[0].wait()
            loads[1].wait()

        def tile(n, carry):
            at = pl.ds(pl.multiple_of(n * TILE, TILE), TILE)
            gate = jnp.dot(low_buf[...], wg[:, at], preferred_element_type=F32)
            up = jnp.dot(low_buf[...], wu[:, at], preferred_element_type=F32)
            gate_buf[:, at] = gate
            up_buf[:, at] = up
            inner_buf[:, at] = (gate * jax.nn.sigmoid(gate) * up).astype(BF16)
            return carry
        lax.fori_loop(0, tiles, tile, 0)
        for buf, dst, i in ((gate_buf, gate_out, 0), (up_buf, up_out, 1), (inner_buf, inner_out, 2)):
            for copy in side_copies(buf, dst, g_sem.at[i], c):
                copy.start()
        if c == 0:
            loads[2].wait()
        if c >= 2:
            core2_copy(c - 2).wait_send()
        branch_copy.wait()

        def down_tile(n, carry):
            at = pl.ds(pl.multiple_of(n * TILE, TILE), TILE)
            part = jnp.dot(inner_buf[...], wd[:, at], preferred_element_type=F32)
            xs[c, :, at] = part[0:chunk]
            cs[c % 2, :, at] = part[chunk : 2 * chunk]
            return carry
        lax.fori_loop(0, wide_tiles, down_tile, 0)
        core2_copy(c).start()
        core2_copy(c).wait_recv()
        xs[c] += crecv[c]
        x2_copy(c).start()

    def finish(c, gain_total):
        x2_copy(c).wait()
        down = xs[c] + xr2[c]
        inv = mean_inverse(down)
        row_load(c, cot_hbm, seed, s_sem).wait()
        seed_rows = seed[c % 2].astype(F32) * seg_live[own_rows(0, c), 1:2].astype(F32)
        if c + 2 < ROW_CHUNKS:
            row_load(c + 2, cot_hbm, seed, s_sem).start()
        normed = down * inv
        gain_total = gain_total + column_sum(seed_rows * normed)
        scaled = seed_rows * mlp_gain[...]
        dot = jnp.sum(scaled * down, axis=1, keepdims=True)
        grad = inv * scaled - down * (inv * inv * inv * dot / down.shape[1])
        hidden_copy(c).wait_send()
        xr2[c] = grad
        grad_copy(c).start()
        xr[c] = xr[c] + normed * mlp_gain[...]
        if c == 0:
            for copy in turned_copies(hlt_buf, hlt_out, h_sem, last):
                copy.wait()
        if c >= 1:
            for copy in turned_copies(hlt_buf, gdrt_out, d_sem.at[0], c - 1):
                copy.wait()
            for copy in side_copies(low_buf, gdr_out, d_sem.at[1], c - 1):
                copy.wait()
        low_buf[0:chunk, :] = grad.astype(BF16)
        hlt_buf[:, 0:chunk] = grad.astype(BF16).T
        grad_copy(c).wait_recv()
        out_copy(c).start()
        low_buf[chunk : 2 * chunk, :] = ag[c % 2].astype(BF16)
        hlt_buf[:, chunk : 2 * chunk] = ag[c % 2].astype(BF16).T
        for copy in turned_copies(hlt_buf, gdrt_out, d_sem.at[0], c):
            copy.start()
        for copy in side_copies(low_buf, gdr_out, d_sem.at[1], c):
            copy.start()
        return gain_total

    def out_copies(c):
        return [
            pltpu.make_async_copy(
                out_buf.at[pl.ds(s * chunk, chunk)], out_out.at[own_rows(s, c)], o_sem.at[s])
            for s in range(2)
        ]

    def place(c):
        if c >= 1:
            for copy in out_copies(c - 1):
                copy.wait()
        out_buf[0:chunk, :] = xr[c].astype(BF16)
        out_copy(c).wait_recv()
        out_buf[chunk : 2 * chunk, :] = crecv[c].astype(BF16)
        for copy in out_copies(c):
            copy.start()

    for c in range(ROW_CHUNKS):
        feed(c)
    gain_total = jnp.zeros(mlp_gain.shape, F32)
    for c in range(ROW_CHUNKS):
        gain_total = finish(c, gain_total)
        if c >= 1:
            place(c - 1)
    place(last)
    gain_out[...] = gain_total
    for buf, dst, i in ((gate_buf, gate_out, 0), (up_buf, up_out, 1), (inner_buf, inner_out, 2)):
        for copy in side_copies(buf, dst, g_sem.at[i], last):
            copy.wait()
    for copy in turned_copies(hlt_buf, gdrt_out, d_sem.at[0], last):
        copy.wait()
    for copy in side_copies(low_buf, gdr_out, d_sem.at[1], last):
        copy.wait()
    for copy in out_copies(last):
        copy.wait()
    core2_copy(last - 1).wait_send()
    core2_copy(last).wait_send()
    for c in range(ROW_CHUNKS):
        grad_copy(c).wait_send()
        out_copy(c).wait_send()


def forward_layer(hbm, vmem_args):
    tokens, w_query, w_gate = hbm[0], hbm[2], hbm[6]
    row_count, width = tokens.shape
    hidden, head_cols = w_gate.shape[1], w_query.shape[1]
    chunk = row_count // 2 // ROW_CHUNKS
    DMA = pltpu.SemaphoreType.DMA
    vmem, any_space = pl.BlockSpec(memory_space=pltpu.VMEM), pl.BlockSpec(memory_space=pl.ANY)

    def shape(*dims, kind=F32):
        return jax.ShapeDtypeStruct(dims, kind)

    per_chunk = DMA((ROW_CHUNKS,))
    return pl.pallas_call(
        forward_kernel,
        out_shape=(
            shape(row_count, hidden),
            shape(row_count, hidden),
            shape(row_count, hidden, kind=BF16),
            shape(width, row_count, kind=BF16),
            shape(row_count, width, kind=BF16),
            shape(width, row_count, kind=BF16),
            shape(row_count // 2, width),
            shape(row_count, width, kind=BF16),
            shape(row_count, head_cols, kind=BF16),
            shape(row_count, head_cols, kind=BF16),
            shape(row_count, head_cols, kind=BF16),
            shape(row_count, head_cols),
            shape(row_count, head_cols),
            shape(row_count, head_cols, kind=BF16),
            shape(1, width),
            shape(row_count, HEAD),
            shape(head_cols // HEAD, row_count),
        ),
        in_specs=[any_space] * len(hbm) + [vmem] * len(vmem_args),
        out_specs=(any_space,) * 14 + (vmem,) * 3,
        scratch_shapes=[
            pltpu.VMEM(w_gate.shape, BF16),
            pltpu.VMEM(w_gate.shape, BF16),
            pltpu.VMEM((2, chunk, width), F32),
            pltpu.VMEM((ROW_CHUNKS, chunk, width), F32),
            pltpu.VMEM((ROW_CHUNKS, chunk, width), F32),
            pltpu.VMEM((ROW_CHUNKS, chunk, width), F32),
            pltpu.VMEM((ROW_CHUNKS, chunk, width), F32),
            pltpu.VMEM((2, chunk, width), F32),
            pltpu.VMEM((ROW_CHUNKS, 2 * chunk, HEAD), F32),
            pltpu.VMEM((2, ROW_CHUNKS, 2 * chunk, HEAD), F32),
            DMA((3,)),
            DMA((2,)),
            DMA((2,)),
            DMA((5,)),
            DMA((3,)),
            DMA((2, 2)),
        ]
        + [per_chunk] * 18
        + [DMA((3, 2)), DMA((2,)), DMA, DMA((2, 2)), DMA((2,))],
        compiler_params=pltpu.CompilerParams(
            collective_id=1, has_side_effects=True, vmem_limit_bytes=VMEM_LIMIT),
    )(*hbm, *vmem_args)


def backward_kernel(
    dp_size, counts,
    gdrt_hbm, hlt_hbm, tok_hbm, inner_hbm, mixed_hbm, gdr_hbm, gate_hbm, up_hbm, branch_hbm, cot_hbm,
    query_hbm, key_hbm, value_hbm, query_raw_hbm, key_raw_hbm,
    w_out_hbm, wg_hbm, wu_hbm, wd_hbm, wq_hbm, wk_hbm, wv_hbm,
    inverses, log_totals, seg_live, seg_row, cosine, sine,
    query_gain, key_gain, attn_gain, gain_mlp_part,
    turned_out, straight_out, token_out, gains_out,
    ggr_hbm, gur_hbm, gbt_hbm, gh_hbm, gqkv_hbm,
    at, bbuf, ysend, yrecv, zsend, zrecv, stage, stage_t, cs, crecv, xs, xr, ag, dots, dots_in,
    vec, vec_in,
    at_sem, b_sem, ys_sem, yr_sem, zs_sem, zr_sem, out_sem,
    cs_sem, cr_sem, xs_sem, xr_sem, as_sem, ar_sem, cs2_sem, cr2_sem, xs2_sem, xr2_sem, as2_sem,
    ar2_sem, ds_sem, dr_sem, vs_sem, vr_sem, w_sem, pre_sem, st_sem, gh_sem, tok_sem,
    y_credit, up_credit, down_credit,
):
    n_down, n_hidden, n_heads, n_out = counts
    first_heads = n_down + n_hidden
    first_out = first_heads + n_heads
    total = first_out + n_out
    line = dp_size // 2
    width = at.shape[1]
    block = width // dp_size
    chunk = xs.shape[1]
    half = chunk * ROW_CHUNKS
    full = 2 * half
    head_cols = query_hbm.shape[1]
    passes = total + total // SPAN
    dp_at = lax.axis_index("dp")
    z, y = dp_at // 2, dp_at % 2
    partner = dp_at + 1 - 2 * y
    below, above = dp_at - 2, dp_at + 2
    has_below, has_above = z > 0, z < line - 1
    core, sibling, across = tensor_peers()
    steps = [1 << s for s in range(dp_size.bit_length() - 1)]
    vec_peers = [dp_at + bit * (1 - 2 * ((dp_at // bit) % 2)) for bit in steps]

    def at_dp(i):
        return {"dp": i}

    def at_tensor(i):
        return {"tensor": i}

    barrier = pltpu.get_barrier_semaphore()

    def greet_one(peer):
        pl.semaphore_signal(barrier, inc=1, device_id=peer, device_id_type=MESH)

    other_z = z - 1 + 2 * lax.rem(z, 2)
    has_other = (other_z >= 0) & (other_z < line)
    for peer in vec_peers:
        greet_one(at_dp(peer))
    greet_one(at_tensor(sibling))
    greet_one(at_tensor(across))

    @pl.when(has_other)
    def _():
        greet_one(at_dp(2 * other_z + y))
    pl.semaphore_wait(barrier, len(steps) + 2 + has_other.astype(jnp.int32))

    def remote(src, dst, send_sem, recv_sem, peer):
        return pltpu.make_async_remote_copy(
            src_ref=src, dst_ref=dst, send_sem=send_sem, recv_sem=recv_sem,
            device_id=peer, device_id_type=MESH)

    def y_copy(p, b):
        return remote(ysend.at[p, b], yrecv.at[p, b], ys_sem.at[p, b], yr_sem.at[p, b], at_dp(partner))

    def z_copy(p, b, slot, target):
        return remote(zsend.at[p, b], zrecv.at[p, slot], zs_sem.at[p, b], zr_sem.at[p, slot], at_dp(target))

    def group_of(k):
        return (
            (k >= n_down).astype(jnp.int32)
            + (k >= first_heads).astype(jnp.int32)
            + (k >= first_out).astype(jnp.int32))

    def product(k, rows_at):
        return jnp.dot(
            at[lax.rem(group_of(k), 2), pl.ds(pl.multiple_of(rows_at * block, block), block), :],
            bbuf[lax.rem(k, B_SLOTS)], preferred_element_type=F32)

    def at_load(i):
        src = (gdrt_hbm, hlt_hbm, None, gbt_hbm)[i]
        return pltpu.make_async_copy(src, at.at[i % 2], at_sem.at[i % 2])

    def b_load(k, act):
        def columns(src, at_chunk):
            act(pltpu.make_async_copy(
                src.at[:, pl.ds(pl.multiple_of(at_chunk * COLS, COLS), COLS)],
                bbuf.at[lax.rem(k, B_SLOTS)], b_sem.at[lax.rem(k, B_SLOTS)]))
        per = n_hidden // 2

        @pl.when(k < n_down)
        def _():
            columns(inner_hbm, k)

        @pl.when((k >= n_down) & (k < n_down + per))
        def _():
            columns(ggr_hbm, k - n_down)

        @pl.when((k >= n_down + per) & (k < first_heads))
        def _():
            columns(gur_hbm, k - n_down - per)

        @pl.when((k >= first_heads) & (k < first_out))
        def _():
            columns(gqkv_hbm, k - first_heads)

        @pl.when((k >= first_out) & (k < total))
        def _():
            columns(mixed_hbm, k - first_out)

    def line_first(k):
        return lax.rem(k, SPAN) == SPAN - 1

    def walk(fn):
        def body(i, carry):
            @pl.when(z <= i)
            def _():
                fn(z + line - 1 - i, True)

            @pl.when(z >= line - 1 - i)
            def _():
                fn(z - (line - 1 - i), False)
            return carry
        lax.fori_loop(0, line - 1, body, 0)

    def pair_send(k):
        p = lax.rem(k, Y_SLOTS)

        @pl.when(k >= Y_SLOTS)
        def _():
            pl.semaphore_wait(y_credit, 1)
        b_load(k, lambda copy: copy.wait())

        @pl.when(jnp.logical_not(line_first(k)))
        def _():
            def one(b, up=None):
                ysend[p, b] = product(k, 2 * b + 1 - y)
                y_copy(p, b).start()
            walk(one)
            one(z)

    def line_send(q, k, source):
        p = lax.rem(q, 2)

        @pl.when(q >= 2)
        def _():
            @pl.when(has_above)
            def _():
                pl.semaphore_wait(up_credit, 1)

            @pl.when(has_below)
            def _():
                pl.semaphore_wait(down_credit, 1)

        def one(b, up):
            has_before, target = (has_below, above) if up else (has_above, below)
            zsend[p, b] = source(b)

            @pl.when(has_before)
            def _():
                z_copy(p, b, b, target).wait_recv()
                zsend[p, b] += zrecv[p, b]
            if up:
                z_copy(p, b, b, target).start()
            else:
                @pl.when(b == z - 1)
                def _():
                    z_copy(p, b, line, target).start()

                @pl.when(b != z - 1)
                def _():
                    z_copy(p, b, b, target).start()
        walk(one)

    def line_own(q, dst):
        p = lax.rem(q, 2)

        @pl.when(has_below)
        def _():
            z_copy(p, z, z, below).wait_recv()
            dst[...] += zrecv[p, z]

        @pl.when(has_above)
        def _():
            z_copy(p, z, line, below).wait_recv()
            dst[...] += zrecv[p, line]

        def drain(b, up):
            z_copy(p, b, b, below).wait_send()
        walk(drain)

        @pl.when(q < passes - 2)
        def _():
            @pl.when(has_below)
            def _():
                pl.semaphore_signal(up_credit, inc=1, device_id=at_dp(below), device_id_type=MESH)

            @pl.when(has_above)
            def _():
                pl.semaphore_signal(down_credit, inc=1, device_id=at_dp(above), device_id_type=MESH)

    def is_turned(k):
        return (k < n_down) | (k >= first_out)

    def out_act(k, act):
        @pl.when(is_turned(k))
        def _():
            first = jnp.where(k < n_down, k, k - first_out + n_down) * COLS
            act(pltpu.make_async_copy(
                stage_t, turned_out.at[pl.ds(pl.multiple_of(first, COLS), COLS)], out_sem))

        @pl.when(jnp.logical_not(is_turned(k)))
        def _():
            cols = pl.ds(pl.multiple_of((k - n_down) * COLS, COLS), COLS)
            act(pltpu.make_async_copy(stage, straight_out.at[:, cols], out_sem))

    def finish_chunk(k, q):
        p = lax.rem(k, Y_SLOTS)

        @pl.when(k >= 1)
        def _():
            out_act(k - 1, lambda copy: copy.wait())
        stage[...] = product(k, 2 * z + y)
        y_copy(p, z).wait_recv()
        stage[...] += yrecv[p, z]
        line_own(q, stage)

        @pl.when(is_turned(k))
        def _():
            stage_t[...] = stage[...].T
        out_act(k, lambda copy: copy.start())

        @pl.when(line_first(k))
        def _():
            y_copy(p, z).wait_send()

        @pl.when(jnp.logical_not(line_first(k)))
        def _():
            for b in range(line):
                y_copy(p, b).wait_send()

        @pl.when(k < total - Y_SLOTS)
        def _():
            pl.semaphore_signal(y_credit, inc=1, device_id=at_dp(partner), device_id_type=MESH)

    def tick(k):
        p = lax.rem(k, Y_SLOTS)
        q = k + k // SPAN
        is_line_first = line_first(k)

        @pl.when(jnp.logical_not(is_line_first))
        def _():
            def mine(b):
                part = product(k, 2 * b + y)
                y_copy(p, b).wait_recv()
                return part + yrecv[p, b]
            line_send(q, k, mine)

        @pl.when(is_line_first)
        def _():
            line_send(q, k, lambda b: product(k, 2 * b + 1 - y))

        @pl.when(k >= 1)
        def _():
            finish_chunk(k - 1, q - 1)

        @pl.when(is_line_first)
        def _():
            line_send(q + 1, k, lambda b: product(k, 2 * b + y))
            ysend[p, z] = product(k, 2 * z + 1 - y)
            line_own(q, ysend.at[p, z])
            y_copy(p, z).start()

        @pl.when(k + 2 < total)
        def _():
            pair_send(k + 2)

        @pl.when(k + 3 < total)
        def _():
            b_load(k + 3, lambda copy: copy.start())

    nt = (((1,), (1,)), ((), ()))

    def copies_of(sem, *pairs):
        return [pltpu.make_async_copy(src, dst, sem.at[i]) for i, (src, dst) in enumerate(pairs)]

    def start(copies):
        for copy in copies:
            copy.start()

    def finish(copies):
        for copy in copies:
            copy.wait()

    def run_ticks(first, last, work):
        def body(k, carry):
            tick(k)
            for when, fn in work.items():
                low, high = when if isinstance(when, tuple) else (when, when + 1)

                @pl.when((k >= low) & (k < high))
                def _(fn=fn, low=low):
                    if isinstance(fn, list):
                        for one in fn:
                            one()
                    elif low + 1 == high:
                        fn()
                    else:
                        fn(k - low)
            return carry
        lax.fori_loop(first, last, body, 0)

    def part(fn, *args):
        return functools.partial(fn, *args)

    def side_rows(s, c):
        return pl.ds(s * half + c * chunk, chunk)

    def both_sides(hbm, buf, c, out=False):
        pairs = [(hbm.at[side_rows(s, c)], buf.at[pl.ds(s * chunk, chunk)]) for s in range(2)]
        return [(b, a) for a, b in pairs] if out else pairs

    def sequence_rows(s, c):
        return pl.ds(pl.multiple_of(2 * c * chunk + jnp.where(core == s, 0, chunk), chunk), chunk)

    def core_copy(c, again):
        ss, rs = (cs2_sem, cr2_sem) if again else (cs_sem, cr_sem)
        return remote(cs.at[c % 2], crecv.at[c], ss.at[c], rs.at[c], at_tensor(sibling))

    def x_copy(c, again):
        ss, rs = (xs2_sem, xr2_sem) if again else (xs_sem, xr_sem)
        return remote(xs.at[c], xr.at[c], ss.at[c], rs.at[c], at_tensor(across))

    def to_sibling(c, again):
        ss, rs = (as2_sem, ar2_sem) if again else (as_sem, ar_sem)
        return remote(xr.at[c], ag.at[c % 2], ss.at[c], rs.at[c], at_tensor(sibling))

    def pass_on(c, again):
        core_copy(c, again).wait_recv()
        xs[c] += crecv[c]
        x_copy(c, again).start()
        core_copy(c, again).wait_send()

    hidden = wd_hbm.shape[0]

    def feed_phase(wd, grads, gates, ups, ggr, gur):
        def loads(c):
            return copies_of(
                pre_sem, *both_sides(gdr_hbm, grads, c), *both_sides(gate_hbm, gates, c),
                *both_sides(up_hbm, ups, c))

        def stores(c):
            return copies_of(
                st_sem, *both_sides(ggr_hbm, ggr, c, True), *both_sides(gur_hbm, gur, c, True))

        def piece(c):
            finish(loads(c))
            if c >= 1:
                finish(stores(c - 1))

            def tile(n, carry):
                cols = pl.ds(pl.multiple_of(n * TILE, TILE), TILE)
                grad = lax.dot_general(grads[...], wd[cols, :], nt, preferred_element_type=F32)
                gate = gates[:, cols]
                sig = jax.nn.sigmoid(gate)
                act = gate * sig
                ggr[:, cols] = (grad * ups[:, cols] * (sig + act * (1.0 - sig))).astype(BF16)
                gur[:, cols] = (grad * act).astype(BF16)
                return carry
            lax.fori_loop(0, hidden // TILE, tile, 0)
            start(stores(c))
            if c + 1 < ROW_CHUNKS:
                start(loads(c + 1))

        load_weight = copies_of(w_sem, (wd_hbm, wd))
        start(load_weight)
        start(loads(0))
        at_load(0).wait()
        pair_send(jnp.int32(0))
        pair_send(jnp.int32(1))
        finish(load_weight)
        piece(0)
        run_ticks(0, FEED_TICK, {c - 1: part(piece, c) for c in range(1, ROW_CHUNKS)})
        finish(stores(ROW_CHUNKS - 1))

    def hidden_phase(weights, ggr, gur):
        load_weights = copies_of(w_sem, (wg_hbm, weights.at[0]), (wu_hbm, weights.at[1]))

        def loads(c):
            return copies_of(pre_sem, *both_sides(ggr_hbm, ggr, c), *both_sides(gur_hbm, gur, c))

        def piece(c):
            if c == 0:
                finish(load_weights)
            else:
                pass_on(c - 1, False)
            finish(loads(c))

            def tile(n, carry):
                rows = pl.ds(pl.multiple_of(n * TILE, TILE), TILE)
                total_part = lax.dot_general(ggr[...], weights[0, rows, :], nt, preferred_element_type=F32)
                total_part = total_part + lax.dot_general(
                    gur[...], weights[1, rows, :], nt, preferred_element_type=F32)
                xs[c, :, rows] = total_part[0:chunk]
                cs[c % 2, :, rows] = total_part[chunk : 2 * chunk]
                return carry
            lax.fori_loop(0, width // TILE, tile, 0)
            core_copy(c, False).start()
            if c + 1 < ROW_CHUNKS:
                start(loads(c + 1))

        start(load_weights)
        start(loads(0))
        run_ticks(
            FEED_TICK, HIDDEN_TICK, {FEED_TICK + c: part(piece, c) for c in range(ROW_CHUNKS)})

    def branch_phase(branch, seed, low, turned, w_out, mixed_grad, token_rows):
        load_weight = copies_of(w_sem, (w_out_hbm, w_out))
        token_piece = full // ROW_CHUNKS

        def loads(c):
            rows = pl.ds(c * chunk, chunk)
            return copies_of(
                pre_sem, (branch_hbm.at[rows], branch), (cot_hbm.at[sequence_rows(0, c)], seed))

        def stores(c):
            i = c % 2
            return copies_of(
                st_sem.at[pl.ds(4 * i, 4)],
                (turned.at[i, :, pl.ds(0, chunk)], gbt_hbm.at[:, side_rows(0, c)]),
                (turned.at[i, :, pl.ds(chunk, chunk)], gbt_hbm.at[:, side_rows(1, c)]),
                *[(
                    mixed_grad.at[i, pl.ds(s * chunk, chunk)],
                    gqkv_hbm.at[sequence_rows(s, c), pl.ds(2 * head_cols, head_cols)],
                ) for s in range(2)])

        def hidden_store(c):
            return copies_of(gh_sem, (xs.at[c], gh_hbm.at[pl.ds(c * chunk, chunk)]))

        def token_load(c):
            return copies_of(tok_sem, (tok_hbm.at[pl.ds(c * token_piece, token_piece)], token_rows))

        def first(c):
            i = c % 2
            finish(loads(c))
            x_copy(c, False).wait()
            live = seg_live[sequence_rows(0, c), 1:2].astype(F32)
            grad_hidden = xs[c] + xr[c] + seed[...].astype(F32) * live
            xs[c] = grad_hidden
            start(hidden_store(c))
            values = branch[...]
            inv = mean_inverse(values)
            vec[1:2, :] += column_sum(grad_hidden * values * inv)
            scaled = grad_hidden * attn_gain[...]
            dot = jnp.sum(scaled * values, axis=1, keepdims=True)
            grad = inv * scaled - values * (inv * inv * inv * dot / width)
            xr[c] = grad
            to_sibling(c, False).start()
            if c >= 2:
                finish(stores(c - 2))
            low[i, 0:chunk, :] = grad.astype(BF16)
            turned[i, :, 0:chunk] = grad.astype(BF16).T
            if c + 1 < ROW_CHUNKS:
                start(loads(c + 1))

        def second(c):
            i = c % 2
            to_sibling(c, False).wait_recv()
            if c == 0:
                finish(load_weight)
            other = ag[i].astype(BF16)
            low[i, chunk : 2 * chunk, :] = other
            turned[i, :, chunk : 2 * chunk] = other.T
            mixed_grad[i] = lax.dot_general(
                low[i], w_out[...], nt, preferred_element_type=F32).astype(BF16)
            start(stores(c))
            finish(hidden_store(c))
            to_sibling(c, False).wait_send()

        def turn(c):
            finish(token_load(c))
            at[0, :, pl.ds(c * token_piece, token_piece)] = token_rows[...].T
            if c + 1 < ROW_CHUNKS:
                start(token_load(c + 1))

        start(load_weight)
        start(loads(0))
        start(token_load(0))
        work = {HIDDEN_TICK + c: [] for c in range(ROW_CHUNKS + 1)}
        work[HIDDEN_TICK].append(part(pass_on, ROW_CHUNKS - 1, False))
        for c in range(ROW_CHUNKS):
            work[HIDDEN_TICK + c].append(part(first, c))
            work[HIDDEN_TICK + c + 1].append(part(second, c))
        work[HIDDEN_TICK + 3] += [part(turn, 0)]
        work[HIDDEN_TICK + 4] += [part(turn, c) for c in range(1, ROW_CHUNKS)]
        run_ticks(HIDDEN_TICK, BRANCH_TICK, work)
        for c in range(ROW_CHUNKS - 2, ROW_CHUNKS):
            finish(stores(c))

    def attention_phase(query, key, value, mixed_grad, dq, dk, dv, raw, bias):
        heads = head_cols // HEAD
        q_rows = min(256, full)
        scale = HEAD ** (-0.5)
        value_cols = pl.ds(2 * head_cols, head_cols)
        loads = copies_of(
            pre_sem, (query_hbm, query), (key_hbm, key), (value_hbm, value),
            (gqkv_hbm.at[:, value_cols], mixed_grad))

        def masks():
            for i in range(full // q_rows):
                rows, keys = slice(i * q_rows, (i + 1) * q_rows), (i + 1) * q_rows
                key_at = lax.broadcasted_iota(jnp.int32, (keys, q_rows), 0)
                query_at = lax.broadcasted_iota(jnp.int32, (keys, q_rows), 1) + i * q_rows
                allowed = (
                    (seg_live[0:keys, 0:1] == seg_row[:, rows])
                    & (key_at <= query_at)
                    & ((seg_live[0:keys, 1:2] > 0) | (key_at == query_at)))
                bias[0:keys, rows] = jnp.where(allowed, 0.0, NEG_FILL)
            finish(loads)

        def head(h):
            cols = pl.ds(pl.multiple_of(h * HEAD, HEAD), HEAD)
            dk[:, cols] = jnp.zeros((full, HEAD), F32)
            dv[...] = jnp.zeros((full, HEAD), F32)
            for i in range(full // q_rows):
                rows, keys = slice(i * q_rows, (i + 1) * q_rows), (i + 1) * q_rows
                q_block, grad_block = query[rows, cols], mixed_grad[rows, cols]
                key_block, value_block = key[0:keys, cols], value[0:keys, cols]
                scores = lax.dot_general(key_block, q_block, nt, preferred_element_type=F32) * scale
                prob = jnp.exp(scores + bias[0:keys, rows] - log_totals[pl.ds(h, 1), rows])
                grad_prob = lax.dot_general(value_block, grad_block, nt, preferred_element_type=F32)
                row_dot = jnp.sum(prob * grad_prob, axis=0, keepdims=True)
                grad_scores = (prob * (grad_prob - row_dot)).astype(BF16)
                dq[rows, cols] = lax.dot_general(
                    grad_scores, key_block, (((0,), (0,)), ((), ())), preferred_element_type=F32) * scale
                dk[0:keys, cols] += jnp.dot(grad_scores, q_block, preferred_element_type=F32) * scale
                dv[0:keys, :] += jnp.dot(prob.astype(BF16), grad_block, preferred_element_type=F32)
            mixed_grad[:, cols] = dv[...].astype(BF16)

        store_value = copies_of(st_sem, (mixed_grad, gqkv_hbm.at[:, value_cols]))
        sides = ((dq, query_raw_hbm, query_gain), (dk, key_raw_hbm, key_gain))

        def load_raw(which):
            return copies_of(pre_sem, (sides[which][1], raw))

        def back(which):
            grads, _, gain = sides[which]
            finish(load_raw(which))
            gains = gain[...].astype(F32)
            lanes = lax.broadcasted_iota(jnp.int32, (q_rows, HEAD), 1)

            def block_back(i, carry):
                rows = pl.ds(pl.multiple_of(i * q_rows, q_rows), q_rows)
                dot = jnp.zeros((q_rows, 1), F32)
                for h in range(heads):
                    cols = slice(h * HEAD, (h + 1) * HEAD)
                    grad = grads[rows, cols]
                    grad = grad * cosine[rows, :] - pltpu.roll(grad, HEAD // 2, 1) * sine[rows, :]
                    raw_rows = raw[rows, cols]
                    gain_cols = slice(which * head_cols + h * HEAD, which * head_cols + (h + 1) * HEAD)
                    vec[2:3, gain_cols] += column_sum(
                        grad * raw_rows * inverses[rows, which : which + 1])
                    scaled = grad * gains[h : h + 1, :]
                    grads[rows, cols] = scaled
                    dot = dot + jnp.sum(scaled * raw_rows, axis=1, keepdims=True)
                if which == 0:
                    dots[rows, :] = jnp.broadcast_to(dot, (q_rows, HEAD))
                else:
                    dots[rows, :] = jnp.where(lanes == 0, dots[rows, :], dot)
                return carry
            lax.fori_loop(0, full // q_rows, block_back, 0)

        def dots_copy(i):
            return remote(
                dots, dots_in.at[i], ds_sem.at[i], dr_sem.at[i], at_tensor((sibling, across)[i]))

        def dots_add(i):
            dots_copy(i).wait()
            dots[...] += dots_in[i]

        def combine(which):
            grads = sides[which][0]
            for i in range(full // q_rows):
                rows = slice(i * q_rows, (i + 1) * q_rows)
                inv_rows = inverses[rows, which : which + 1]
                dot = dots[rows, which : which + 1]
                mixed_grad[rows, :] = (
                    inv_rows * grads[rows, :]
                    - raw[rows, :] * (inv_rows * inv_rows * inv_rows * dot / width)
                ).astype(BF16)

        def store_grads(which):
            return copies_of(
                st_sem, (mixed_grad, gqkv_hbm.at[:, pl.ds(which * head_cols, head_cols)]))

        def after_heads():
            start(store_value)
            start(load_raw(0))

        def back_query():
            back(0)
            start(load_raw(1))

        def back_key():
            back(1)
            dots_copy(0).start()
            finish(store_value)

        def first_sum():
            dots_add(0)
            dots_copy(1).start()

        def second_sum():
            dots_add(1)
            combine(1)
            start(store_grads(1))
            start(load_raw(0))

        def last_part():
            finish(store_grads(1))
            finish(load_raw(0))
            combine(0)
            start(store_grads(0))

        start(loads)
        t = BRANCH_TICK
        run_ticks(t, INPUT_TICK, {
            t: masks,
            (t + 1, t + 1 + heads): head,
            t + heads: after_heads,
            t + heads + 1: back_query,
            t + heads + 2: back_key,
            t + heads + 3: first_sum,
            t + heads + 4: [second_sum, last_part],
        })
        finish(store_grads(0))

    def input_phase(weights, grads, grad_hidden, low):
        loads = copies_of(
            w_sem, *[(w, weights.at[i]) for i, w in enumerate((wq_hbm, wk_hbm, wv_hbm))],
            (gqkv_hbm, grads))

        def piece(c):
            if c == 0:
                finish(loads)
            else:
                pass_on(c - 1, True)
            for s in range(2):
                rows = sequence_rows(s, c)

                def tile(n, carry):
                    cols = pl.ds(pl.multiple_of(n * TILE, TILE), TILE)
                    total_part = jnp.zeros((chunk, TILE), F32)
                    for i in range(3):
                        total_part = total_part + lax.dot_general(
                            grads[rows, i * head_cols : (i + 1) * head_cols], weights[i, cols, :],
                            nt, preferred_element_type=F32)
                    if s == 0:
                        xs[c, :, cols] = total_part
                    else:
                        cs[c % 2, :, cols] = total_part
                    return carry
                lax.fori_loop(0, width // TILE, tile, 0)
            core_copy(c, True).start()

        def hidden_load(c):
            return copies_of(gh_sem, (gh_hbm.at[pl.ds(c * chunk, chunk)], grad_hidden))

        def stores(c):
            return copies_of(
                st_sem, *[(low.at[s], token_out.at[sequence_rows(s, c)]) for s in range(2)])

        def first(c):
            finish(hidden_load(c))
            x_copy(c, True).wait()
            xr[c] = xs[c] + xr[c] + grad_hidden[...]
            to_sibling(c, True).start()
            if c + 1 < ROW_CHUNKS:
                start(hidden_load(c + 1))

        def second(c):
            if c >= 1:
                finish(stores(c - 1))
            low[0] = xr[c].astype(BF16)
            to_sibling(c, True).wait_recv()
            low[1] = ag[c % 2].astype(BF16)
            start(stores(c))
            to_sibling(c, True).wait_send()

        vec_peer_ids = [at_tensor(sibling)] + [at_dp(peer) for peer in vec_peers]

        def vec_copy(i):
            return remote(vec, vec_in.at[i], vs_sem.at[i], vr_sem.at[i], vec_peer_ids[i])

        def vec_step(i):
            if i >= 1:
                vec_copy(i - 1).wait()
                if i == 1:
                    vec[0:2, :] += vec_in[0, 0:2, :]
                else:
                    vec[...] += vec_in[i - 1]
            if i < len(vec_peer_ids):
                vec_copy(i).start()

        start(loads)
        start(hidden_load(0))
        work = {k: [] for k in range(INPUT_TICK, total)}
        for c in range(ROW_CHUNKS):
            work[INPUT_TICK + c].append(part(piece, c))
            work[TOKEN_TICK + c].append(part(first, c))
            work[TOKEN_TICK + c + 1].append(part(second, c))
        work[INPUT_TICK + ROW_CHUNKS].append(part(pass_on, ROW_CHUNKS - 1, True))
        for i in range(len(vec_peer_ids) + 1):
            work[INPUT_TICK + 2 + i].append(part(vec_step, i))
        work[first_heads + 1].append(lambda: at_load(3).start())
        work[first_heads + 2].append(lambda: at_load(3).wait())
        run_ticks(INPUT_TICK, total, {k: fns for k, fns in work.items() if fns})
        finish(stores(ROW_CHUNKS - 1))

    vec[...] = jnp.zeros(vec.shape, F32)
    vec[0:1, :] = gain_mlp_part[...]
    at_load(0).start()
    at_load(1).start()
    for k in range(3):
        b_load(jnp.int32(k), lambda copy: copy.start())
    both = 2 * chunk
    rows_of = (full, head_cols)
    pl.run_scoped(
        feed_phase, pltpu.VMEM(wd_hbm.shape, BF16), pltpu.VMEM((both, width), BF16),
        pltpu.VMEM((both, hidden), F32), pltpu.VMEM((both, hidden), F32),
        pltpu.VMEM((both, hidden), BF16), pltpu.VMEM((both, hidden), BF16))
    at_load(1).wait()
    pl.run_scoped(
        hidden_phase, pltpu.VMEM((2,) + wg_hbm.shape, BF16), pltpu.VMEM((both, hidden), BF16),
        pltpu.VMEM((both, hidden), BF16))
    pl.run_scoped(
        branch_phase, pltpu.VMEM((chunk, width), F32), pltpu.VMEM((chunk, width), BF16),
        pltpu.VMEM((2, both, width), BF16), pltpu.VMEM((2, width, both), BF16),
        pltpu.VMEM(w_out_hbm.shape, BF16), pltpu.VMEM((2, both, head_cols), BF16),
        pltpu.VMEM((full // ROW_CHUNKS, width), BF16))
    pl.run_scoped(
        attention_phase, pltpu.VMEM(rows_of, BF16), pltpu.VMEM(rows_of, BF16), pltpu.VMEM(rows_of, BF16),
        pltpu.VMEM(rows_of, BF16), pltpu.VMEM(rows_of, F32), pltpu.VMEM(rows_of, F32),
        pltpu.VMEM((full, HEAD), F32), pltpu.VMEM(rows_of, F32), pltpu.VMEM((full, full), F32))
    pl.run_scoped(
        input_phase, pltpu.VMEM((3,) + wq_hbm.shape, BF16), pltpu.VMEM((full, 3 * head_cols), BF16),
        pltpu.VMEM((chunk, width), F32), pltpu.VMEM((2, chunk, width), BF16))
    finish_chunk(jnp.int32(total - 1), jnp.int32(passes - 1))
    out_act(jnp.int32(total - 1), lambda copy: copy.wait())
    gains_out[...] = vec[...]


def backward_layer(dp_size, hbm, vmem_args):
    names = dict(zip(HBM_NAMES, hbm, strict=True))
    width, row_count = names["gdrt"].shape
    hidden, head_cols = names["inner"].shape[1], names["query"].shape[1]
    line, block = dp_size // 2, width // dp_size
    chunk = row_count // 2 // ROW_CHUNKS
    counts = (hidden // COLS, 2 * hidden // COLS, 3 * head_cols // COLS, head_cols // COLS)
    DMA, REG = pltpu.SemaphoreType.DMA, pltpu.SemaphoreType.REGULAR
    vmem, any_space = pl.BlockSpec(memory_space=pltpu.VMEM), pl.BlockSpec(memory_space=pl.ANY)

    def shape(*dims, kind=F32):
        return jax.ShapeDtypeStruct(dims, kind)

    slot = (block, COLS)
    per_chunk = DMA((ROW_CHUNKS,))
    steps = dp_size.bit_length() - 1
    results = pl.pallas_call(
        functools.partial(backward_kernel, dp_size, counts),
        out_shape=(
            shape((counts[0] + counts[3]) * COLS, block),
            shape(block, (counts[1] + counts[2]) * COLS),
            shape(row_count, width, kind=BF16),
            shape(8, width),
            shape(row_count, hidden, kind=BF16),
            shape(row_count, hidden, kind=BF16),
            shape(width, row_count, kind=BF16),
            shape(row_count // 2, width),
            shape(row_count, 3 * head_cols, kind=BF16),
        ),
        in_specs=[any_space] * len(hbm) + [vmem] * len(vmem_args),
        out_specs=(any_space,) * 3 + (vmem,) + (any_space,) * 5,
        scratch_shapes=[
            pltpu.VMEM((2, width, row_count), BF16),
            pltpu.VMEM((B_SLOTS, row_count, COLS), BF16),
            pltpu.VMEM((Y_SLOTS, line) + slot, F32),
            pltpu.VMEM((Y_SLOTS, line) + slot, F32),
            pltpu.VMEM((2, line) + slot, F32),
            pltpu.VMEM((2, line + 1) + slot, F32),
            pltpu.VMEM(slot, F32),
            pltpu.VMEM((COLS, block), F32),
            pltpu.VMEM((2, chunk, width), F32),
            pltpu.VMEM((ROW_CHUNKS, chunk, width), F32),
            pltpu.VMEM((ROW_CHUNKS, chunk, width), F32),
            pltpu.VMEM((ROW_CHUNKS, chunk, width), F32),
            pltpu.VMEM((2, chunk, width), F32),
            pltpu.VMEM((row_count, HEAD), F32),
            pltpu.VMEM((2, row_count, HEAD), F32),
            pltpu.VMEM((8, width), F32),
            pltpu.VMEM((steps + 1, 8, width), F32),
            DMA((2,)),
            DMA((B_SLOTS,)),
            DMA((Y_SLOTS, line)),
            DMA((Y_SLOTS, line)),
            DMA((2, line)),
            DMA((2, line + 1)),
            DMA,
        ]
        + [per_chunk] * 12
        + [DMA((2,)), DMA((2,)), DMA((steps + 1,)), DMA((steps + 1,)), DMA((4,)), DMA((6,)), DMA((8,)), DMA((1,)), DMA((1,)),
           REG, REG, REG],
        compiler_params=pltpu.CompilerParams(
            collective_id=2, has_side_effects=True, vmem_limit_bytes=VMEM_LIMIT),
    )(*hbm, *vmem_args)
    return results[:4]


def rope_tables():
    half_size = HEAD // 2
    freq_row = ROPE_BASE ** (-(jnp.arange(half_size, dtype=F32) * 2.0) / HEAD)
    angle = jnp.arange(LENGTH, dtype=F32)[:, None] * freq_row[None, :]
    cosine, sine = jnp.cos(angle), jnp.sin(angle)
    return jnp.concatenate((cosine, cosine), 1), jnp.concatenate((-sine, sine), 1)


def make_shards(dp_size):
    def shards(
        tokens,
        segments,
        pad_mask,
        w_query,
        w_key,
        w_value,
        w_out,
        gain_query,
        gain_key,
        gain_attn,
        w_gate,
        w_up,
        w_down,
        gain_mlp,
        cotangent,
    ):
        block = tokens.shape[1] // dp_size
        cosine, sine = rope_tables()
        seg_live = jnp.stack((segments, pad_mask), 1)
        seg_row = segments[None, :]
        attn_gain = gain_attn.astype(F32)[None, :]
        mlp_gain = gain_mlp.astype(F32)[None, :]
        (
            gate_rows,
            up_rows,
            inner_rows,
            hidden_turned,
            grad_down_rows,
            grad_down_turned,
            branch_rows,
            output,
            query_norm,
            key_norm,
            value_rows,
            query_raw,
            key_raw,
            mixed_rows,
            gain_mlp_part,
            inverses,
            log_totals,
        ) = forward_layer(
            (
                tokens, cotangent, w_query, w_key, w_value, w_out, w_gate, w_up, w_down, cosine, sine,
            ),
            (seg_live, seg_row, gain_query, gain_key, attn_gain, mlp_gain),
        )
        turned, straight, grad_tokens, gains = backward_layer(
            dp_size,
            (
                grad_down_turned, hidden_turned, tokens, inner_rows, mixed_rows, grad_down_rows,
                gate_rows, up_rows, branch_rows, cotangent,
                query_norm, key_norm, value_rows, query_raw, key_raw,
                w_out, w_gate, w_up, w_down, w_query, w_key, w_value,
            ),
            (
                inverses, log_totals, seg_live, seg_row, cosine, sine,
                gain_query, gain_key, attn_gain, gain_mlp_part,
            ),
        )
        hidden, head_cols = w_gate.shape[1], w_query.shape[1]
        grad_gate, grad_up = straight[:, :hidden], straight[:, hidden : 2 * hidden]
        grad_query, grad_key, grad_value = (
            straight[:, 2 * hidden + i * head_cols : 2 * hidden + (i + 1) * head_cols]
            for i in range(3)
        )
        dp_at = lax.axis_index("dp")
        wide = lax.dynamic_slice_in_dim(gains[:2], dp_at * block, block, 1)
        head_gains = gains[2, : 2 * head_cols].reshape(2 * gain_query.shape[0], HEAD)
        head_gains = lax.dynamic_slice_in_dim(head_gains, dp_at * (HEAD // dp_size), HEAD // dp_size, 1)
        return (
            output,
            grad_tokens,
            grad_query,
            grad_key,
            grad_value,
            turned[hidden:],
            head_gains[: gain_query.shape[0]],
            head_gains[gain_query.shape[0] :],
            wide[1],
            grad_gate,
            grad_up,
            turned[:hidden],
            wide[0],
        )

    return shards


def solution(mesh):
    in_specs = (
        P("dp", None),
        P("dp"),
        P("dp"),
        P(None, "tensor"),
        P(None, "tensor"),
        P(None, "tensor"),
        P("tensor", None),
        P("tensor", None),
        P("tensor", None),
        P(),
        P(None, "tensor"),
        P(None, "tensor"),
        P("tensor", None),
        P(),
        P("dp", None),
    )
    out_specs = (
        P("dp", None),
        P("dp", None),
        P("dp", "tensor"),
        P("dp", "tensor"),
        P("dp", "tensor"),
        P("tensor", "dp"),
        P("tensor", "dp"),
        P("tensor", "dp"),
        P("dp"),
        P("dp", "tensor"),
        P("dp", "tensor"),
        P("tensor", "dp"),
        P("dp"),
    )
    shards = make_shards(mesh.shape["dp"])
    return jax.shard_map(shards, mesh=mesh, in_specs=in_specs, out_specs=out_specs, check_vma=False)
```

```python
import functools

import jax
import jax.numpy as jnp
from jax import lax
from jax.experimental import pallas as pl
from jax.experimental.pallas import tpu as pltpu
from jax.sharding import PartitionSpec as P

HEAD = 128
LENGTH = 1024
EPSILON = 1e-06
NEG_FILL = -1e30
ROPE_BASE = 500000.0
ROW_CHUNKS = 4
F32 = jnp.float32
BF16 = jnp.bfloat16


COLS = 256
LINE_FIRST = (1, 23)
Y_SLOTS = 3
B_SLOTS = 3
FEED_TICK = 3
HIDDEN_TICK = 7
BRANCH_TICK = 12
INPUT_TICK = 20
TOKEN_TICK = 25
HBM_NAMES = (
    "gdrt", "hlt", "tokens", "inner", "mixed", "gdr", "gate", "up", "branch", "cotangent",
    "query", "key", "value", "query_raw", "key_raw", "partner",
    "inverses", "seg_live", "cosine", "sine",
    "w_out", "w_gate", "w_up", "w_down", "w_query", "w_key", "w_value",
)
TILE = 512
VMEM_LIMIT = 65400 * 1024
MESH = pl.DeviceIdType.MESH

def column_sum(values):
    return jnp.sum(values, axis=0, keepdims=True)


def mean_inverse(values):
    return lax.rsqrt(jnp.mean(values * values, axis=1, keepdims=True) + EPSILON)


def tensor_peers():
    at = lax.axis_index("tensor")
    core = lax.rem(at, 2)
    return core, at + 1 - 2 * core, lax.rem(at + 2, 4)


def greet(*peers):
    barrier = pltpu.get_barrier_semaphore()
    for peer in peers:
        pl.semaphore_signal(barrier, inc=1, device_id=peer, device_id_type=MESH)
    pl.semaphore_wait(barrier, len(peers))


def forward_kernel(
    tok_hbm, cot_hbm, wq_hbm, wk_hbm, wv_hbm, wo_hbm, wg_hbm, wu_hbm, wd_hbm, cos_hbm, sin_hbm,
    seg_live, seg_row, query_gain, key_gain, attn_gain, mlp_gain,
    gate_out, up_out, inner_out, hlt_out, gdr_out, gdrt_out, branch_out, out_out,
    query_out, key_out, value_out, query_raw_out, key_raw_out, mixed_out, partner_out,
    gain_out, inverse_out, log_out,
    wg, wu, cs, crecv, xs, xr, xr2, ag, squares, squares_in,
    w_sem, t_sem, s_sem, a_sem, r_sem, m_sem, sq_s_sem, sq_r_sem, sx_s_sem, sx_r_sem,
    cs_sem, cr_sem, xs_sem, xr_sem, as_sem, ar_sem, cs2_sem, cr2_sem, xs2_sem, xr2_sem,
    gs_sem, gr_sem, os_sem, or_sem, hs_sem, hr_sem, fs_sem, fr_sem, g_sem, h_sem, b_sem, d_sem, o_sem,
):
    core, sibling, across = tensor_peers()
    dp_at = lax.axis_index("dp")
    partner = dp_at + 1 - 2 * lax.rem(dp_at, 2)
    chunk = xs.shape[1]
    half = chunk * ROW_CHUNKS
    full = 2 * half
    both = 2 * chunk
    width, hidden = xs.shape[2], wg.shape[1]
    head_cols = wq_hbm.shape[1]
    heads = head_cols // HEAD
    tiles = hidden // TILE
    wide_tiles = width // TILE
    last = ROW_CHUNKS - 1
    nt = (((1,), (1,)), ((), ()))

    def start(copies):
        for copy in copies:
            copy.start()

    def finish(copies):
        for copy in copies:
            copy.wait()

    def own_rows(s, c):
        return pl.ds(pl.multiple_of(c * both + jnp.where(core == s, 0, chunk), chunk), chunk)

    def row_load(c, src, dst, sem):
        return pltpu.make_async_copy(src.at[own_rows(0, c)], dst.at[c % 2], sem.at[c % 2])

    wide_loads = [
        pltpu.make_async_copy(src, dst, w_sem.at[i])
        for i, (src, dst) in enumerate(((wg_hbm, wg), (wu_hbm, wu)))
    ]

    def remote(src, dst, send_sem, recv_sem, peer):
        return pltpu.make_async_remote_copy(
            src_ref=src, dst_ref=dst, send_sem=send_sem, recv_sem=recv_sem,
            device_id={"tensor": peer}, device_id_type=MESH)

    def partner_copy(c):
        return pltpu.make_async_remote_copy(
            src_ref=xr.at[c], dst_ref=partner_out.at[rows(c * chunk)], send_sem=hs_sem.at[c],
            recv_sem=hr_sem.at[c], device_id={"dp": partner}, device_id_type=MESH)

    def hand_copy(c):
        return remote(
            partner_out.at[rows(c * chunk)], partner_out.at[rows(half + c * chunk)],
            fs_sem.at[c], fr_sem.at[c], sibling)

    def core_copy(c):
        return remote(cs.at[c % 2], crecv.at[c], cs_sem.at[c], cr_sem.at[c], sibling)

    def x_copy(c):
        return remote(xs.at[c], xr.at[c], xs_sem.at[c], xr_sem.at[c], across)

    def hidden_copy(c):
        return remote(xr.at[c], ag.at[c % 2], as_sem.at[c], ar_sem.at[c], sibling)

    def core2_copy(c):
        return remote(cs.at[c % 2], crecv.at[c], cs2_sem.at[c], cr2_sem.at[c], sibling)

    def x2_copy(c):
        return remote(xs.at[c], xr2.at[c], xs2_sem.at[c], xr2_sem.at[c], across)

    def grad_copy(c):
        return remote(xr2.at[c], ag.at[c % 2], gs_sem.at[c], gr_sem.at[c], sibling)

    def out_copy(c):
        return remote(xr.at[c], crecv.at[c], os_sem.at[c], or_sem.at[c], sibling)

    def rows(first):
        return pl.ds(first, chunk)

    def side_copies(buf, dst, sem, c):
        return [
            pltpu.make_async_copy(
                buf.at[pl.ds(s * chunk, chunk)], dst.at[rows(s * half + c * chunk)], sem.at[s])
            for s in range(2)
        ]

    def turned_copies(buf, dst, sem, c):
        return [
            pltpu.make_async_copy(
                buf.at[:, pl.ds(s * chunk, chunk)], dst.at[:, rows(s * half + c * chunk)], sem.at[s])
            for s in range(2)
        ]

    def square_copy(c):
        return remote(
            squares.at[c], squares_in.at[0, c], sq_s_sem.at[c], sq_r_sem.at[c], sibling)

    def square_x_copy(c):
        return remote(
            squares.at[c], squares_in.at[1, c], sx_s_sem.at[c], sx_r_sem.at[c], across)

    def square_pass_on(c):
        square_copy(c).wait()
        squares[c] += squares_in[0, c]
        square_x_copy(c).start()

    def projections(weights, tok, query_raw, key_raw, value, value_turned):
        def tok_load(c):
            return pltpu.make_async_copy(
                tok_hbm.at[pl.ds(c * both, both)], tok.at[c % 2], t_sem.at[c % 2])

        loads = [
            pltpu.make_async_copy(w, weights.at[i], a_sem.at[i])
            for i, w in enumerate((wq_hbm, wk_hbm, wv_hbm))
        ]
        tok_load(0).start()
        start(loads)
        tok_load(1).start()
        greet({"tensor": sibling}, {"tensor": across}, {"dp": partner})
        lanes = lax.broadcasted_iota(jnp.int32, (both, HEAD), 1)
        for c in range(ROW_CHUNKS):
            at = slice(c * both, (c + 1) * both)
            tok_load(c).wait()
            if c == 0:
                loads[0].wait()
            query_raw[at, :] = jnp.dot(tok[c % 2], weights[0], preferred_element_type=F32)
            if c == 0:
                loads[1].wait()
            key_raw[at, :] = jnp.dot(tok[c % 2], weights[1], preferred_element_type=F32)
            query_square = jnp.sum(query_raw[at, :] * query_raw[at, :], axis=1, keepdims=True)
            key_square = jnp.sum(key_raw[at, :] * key_raw[at, :], axis=1, keepdims=True)
            squares[c] = jnp.where(lanes == 0, query_square, key_square)
            square_copy(c).start()
            if c == 0:
                loads[2].wait()
                start(wide_loads)
            value[at, :] = jnp.dot(tok[c % 2], weights[2], preferred_element_type=F32).astype(BF16)
            value_turned[:, at] = value[at, :].T
            if c + 2 < ROW_CHUNKS:
                tok_load(c + 2).start()
            if c >= 1:
                square_pass_on(c - 1)
        square_pass_on(last)

    def attend(c, query_raw, key_raw, query, key, value_turned, cosine, sine, w_out, mixed, bias):
        first, keys = c * both, (c + 1) * both
        at = slice(first, keys)
        square_x_copy(c).wait()
        squares[c] += squares_in[1, c]
        inverse = lax.rsqrt(squares[c] / width + EPSILON)
        inverse_out[at, :] = inverse
        for raw, gain, lane, dst in (
            (query_raw, query_gain, 0, query), (key_raw, key_gain, 1, key)):
            gains = gain[...].astype(F32)
            for h in range(heads):
                cols = slice(h * HEAD, (h + 1) * HEAD)
                normed = raw[at, cols] * inverse[:, lane : lane + 1] * gains[h : h + 1, :]
                turned = normed * cosine[at, :] + pltpu.roll(normed, HEAD // 2, 1) * sine[at, :]
                dst[at, cols] = turned.astype(BF16)
        key_at = lax.broadcasted_iota(jnp.int32, (keys, both), 0)
        query_at = lax.broadcasted_iota(jnp.int32, (keys, both), 1) + first
        allowed = (
            (seg_live[0:keys, 0:1] == seg_row[:, at])
            & (key_at <= query_at)
            & ((seg_live[0:keys, 1:2] > 0) | (key_at == query_at)))
        bias[0:keys, :] = jnp.where(allowed, 0.0, NEG_FILL)

        def head(h, carry):
            cols = pl.ds(pl.multiple_of(h * HEAD, HEAD), HEAD)
            scores = lax.dot_general(
                key[0:keys, cols], query[at, cols], nt, preferred_element_type=F32) * HEAD ** (-0.5)
            scores = scores + bias[0:keys, :]
            top = jnp.max(scores, axis=0, keepdims=True)
            powers = jnp.exp(scores - top)
            total = jnp.sum(powers, axis=0, keepdims=True)
            prob = (powers / total).astype(BF16)
            log_out[pl.ds(h, 1), at] = top + jnp.log(total)
            turned = jnp.dot(value_turned[cols, 0:keys], prob, preferred_element_type=F32)
            mixed[c % 2, :, cols] = turned.T.astype(BF16)
            return carry
        lax.fori_loop(0, heads, head, 0)

        def mixed_rows(s):
            return pl.ds(pl.multiple_of(jnp.where(core == s, 0, chunk), chunk), chunk)
        if c >= 2:
            core_copy(c - 2).wait_send()
        cs[c % 2] = jnp.dot(mixed[c % 2, mixed_rows(1), :], w_out[...], preferred_element_type=F32)
        core_copy(c).start()
        xs[c] = jnp.dot(mixed[c % 2, mixed_rows(0), :], w_out[...], preferred_element_type=F32)
        start(mixed_copies(c, mixed))
        if c >= 1:
            pass_on(c - 1)

    def mixed_copies(c, mixed):
        return [
            pltpu.make_async_copy(
                mixed.at[c % 2, pl.ds(pl.multiple_of(jnp.where(core == s, 0, chunk), chunk), chunk)],
                mixed_out.at[rows(s * half + c * chunk)], m_sem.at[c % 2, s])
            for s in range(2)
        ]

    def pass_on(c):
        core_copy(c).wait_recv()
        xs[c] += crecv[c]
        x_copy(c).start()

    def attention(query_raw, key_raw, query, key, value, value_turned, cosine, sine, w_out):
        tables = [
            pltpu.make_async_copy(src, dst, r_sem.at[i])
            for i, (src, dst) in enumerate(((cos_hbm, cosine), (sin_hbm, sine), (wo_hbm, w_out)))
        ]
        start(tables)
        pl.run_scoped(
            functools.partial(
                projections, query_raw=query_raw, key_raw=key_raw, value=value,
                value_turned=value_turned),
            pltpu.VMEM((3,) + wq_hbm.shape, BF16), pltpu.VMEM((2, both, width), BF16))
        finish(tables)
        results = [
            pltpu.make_async_copy(src, dst, a_sem.at[i])
            for i, (src, dst) in enumerate((
                (value, value_out), (query_raw, query_raw_out), (key_raw, key_raw_out),
                (query, query_out), (key, key_out)))
        ]
        start(results[:3])

        def chunks(mixed, bias):
            for c in range(ROW_CHUNKS):
                if c >= 2:
                    finish(mixed_copies(c - 2, mixed))
                attend(
                    c, query_raw, key_raw, query, key, value_turned, cosine, sine, w_out, mixed, bias)
            start(results[3:])
            pass_on(last)
            for c in range(last - 1, ROW_CHUNKS):
                core_copy(c).wait_send()
                finish(mixed_copies(c, mixed))
            finish(results)
        pl.run_scoped(
            chunks, pltpu.VMEM((2, both, head_cols), BF16), pltpu.VMEM((full, both), F32))

    rows_of = (full, head_cols)
    pl.run_scoped(
        attention, pltpu.VMEM(rows_of, F32), pltpu.VMEM(rows_of, F32), pltpu.VMEM(rows_of, BF16),
        pltpu.VMEM(rows_of, BF16), pltpu.VMEM(rows_of, BF16), pltpu.VMEM((head_cols, full), BF16),
        pltpu.VMEM((full, HEAD), F32), pltpu.VMEM((full, HEAD), F32), pltpu.VMEM(wo_hbm.shape, BF16))
    pl.run_scoped(
        functools.partial(
            feed_forward, core, chunk, own_rows, row_load, rows, side_copies, turned_copies,
            (x_copy, hidden_copy, core2_copy, x2_copy, grad_copy, out_copy, partner_copy, hand_copy), wide_loads, seg_live,
            (tok_hbm, cot_hbm, wd_hbm, attn_gain, mlp_gain, wg, wu),
            (gate_out, up_out, inner_out, hlt_out, gdr_out, gdrt_out, branch_out, out_out, gain_out),
            (cs, crecv, xs, xr, xr2, ag),
            (w_sem, t_sem, s_sem, g_sem, h_sem, b_sem, d_sem, o_sem)),
        pltpu.VMEM(wd_hbm.shape, BF16), pltpu.VMEM((both, hidden), F32), pltpu.VMEM((both, hidden), F32),
        pltpu.VMEM((both, hidden), BF16), pltpu.VMEM((both, width), BF16), pltpu.VMEM((width, both), BF16),
        pltpu.VMEM((both, width), BF16), pltpu.VMEM((2, chunk, width), BF16),
        pltpu.VMEM((2, chunk, width), BF16))


def feed_forward(
    core, chunk, own_rows, row_load, rows, side_copies, turned_copies, remote_copies, wide_loads, seg_live,
    operands, results, buffers, sems,
    wd, gate_buf, up_buf, inner_buf, low_buf, hlt_buf, out_buf, tok, seed,
):
    x_copy, hidden_copy, core2_copy, x2_copy, grad_copy, out_copy, partner_copy, hand_copy = remote_copies
    tok_hbm, cot_hbm, wd_hbm, attn_gain, mlp_gain, wg, wu = operands
    gate_out, up_out, inner_out, hlt_out, gdr_out, gdrt_out, branch_out, out_out, gain_out = results
    cs, crecv, xs, xr, xr2, ag = buffers
    w_sem, t_sem, s_sem, g_sem, h_sem, b_sem, d_sem, o_sem = sems
    last = ROW_CHUNKS - 1
    tiles, wide_tiles = wg.shape[1] // TILE, wd.shape[1] // TILE
    loads = wide_loads + [pltpu.make_async_copy(wd_hbm, wd, w_sem.at[2])]
    loads[2].start()
    for c in range(2):
        row_load(c, tok_hbm, tok, t_sem).start()
        row_load(c, cot_hbm, seed, s_sem).start()

    def hand_on(c):
        partner_copy(c).wait_recv()
        hand_copy(c).start()

    def feed(c):
        x_copy(c).wait()
        total = xs[c] + xr[c]
        xs[c] = total
        branch_copy = pltpu.make_async_copy(xs.at[c], branch_out.at[rows(c * chunk)], b_sem)
        branch_copy.start()
        row_load(c, tok_hbm, tok, t_sem).wait()
        hidden = tok[c % 2].astype(F32) + total * mean_inverse(total) * attn_gain[...]
        if c + 2 < ROW_CHUNKS:
            row_load(c + 2, tok_hbm, tok, t_sem).start()
        xr[c] = hidden
        hidden_copy(c).start()
        partner_copy(c).start()
        low_buf[0:chunk, :] = hidden.astype(BF16)
        if c >= 1:
            for copy in turned_copies(hlt_buf, hlt_out, h_sem, c - 1):
                copy.wait()
            for buf, dst, i in ((gate_buf, gate_out, 0), (up_buf, up_out, 1), (inner_buf, inner_out, 2)):
                for copy in side_copies(buf, dst, g_sem.at[i], c - 1):
                    copy.wait()
        hlt_buf[:, 0:chunk] = hidden.astype(BF16).T
        hidden_copy(c).wait_recv()
        low_buf[chunk : 2 * chunk, :] = ag[c % 2].astype(BF16)
        hlt_buf[:, chunk : 2 * chunk] = ag[c % 2].astype(BF16).T
        for copy in turned_copies(hlt_buf, hlt_out, h_sem, c):
            copy.start()
        if c == 0:
            loads[0].wait()
            loads[1].wait()

        def tile(n, carry):
            at = pl.ds(pl.multiple_of(n * TILE, TILE), TILE)
            gate = jnp.dot(low_buf[...], wg[:, at], preferred_element_type=F32)
            up = jnp.dot(low_buf[...], wu[:, at], preferred_element_type=F32)
            gate_buf[:, at] = gate
            up_buf[:, at] = up
            inner_buf[:, at] = (gate * jax.nn.sigmoid(gate) * up).astype(BF16)
            return carry
        lax.fori_loop(0, tiles, tile, 0)
        for buf, dst, i in ((gate_buf, gate_out, 0), (up_buf, up_out, 1), (inner_buf, inner_out, 2)):
            for copy in side_copies(buf, dst, g_sem.at[i], c):
                copy.start()
        if c == 0:
            loads[2].wait()
        if c >= 2:
            core2_copy(c - 2).wait_send()
        branch_copy.wait()

        def down_tile(n, carry):
            at = pl.ds(pl.multiple_of(n * TILE, TILE), TILE)
            part = jnp.dot(inner_buf[...], wd[:, at], preferred_element_type=F32)
            xs[c, :, at] = part[0:chunk]
            cs[c % 2, :, at] = part[chunk : 2 * chunk]
            return carry
        lax.fori_loop(0, wide_tiles, down_tile, 0)
        core2_copy(c).start()
        core2_copy(c).wait_recv()
        xs[c] += crecv[c]
        x2_copy(c).start()
        if c >= 1:
            hand_on(c - 1)

    def finish(c, gain_total):
        x2_copy(c).wait()
        down = xs[c] + xr2[c]
        inv = mean_inverse(down)
        row_load(c, cot_hbm, seed, s_sem).wait()
        seed_rows = seed[c % 2].astype(F32) * seg_live[own_rows(0, c), 1:2].astype(F32)
        if c + 2 < ROW_CHUNKS:
            row_load(c + 2, cot_hbm, seed, s_sem).start()
        normed = down * inv
        gain_total = gain_total + column_sum(seed_rows * normed)
        scaled = seed_rows * mlp_gain[...]
        dot = jnp.sum(scaled * down, axis=1, keepdims=True)
        grad = inv * scaled - down * (inv * inv * inv * dot / down.shape[1])
        hidden_copy(c).wait_send()
        partner_copy(c).wait_send()
        xr2[c] = grad
        grad_copy(c).start()
        xr[c] = xr[c] + normed * mlp_gain[...]
        if c == 0:
            for copy in turned_copies(hlt_buf, hlt_out, h_sem, last):
                copy.wait()
        if c >= 1:
            for copy in turned_copies(hlt_buf, gdrt_out, d_sem.at[0], c - 1):
                copy.wait()
            for copy in side_copies(low_buf, gdr_out, d_sem.at[1], c - 1):
                copy.wait()
        low_buf[0:chunk, :] = grad.astype(BF16)
        hlt_buf[:, 0:chunk] = grad.astype(BF16).T
        grad_copy(c).wait_recv()
        out_copy(c).start()
        low_buf[chunk : 2 * chunk, :] = ag[c % 2].astype(BF16)
        hlt_buf[:, chunk : 2 * chunk] = ag[c % 2].astype(BF16).T
        for copy in turned_copies(hlt_buf, gdrt_out, d_sem.at[0], c):
            copy.start()
        for copy in side_copies(low_buf, gdr_out, d_sem.at[1], c):
            copy.start()
        return gain_total

    def out_copies(c):
        return [
            pltpu.make_async_copy(
                out_buf.at[pl.ds(s * chunk, chunk)], out_out.at[own_rows(s, c)], o_sem.at[s])
            for s in range(2)
        ]

    def place(c):
        if c >= 1:
            for copy in out_copies(c - 1):
                copy.wait()
        out_buf[0:chunk, :] = xr[c].astype(BF16)
        out_copy(c).wait_recv()
        out_buf[chunk : 2 * chunk, :] = crecv[c].astype(BF16)
        for copy in out_copies(c):
            copy.start()

    for c in range(ROW_CHUNKS):
        feed(c)
    gain_total = jnp.zeros(mlp_gain.shape, F32)
    for c in range(ROW_CHUNKS):
        gain_total = finish(c, gain_total)
        if c >= 1:
            place(c - 1)
        if c == 1:
            hand_on(last)
    place(last)
    gain_out[...] = gain_total
    for buf, dst, i in ((gate_buf, gate_out, 0), (up_buf, up_out, 1), (inner_buf, inner_out, 2)):
        for copy in side_copies(buf, dst, g_sem.at[i], last):
            copy.wait()
    for copy in turned_copies(hlt_buf, gdrt_out, d_sem.at[0], last):
        copy.wait()
    for copy in side_copies(low_buf, gdr_out, d_sem.at[1], last):
        copy.wait()
    for copy in out_copies(last):
        copy.wait()
    core2_copy(last - 1).wait_send()
    core2_copy(last).wait_send()
    for c in range(ROW_CHUNKS):
        grad_copy(c).wait_send()
        out_copy(c).wait_send()
        hand_copy(c).wait()


def forward_layer(hbm, vmem_args):
    tokens, w_query, w_gate = hbm[0], hbm[2], hbm[6]
    row_count, width = tokens.shape
    hidden, head_cols = w_gate.shape[1], w_query.shape[1]
    chunk = row_count // 2 // ROW_CHUNKS
    DMA = pltpu.SemaphoreType.DMA
    vmem, any_space = pl.BlockSpec(memory_space=pltpu.VMEM), pl.BlockSpec(memory_space=pl.ANY)

    def shape(*dims, kind=F32):
        return jax.ShapeDtypeStruct(dims, kind)

    per_chunk = DMA((ROW_CHUNKS,))
    return pl.pallas_call(
        forward_kernel,
        out_shape=(
            shape(row_count, hidden),
            shape(row_count, hidden),
            shape(row_count, hidden, kind=BF16),
            shape(width, row_count, kind=BF16),
            shape(row_count, width, kind=BF16),
            shape(width, row_count, kind=BF16),
            shape(row_count // 2, width),
            shape(row_count, width, kind=BF16),
            shape(row_count, head_cols, kind=BF16),
            shape(row_count, head_cols, kind=BF16),
            shape(row_count, head_cols, kind=BF16),
            shape(row_count, head_cols),
            shape(row_count, head_cols),
            shape(row_count, head_cols, kind=BF16),
            shape(row_count, width),
            shape(1, width),
            shape(row_count, HEAD),
            shape(head_cols // HEAD, row_count),
        ),
        in_specs=[any_space] * len(hbm) + [vmem] * len(vmem_args),
        out_specs=(any_space,) * 15 + (vmem,) * 3,
        scratch_shapes=[
            pltpu.VMEM(w_gate.shape, BF16),
            pltpu.VMEM(w_gate.shape, BF16),
            pltpu.VMEM((2, chunk, width), F32),
            pltpu.VMEM((ROW_CHUNKS, chunk, width), F32),
            pltpu.VMEM((ROW_CHUNKS, chunk, width), F32),
            pltpu.VMEM((ROW_CHUNKS, chunk, width), F32),
            pltpu.VMEM((ROW_CHUNKS, chunk, width), F32),
            pltpu.VMEM((2, chunk, width), F32),
            pltpu.VMEM((ROW_CHUNKS, 2 * chunk, HEAD), F32),
            pltpu.VMEM((2, ROW_CHUNKS, 2 * chunk, HEAD), F32),
            DMA((3,)),
            DMA((2,)),
            DMA((2,)),
            DMA((5,)),
            DMA((3,)),
            DMA((2, 2)),
        ]
        + [per_chunk] * 22
        + [DMA((3, 2)), DMA((2,)), DMA, DMA((2, 2)), DMA((2,))],
        compiler_params=pltpu.CompilerParams(
            collective_id=1, has_side_effects=True, vmem_limit_bytes=VMEM_LIMIT),
    )(*hbm, *vmem_args)


def backward_kernel(
    dp_size, counts,
    gdrt_hbm, hlt_hbm, tok_hbm, inner_hbm, mixed_hbm, gdr_hbm, gate_hbm, up_hbm, branch_hbm, cot_hbm,
    query_hbm, key_hbm, value_hbm, query_raw_hbm, key_raw_hbm, partner_hbm,
    inverses_hbm, seg_live_hbm, cos_hbm, sin_hbm,
    w_out_hbm, wg_hbm, wu_hbm, wd_hbm, wq_hbm, wk_hbm, wv_hbm,
    log_totals, seg_row,
    query_gain, key_gain, attn_gain, gain_mlp_part,
    down_out, out_out, gate_out, up_out, query_out, key_out, value_out, token_out, gains_out,
    ggr_hbm, gur_hbm, gbt_hbm, gh_hbm, gqkv_hbm,
    at, bbuf, bsend, bpar, own, ysend, yrecv, fsend, frecv, zsend, zrecv, stage, stage_t, cs, crecv, xs, xr, ag, dots, dots_in,
    vec, vec_in,
    at_sem, b_sem, bs_sem, ys_sem, yr_sem, fs_sem, fr_sem, zs_sem, zr_sem, out_sem, far_sem,
    cs_sem, cr_sem, xs_sem, xr_sem, as_sem, ar_sem, cs2_sem, cr2_sem, xs2_sem, xr2_sem, as2_sem,
    ar2_sem, ds_sem, dr_sem, vs_sem, vr_sem, w_sem, pre_sem, st_sem, gh_sem, tok_sem, live_sem,
    y_credit, up_credit, down_credit,
):
    n_down, n_pairs, n_heads, n_out = counts
    first_heads = n_down + n_pairs
    first_out = first_heads + n_heads
    total = first_out + n_out
    line = dp_size // 2
    width = at.shape[1]
    block = width // dp_size
    chunk = xs.shape[1]
    half = chunk * ROW_CHUNKS
    full = 2 * half
    head_cols = query_hbm.shape[1]
    passes = total + n_pairs + len(LINE_FIRST)
    dp_at = lax.axis_index("dp")
    z, y = dp_at // 2, dp_at % 2
    partner = dp_at + 1 - 2 * y
    below, above = dp_at - 2, dp_at + 2
    has_below, has_above = z > 0, z < line - 1
    core, sibling, across = tensor_peers()
    steps = [1 << s for s in range(dp_size.bit_length() - 1)]
    vec_peers = [dp_at + bit * (1 - 2 * ((dp_at // bit) % 2)) for bit in steps]

    def at_dp(i):
        return {"dp": i}

    def at_tensor(i):
        return {"tensor": i}

    def remote(src, dst, send_sem, recv_sem, peer):
        return pltpu.make_async_remote_copy(
            src_ref=src, dst_ref=dst, send_sem=send_sem, recv_sem=recv_sem,
            device_id=peer, device_id_type=MESH)

    def y_copy(p, b):
        return remote(ysend.at[p, b], yrecv.at[p, b], ys_sem.at[p, b], yr_sem.at[p, b], at_dp(partner))

    def z_copy(p, b, slot, target):
        return remote(zsend.at[p, b], zrecv.at[p, slot], zs_sem.at[p, b], zr_sem.at[p, slot], at_dp(target))

    def final_copy(p):
        return remote(fsend.at[p], frecv.at[p], fs_sem.at[p], fr_sem.at[p], at_dp(partner))

    def is_pair(k):
        return (k >= n_down) & (k < first_heads)

    def slot_of(k):
        return lax.rem(
            (k >= n_down).astype(jnp.int32) + (k >= first_heads).astype(jnp.int32)
            + (k >= first_out).astype(jnp.int32), 2)

    def row_block(rows_at):
        return pl.ds(pl.multiple_of(rows_at * block, block), block)

    def product(k, rows_at):
        return jnp.dot(
            at[slot_of(k), row_block(rows_at), :], bbuf[lax.rem(k, B_SLOTS)],
            preferred_element_type=F32)

    def pair_product(k, rows_at):
        return product(k, rows_at) + jnp.dot(
            at[2, row_block(rows_at), :], bpar[...], preferred_element_type=F32)

    def at_load(i):
        src = (gdrt_hbm, hlt_hbm, None, gbt_hbm)[i]
        return pltpu.make_async_copy(src, at.at[i % 2], at_sem.at[i % 2])

    def b_load(k, act):
        def columns(src, at_chunk, dst, sem):
            act(pltpu.make_async_copy(
                src.at[:, pl.ds(pl.multiple_of(at_chunk * COLS, COLS), COLS)], dst, sem))
        own_dst, own_sem = bbuf.at[lax.rem(k, B_SLOTS)], b_sem.at[lax.rem(k, B_SLOTS)]

        @pl.when(k < n_down)
        def _():
            columns(inner_hbm, k, own_dst, own_sem)

        for first, src in ((n_down, ggr_hbm), (n_down + n_pairs // 2, gur_hbm)):
            @pl.when((k >= first) & (k < first + n_pairs // 2))
            def _(first=first, src=src):
                columns(src, 2 * (k - first) + y, own_dst, own_sem)
                columns(src, 2 * (k - first) + 1 - y, bsend, bs_sem)

        @pl.when((k >= first_heads) & (k < first_out))
        def _():
            columns(gqkv_hbm, k - first_heads, own_dst, own_sem)

        @pl.when((k >= first_out) & (k < total))
        def _():
            columns(mixed_hbm, k - first_out, own_dst, own_sem)

    def line_first(k):
        return functools.reduce(jnp.logical_or, [k == at_chunk for at_chunk in LINE_FIRST])

    def walk(fn):
        def body(i, carry):
            @pl.when(z <= i)
            def _():
                fn(z + line - 1 - i, True)

            @pl.when(z >= line - 1 - i)
            def _():
                fn(z - (line - 1 - i), False)
            return carry
        lax.fori_loop(0, line - 1, body, 0)

    def pair_send(k):
        p = lax.rem(k, Y_SLOTS)

        @pl.when(k >= Y_SLOTS)
        def _():
            pl.semaphore_wait(y_credit, 1)
        b_load(k, lambda copy: copy.wait())

        @pl.when(jnp.logical_not(line_first(k) | is_pair(k)))
        def _():
            def one(b, up=None):
                ysend[p, b] = product(k, 2 * b + 1 - y)
                y_copy(p, b).start()
            walk(one)
            one(z)

        @pl.when(is_pair(k))
        def _():
            def rows_out(b, carry):
                ysend[p, b] = bsend[row_block(b), :].astype(F32)
                y_copy(p, b).start()
                return carry
            lax.fori_loop(0, line, rows_out, 0)

    def line_send(q, k, source):
        p = lax.rem(q, 2)

        @pl.when(q >= 2)
        def _():
            @pl.when(has_above)
            def _():
                pl.semaphore_wait(up_credit, 1)

            @pl.when(has_below)
            def _():
                pl.semaphore_wait(down_credit, 1)

        def one(b, up):
            has_before, target = (has_below, above) if up else (has_above, below)
            zsend[p, b] = source(b)

            @pl.when(has_before)
            def _():
                z_copy(p, b, b, target).wait_recv()
                zsend[p, b] += zrecv[p, b]
            if up:
                z_copy(p, b, b, target).start()
            else:
                @pl.when(b == z - 1)
                def _():
                    z_copy(p, b, line, target).start()

                @pl.when(b != z - 1)
                def _():
                    z_copy(p, b, b, target).start()
        walk(one)

    def line_own(q, dst):
        p = lax.rem(q, 2)

        @pl.when(has_below)
        def _():
            z_copy(p, z, z, below).wait_recv()
            dst[...] += zrecv[p, z]

        @pl.when(has_above)
        def _():
            z_copy(p, z, line, below).wait_recv()
            dst[...] += zrecv[p, line]

        def drain(b, up):
            z_copy(p, b, b, below).wait_send()
        walk(drain)

        @pl.when(q < passes - 2)
        def _():
            @pl.when(has_below)
            def _():
                pl.semaphore_signal(up_credit, inc=1, device_id=at_dp(below), device_id_type=MESH)

            @pl.when(has_above)
            def _():
                pl.semaphore_signal(down_credit, inc=1, device_id=at_dp(above), device_id_type=MESH)

    def is_turned(k):
        return (k < n_down) | (k >= first_out)

    per_head = n_heads // 3
    results = (
        (0, n_down, down_out, True),
        (first_heads, per_head, query_out, False),
        (first_heads + per_head, per_head, key_out, False),
        (first_heads + 2 * per_head, per_head, value_out, False),
        (first_out, n_out, out_out, True),
    )
    pair_results = ((n_down, gate_out), (n_down + n_pairs // 2, up_out))

    def out_act(k, act):
        def place(at_chunk):
            return pl.ds(pl.multiple_of(at_chunk * COLS, COLS), COLS)

        for first, count, dst, turned in results:
            @pl.when((k >= first) & (k < first + count))
            def _(first=first, dst=dst, turned=turned):
                if turned:
                    act(pltpu.make_async_copy(stage_t, dst.at[place(k - first)], out_sem))
                else:
                    act(pltpu.make_async_copy(stage, dst.at[:, place(k - first)], out_sem))

        for first, dst in pair_results:
            @pl.when((k >= first) & (k < first + n_pairs // 2))
            def _(first=first, dst=dst):
                act(pltpu.make_async_copy(stage, dst.at[:, place(2 * (k - first) + y)], out_sem))

    def far_out(k):
        for first, dst in pair_results:
            @pl.when((k >= first) & (k < first + n_pairs // 2))
            def _(first=first, dst=dst):
                cols = pl.ds(pl.multiple_of((2 * (k - first) + 1 - y) * COLS, COLS), COLS)
                copy = pltpu.make_async_copy(frecv.at[lax.rem(k, Y_SLOTS)], dst.at[:, cols], far_sem)
                copy.start()
                copy.wait()

    def finish_chunk(k, q):
        p = lax.rem(k, Y_SLOTS)

        @pl.when(k >= 1)
        def _():
            out_act(k - 1, lambda copy: copy.wait())
        stage[...] = own[...]

        @pl.when(jnp.logical_not(is_pair(k)))
        def _():
            y_copy(p, z).wait_recv()
            stage[...] += yrecv[p, z]
        line_own(q, stage)

        @pl.when((k < n_down) | (k >= first_out))
        def _():
            stage_t[...] = stage[...].T
        out_act(k, lambda copy: copy.start())

        @pl.when(line_first(k))
        def _():
            y_copy(p, z).wait_send()

        @pl.when(jnp.logical_not(line_first(k)))
        def _():
            for b in range(line):
                y_copy(p, b).wait_send()

        @pl.when(is_pair(k))
        def _():
            final_copy(p).wait()
            far_out(k)

        @pl.when(k < total - Y_SLOTS)
        def _():
            pl.semaphore_signal(y_credit, inc=1, device_id=at_dp(partner), device_id_type=MESH)

    def pass_of(k):
        return (
            k + jnp.clip(k - n_down, 0, n_pairs)
            + sum((k > at_chunk).astype(jnp.int32) for at_chunk in LINE_FIRST))

    def prefetch(k):
        @pl.when(k + 2 < total)
        def _():
            b_load(k + 2, lambda copy: copy.start())

    def send_ahead(k):
        @pl.when(k + 2 < total)
        def _():
            pair_send(k + 2)

    def tick(k):
        p = lax.rem(k, Y_SLOTS)
        q = pass_of(k)
        is_line_first = line_first(k)
        prefetch(k)

        @pl.when(jnp.logical_not(is_line_first))
        def _():
            def mine(b):
                part = product(k, 2 * b + y)
                y_copy(p, b).wait_recv()
                return part + yrecv[p, b]
            line_send(q, k, mine)

        @pl.when(is_line_first)
        def _():
            line_send(q, k, lambda b: product(k, 2 * b + 1 - y))

        @pl.when(k >= 1)
        def _():
            finish_chunk(k - 1, q - 1)
        own[...] = product(k, 2 * z + y)

        @pl.when(is_line_first)
        def _():
            line_send(q + 1, k, lambda b: product(k, 2 * b + y))
            ysend[p, z] = product(k, 2 * z + 1 - y)
            line_own(q, ysend.at[p, z])
            y_copy(p, z).start()
        send_ahead(k)

    def pair_tick(k, work):
        p = lax.rem(k, Y_SLOTS)
        q = pass_of(k)
        prefetch(k)

        def rows_in(b, carry):
            y_copy(p, b).wait_recv()
            bpar[row_block(b), :] = yrecv[p, b].astype(BF16)
            return carry
        lax.fori_loop(0, line, rows_in, 0)
        line_send(q, k, lambda b: pair_product(k, 2 * b + 1 - y))
        finish_chunk(k - 1, q - 1)
        work(q)
        line_send(q + 1, k, lambda b: pair_product(k, 2 * b + y))
        own[...] = pair_product(k, 2 * z + y)
        fsend[p] = pair_product(k, 2 * z + 1 - y)
        line_own(q, fsend.at[p])
        final_copy(p).start()
        send_ahead(k)

    nt = (((1,), (1,)), ((), ()))

    def copies_of(sem, *pairs):
        return [pltpu.make_async_copy(src, dst, sem.at[i]) for i, (src, dst) in enumerate(pairs)]

    def start(copies):
        for copy in copies:
            copy.start()

    def finish(copies):
        for copy in copies:
            copy.wait()

    first_pair, last_pair = n_down, n_down + 2 * n_pairs

    def run_ticks(first, last, work):
        def do_work(at_half):
            for when, fn in work.items():
                low, high = when if isinstance(when, tuple) else (when, when + 1)

                @pl.when((at_half >= low) & (at_half < high))
                def _(fn=fn, low=low, high=high):
                    if isinstance(fn, list):
                        for one in fn:
                            one()
                    elif low + 1 == high:
                        fn()
                    else:
                        fn(at_half - low)

        def single(at_half, carry):
            k = jnp.where(at_half < first_pair, at_half, at_half - n_pairs)
            tick(k)
            do_work(at_half)
            return carry

        def double(m, carry):
            at_half = first_pair + 2 * m
            pair_tick(first_pair + m, lambda q: do_work(at_half))
            do_work(at_half + 1)
            return carry
        if first < first_pair:
            lax.fori_loop(first, min(last, first_pair), single, 0)
        low, high = max(first, first_pair), min(last, last_pair)
        if low < high:
            lax.fori_loop((low - first_pair) // 2, (high - first_pair) // 2, double, 0)
        if last > last_pair:
            lax.fori_loop(max(first, last_pair), last, single, 0)

    def part(fn, *args):
        return functools.partial(fn, *args)

    def side_rows(s, c):
        return pl.ds(s * half + c * chunk, chunk)

    def both_sides(hbm, buf, c, out=False):
        pairs = [(hbm.at[side_rows(s, c)], buf.at[pl.ds(s * chunk, chunk)]) for s in range(2)]
        return [(b, a) for a, b in pairs] if out else pairs

    def sequence_rows(s, c):
        return pl.ds(pl.multiple_of(2 * c * chunk + jnp.where(core == s, 0, chunk), chunk), chunk)

    def core_copy(c, again):
        ss, rs = (cs2_sem, cr2_sem) if again else (cs_sem, cr_sem)
        return remote(cs, crecv.at[c], ss.at[c], rs.at[c], at_tensor(sibling))

    def x_copy(c, again):
        ss, rs = (xs2_sem, xr2_sem) if again else (xs_sem, xr_sem)
        return remote(xs.at[c], xr.at[c], ss.at[c], rs.at[c], at_tensor(across))

    def to_sibling(c, again):
        ss, rs = (as2_sem, ar2_sem) if again else (as_sem, ar_sem)
        return remote(xr.at[c], ag.at[c % 2], ss.at[c], rs.at[c], at_tensor(sibling))

    def pass_on(c, again):
        core_copy(c, again).wait_recv()
        xs[c] += crecv[c]
        x_copy(c, again).start()
        core_copy(c, again).wait_send()

    hidden = wd_hbm.shape[0]

    def feed_phase(wd, grads, gates, ups, ggr, gur, far_rows):
        far_piece = full // ROW_CHUNKS

        def far_load(c):
            return copies_of(
                tok_sem, (partner_hbm.at[pl.ds(c * far_piece, far_piece)], far_rows))

        def far_turn(c):
            finish(far_load(c))
            at[2, :, pl.ds(c * far_piece, far_piece)] = far_rows[...].astype(BF16).T
            if c + 1 < ROW_CHUNKS:
                start(far_load(c + 1))

        def loads(c):
            return copies_of(
                pre_sem, *both_sides(gdr_hbm, grads, c), *both_sides(gate_hbm, gates, c),
                *both_sides(up_hbm, ups, c))

        def stores(c):
            return copies_of(
                st_sem, *both_sides(ggr_hbm, ggr, c, True), *both_sides(gur_hbm, gur, c, True))

        def piece(c):
            finish(loads(c))
            if c >= 1:
                finish(stores(c - 1))

            def tile(n, carry):
                cols = pl.ds(pl.multiple_of(n * TILE, TILE), TILE)
                grad = lax.dot_general(grads[...], wd[cols, :], nt, preferred_element_type=F32)
                gate = gates[:, cols]
                sig = jax.nn.sigmoid(gate)
                act = gate * sig
                ggr[:, cols] = (grad * ups[:, cols] * (sig + act * (1.0 - sig))).astype(BF16)
                gur[:, cols] = (grad * act).astype(BF16)
                return carry
            lax.fori_loop(0, hidden // TILE, tile, 0)
            start(stores(c))
            if c + 1 < ROW_CHUNKS:
                start(loads(c + 1))

        load_weight = copies_of(w_sem, (wd_hbm, wd))
        start(load_weight)
        start(loads(0))
        start(far_load(0))
        at_load(0).wait()
        pair_send(jnp.int32(0))
        pair_send(jnp.int32(1))
        finish(load_weight)
        piece(0)
        far_turn(0)
        run_ticks(0, FEED_TICK, {
            c - 1: [part(piece, c), part(far_turn, c)] for c in range(1, ROW_CHUNKS)})
        finish(stores(ROW_CHUNKS - 1))

    def hidden_phase(weights, ggr, gur):
        load_weights = copies_of(w_sem, (wg_hbm, weights.at[0]), (wu_hbm, weights.at[1]))

        def loads(c):
            return copies_of(pre_sem, *both_sides(ggr_hbm, ggr, c), *both_sides(gur_hbm, gur, c))

        def piece(c):
            if c == 0:
                finish(load_weights)
            else:
                pass_on(c - 1, False)
            finish(loads(c))

            def tile(n, carry):
                rows = pl.ds(pl.multiple_of(n * TILE, TILE), TILE)
                total_part = lax.dot_general(ggr[...], weights[0, rows, :], nt, preferred_element_type=F32)
                total_part = total_part + lax.dot_general(
                    gur[...], weights[1, rows, :], nt, preferred_element_type=F32)
                xs[c, :, rows] = total_part[0:chunk]
                cs[:, rows] = total_part[chunk : 2 * chunk]
                return carry
            lax.fori_loop(0, width // TILE, tile, 0)
            core_copy(c, False).start()
            if c + 1 < ROW_CHUNKS:
                start(loads(c + 1))

        start(load_weights)
        start(loads(0))
        run_ticks(
            FEED_TICK, HIDDEN_TICK, {FEED_TICK + c: part(piece, c) for c in range(ROW_CHUNKS)})

    def branch_phase(branch, seed, low, turned, w_out, mixed_grad, token_rows, seg_live):
        load_weight = copies_of(w_sem, (w_out_hbm, w_out))
        load_live = copies_of(live_sem, (seg_live_hbm, seg_live))
        token_piece = full // ROW_CHUNKS

        def loads(c):
            rows = pl.ds(c * chunk, chunk)
            return copies_of(
                pre_sem, (branch_hbm.at[rows], branch), (cot_hbm.at[sequence_rows(0, c)], seed))

        def stores(c):
            i = c % 2
            return copies_of(
                st_sem.at[pl.ds(4 * i, 4)],
                (turned.at[i, :, pl.ds(0, chunk)], gbt_hbm.at[:, side_rows(0, c)]),
                (turned.at[i, :, pl.ds(chunk, chunk)], gbt_hbm.at[:, side_rows(1, c)]),
                *[(
                    mixed_grad.at[i, pl.ds(s * chunk, chunk)],
                    gqkv_hbm.at[sequence_rows(s, c), pl.ds(2 * head_cols, head_cols)],
                ) for s in range(2)])

        def hidden_store(c):
            return copies_of(gh_sem, (xs.at[c], gh_hbm.at[pl.ds(c * chunk, chunk)]))

        def token_load(c):
            return copies_of(tok_sem, (tok_hbm.at[pl.ds(c * token_piece, token_piece)], token_rows))

        def first(c):
            i = c % 2
            finish(loads(c))
            if c == 0:
                finish(load_live)
            x_copy(c, False).wait()
            live = seg_live[sequence_rows(0, c), 1:2].astype(F32)
            grad_hidden = xs[c] + xr[c] + seed[...].astype(F32) * live
            xs[c] = grad_hidden
            start(hidden_store(c))
            values = branch[...]
            inv = mean_inverse(values)
            vec[1:2, :] += column_sum(grad_hidden * values * inv)
            scaled = grad_hidden * attn_gain[...]
            dot = jnp.sum(scaled * values, axis=1, keepdims=True)
            grad = inv * scaled - values * (inv * inv * inv * dot / width)
            xr[c] = grad
            to_sibling(c, False).start()
            if c >= 2:
                finish(stores(c - 2))
            low[i, 0:chunk, :] = grad.astype(BF16)
            turned[i, :, 0:chunk] = grad.astype(BF16).T
            if c + 1 < ROW_CHUNKS:
                start(loads(c + 1))

        def second(c):
            i = c % 2
            to_sibling(c, False).wait_recv()
            if c == 0:
                finish(load_weight)
            other = ag[i].astype(BF16)
            low[i, chunk : 2 * chunk, :] = other
            turned[i, :, chunk : 2 * chunk] = other.T
            mixed_grad[i] = lax.dot_general(
                low[i], w_out[...], nt, preferred_element_type=F32).astype(BF16)
            start(stores(c))
            finish(hidden_store(c))
            to_sibling(c, False).wait_send()

        def turn(c):
            finish(token_load(c))
            at[0, :, pl.ds(c * token_piece, token_piece)] = token_rows[...].T
            if c + 1 < ROW_CHUNKS:
                start(token_load(c + 1))

        start(load_weight)
        start(load_live)
        start(loads(0))
        start(token_load(0))
        work = {HIDDEN_TICK + c: [] for c in range(ROW_CHUNKS + 1)}
        work[HIDDEN_TICK].append(part(pass_on, ROW_CHUNKS - 1, False))
        for c in range(ROW_CHUNKS):
            work[HIDDEN_TICK + c].append(part(first, c))
            work[HIDDEN_TICK + c + 1].append(part(second, c))
        work[HIDDEN_TICK + 3] += [part(turn, 0)]
        work[HIDDEN_TICK + 4] += [part(turn, c) for c in range(1, ROW_CHUNKS)]
        run_ticks(HIDDEN_TICK, BRANCH_TICK, work)
        for c in range(ROW_CHUNKS - 2, ROW_CHUNKS):
            finish(stores(c))

    def attention_phase(
        query, key, value, mixed_grad, dq, dk, dv, raw, bias, inverses, seg_live, cosine, sine,
    ):
        heads = head_cols // HEAD
        q_rows = min(256, full)
        scale = HEAD ** (-0.5)
        value_cols = pl.ds(2 * head_cols, head_cols)
        loads = copies_of(
            pre_sem, (query_hbm, query), (key_hbm, key), (value_hbm, value),
            (gqkv_hbm.at[:, value_cols], mixed_grad))
        load_tables = copies_of(
            w_sem, (inverses_hbm, inverses), (seg_live_hbm, seg_live), (cos_hbm, cosine), (sin_hbm, sine))

        def masks():
            finish(load_tables)
            for i in range(full // q_rows):
                rows, keys = slice(i * q_rows, (i + 1) * q_rows), (i + 1) * q_rows
                key_at = lax.broadcasted_iota(jnp.int32, (keys, q_rows), 0)
                query_at = lax.broadcasted_iota(jnp.int32, (keys, q_rows), 1) + i * q_rows
                allowed = (
                    (seg_live[0:keys, 0:1] == seg_row[:, rows])
                    & (key_at <= query_at)
                    & ((seg_live[0:keys, 1:2] > 0) | (key_at == query_at)))
                bias[0:keys, rows] = jnp.where(allowed, 0.0, NEG_FILL).astype(BF16)
            finish(loads)

        def head(h):
            cols = pl.ds(pl.multiple_of(h * HEAD, HEAD), HEAD)
            dk[:, cols] = jnp.zeros((full, HEAD), F32)
            dv[...] = jnp.zeros((full, HEAD), F32)
            for i in range(full // q_rows):
                rows, keys = slice(i * q_rows, (i + 1) * q_rows), (i + 1) * q_rows
                q_block, grad_block = query[rows, cols], mixed_grad[rows, cols]
                key_block, value_block = key[0:keys, cols], value[0:keys, cols]
                scores = lax.dot_general(key_block, q_block, nt, preferred_element_type=F32) * scale
                prob = jnp.exp(scores + bias[0:keys, rows].astype(F32) - log_totals[pl.ds(h, 1), rows])
                grad_prob = lax.dot_general(value_block, grad_block, nt, preferred_element_type=F32)
                row_dot = jnp.sum(prob * grad_prob, axis=0, keepdims=True)
                grad_scores = (prob * (grad_prob - row_dot)).astype(BF16)
                dq[rows, cols] = lax.dot_general(
                    grad_scores, key_block, (((0,), (0,)), ((), ())), preferred_element_type=F32) * scale
                dk[0:keys, cols] += jnp.dot(grad_scores, q_block, preferred_element_type=F32) * scale
                dv[0:keys, :] += jnp.dot(prob.astype(BF16), grad_block, preferred_element_type=F32)
            mixed_grad[:, cols] = dv[...].astype(BF16)

        store_value = copies_of(st_sem, (mixed_grad, gqkv_hbm.at[:, value_cols]))
        sides = ((dq, query_raw_hbm, query_gain), (dk, key_raw_hbm, key_gain))

        def load_raw(which):
            return copies_of(pre_sem, (sides[which][1], raw))

        def back(which):
            grads, _, gain = sides[which]
            finish(load_raw(which))
            gains = gain[...].astype(F32)
            lanes = lax.broadcasted_iota(jnp.int32, (q_rows, HEAD), 1)

            def block_back(i, carry):
                rows = pl.ds(pl.multiple_of(i * q_rows, q_rows), q_rows)
                dot = jnp.zeros((q_rows, 1), F32)
                for h in range(heads):
                    cols = slice(h * HEAD, (h + 1) * HEAD)
                    grad = grads[rows, cols]
                    grad = grad * cosine[rows, :] - pltpu.roll(grad, HEAD // 2, 1) * sine[rows, :]
                    raw_rows = raw[rows, cols]
                    gain_cols = slice(which * head_cols + h * HEAD, which * head_cols + (h + 1) * HEAD)
                    vec[2:3, gain_cols] += column_sum(
                        grad * raw_rows * inverses[rows, which : which + 1])
                    scaled = grad * gains[h : h + 1, :]
                    grads[rows, cols] = scaled
                    dot = dot + jnp.sum(scaled * raw_rows, axis=1, keepdims=True)
                if which == 0:
                    dots[rows, :] = jnp.broadcast_to(dot, (q_rows, HEAD))
                else:
                    dots[rows, :] = jnp.where(lanes == 0, dots[rows, :], dot)
                return carry
            lax.fori_loop(0, full // q_rows, block_back, 0)

        def dots_copy(i):
            return remote(
                dots, dots_in.at[i], ds_sem.at[i], dr_sem.at[i], at_tensor((sibling, across)[i]))

        def dots_add(i):
            dots_copy(i).wait()
            dots[...] += dots_in[i]

        def combine(which):
            grads = sides[which][0]
            for i in range(full // q_rows):
                rows = slice(i * q_rows, (i + 1) * q_rows)
                inv_rows = inverses[rows, which : which + 1]
                dot = dots[rows, which : which + 1]
                mixed_grad[rows, :] = (
                    inv_rows * grads[rows, :]
                    - raw[rows, :] * (inv_rows * inv_rows * inv_rows * dot / width)
                ).astype(BF16)

        def store_grads(which):
            return copies_of(
                st_sem, (mixed_grad, gqkv_hbm.at[:, pl.ds(which * head_cols, head_cols)]))

        def after_heads():
            start(store_value)
            start(load_raw(0))

        def back_query():
            back(0)
            start(load_raw(1))

        def back_key():
            back(1)
            dots_copy(0).start()
            finish(store_value)

        def first_sum():
            dots_add(0)
            dots_copy(1).start()

        def second_sum():
            dots_add(1)
            combine(1)
            start(store_grads(1))
            start(load_raw(0))

        def last_part():
            finish(store_grads(1))
            finish(load_raw(0))
            combine(0)
            start(store_grads(0))

        start(loads)
        start(load_tables)
        t = BRANCH_TICK
        run_ticks(t, INPUT_TICK, {
            t: masks,
            (t, t + heads): head,
            t + heads - 1: after_heads,
            t + heads: back_query,
            t + heads + 1: back_key,
            t + heads + 2: first_sum,
            t + heads + 3: [second_sum, last_part],
        })
        finish(store_grads(0))

    def input_phase(weights, grads, grad_hidden, low):
        loads = copies_of(
            w_sem, *[(w, weights.at[i]) for i, w in enumerate((wq_hbm, wk_hbm, wv_hbm))],
            (gqkv_hbm, grads))

        def piece(c):
            if c == 0:
                finish(loads)
            else:
                pass_on(c - 1, True)
            for s in range(2):
                rows = sequence_rows(s, c)

                def tile(n, carry):
                    cols = pl.ds(pl.multiple_of(n * TILE, TILE), TILE)
                    total_part = jnp.zeros((chunk, TILE), F32)
                    for i in range(3):
                        total_part = total_part + lax.dot_general(
                            grads[rows, i * head_cols : (i + 1) * head_cols], weights[i, cols, :],
                            nt, preferred_element_type=F32)
                    if s == 0:
                        xs[c, :, cols] = total_part
                    else:
                        cs[:, cols] = total_part
                    return carry
                lax.fori_loop(0, width // TILE, tile, 0)
            core_copy(c, True).start()

        def hidden_load(c):
            return copies_of(gh_sem, (gh_hbm.at[pl.ds(c * chunk, chunk)], grad_hidden))

        def stores(c):
            return copies_of(
                st_sem, *[(low.at[s], token_out.at[sequence_rows(s, c)]) for s in range(2)])

        def first(c):
            finish(hidden_load(c))
            x_copy(c, True).wait()
            xr[c] = xs[c] + xr[c] + grad_hidden[...]
            to_sibling(c, True).start()
            if c + 1 < ROW_CHUNKS:
                start(hidden_load(c + 1))

        def second(c):
            if c >= 1:
                finish(stores(c - 1))
            low[0] = xr[c].astype(BF16)
            to_sibling(c, True).wait_recv()
            low[1] = ag[c % 2].astype(BF16)
            start(stores(c))
            to_sibling(c, True).wait_send()

        vec_peer_ids = [at_tensor(sibling)] + [at_dp(peer) for peer in vec_peers]

        def vec_copy(i):
            return remote(vec, vec_in.at[i], vs_sem.at[i], vr_sem.at[i], vec_peer_ids[i])

        def vec_step(i):
            if i >= 1:
                vec_copy(i - 1).wait()
                if i == 1:
                    vec[0:2, :] += vec_in[0, 0:2, :]
                else:
                    vec[...] += vec_in[i - 1]
            if i < len(vec_peer_ids):
                vec_copy(i).start()

        start(loads)
        start(hidden_load(0))
        halves = total + n_pairs
        work = {k: [] for k in range(INPUT_TICK, halves)}
        for c in range(ROW_CHUNKS):
            work[INPUT_TICK + c].append(part(piece, c))
            work[TOKEN_TICK + c].append(part(first, c))
            work[TOKEN_TICK + c + 1].append(part(second, c))
        work[INPUT_TICK + ROW_CHUNKS].append(part(pass_on, ROW_CHUNKS - 1, True))
        for i in range(len(vec_peer_ids) + 1):
            work[INPUT_TICK + 2 + i].append(part(vec_step, i))
        work[last_pair + 1].append(lambda: at_load(3).start())
        work[last_pair + 2].append(lambda: at_load(3).wait())
        run_ticks(INPUT_TICK, halves, {k: fns for k, fns in work.items() if fns})
        finish(stores(ROW_CHUNKS - 1))

    vec[...] = jnp.zeros(vec.shape, F32)
    vec[0:1, :] = gain_mlp_part[...]
    at_load(0).start()
    at_load(1).start()
    for k in range(2):
        b_load(jnp.int32(k), lambda copy: copy.start())
    barrier = pltpu.get_barrier_semaphore()

    def greet_one(peer):
        pl.semaphore_signal(barrier, inc=1, device_id=peer, device_id_type=MESH)

    other_z = z - 1 + 2 * lax.rem(z, 2)
    has_other = (other_z >= 0) & (other_z < line)
    for peer in vec_peers:
        greet_one(at_dp(peer))
    greet_one(at_tensor(sibling))
    greet_one(at_tensor(across))

    @pl.when(has_other)
    def _():
        greet_one(at_dp(2 * other_z + y))
    pl.semaphore_wait(barrier, len(steps) + 2 + has_other.astype(jnp.int32))

    both = 2 * chunk
    rows_of = (full, head_cols)
    pl.run_scoped(
        feed_phase, pltpu.VMEM(wd_hbm.shape, BF16), pltpu.VMEM((both, width), BF16),
        pltpu.VMEM((both, hidden), F32), pltpu.VMEM((both, hidden), F32),
        pltpu.VMEM((both, hidden), BF16), pltpu.VMEM((both, hidden), BF16),
        pltpu.VMEM((full // ROW_CHUNKS, width), F32))
    at_load(1).wait()
    pl.run_scoped(
        hidden_phase, pltpu.VMEM((2,) + wg_hbm.shape, BF16), pltpu.VMEM((both, hidden), BF16),
        pltpu.VMEM((both, hidden), BF16))
    pl.run_scoped(
        branch_phase, pltpu.VMEM((chunk, width), F32), pltpu.VMEM((chunk, width), BF16),
        pltpu.VMEM((2, both, width), BF16), pltpu.VMEM((2, width, both), BF16),
        pltpu.VMEM(w_out_hbm.shape, BF16), pltpu.VMEM((2, both, head_cols), BF16),
        pltpu.VMEM((full // ROW_CHUNKS, width), BF16), pltpu.VMEM(seg_live_hbm.shape, jnp.int32))
    pl.run_scoped(
        attention_phase, pltpu.VMEM(rows_of, BF16), pltpu.VMEM(rows_of, BF16), pltpu.VMEM(rows_of, BF16),
        pltpu.VMEM(rows_of, BF16), pltpu.VMEM(rows_of, F32), pltpu.VMEM(rows_of, F32),
        pltpu.VMEM((full, HEAD), F32), pltpu.VMEM(rows_of, F32), pltpu.VMEM((full, full), BF16),
        pltpu.VMEM((full, HEAD), F32), pltpu.VMEM(seg_live_hbm.shape, jnp.int32),
        pltpu.VMEM((full, HEAD), F32), pltpu.VMEM((full, HEAD), F32))
    pl.run_scoped(
        input_phase, pltpu.VMEM((3,) + wq_hbm.shape, BF16), pltpu.VMEM((full, 3 * head_cols), BF16),
        pltpu.VMEM((chunk, width), F32), pltpu.VMEM((2, chunk, width), BF16))
    finish_chunk(jnp.int32(total - 1), jnp.int32(passes - 1))
    out_act(jnp.int32(total - 1), lambda copy: copy.wait())
    gains_out[...] = jnp.zeros(gains_out.shape, F32)
    gains_out[0:8, :] = vec[...]
    for h in range(2 * head_cols // HEAD):
        gains_out[8 + h : 9 + h, 0:HEAD] = vec[2:3, h * HEAD : (h + 1) * HEAD]


def backward_layer(dp_size, hbm, vmem_args):
    names = dict(zip(HBM_NAMES, hbm, strict=True))
    width, row_count = names["gdrt"].shape
    hidden, head_cols = names["inner"].shape[1], names["query"].shape[1]
    line, block = dp_size // 2, width // dp_size
    chunk = row_count // 2 // ROW_CHUNKS
    counts = (hidden // COLS, hidden // COLS, 3 * head_cols // COLS, head_cols // COLS)
    DMA, REG = pltpu.SemaphoreType.DMA, pltpu.SemaphoreType.REGULAR
    vmem, any_space = pl.BlockSpec(memory_space=pltpu.VMEM), pl.BlockSpec(memory_space=pl.ANY)

    def shape(*dims, kind=F32):
        return jax.ShapeDtypeStruct(dims, kind)

    slot = (block, COLS)
    per_chunk = DMA((ROW_CHUNKS,))
    steps = dp_size.bit_length() - 1
    results = pl.pallas_call(
        functools.partial(backward_kernel, dp_size, counts),
        out_shape=(
            shape(hidden, block),
            shape(head_cols, block),
            shape(block, hidden),
            shape(block, hidden),
            shape(block, head_cols),
            shape(block, head_cols),
            shape(block, head_cols),
            shape(row_count, width, kind=BF16),
            shape(8 + 2 * head_cols // HEAD, width),
            shape(row_count, hidden, kind=BF16),
            shape(row_count, hidden, kind=BF16),
            shape(width, row_count, kind=BF16),
            shape(row_count // 2, width),
            shape(row_count, 3 * head_cols, kind=BF16),
        ),
        in_specs=[any_space] * len(hbm) + [vmem] * len(vmem_args),
        out_specs=(any_space,) * 8 + (vmem,) + (any_space,) * 5,
        scratch_shapes=[
            pltpu.VMEM((3, width, row_count), BF16),
            pltpu.VMEM((B_SLOTS, row_count, COLS), BF16),
            pltpu.VMEM((row_count, COLS), BF16),
            pltpu.VMEM((row_count, COLS), BF16),
            pltpu.VMEM(slot, F32),
            pltpu.VMEM((Y_SLOTS, line) + slot, F32),
            pltpu.VMEM((Y_SLOTS, line) + slot, F32),
            pltpu.VMEM((Y_SLOTS,) + slot, F32),
            pltpu.VMEM((Y_SLOTS,) + slot, F32),
            pltpu.VMEM((2, line) + slot, F32),
            pltpu.VMEM((2, line + 1) + slot, F32),
            pltpu.VMEM(slot, F32),
            pltpu.VMEM((COLS, block), F32),
            pltpu.VMEM((chunk, width), F32),
            pltpu.VMEM((ROW_CHUNKS, chunk, width), F32),
            pltpu.VMEM((ROW_CHUNKS, chunk, width), F32),
            pltpu.VMEM((ROW_CHUNKS, chunk, width), F32),
            pltpu.VMEM((2, chunk, width), F32),
            pltpu.VMEM((row_count, HEAD), F32),
            pltpu.VMEM((2, row_count, HEAD), F32),
            pltpu.VMEM((8, width), F32),
            pltpu.VMEM((steps + 1, 8, width), F32),
            DMA((2,)),
            DMA((B_SLOTS,)),
            DMA,
            DMA((Y_SLOTS, line)),
            DMA((Y_SLOTS, line)),
            DMA((Y_SLOTS,)),
            DMA((Y_SLOTS,)),
            DMA((2, line)),
            DMA((2, line + 1)),
            DMA,
            DMA,
        ]
        + [per_chunk] * 12
        + [DMA((2,)), DMA((2,)), DMA((steps + 1,)), DMA((steps + 1,)), DMA((4,)), DMA((6,)), DMA((8,)), DMA((1,)), DMA((1,)), DMA((1,)),
           REG, REG, REG],
        compiler_params=pltpu.CompilerParams(
            collective_id=2, has_side_effects=True, vmem_limit_bytes=VMEM_LIMIT),
    )(*hbm, *vmem_args)
    return results[:9]


def rope_tables():
    half_size = HEAD // 2
    freq_row = ROPE_BASE ** (-(jnp.arange(half_size, dtype=F32) * 2.0) / HEAD)
    angle = jnp.arange(LENGTH, dtype=F32)[:, None] * freq_row[None, :]
    cosine, sine = jnp.cos(angle), jnp.sin(angle)
    return jnp.concatenate((cosine, cosine), 1), jnp.concatenate((-sine, sine), 1)


def make_shards(dp_size):
    def shards(
        tokens,
        segments,
        pad_mask,
        w_query,
        w_key,
        w_value,
        w_out,
        gain_query,
        gain_key,
        gain_attn,
        w_gate,
        w_up,
        w_down,
        gain_mlp,
        cotangent,
    ):
        block = tokens.shape[1] // dp_size
        cosine, sine = rope_tables()
        seg_live = jnp.stack((segments, pad_mask), 1)
        seg_row = segments[None, :]
        attn_gain = gain_attn.astype(F32)[None, :]
        mlp_gain = gain_mlp.astype(F32)[None, :]
        (
            gate_rows,
            up_rows,
            inner_rows,
            hidden_turned,
            grad_down_rows,
            grad_down_turned,
            branch_rows,
            output,
            query_norm,
            key_norm,
            value_rows,
            query_raw,
            key_raw,
            mixed_rows,
            partner_rows,
            gain_mlp_part,
            inverses,
            log_totals,
        ) = forward_layer(
            (
                tokens, cotangent, w_query, w_key, w_value, w_out, w_gate, w_up, w_down, cosine, sine,
            ),
            (seg_live, seg_row, gain_query, gain_key, attn_gain, mlp_gain),
        )
        (
            grad_down,
            grad_out,
            grad_gate,
            grad_up,
            grad_query,
            grad_key,
            grad_value,
            grad_tokens,
            gains,
        ) = backward_layer(
            dp_size,
            (
                grad_down_turned, hidden_turned, tokens, inner_rows, mixed_rows, grad_down_rows,
                gate_rows, up_rows, branch_rows, cotangent,
                query_norm, key_norm, value_rows, query_raw, key_raw, partner_rows,
                inverses, seg_live, cosine, sine,
                w_out, w_gate, w_up, w_down, w_query, w_key, w_value,
            ),
            (
                log_totals, seg_row, gain_query, gain_key, attn_gain, gain_mlp_part,
            ),
        )
        heads, head_block = gain_query.shape[0], HEAD // dp_size
        dp_at = lax.axis_index("dp")
        wide = lax.dynamic_slice(gains, (0, dp_at * block), (2, block))
        head_gains = lax.dynamic_slice(gains, (8, dp_at * head_block), (2 * heads, head_block))
        return (
            output,
            grad_tokens,
            grad_query,
            grad_key,
            grad_value,
            grad_out,
            head_gains[:heads],
            head_gains[heads:],
            wide[1],
            grad_gate,
            grad_up,
            grad_down,
            wide[0],
        )

    return shards


def solution(mesh):
    in_specs = (
        P("dp", None),
        P("dp"),
        P("dp"),
        P(None, "tensor"),
        P(None, "tensor"),
        P(None, "tensor"),
        P("tensor", None),
        P("tensor", None),
        P("tensor", None),
        P(),
        P(None, "tensor"),
        P(None, "tensor"),
        P("tensor", None),
        P(),
        P("dp", None),
    )
    out_specs = (
        P("dp", None),
        P("dp", None),
        P("dp", "tensor"),
        P("dp", "tensor"),
        P("dp", "tensor"),
        P("tensor", "dp"),
        P("tensor", "dp"),
        P("tensor", "dp"),
        P("dp"),
        P("dp", "tensor"),
        P("dp", "tensor"),
        P("tensor", "dp"),
        P("dp"),
    )
    shards = make_shards(mesh.shape["dp"])
    return jax.shard_map(shards, mesh=mesh, in_specs=in_specs, out_specs=out_specs, check_vma=False)
```

```python
import functools

import jax
import jax.numpy as jnp
import numpy as np
from jax import lax
from jax.experimental import pallas as pl
from jax.experimental.pallas import tpu as pltpu
from jax.sharding import PartitionSpec as P

HEAD = 128
LENGTH = 1024
EPSILON = 1e-06
NEG_FILL = -1e30
ROPE_BASE = 500000.0
ROW_CHUNKS = 4
F32 = jnp.float32
BF16 = jnp.bfloat16


COLS = 256
LINE_FIRST = (1, 5, 23)
Y_SLOTS = 3
B_SLOTS = 3
FEED_TICK = 3
HIDDEN_TICK = 7
BRANCH_TICK = 12
INPUT_TICK = 20
TOKEN_TICK = 25
HBM_NAMES = (
    "gdrt", "hlt", "tokens", "inner", "mixed", "gdr", "gate", "up", "branch", "cotangent",
    "query", "key", "value", "query_raw", "key_raw", "partner",
    "inverses", "seg_live", "cosine", "sine",
    "w_out", "w_gate", "w_up", "w_down", "w_query", "w_key", "w_value",
)
TILE = 512
VMEM_LIMIT = 65400 * 1024
MESH = pl.DeviceIdType.MESH

def column_sum(values):
    return jnp.sum(values, axis=0, keepdims=True)


def mean_inverse(values):
    return lax.rsqrt(jnp.mean(values * values, axis=1, keepdims=True) + EPSILON)


def tensor_peers():
    at = lax.axis_index("tensor")
    core = lax.rem(at, 2)
    return core, at + 1 - 2 * core, lax.rem(at + 2, 4)


def greet(*peers):
    barrier = pltpu.get_barrier_semaphore()
    for peer in peers:
        pl.semaphore_signal(barrier, inc=1, device_id=peer, device_id_type=MESH)
    pl.semaphore_wait(barrier, len(peers))


def forward_kernel(
    tok_hbm, cot_hbm, wq_hbm, wk_hbm, wv_hbm, wo_hbm, wg_hbm, wu_hbm, wd_hbm, cos_hbm, sin_hbm,
    seg_live, seg_row, query_gain, key_gain, attn_gain, mlp_gain,
    gate_out, up_out, inner_out, hlt_out, gdr_out, gdrt_out, branch_out, out_out,
    query_out, key_out, value_out, query_raw_out, key_raw_out, mixed_out, partner_out,
    gain_out, inverse_out, log_out,
    wg, cs, crecv, xs, xr, xr2, ag, squares, squares_in,
    w_sem, t_sem, s_sem, a_sem, r_sem, m_sem, sq_s_sem, sq_r_sem, sx_s_sem, sx_r_sem,
    cs_sem, cr_sem, xs_sem, xr_sem, as_sem, ar_sem, cs2_sem, cr2_sem, xs2_sem, xr2_sem,
    gs_sem, gr_sem, os_sem, or_sem, hs_sem, hr_sem, fs_sem, fr_sem, g_sem, h_sem, b_sem, d_sem, o_sem,
):
    core, sibling, across = tensor_peers()
    dp_at = lax.axis_index("dp")
    partner = dp_at + 1 - 2 * lax.rem(dp_at, 2)
    chunk = xs.shape[1]
    half = chunk * ROW_CHUNKS
    full = 2 * half
    both = 2 * chunk
    width, hidden = xs.shape[2], wg.shape[1]
    head_cols = wq_hbm.shape[1]
    heads = head_cols // HEAD
    tiles = hidden // TILE
    wide_tiles = width // TILE
    last = ROW_CHUNKS - 1
    nt = (((1,), (1,)), ((), ()))

    def start(copies):
        for copy in copies:
            copy.start()

    def finish(copies):
        for copy in copies:
            copy.wait()

    def own_rows(s, c):
        return pl.ds(pl.multiple_of(c * both + jnp.where(core == s, 0, chunk), chunk), chunk)

    def row_load(c, src, dst, sem):
        return pltpu.make_async_copy(src.at[own_rows(0, c)], dst.at[c % 2], sem.at[c % 2])

    wide_loads = [pltpu.make_async_copy(wg_hbm, wg, w_sem.at[0])]

    def remote(src, dst, send_sem, recv_sem, peer):
        return pltpu.make_async_remote_copy(
            src_ref=src, dst_ref=dst, send_sem=send_sem, recv_sem=recv_sem,
            device_id={"tensor": peer}, device_id_type=MESH)

    def partner_copy(c):
        return pltpu.make_async_remote_copy(
            src_ref=xr.at[c], dst_ref=partner_out.at[rows(c * chunk)], send_sem=hs_sem.at[c],
            recv_sem=hr_sem.at[c], device_id={"dp": partner}, device_id_type=MESH)

    def hand_copy(c):
        return remote(
            partner_out.at[rows(c * chunk)], partner_out.at[rows(half + c * chunk)],
            fs_sem.at[c], fr_sem.at[c], sibling)

    def core_copy(c):
        return remote(cs.at[c % 2], crecv.at[c], cs_sem.at[c], cr_sem.at[c], sibling)

    def x_copy(c):
        return remote(xs.at[c], xr.at[c], xs_sem.at[c], xr_sem.at[c], across)

    def hidden_copy(c):
        return remote(xr.at[c], ag.at[c % 2], as_sem.at[c], ar_sem.at[c], sibling)

    def core2_copy(c):
        return remote(cs.at[c % 2], crecv.at[c], cs2_sem.at[c], cr2_sem.at[c], sibling)

    def x2_copy(c):
        return remote(xs.at[c], xr2.at[c], xs2_sem.at[c], xr2_sem.at[c], across)

    def grad_copy(c):
        return remote(xr2.at[c], ag.at[c % 2], gs_sem.at[c], gr_sem.at[c], sibling)

    def out_copy(c):
        return remote(xr.at[c], crecv.at[c], os_sem.at[c], or_sem.at[c], sibling)

    def rows(first):
        return pl.ds(first, chunk)

    def side_copies(buf, dst, sem, c):
        return [
            pltpu.make_async_copy(
                buf.at[pl.ds(s * chunk, chunk)], dst.at[rows(s * half + c * chunk)], sem.at[s])
            for s in range(2)
        ]

    def turned_copies(buf, dst, sem, c):
        return [
            pltpu.make_async_copy(
                buf.at[:, pl.ds(s * chunk, chunk)], dst.at[:, rows(s * half + c * chunk)], sem.at[s])
            for s in range(2)
        ]

    def square_copy(c):
        return remote(
            squares.at[c], squares_in.at[0, c], sq_s_sem.at[c], sq_r_sem.at[c], sibling)

    def square_x_copy(c):
        return remote(
            squares.at[c], squares_in.at[1, c], sx_s_sem.at[c], sx_r_sem.at[c], across)

    def square_pass_on(c):
        square_copy(c).wait()
        squares[c] += squares_in[0, c]
        square_x_copy(c).start()

    def project(c, weights, loads, tok, tok_load, query_raw, key_raw, value, value_turned):
        at = slice(c * both, (c + 1) * both)
        lanes = lax.broadcasted_iota(jnp.int32, (both, HEAD), 1)
        tok_load(c).wait()
        if c == 0:
            loads[0].wait()
        query_raw[at, :] = jnp.dot(tok[c % 2], weights[0], preferred_element_type=F32)
        if c == 0:
            loads[1].wait()
        key_raw[at, :] = jnp.dot(tok[c % 2], weights[1], preferred_element_type=F32)
        query_square = jnp.sum(query_raw[at, :] * query_raw[at, :], axis=1, keepdims=True)
        key_square = jnp.sum(key_raw[at, :] * key_raw[at, :], axis=1, keepdims=True)
        squares[c] = jnp.where(lanes == 0, query_square, key_square)
        square_copy(c).start()
        if c == 0:
            loads[2].wait()
            start(wide_loads)
        if c == 1:
            square_pass_on(0)
        value[at, :] = jnp.dot(tok[c % 2], weights[2], preferred_element_type=F32).astype(BF16)
        value_turned[:, at] = value[at, :].T
        if c + 2 < ROW_CHUNKS:
            tok_load(c + 2).start()

    def attend(c, query_raw, key_raw, query, key, value_turned, cosine, sine, w_out, mixed, bias):
        first, keys = c * both, (c + 1) * both
        at = slice(first, keys)
        square_x_copy(c).wait()
        squares[c] += squares_in[1, c]
        inverse = lax.rsqrt(squares[c] / width + EPSILON)
        inverse_out[at, :] = inverse
        for raw, gain, lane, dst in (
            (query_raw, query_gain, 0, query), (key_raw, key_gain, 1, key)):
            gains = gain[...].astype(F32)
            for h in range(heads):
                cols = slice(h * HEAD, (h + 1) * HEAD)
                normed = raw[at, cols] * inverse[:, lane : lane + 1] * gains[h : h + 1, :]
                turned = normed * cosine[at, :] + pltpu.roll(normed, HEAD // 2, 1) * sine[at, :]
                dst[at, cols] = turned.astype(BF16)
        key_at = lax.broadcasted_iota(jnp.int32, (keys, both), 0)
        query_at = lax.broadcasted_iota(jnp.int32, (keys, both), 1) + first
        allowed = (
            (seg_live[0:keys, 0:1] == seg_row[:, at])
            & (key_at <= query_at)
            & ((seg_live[0:keys, 1:2] > 0) | (key_at == query_at)))
        bias[0:keys, :] = jnp.where(allowed, 0.0, NEG_FILL)

        def head(h, carry):
            cols = pl.ds(pl.multiple_of(h * HEAD, HEAD), HEAD)
            scores = lax.dot_general(
                key[0:keys, cols], query[at, cols], nt, preferred_element_type=F32) * HEAD ** (-0.5)
            scores = scores + bias[0:keys, :]
            top = jnp.max(scores, axis=0, keepdims=True)
            powers = jnp.exp(scores - top)
            total = jnp.sum(powers, axis=0, keepdims=True)
            prob = (powers / total).astype(BF16)
            log_out[pl.ds(h, 1), at] = top + jnp.log(total)
            turned = jnp.dot(value_turned[cols, 0:keys], prob, preferred_element_type=F32)
            mixed[c % 2, :, cols] = turned.T.astype(BF16)
            return carry
        lax.fori_loop(0, heads, head, 0)

        def mixed_rows(s):
            return pl.ds(pl.multiple_of(jnp.where(core == s, 0, chunk), chunk), chunk)
        if c + 1 < ROW_CHUNKS:
            square_pass_on(c + 1)
        if c >= 2:
            core_copy(c - 2).wait_send()
        cs[c % 2] = jnp.dot(mixed[c % 2, mixed_rows(1), :], w_out[...], preferred_element_type=F32)
        core_copy(c).start()
        xs[c] = jnp.dot(mixed[c % 2, mixed_rows(0), :], w_out[...], preferred_element_type=F32)
        start(mixed_copies(c, mixed))
        pass_on(c)

    def mixed_copies(c, mixed):
        return [
            pltpu.make_async_copy(
                mixed.at[c % 2, pl.ds(pl.multiple_of(jnp.where(core == s, 0, chunk), chunk), chunk)],
                mixed_out.at[rows(s * half + c * chunk)], m_sem.at[c % 2, s])
            for s in range(2)
        ]

    def pass_on(c):
        core_copy(c).wait_recv()
        xs[c] += crecv[c]
        x_copy(c).start()

    def attention(
        query_raw, key_raw, query, key, value, value_turned, cosine, sine, w_out, weights, tok, mixed, bias,
    ):
        def tok_load(c):
            return pltpu.make_async_copy(
                tok_hbm.at[pl.ds(c * both, both)], tok.at[c % 2], t_sem.at[c % 2])

        loads = [
            pltpu.make_async_copy(w, weights.at[i], a_sem.at[i])
            for i, w in enumerate((wq_hbm, wk_hbm, wv_hbm))
        ]
        tables = [
            pltpu.make_async_copy(src, dst, r_sem.at[i])
            for i, (src, dst) in enumerate(((cos_hbm, cosine), (sin_hbm, sine), (wo_hbm, w_out)))
        ]
        tok_load(0).start()
        start(loads)
        tok_load(1).start()
        start(tables)
        greet({"tensor": sibling}, {"tensor": across}, {"dp": partner})
        results = [
            pltpu.make_async_copy(src, dst, a_sem.at[i])
            for i, (src, dst) in enumerate((
                (value, value_out), (query_raw, query_raw_out), (key_raw, key_raw_out),
                (query, query_out), (key, key_out)))
        ]
        for c in range(ROW_CHUNKS + 1):
            if c < ROW_CHUNKS:
                project(c, weights, loads, tok, tok_load, query_raw, key_raw, value, value_turned)
            if c == 1:
                finish(tables)
            if c == last:
                start(results[:3])
            if c >= 1:
                if c >= 3:
                    finish(mixed_copies(c - 3, mixed))
                attend(
                    c - 1, query_raw, key_raw, query, key, value_turned, cosine, sine, w_out, mixed, bias)
        start(results[3:])
        for c in range(last - 1, ROW_CHUNKS):
            core_copy(c).wait_send()
            finish(mixed_copies(c, mixed))
        finish(results)

    rows_of = (full, head_cols)
    pl.run_scoped(
        attention, pltpu.VMEM(rows_of, F32), pltpu.VMEM(rows_of, F32), pltpu.VMEM(rows_of, BF16),
        pltpu.VMEM(rows_of, BF16), pltpu.VMEM(rows_of, BF16), pltpu.VMEM((head_cols, full), BF16),
        pltpu.VMEM((full, HEAD), F32), pltpu.VMEM((full, HEAD), F32), pltpu.VMEM(wo_hbm.shape, BF16),
        pltpu.VMEM((3,) + wq_hbm.shape, BF16), pltpu.VMEM((2, both, width), BF16),
        pltpu.VMEM((2, both, head_cols), BF16), pltpu.VMEM((full, both), F32))
    pl.run_scoped(
        functools.partial(
            feed_forward, core, chunk, own_rows, row_load, rows, side_copies, turned_copies,
            (x_copy, hidden_copy, core2_copy, x2_copy, grad_copy, out_copy, partner_copy, hand_copy), wide_loads, seg_live,
            (tok_hbm, cot_hbm, wu_hbm, wd_hbm, attn_gain, mlp_gain, wg),
            (gate_out, up_out, inner_out, hlt_out, gdr_out, gdrt_out, branch_out, out_out, gain_out),
            (cs, crecv, xs, xr, xr2, ag),
            (w_sem, t_sem, s_sem, g_sem, h_sem, b_sem, d_sem, o_sem)),
        pltpu.VMEM(wu_hbm.shape, BF16), pltpu.VMEM(wd_hbm.shape, BF16),
        pltpu.VMEM((both, hidden), F32), pltpu.VMEM((both, hidden), F32),
        pltpu.VMEM((both, hidden), BF16), pltpu.VMEM((both, width), BF16), pltpu.VMEM((width, both), BF16),
        pltpu.VMEM((both, width), BF16), pltpu.VMEM((2, chunk, width), BF16),
        pltpu.VMEM((2, chunk, width), BF16))


def feed_forward(
    core, chunk, own_rows, row_load, rows, side_copies, turned_copies, remote_copies, wide_loads, seg_live,
    operands, results, buffers, sems,
    wu, wd, gate_buf, up_buf, inner_buf, low_buf, hlt_buf, out_buf, tok, seed,
):
    x_copy, hidden_copy, core2_copy, x2_copy, grad_copy, out_copy, partner_copy, hand_copy = remote_copies
    tok_hbm, cot_hbm, wu_hbm, wd_hbm, attn_gain, mlp_gain, wg = operands
    gate_out, up_out, inner_out, hlt_out, gdr_out, gdrt_out, branch_out, out_out, gain_out = results
    cs, crecv, xs, xr, xr2, ag = buffers
    w_sem, t_sem, s_sem, g_sem, h_sem, b_sem, d_sem, o_sem = sems
    last = ROW_CHUNKS - 1
    tiles, wide_tiles = wg.shape[1] // TILE, wd.shape[1] // TILE
    loads = wide_loads + [
        pltpu.make_async_copy(wu_hbm, wu, w_sem.at[1]),
        pltpu.make_async_copy(wd_hbm, wd, w_sem.at[2]),
    ]
    loads[1].start()
    loads[2].start()
    for c in range(2):
        row_load(c, tok_hbm, tok, t_sem).start()
        row_load(c, cot_hbm, seed, s_sem).start()

    def hand_on(c):
        partner_copy(c).wait_recv()
        hand_copy(c).start()

    def feed(c):
        x_copy(c).wait()
        total = xs[c] + xr[c]
        xs[c] = total
        branch_copy = pltpu.make_async_copy(xs.at[c], branch_out.at[rows(c * chunk)], b_sem)
        branch_copy.start()
        row_load(c, tok_hbm, tok, t_sem).wait()
        hidden = tok[c % 2].astype(F32) + total * mean_inverse(total) * attn_gain[...]
        if c + 2 < ROW_CHUNKS:
            row_load(c + 2, tok_hbm, tok, t_sem).start()
        xr[c] = hidden
        hidden_copy(c).start()
        partner_copy(c).start()
        low_buf[0:chunk, :] = hidden.astype(BF16)
        if c >= 1:
            for copy in turned_copies(hlt_buf, hlt_out, h_sem, c - 1):
                copy.wait()
            for buf, dst, i in ((gate_buf, gate_out, 0), (up_buf, up_out, 1), (inner_buf, inner_out, 2)):
                for copy in side_copies(buf, dst, g_sem.at[i], c - 1):
                    copy.wait()
        hlt_buf[:, 0:chunk] = hidden.astype(BF16).T
        hidden_copy(c).wait_recv()
        low_buf[chunk : 2 * chunk, :] = ag[c % 2].astype(BF16)
        hlt_buf[:, chunk : 2 * chunk] = ag[c % 2].astype(BF16).T
        for copy in turned_copies(hlt_buf, hlt_out, h_sem, c):
            copy.start()
        if c == 0:
            loads[0].wait()
            loads[1].wait()

        def tile(n, carry):
            at = pl.ds(pl.multiple_of(n * TILE, TILE), TILE)
            gate = jnp.dot(low_buf[...], wg[:, at], preferred_element_type=F32)
            up = jnp.dot(low_buf[...], wu[:, at], preferred_element_type=F32)
            gate_buf[:, at] = gate
            up_buf[:, at] = up
            inner_buf[:, at] = (gate * jax.nn.sigmoid(gate) * up).astype(BF16)
            return carry
        lax.fori_loop(0, tiles, tile, 0)
        for buf, dst, i in ((gate_buf, gate_out, 0), (up_buf, up_out, 1), (inner_buf, inner_out, 2)):
            for copy in side_copies(buf, dst, g_sem.at[i], c):
                copy.start()
        if c == 0:
            loads[2].wait()
        if c >= 2:
            core2_copy(c - 2).wait_send()
        branch_copy.wait()

        def down_tile(n, carry):
            at = pl.ds(pl.multiple_of(n * TILE, TILE), TILE)
            part = jnp.dot(inner_buf[...], wd[:, at], preferred_element_type=F32)
            xs[c, :, at] = part[0:chunk]
            cs[c % 2, :, at] = part[chunk : 2 * chunk]
            return carry
        lax.fori_loop(0, wide_tiles, down_tile, 0)
        core2_copy(c).start()
        core2_copy(c).wait_recv()
        xs[c] += crecv[c]
        x2_copy(c).start()
        if c >= 1:
            hand_on(c - 1)

    def finish(c, gain_total):
        x2_copy(c).wait()
        down = xs[c] + xr2[c]
        inv = mean_inverse(down)
        row_load(c, cot_hbm, seed, s_sem).wait()
        seed_rows = seed[c % 2].astype(F32) * seg_live[own_rows(0, c), 1:2].astype(F32)
        if c + 2 < ROW_CHUNKS:
            row_load(c + 2, cot_hbm, seed, s_sem).start()
        normed = down * inv
        gain_total = gain_total + column_sum(seed_rows * normed)
        scaled = seed_rows * mlp_gain[...]
        dot = jnp.sum(scaled * down, axis=1, keepdims=True)
        grad = inv * scaled - down * (inv * inv * inv * dot / down.shape[1])
        hidden_copy(c).wait_send()
        partner_copy(c).wait_send()
        xr2[c] = grad
        grad_copy(c).start()
        xr[c] = xr[c] + normed * mlp_gain[...]
        if c == 0:
            for copy in turned_copies(hlt_buf, hlt_out, h_sem, last):
                copy.wait()
        if c >= 1:
            for copy in turned_copies(hlt_buf, gdrt_out, d_sem.at[0], c - 1):
                copy.wait()
            for copy in side_copies(low_buf, gdr_out, d_sem.at[1], c - 1):
                copy.wait()
        low_buf[0:chunk, :] = grad.astype(BF16)
        hlt_buf[:, 0:chunk] = grad.astype(BF16).T
        grad_copy(c).wait_recv()
        out_copy(c).start()
        low_buf[chunk : 2 * chunk, :] = ag[c % 2].astype(BF16)
        hlt_buf[:, chunk : 2 * chunk] = ag[c % 2].astype(BF16).T
        for copy in turned_copies(hlt_buf, gdrt_out, d_sem.at[0], c):
            copy.start()
        for copy in side_copies(low_buf, gdr_out, d_sem.at[1], c):
            copy.start()
        return gain_total

    def out_copies(c):
        return [
            pltpu.make_async_copy(
                out_buf.at[pl.ds(s * chunk, chunk)], out_out.at[own_rows(s, c)], o_sem.at[s])
            for s in range(2)
        ]

    def place(c):
        if c >= 1:
            for copy in out_copies(c - 1):
                copy.wait()
        out_buf[0:chunk, :] = xr[c].astype(BF16)
        out_copy(c).wait_recv()
        out_buf[chunk : 2 * chunk, :] = crecv[c].astype(BF16)
        for copy in out_copies(c):
            copy.start()

    for c in range(ROW_CHUNKS):
        feed(c)
    gain_total = jnp.zeros(mlp_gain.shape, F32)
    for c in range(ROW_CHUNKS):
        gain_total = finish(c, gain_total)
        if c >= 1:
            place(c - 1)
        if c == 1:
            hand_on(last)
    place(last)
    gain_out[...] = gain_total
    for buf, dst, i in ((gate_buf, gate_out, 0), (up_buf, up_out, 1), (inner_buf, inner_out, 2)):
        for copy in side_copies(buf, dst, g_sem.at[i], last):
            copy.wait()
    for copy in turned_copies(hlt_buf, gdrt_out, d_sem.at[0], last):
        copy.wait()
    for copy in side_copies(low_buf, gdr_out, d_sem.at[1], last):
        copy.wait()
    for copy in out_copies(last):
        copy.wait()
    core2_copy(last - 1).wait_send()
    core2_copy(last).wait_send()
    for c in range(ROW_CHUNKS):
        grad_copy(c).wait_send()
        out_copy(c).wait_send()
        hand_copy(c).wait()


def forward_layer(hbm, vmem_args):
    tokens, w_query, w_gate = hbm[0], hbm[2], hbm[6]
    row_count, width = tokens.shape
    hidden, head_cols = w_gate.shape[1], w_query.shape[1]
    chunk = row_count // 2 // ROW_CHUNKS
    DMA = pltpu.SemaphoreType.DMA
    vmem, any_space = pl.BlockSpec(memory_space=pltpu.VMEM), pl.BlockSpec(memory_space=pl.ANY)

    def shape(*dims, kind=F32):
        return jax.ShapeDtypeStruct(dims, kind)

    per_chunk = DMA((ROW_CHUNKS,))
    return pl.pallas_call(
        forward_kernel,
        out_shape=(
            shape(row_count, hidden),
            shape(row_count, hidden),
            shape(row_count, hidden, kind=BF16),
            shape(width, row_count, kind=BF16),
            shape(row_count, width, kind=BF16),
            shape(width, row_count, kind=BF16),
            shape(row_count // 2, width),
            shape(row_count, width, kind=BF16),
            shape(row_count, head_cols, kind=BF16),
            shape(row_count, head_cols, kind=BF16),
            shape(row_count, head_cols, kind=BF16),
            shape(row_count, head_cols),
            shape(row_count, head_cols),
            shape(row_count, head_cols, kind=BF16),
            shape(row_count, width),
            shape(1, width),
            shape(row_count, HEAD),
            shape(head_cols // HEAD, row_count),
        ),
        in_specs=[any_space] * len(hbm) + [vmem] * len(vmem_args),
        out_specs=(any_space,) * 15 + (vmem,) * 3,
        scratch_shapes=[
            pltpu.VMEM(w_gate.shape, BF16),
            pltpu.VMEM((2, chunk, width), F32),
            pltpu.VMEM((ROW_CHUNKS, chunk, width), F32),
            pltpu.VMEM((ROW_CHUNKS, chunk, width), F32),
            pltpu.VMEM((ROW_CHUNKS, chunk, width), F32),
            pltpu.VMEM((ROW_CHUNKS, chunk, width), F32),
            pltpu.VMEM((2, chunk, width), F32),
            pltpu.VMEM((ROW_CHUNKS, 2 * chunk, HEAD), F32),
            pltpu.VMEM((2, ROW_CHUNKS, 2 * chunk, HEAD), F32),
            DMA((3,)),
            DMA((2,)),
            DMA((2,)),
            DMA((5,)),
            DMA((3,)),
            DMA((2, 2)),
        ]
        + [per_chunk] * 22
        + [DMA((3, 2)), DMA((2,)), DMA, DMA((2, 2)), DMA((2,))],
        compiler_params=pltpu.CompilerParams(
            collective_id=1, has_side_effects=True, vmem_limit_bytes=VMEM_LIMIT),
    )(*hbm, *vmem_args)


def backward_kernel(
    dp_size, counts,
    gdrt_hbm, hlt_hbm, tok_hbm, inner_hbm, mixed_hbm, gdr_hbm, gate_hbm, up_hbm, branch_hbm, cot_hbm,
    query_hbm, key_hbm, value_hbm, query_raw_hbm, key_raw_hbm, partner_hbm,
    inverses_hbm, seg_live_hbm, cos_hbm, sin_hbm,
    w_out_hbm, wg_hbm, wu_hbm, wd_hbm, wq_hbm, wk_hbm, wv_hbm,
    log_totals, seg_row,
    query_gain, key_gain, attn_gain, gain_mlp_part,
    down_out, out_out, gate_out, up_out, query_out, key_out, value_out, token_out, gains_out,
    ggr_hbm, gur_hbm, gbt_hbm, gh_hbm, gqkv_hbm,
    at, bbuf, bsend, bpar, own, ysend, yrecv, fsend, frecv, zsend, zrecv, stage, stage_t, cs, crecv, xs, xr, ag, dots, dots_in,
    vec, vec_in,
    at_sem, b_sem, bs_sem, ys_sem, yr_sem, fs_sem, fr_sem, zs_sem, zr_sem, out_sem, far_sem,
    cs_sem, cr_sem, xs_sem, xr_sem, as_sem, ar_sem, cs2_sem, cr2_sem, xs2_sem, xr2_sem, as2_sem,
    ar2_sem, ds_sem, dr_sem, vs_sem, vr_sem, w_sem, pre_sem, st_sem, gh_sem, tok_sem, live_sem,
    y_credit, up_credit, down_credit,
):
    n_down, n_pairs, n_heads, n_out = counts
    first_heads = n_down + n_pairs
    first_out = first_heads + n_heads
    total = first_out + n_out
    line = dp_size // 2
    width = at.shape[1]
    block = width // dp_size
    chunk = xs.shape[1]
    half = chunk * ROW_CHUNKS
    full = 2 * half
    head_cols = query_hbm.shape[1]
    passes = total + n_pairs + len(LINE_FIRST)
    dp_at = lax.axis_index("dp")
    z, y = dp_at // 2, dp_at % 2
    partner = dp_at + 1 - 2 * y
    below, above = dp_at - 2, dp_at + 2
    has_below, has_above = z > 0, z < line - 1
    core, sibling, across = tensor_peers()
    steps = [1 << s for s in range(dp_size.bit_length() - 1)]
    vec_peers = [dp_at + bit * (1 - 2 * ((dp_at // bit) % 2)) for bit in steps]

    def at_dp(i):
        return {"dp": i}

    def at_tensor(i):
        return {"tensor": i}

    def remote(src, dst, send_sem, recv_sem, peer):
        return pltpu.make_async_remote_copy(
            src_ref=src, dst_ref=dst, send_sem=send_sem, recv_sem=recv_sem,
            device_id=peer, device_id_type=MESH)

    def y_copy(p, b):
        return remote(ysend.at[p, b], yrecv.at[p, b], ys_sem.at[p, b], yr_sem.at[p, b], at_dp(partner))

    def z_copy(p, b, slot, target):
        return remote(zsend.at[p, b], zrecv.at[p, slot], zs_sem.at[p, b], zr_sem.at[p, slot], at_dp(target))

    def final_copy(p):
        return remote(fsend.at[p], frecv.at[p], fs_sem.at[p], fr_sem.at[p], at_dp(partner))

    def is_pair(k):
        return (k >= n_down) & (k < first_heads)

    def slot_of(k):
        return lax.rem(
            (k >= n_down).astype(jnp.int32) + (k >= first_heads).astype(jnp.int32)
            + (k >= first_out).astype(jnp.int32), 2)

    def row_block(rows_at):
        return pl.ds(pl.multiple_of(rows_at * block, block), block)

    def product(k, rows_at):
        return jnp.dot(
            at[slot_of(k), row_block(rows_at), :], bbuf[lax.rem(k, B_SLOTS)],
            preferred_element_type=F32)

    def pair_product(k, rows_at):
        return product(k, rows_at) + jnp.dot(
            at[2, row_block(rows_at), :], bpar[...], preferred_element_type=F32)

    def at_load(i):
        src = (gdrt_hbm, hlt_hbm, None, gbt_hbm)[i]
        return pltpu.make_async_copy(src, at.at[i % 2], at_sem.at[i % 2])

    def b_load(k, act):
        def columns(src, at_chunk, dst, sem):
            act(pltpu.make_async_copy(
                src.at[:, pl.ds(pl.multiple_of(at_chunk * COLS, COLS), COLS)], dst, sem))
        own_dst, own_sem = bbuf.at[lax.rem(k, B_SLOTS)], b_sem.at[lax.rem(k, B_SLOTS)]

        @pl.when(k < n_down)
        def _():
            columns(inner_hbm, k, own_dst, own_sem)

        for first, src in ((n_down, ggr_hbm), (n_down + n_pairs // 2, gur_hbm)):
            @pl.when((k >= first) & (k < first + n_pairs // 2))
            def _(first=first, src=src):
                columns(src, 2 * (k - first) + y, own_dst, own_sem)
                columns(src, 2 * (k - first) + 1 - y, bsend, bs_sem)

        @pl.when((k >= first_heads) & (k < first_out))
        def _():
            columns(gqkv_hbm, k - first_heads, own_dst, own_sem)

        @pl.when((k >= first_out) & (k < total))
        def _():
            columns(mixed_hbm, k - first_out, own_dst, own_sem)

    def line_first(k):
        return functools.reduce(jnp.logical_or, [k == at_chunk for at_chunk in LINE_FIRST])

    def walk(fn):
        def body(i, carry):
            @pl.when(z <= i)
            def _():
                fn(z + line - 1 - i, True)

            @pl.when(z >= line - 1 - i)
            def _():
                fn(z - (line - 1 - i), False)
            return carry
        lax.fori_loop(0, line - 1, body, 0)

    def pair_send(k):
        p = lax.rem(k, Y_SLOTS)

        @pl.when(k >= Y_SLOTS)
        def _():
            pl.semaphore_wait(y_credit, 1)
        b_load(k, lambda copy: copy.wait())

        @pl.when(jnp.logical_not(line_first(k) | is_pair(k)))
        def _():
            def one(b, up=None):
                ysend[p, b] = product(k, 2 * b + 1 - y)
                y_copy(p, b).start()
            walk(one)
            one(z)

        @pl.when(is_pair(k))
        def _():
            def rows_out(b, carry):
                ysend[p, b] = bsend[row_block(b), :].astype(F32)
                y_copy(p, b).start()
                return carry
            lax.fori_loop(0, line, rows_out, 0)

    def line_send(q, k, source):
        p = lax.rem(q, 2)

        @pl.when(q >= 2)
        def _():
            @pl.when(has_above)
            def _():
                pl.semaphore_wait(up_credit, 1)

            @pl.when(has_below)
            def _():
                pl.semaphore_wait(down_credit, 1)

        def one(b, up):
            has_before, target = (has_below, above) if up else (has_above, below)
            zsend[p, b] = source(b)

            @pl.when(has_before)
            def _():
                z_copy(p, b, b, target).wait_recv()
                zsend[p, b] += zrecv[p, b]
            if up:
                z_copy(p, b, b, target).start()
            else:
                @pl.when(b == z - 1)
                def _():
                    z_copy(p, b, line, target).start()

                @pl.when(b != z - 1)
                def _():
                    z_copy(p, b, b, target).start()
        walk(one)

    def line_own(q, dst):
        p = lax.rem(q, 2)

        @pl.when(has_below)
        def _():
            z_copy(p, z, z, below).wait_recv()
            dst[...] += zrecv[p, z]

        @pl.when(has_above)
        def _():
            z_copy(p, z, line, below).wait_recv()
            dst[...] += zrecv[p, line]

        def drain(b, up):
            z_copy(p, b, b, below).wait_send()
        walk(drain)

        @pl.when(q < passes - 2)
        def _():
            @pl.when(has_below)
            def _():
                pl.semaphore_signal(up_credit, inc=1, device_id=at_dp(below), device_id_type=MESH)

            @pl.when(has_above)
            def _():
                pl.semaphore_signal(down_credit, inc=1, device_id=at_dp(above), device_id_type=MESH)

    def is_turned(k):
        return (k < n_down) | (k >= first_out)

    per_head = n_heads // 3
    results = (
        (0, n_down, down_out, True),
        (first_heads, per_head, query_out, False),
        (first_heads + per_head, per_head, key_out, False),
        (first_heads + 2 * per_head, per_head, value_out, False),
        (first_out, n_out, out_out, True),
    )
    pair_results = ((n_down, gate_out), (n_down + n_pairs // 2, up_out))

    def out_act(k, act):
        def place(at_chunk):
            return pl.ds(pl.multiple_of(at_chunk * COLS, COLS), COLS)

        for first, count, dst, turned in results:
            @pl.when((k >= first) & (k < first + count))
            def _(first=first, dst=dst, turned=turned):
                if turned:
                    act(pltpu.make_async_copy(stage_t, dst.at[place(k - first)], out_sem))
                else:
                    act(pltpu.make_async_copy(stage, dst.at[:, place(k - first)], out_sem))

        for first, dst in pair_results:
            @pl.when((k >= first) & (k < first + n_pairs // 2))
            def _(first=first, dst=dst):
                act(pltpu.make_async_copy(stage, dst.at[:, place(2 * (k - first) + y)], out_sem))

    def far_out(k):
        for first, dst in pair_results:
            @pl.when((k >= first) & (k < first + n_pairs // 2))
            def _(first=first, dst=dst):
                cols = pl.ds(pl.multiple_of((2 * (k - first) + 1 - y) * COLS, COLS), COLS)
                copy = pltpu.make_async_copy(frecv.at[lax.rem(k, Y_SLOTS)], dst.at[:, cols], far_sem)
                copy.start()
                copy.wait()

    def finish_chunk(k, q):
        p = lax.rem(k, Y_SLOTS)

        @pl.when(k >= 1)
        def _():
            out_act(k - 1, lambda copy: copy.wait())
        stage[...] = own[...]

        @pl.when(jnp.logical_not(is_pair(k)))
        def _():
            y_copy(p, z).wait_recv()
            stage[...] += yrecv[p, z]
        line_own(q, stage)

        @pl.when((k < n_down) | (k >= first_out))
        def _():
            stage_t[...] = stage[...].T
        out_act(k, lambda copy: copy.start())

        @pl.when(line_first(k))
        def _():
            y_copy(p, z).wait_send()

        @pl.when(jnp.logical_not(line_first(k)))
        def _():
            for b in range(line):
                y_copy(p, b).wait_send()

        @pl.when(is_pair(k))
        def _():
            final_copy(p).wait()
            far_out(k)

        @pl.when(k < total - Y_SLOTS)
        def _():
            pl.semaphore_signal(y_credit, inc=1, device_id=at_dp(partner), device_id_type=MESH)

    def pass_of(k):
        return (
            k + jnp.clip(k - n_down, 0, n_pairs)
            + sum((k > at_chunk).astype(jnp.int32) for at_chunk in LINE_FIRST))

    def prefetch(k):
        @pl.when(k + 2 < total)
        def _():
            b_load(k + 2, lambda copy: copy.start())

    def send_ahead(k):
        @pl.when(k + 2 < total)
        def _():
            pair_send(k + 2)

    def tick(k):
        p = lax.rem(k, Y_SLOTS)
        q = pass_of(k)
        is_line_first = line_first(k)
        prefetch(k)

        @pl.when(jnp.logical_not(is_line_first))
        def _():
            def mine(b):
                part = product(k, 2 * b + y)
                y_copy(p, b).wait_recv()
                return part + yrecv[p, b]
            line_send(q, k, mine)

        @pl.when(is_line_first)
        def _():
            line_send(q, k, lambda b: product(k, 2 * b + 1 - y))

        @pl.when(k >= 1)
        def _():
            finish_chunk(k - 1, q - 1)
        send_ahead(k)
        own[...] = product(k, 2 * z + y)

        @pl.when(is_line_first)
        def _():
            line_send(q + 1, k, lambda b: product(k, 2 * b + y))
            ysend[p, z] = product(k, 2 * z + 1 - y)
            line_own(q, ysend.at[p, z])
            y_copy(p, z).start()

    def pair_tick(k, work):
        p = lax.rem(k, Y_SLOTS)
        q = pass_of(k)
        prefetch(k)

        def rows_in(b, carry):
            y_copy(p, b).wait_recv()
            bpar[row_block(b), :] = yrecv[p, b].astype(BF16)
            return carry
        lax.fori_loop(0, line, rows_in, 0)
        line_send(q, k, lambda b: pair_product(k, 2 * b + 1 - y))
        finish_chunk(k - 1, q - 1)
        send_ahead(k)
        work(q)
        line_send(q + 1, k, lambda b: pair_product(k, 2 * b + y))
        own[...] = pair_product(k, 2 * z + y)
        fsend[p] = pair_product(k, 2 * z + 1 - y)
        line_own(q, fsend.at[p])
        final_copy(p).start()

    nt = (((1,), (1,)), ((), ()))

    def copies_of(sem, *pairs):
        return [pltpu.make_async_copy(src, dst, sem.at[i]) for i, (src, dst) in enumerate(pairs)]

    def start(copies):
        for copy in copies:
            copy.start()

    def finish(copies):
        for copy in copies:
            copy.wait()

    first_pair, last_pair = n_down, n_down + 2 * n_pairs

    def run_ticks(first, last, work):
        def do_work(at_half):
            for when, fn in work.items():
                low, high = when if isinstance(when, tuple) else (when, when + 1)

                @pl.when((at_half >= low) & (at_half < high))
                def _(fn=fn, low=low, high=high):
                    if isinstance(fn, list):
                        for one in fn:
                            one()
                    elif low + 1 == high:
                        fn()
                    else:
                        fn(at_half - low)

        def single(at_half, carry):
            k = jnp.where(at_half < first_pair, at_half, at_half - n_pairs)
            tick(k)
            do_work(at_half)
            return carry

        def double(m, carry):
            at_half = first_pair + 2 * m
            pair_tick(first_pair + m, lambda q: do_work(at_half))
            do_work(at_half + 1)
            return carry
        if first < first_pair:
            lax.fori_loop(first, min(last, first_pair), single, 0)
        low, high = max(first, first_pair), min(last, last_pair)
        if low < high:
            lax.fori_loop((low - first_pair) // 2, (high - first_pair) // 2, double, 0)
        if last > last_pair:
            lax.fori_loop(max(first, last_pair), last, single, 0)

    def part(fn, *args):
        return functools.partial(fn, *args)

    def side_rows(s, c):
        return pl.ds(s * half + c * chunk, chunk)

    def both_sides(hbm, buf, c, out=False):
        pairs = [(hbm.at[side_rows(s, c)], buf.at[pl.ds(s * chunk, chunk)]) for s in range(2)]
        return [(b, a) for a, b in pairs] if out else pairs

    def sequence_rows(s, c):
        return pl.ds(pl.multiple_of(2 * c * chunk + jnp.where(core == s, 0, chunk), chunk), chunk)

    def core_copy(c, again):
        ss, rs = (cs2_sem, cr2_sem) if again else (cs_sem, cr_sem)
        return remote(cs, crecv.at[c], ss.at[c], rs.at[c], at_tensor(sibling))

    def x_copy(c, again):
        ss, rs = (xs2_sem, xr2_sem) if again else (xs_sem, xr_sem)
        return remote(xs.at[c], xr.at[c], ss.at[c], rs.at[c], at_tensor(across))

    def to_sibling(c, again):
        ss, rs = (as2_sem, ar2_sem) if again else (as_sem, ar_sem)
        return remote(xr.at[c], ag.at[c % 2], ss.at[c], rs.at[c], at_tensor(sibling))

    def pass_on(c, again):
        core_copy(c, again).wait_recv()
        xs[c] += crecv[c]
        x_copy(c, again).start()
        core_copy(c, again).wait_send()

    hidden = wd_hbm.shape[0]

    def feed_phase(wd, grads, gates, ups, ggr, gur, far_rows):
        far_piece = full // ROW_CHUNKS

        def far_load(c):
            return copies_of(
                tok_sem, (partner_hbm.at[pl.ds(c * far_piece, far_piece)], far_rows))

        def far_turn(c):
            finish(far_load(c))
            at[2, :, pl.ds(c * far_piece, far_piece)] = far_rows[...].astype(BF16).T
            if c + 1 < ROW_CHUNKS:
                start(far_load(c + 1))

        def loads(c):
            return copies_of(
                pre_sem, *both_sides(gdr_hbm, grads, c), *both_sides(gate_hbm, gates, c),
                *both_sides(up_hbm, ups, c))

        def stores(c):
            return copies_of(
                st_sem, *both_sides(ggr_hbm, ggr, c, True), *both_sides(gur_hbm, gur, c, True))

        def piece(c):
            finish(loads(c))
            if c >= 1:
                finish(stores(c - 1))

            def tile(n, carry):
                cols = pl.ds(pl.multiple_of(n * TILE, TILE), TILE)
                grad = lax.dot_general(grads[...], wd[cols, :], nt, preferred_element_type=F32)
                gate = gates[:, cols]
                sig = jax.nn.sigmoid(gate)
                act = gate * sig
                ggr[:, cols] = (grad * ups[:, cols] * (sig + act * (1.0 - sig))).astype(BF16)
                gur[:, cols] = (grad * act).astype(BF16)
                return carry
            lax.fori_loop(0, hidden // TILE, tile, 0)
            start(stores(c))
            if c + 1 < ROW_CHUNKS:
                start(loads(c + 1))

        load_weight = copies_of(w_sem, (wd_hbm, wd))
        start(load_weight)
        start(loads(0))
        start(far_load(0))
        at_load(0).wait()
        pair_send(jnp.int32(0))
        pair_send(jnp.int32(1))
        finish(load_weight)
        piece(0)
        far_turn(0)
        run_ticks(0, FEED_TICK, {
            c - 1: [part(piece, c), part(far_turn, c)] for c in range(1, ROW_CHUNKS)})
        finish(stores(ROW_CHUNKS - 1))

    def hidden_phase(weights, ggr, gur):
        load_weights = copies_of(w_sem, (wg_hbm, weights.at[0]), (wu_hbm, weights.at[1]))

        def loads(c):
            return copies_of(pre_sem, *both_sides(ggr_hbm, ggr, c), *both_sides(gur_hbm, gur, c))

        def piece(c):
            if c == 0:
                finish(load_weights)
            else:
                pass_on(c - 1, False)
            finish(loads(c))

            def tile(n, carry):
                rows = pl.ds(pl.multiple_of(n * TILE, TILE), TILE)
                total_part = lax.dot_general(ggr[...], weights[0, rows, :], nt, preferred_element_type=F32)
                total_part = total_part + lax.dot_general(
                    gur[...], weights[1, rows, :], nt, preferred_element_type=F32)
                xs[c, :, rows] = total_part[0:chunk]
                cs[:, rows] = total_part[chunk : 2 * chunk]
                return carry
            lax.fori_loop(0, width // TILE, tile, 0)
            core_copy(c, False).start()
            if c + 1 < ROW_CHUNKS:
                start(loads(c + 1))

        start(load_weights)
        start(loads(0))
        run_ticks(
            FEED_TICK, HIDDEN_TICK, {FEED_TICK + c: part(piece, c) for c in range(ROW_CHUNKS)})

    def branch_phase(branch, seed, low, turned, w_out, mixed_grad, token_rows, seg_live):
        load_weight = copies_of(w_sem, (w_out_hbm, w_out))
        load_live = copies_of(live_sem, (seg_live_hbm, seg_live))
        token_piece = full // ROW_CHUNKS

        def loads(c):
            rows = pl.ds(c * chunk, chunk)
            return copies_of(
                pre_sem, (branch_hbm.at[rows], branch), (cot_hbm.at[sequence_rows(0, c)], seed))

        def stores(c):
            i = c % 2
            return copies_of(
                st_sem.at[pl.ds(4 * i, 4)],
                (turned.at[i, :, pl.ds(0, chunk)], gbt_hbm.at[:, side_rows(0, c)]),
                (turned.at[i, :, pl.ds(chunk, chunk)], gbt_hbm.at[:, side_rows(1, c)]),
                *[(
                    mixed_grad.at[i, pl.ds(s * chunk, chunk)],
                    gqkv_hbm.at[sequence_rows(s, c), pl.ds(2 * head_cols, head_cols)],
                ) for s in range(2)])

        def hidden_store(c):
            return copies_of(gh_sem, (xs.at[c], gh_hbm.at[pl.ds(c * chunk, chunk)]))

        def token_load(c):
            return copies_of(tok_sem, (tok_hbm.at[pl.ds(c * token_piece, token_piece)], token_rows))

        def first(c):
            i = c % 2
            finish(loads(c))
            if c == 0:
                finish(load_live)
            x_copy(c, False).wait()
            live = seg_live[sequence_rows(0, c), 1:2].astype(F32)
            grad_hidden = xs[c] + xr[c] + seed[...].astype(F32) * live
            xs[c] = grad_hidden
            start(hidden_store(c))
            values = branch[...]
            inv = mean_inverse(values)
            vec[1:2, :] += column_sum(grad_hidden * values * inv)
            scaled = grad_hidden * attn_gain[...]
            dot = jnp.sum(scaled * values, axis=1, keepdims=True)
            grad = inv * scaled - values * (inv * inv * inv * dot / width)
            xr[c] = grad
            to_sibling(c, False).start()
            if c >= 2:
                finish(stores(c - 2))
            low[i, 0:chunk, :] = grad.astype(BF16)
            turned[i, :, 0:chunk] = grad.astype(BF16).T
            if c + 1 < ROW_CHUNKS:
                start(loads(c + 1))

        def second(c):
            i = c % 2
            to_sibling(c, False).wait_recv()
            if c == 0:
                finish(load_weight)
            other = ag[i].astype(BF16)
            low[i, chunk : 2 * chunk, :] = other
            turned[i, :, chunk : 2 * chunk] = other.T
            mixed_grad[i] = lax.dot_general(
                low[i], w_out[...], nt, preferred_element_type=F32).astype(BF16)
            start(stores(c))
            finish(hidden_store(c))
            to_sibling(c, False).wait_send()

        def turn(c):
            finish(token_load(c))
            at[0, :, pl.ds(c * token_piece, token_piece)] = token_rows[...].T
            if c + 1 < ROW_CHUNKS:
                start(token_load(c + 1))

        start(load_weight)
        start(load_live)
        start(loads(0))
        start(token_load(0))
        work = {HIDDEN_TICK + c: [] for c in range(ROW_CHUNKS + 1)}
        work[HIDDEN_TICK].append(part(pass_on, ROW_CHUNKS - 1, False))
        for c in range(ROW_CHUNKS):
            work[HIDDEN_TICK + c].append(part(first, c))
            work[HIDDEN_TICK + c + 1].append(part(second, c))
        work[HIDDEN_TICK + 3] += [part(turn, 0)]
        work[HIDDEN_TICK + 4] += [part(turn, c) for c in range(1, ROW_CHUNKS)]
        run_ticks(HIDDEN_TICK, BRANCH_TICK, work)
        for c in range(ROW_CHUNKS - 2, ROW_CHUNKS):
            finish(stores(c))

    def attention_phase(
        query, key, value, mixed_grad, dq, dk, dv, raw, bias, inverses, seg_live, cosine, sine,
    ):
        heads = head_cols // HEAD
        q_rows = min(256, full)
        scale = HEAD ** (-0.5)
        value_cols = pl.ds(2 * head_cols, head_cols)
        loads = copies_of(
            pre_sem, (query_hbm, query), (key_hbm, key), (value_hbm, value),
            (gqkv_hbm.at[:, value_cols], mixed_grad))
        load_tables = copies_of(
            w_sem, (inverses_hbm, inverses), (seg_live_hbm, seg_live), (cos_hbm, cosine), (sin_hbm, sine))

        def masks():
            finish(load_tables)
            for i in range(full // q_rows):
                rows, keys = slice(i * q_rows, (i + 1) * q_rows), (i + 1) * q_rows
                key_at = lax.broadcasted_iota(jnp.int32, (keys, q_rows), 0)
                query_at = lax.broadcasted_iota(jnp.int32, (keys, q_rows), 1) + i * q_rows
                allowed = (
                    (seg_live[0:keys, 0:1] == seg_row[:, rows])
                    & (key_at <= query_at)
                    & ((seg_live[0:keys, 1:2] > 0) | (key_at == query_at)))
                bias[0:keys, rows] = jnp.where(allowed, 0.0, NEG_FILL).astype(BF16)
            finish(loads)

        def head(h):
            cols = pl.ds(pl.multiple_of(h * HEAD, HEAD), HEAD)
            dk[:, cols] = jnp.zeros((full, HEAD), F32)
            dv[...] = jnp.zeros((full, HEAD), F32)
            for i in range(full // q_rows):
                rows, keys = slice(i * q_rows, (i + 1) * q_rows), (i + 1) * q_rows
                q_block, grad_block = query[rows, cols], mixed_grad[rows, cols]
                key_block, value_block = key[0:keys, cols], value[0:keys, cols]
                scores = lax.dot_general(key_block, q_block, nt, preferred_element_type=F32) * scale
                prob = jnp.exp(scores + bias[0:keys, rows].astype(F32) - log_totals[pl.ds(h, 1), rows])
                grad_prob = lax.dot_general(value_block, grad_block, nt, preferred_element_type=F32)
                row_dot = jnp.sum(prob * grad_prob, axis=0, keepdims=True)
                grad_scores = (prob * (grad_prob - row_dot)).astype(BF16)
                dq[rows, cols] = lax.dot_general(
                    grad_scores, key_block, (((0,), (0,)), ((), ())), preferred_element_type=F32) * scale
                dk[0:keys, cols] += jnp.dot(grad_scores, q_block, preferred_element_type=F32) * scale
                dv[0:keys, :] += jnp.dot(prob.astype(BF16), grad_block, preferred_element_type=F32)
            mixed_grad[:, cols] = dv[...].astype(BF16)

        store_value = copies_of(st_sem, (mixed_grad, gqkv_hbm.at[:, value_cols]))
        sides = ((dq, query_raw_hbm, query_gain), (dk, key_raw_hbm, key_gain))

        def load_raw(which):
            return copies_of(pre_sem, (sides[which][1], raw))

        def back(which):
            grads, _, gain = sides[which]
            finish(load_raw(which))
            gains = gain[...].astype(F32)
            lanes = lax.broadcasted_iota(jnp.int32, (q_rows, HEAD), 1)

            def block_back(i, carry):
                rows = pl.ds(pl.multiple_of(i * q_rows, q_rows), q_rows)
                dot = jnp.zeros((q_rows, 1), F32)
                for h in range(heads):
                    cols = slice(h * HEAD, (h + 1) * HEAD)
                    grad = grads[rows, cols]
                    grad = grad * cosine[rows, :] - pltpu.roll(grad, HEAD // 2, 1) * sine[rows, :]
                    raw_rows = raw[rows, cols]
                    gain_cols = slice(which * head_cols + h * HEAD, which * head_cols + (h + 1) * HEAD)
                    vec[2:3, gain_cols] += column_sum(
                        grad * raw_rows * inverses[rows, which : which + 1])
                    scaled = grad * gains[h : h + 1, :]
                    grads[rows, cols] = scaled
                    dot = dot + jnp.sum(scaled * raw_rows, axis=1, keepdims=True)
                if which == 0:
                    dots[rows, :] = jnp.broadcast_to(dot, (q_rows, HEAD))
                else:
                    dots[rows, :] = jnp.where(lanes == 0, dots[rows, :], dot)
                return carry
            lax.fori_loop(0, full // q_rows, block_back, 0)

        def dots_copy(i):
            return remote(
                dots, dots_in.at[i], ds_sem.at[i], dr_sem.at[i], at_tensor((sibling, across)[i]))

        def dots_add(i):
            dots_copy(i).wait()
            dots[...] += dots_in[i]

        def combine(which):
            grads = sides[which][0]
            for i in range(full // q_rows):
                rows = slice(i * q_rows, (i + 1) * q_rows)
                inv_rows = inverses[rows, which : which + 1]
                dot = dots[rows, which : which + 1]
                mixed_grad[rows, :] = (
                    inv_rows * grads[rows, :]
                    - raw[rows, :] * (inv_rows * inv_rows * inv_rows * dot / width)
                ).astype(BF16)

        def store_grads(which):
            return copies_of(
                st_sem, (mixed_grad, gqkv_hbm.at[:, pl.ds(which * head_cols, head_cols)]))

        def after_heads():
            start(store_value)
            start(load_raw(0))

        def back_query():
            back(0)
            start(load_raw(1))

        def back_key():
            back(1)
            dots_copy(0).start()
            finish(store_value)

        def first_sum():
            dots_add(0)
            dots_copy(1).start()

        def second_sum():
            dots_add(1)
            combine(1)
            start(store_grads(1))
            start(load_raw(0))

        def last_part():
            finish(store_grads(1))
            finish(load_raw(0))
            combine(0)
            start(store_grads(0))

        start(loads)
        start(load_tables)
        t = BRANCH_TICK
        run_ticks(t, INPUT_TICK, {
            t: masks,
            (t, t + heads): head,
            t + heads - 1: after_heads,
            t + heads: back_query,
            t + heads + 1: back_key,
            t + heads + 2: first_sum,
            t + heads + 3: [second_sum, last_part],
        })
        finish(store_grads(0))

    def input_phase(weights, grads, grad_hidden, low):
        loads = copies_of(
            w_sem, *[(w, weights.at[i]) for i, w in enumerate((wq_hbm, wk_hbm, wv_hbm))],
            (gqkv_hbm, grads))

        def piece(c):
            if c == 0:
                finish(loads)
            else:
                pass_on(c - 1, True)
            for s in range(2):
                rows = sequence_rows(s, c)

                def tile(n, carry):
                    cols = pl.ds(pl.multiple_of(n * TILE, TILE), TILE)
                    total_part = jnp.zeros((chunk, TILE), F32)
                    for i in range(3):
                        total_part = total_part + lax.dot_general(
                            grads[rows, i * head_cols : (i + 1) * head_cols], weights[i, cols, :],
                            nt, preferred_element_type=F32)
                    if s == 0:
                        xs[c, :, cols] = total_part
                    else:
                        cs[:, cols] = total_part
                    return carry
                lax.fori_loop(0, width // TILE, tile, 0)
            core_copy(c, True).start()

        def hidden_load(c):
            return copies_of(gh_sem, (gh_hbm.at[pl.ds(c * chunk, chunk)], grad_hidden))

        def stores(c):
            return copies_of(
                st_sem, *[(low.at[s], token_out.at[sequence_rows(s, c)]) for s in range(2)])

        def first(c):
            finish(hidden_load(c))
            x_copy(c, True).wait()
            xr[c] = xs[c] + xr[c] + grad_hidden[...]
            to_sibling(c, True).start()
            if c + 1 < ROW_CHUNKS:
                start(hidden_load(c + 1))

        def second(c):
            if c >= 1:
                finish(stores(c - 1))
            low[0] = xr[c].astype(BF16)
            to_sibling(c, True).wait_recv()
            low[1] = ag[c % 2].astype(BF16)
            start(stores(c))
            to_sibling(c, True).wait_send()

        vec_peer_ids = [at_tensor(sibling)] + [at_dp(peer) for peer in vec_peers]

        def vec_copy(i):
            return remote(vec, vec_in.at[i], vs_sem.at[i], vr_sem.at[i], vec_peer_ids[i])

        def vec_step(i):
            if i >= 1:
                vec_copy(i - 1).wait()
                if i == 1:
                    vec[0:2, :] += vec_in[0, 0:2, :]
                else:
                    vec[...] += vec_in[i - 1]
            if i < len(vec_peer_ids):
                vec_copy(i).start()

        start(loads)
        start(hidden_load(0))
        halves = total + n_pairs
        work = {k: [] for k in range(INPUT_TICK, halves)}
        for c in range(ROW_CHUNKS):
            work[INPUT_TICK + c].append(part(piece, c))
            work[TOKEN_TICK + c].append(part(first, c))
            work[TOKEN_TICK + c + 1].append(part(second, c))
        work[INPUT_TICK + ROW_CHUNKS].append(part(pass_on, ROW_CHUNKS - 1, True))
        for i in range(len(vec_peer_ids) + 1):
            work[INPUT_TICK + 2 + i].append(part(vec_step, i))
        work[last_pair + 1].append(lambda: at_load(3).start())
        work[last_pair + 2].append(lambda: at_load(3).wait())
        run_ticks(INPUT_TICK, halves, {k: fns for k, fns in work.items() if fns})
        finish(stores(ROW_CHUNKS - 1))

    vec[...] = jnp.zeros(vec.shape, F32)
    vec[0:1, :] = gain_mlp_part[...]
    at_load(0).start()
    at_load(1).start()
    for k in range(2):
        b_load(jnp.int32(k), lambda copy: copy.start())
    barrier = pltpu.get_barrier_semaphore()

    def greet_one(peer):
        pl.semaphore_signal(barrier, inc=1, device_id=peer, device_id_type=MESH)

    other_z = z - 1 + 2 * lax.rem(z, 2)
    has_other = (other_z >= 0) & (other_z < line)
    for peer in vec_peers:
        greet_one(at_dp(peer))
    greet_one(at_tensor(sibling))
    greet_one(at_tensor(across))

    @pl.when(has_other)
    def _():
        greet_one(at_dp(2 * other_z + y))
    pl.semaphore_wait(barrier, len(steps) + 2 + has_other.astype(jnp.int32))

    both = 2 * chunk
    rows_of = (full, head_cols)
    pl.run_scoped(
        feed_phase, pltpu.VMEM(wd_hbm.shape, BF16), pltpu.VMEM((both, width), BF16),
        pltpu.VMEM((both, hidden), F32), pltpu.VMEM((both, hidden), F32),
        pltpu.VMEM((both, hidden), BF16), pltpu.VMEM((both, hidden), BF16),
        pltpu.VMEM((full // ROW_CHUNKS, width), F32))
    at_load(1).wait()
    pl.run_scoped(
        hidden_phase, pltpu.VMEM((2,) + wg_hbm.shape, BF16), pltpu.VMEM((both, hidden), BF16),
        pltpu.VMEM((both, hidden), BF16))
    pl.run_scoped(
        branch_phase, pltpu.VMEM((chunk, width), F32), pltpu.VMEM((chunk, width), BF16),
        pltpu.VMEM((2, both, width), BF16), pltpu.VMEM((2, width, both), BF16),
        pltpu.VMEM(w_out_hbm.shape, BF16), pltpu.VMEM((2, both, head_cols), BF16),
        pltpu.VMEM((full // ROW_CHUNKS, width), BF16), pltpu.VMEM(seg_live_hbm.shape, jnp.int32))
    pl.run_scoped(
        attention_phase, pltpu.VMEM(rows_of, BF16), pltpu.VMEM(rows_of, BF16), pltpu.VMEM(rows_of, BF16),
        pltpu.VMEM(rows_of, BF16), pltpu.VMEM(rows_of, F32), pltpu.VMEM(rows_of, F32),
        pltpu.VMEM((full, HEAD), F32), pltpu.VMEM(rows_of, F32), pltpu.VMEM((full, full), BF16),
        pltpu.VMEM((full, HEAD), F32), pltpu.VMEM(seg_live_hbm.shape, jnp.int32),
        pltpu.VMEM((full, HEAD), F32), pltpu.VMEM((full, HEAD), F32))
    pl.run_scoped(
        input_phase, pltpu.VMEM((3,) + wq_hbm.shape, BF16), pltpu.VMEM((full, 3 * head_cols), BF16),
        pltpu.VMEM((chunk, width), F32), pltpu.VMEM((2, chunk, width), BF16))
    finish_chunk(jnp.int32(total - 1), jnp.int32(passes - 1))
    out_act(jnp.int32(total - 1), lambda copy: copy.wait())
    gains_out[...] = jnp.zeros(gains_out.shape, F32)
    gains_out[0:8, :] = vec[...]
    for h in range(2 * head_cols // HEAD):
        gains_out[8 + h : 9 + h, 0:HEAD] = vec[2:3, h * HEAD : (h + 1) * HEAD]


def backward_layer(dp_size, hbm, vmem_args):
    names = dict(zip(HBM_NAMES, hbm, strict=True))
    width, row_count = names["gdrt"].shape
    hidden, head_cols = names["inner"].shape[1], names["query"].shape[1]
    line, block = dp_size // 2, width // dp_size
    chunk = row_count // 2 // ROW_CHUNKS
    counts = (hidden // COLS, hidden // COLS, 3 * head_cols // COLS, head_cols // COLS)
    DMA, REG = pltpu.SemaphoreType.DMA, pltpu.SemaphoreType.REGULAR
    vmem, any_space = pl.BlockSpec(memory_space=pltpu.VMEM), pl.BlockSpec(memory_space=pl.ANY)

    def shape(*dims, kind=F32):
        return jax.ShapeDtypeStruct(dims, kind)

    slot = (block, COLS)
    per_chunk = DMA((ROW_CHUNKS,))
    steps = dp_size.bit_length() - 1
    results = pl.pallas_call(
        functools.partial(backward_kernel, dp_size, counts),
        out_shape=(
            shape(hidden, block),
            shape(head_cols, block),
            shape(block, hidden),
            shape(block, hidden),
            shape(block, head_cols),
            shape(block, head_cols),
            shape(block, head_cols),
            shape(row_count, width, kind=BF16),
            shape(8 + 2 * head_cols // HEAD, width),
            shape(row_count, hidden, kind=BF16),
            shape(row_count, hidden, kind=BF16),
            shape(width, row_count, kind=BF16),
            shape(row_count // 2, width),
            shape(row_count, 3 * head_cols, kind=BF16),
        ),
        in_specs=[any_space] * len(hbm) + [vmem] * len(vmem_args),
        out_specs=(any_space,) * 8 + (vmem,) + (any_space,) * 5,
        scratch_shapes=[
            pltpu.VMEM((3, width, row_count), BF16),
            pltpu.VMEM((B_SLOTS, row_count, COLS), BF16),
            pltpu.VMEM((row_count, COLS), BF16),
            pltpu.VMEM((row_count, COLS), BF16),
            pltpu.VMEM(slot, F32),
            pltpu.VMEM((Y_SLOTS, line) + slot, F32),
            pltpu.VMEM((Y_SLOTS, line) + slot, F32),
            pltpu.VMEM((Y_SLOTS,) + slot, F32),
            pltpu.VMEM((Y_SLOTS,) + slot, F32),
            pltpu.VMEM((2, line) + slot, F32),
            pltpu.VMEM((2, line + 1) + slot, F32),
            pltpu.VMEM(slot, F32),
            pltpu.VMEM((COLS, block), F32),
            pltpu.VMEM((chunk, width), F32),
            pltpu.VMEM((ROW_CHUNKS, chunk, width), F32),
            pltpu.VMEM((ROW_CHUNKS, chunk, width), F32),
            pltpu.VMEM((ROW_CHUNKS, chunk, width), F32),
            pltpu.VMEM((2, chunk, width), F32),
            pltpu.VMEM((row_count, HEAD), F32),
            pltpu.VMEM((2, row_count, HEAD), F32),
            pltpu.VMEM((8, width), F32),
            pltpu.VMEM((steps + 1, 8, width), F32),
            DMA((2,)),
            DMA((B_SLOTS,)),
            DMA,
            DMA((Y_SLOTS, line)),
            DMA((Y_SLOTS, line)),
            DMA((Y_SLOTS,)),
            DMA((Y_SLOTS,)),
            DMA((2, line)),
            DMA((2, line + 1)),
            DMA,
            DMA,
        ]
        + [per_chunk] * 12
        + [DMA((2,)), DMA((2,)), DMA((steps + 1,)), DMA((steps + 1,)), DMA((4,)), DMA((6,)), DMA((8,)), DMA((1,)), DMA((1,)), DMA((1,)),
           REG, REG, REG],
        compiler_params=pltpu.CompilerParams(
            collective_id=2, has_side_effects=True, vmem_limit_bytes=VMEM_LIMIT),
    )(*hbm, *vmem_args)
    return results[:9]


def rope_tables():
    half_size = HEAD // 2
    freq_row = ROPE_BASE ** (-(np.arange(half_size, dtype=np.float64) * 2.0) / HEAD)
    angle = (np.arange(LENGTH, dtype=np.float64)[:, None] * freq_row[None, :]).astype(np.float32)
    cosine, sine = np.cos(angle), np.sin(angle)
    return np.concatenate((cosine, cosine), 1), np.concatenate((-sine, sine), 1)


def make_shards(dp_size):
    def shards(
        tokens,
        segments,
        pad_mask,
        w_query,
        w_key,
        w_value,
        w_out,
        gain_query,
        gain_key,
        gain_attn,
        w_gate,
        w_up,
        w_down,
        gain_mlp,
        cotangent,
    ):
        block = tokens.shape[1] // dp_size
        cosine, sine = (jnp.asarray(table, F32) for table in rope_tables())
        seg_live = jnp.stack((segments, pad_mask), 1)
        seg_row = segments[None, :]
        attn_gain = gain_attn.astype(F32)[None, :]
        mlp_gain = gain_mlp.astype(F32)[None, :]
        (
            gate_rows,
            up_rows,
            inner_rows,
            hidden_turned,
            grad_down_rows,
            grad_down_turned,
            branch_rows,
            output,
            query_norm,
            key_norm,
            value_rows,
            query_raw,
            key_raw,
            mixed_rows,
            partner_rows,
            gain_mlp_part,
            inverses,
            log_totals,
        ) = forward_layer(
            (
                tokens, cotangent, w_query, w_key, w_value, w_out, w_gate, w_up, w_down, cosine, sine,
            ),
            (seg_live, seg_row, gain_query, gain_key, attn_gain, mlp_gain),
        )
        (
            grad_down,
            grad_out,
            grad_gate,
            grad_up,
            grad_query,
            grad_key,
            grad_value,
            grad_tokens,
            gains,
        ) = backward_layer(
            dp_size,
            (
                grad_down_turned, hidden_turned, tokens, inner_rows, mixed_rows, grad_down_rows,
                gate_rows, up_rows, branch_rows, cotangent,
                query_norm, key_norm, value_rows, query_raw, key_raw, partner_rows,
                inverses, seg_live, cosine, sine,
                w_out, w_gate, w_up, w_down, w_query, w_key, w_value,
            ),
            (
                log_totals, seg_row, gain_query, gain_key, attn_gain, gain_mlp_part,
            ),
        )
        heads, head_block = gain_query.shape[0], HEAD // dp_size
        dp_at = lax.axis_index("dp")
        wide = lax.dynamic_slice(gains, (0, dp_at * block), (2, block))
        head_gains = lax.dynamic_slice(gains, (8, dp_at * head_block), (2 * heads, head_block))
        return (
            output,
            grad_tokens,
            grad_query,
            grad_key,
            grad_value,
            grad_out,
            head_gains[:heads],
            head_gains[heads:],
            wide[1],
            grad_gate,
            grad_up,
            grad_down,
            wide[0],
        )

    return shards


def solution(mesh):
    in_specs = (
        P("dp", None),
        P("dp"),
        P("dp"),
        P(None, "tensor"),
        P(None, "tensor"),
        P(None, "tensor"),
        P("tensor", None),
        P("tensor", None),
        P("tensor", None),
        P(),
        P(None, "tensor"),
        P(None, "tensor"),
        P("tensor", None),
        P(),
        P("dp", None),
    )
    out_specs = (
        P("dp", None),
        P("dp", None),
        P("dp", "tensor"),
        P("dp", "tensor"),
        P("dp", "tensor"),
        P("tensor", "dp"),
        P("tensor", "dp"),
        P("tensor", "dp"),
        P("dp"),
        P("dp", "tensor"),
        P("dp", "tensor"),
        P("tensor", "dp"),
        P("dp"),
    )
    shards = make_shards(mesh.shape["dp"])
    return jax.shard_map(shards, mesh=mesh, in_specs=in_specs, out_specs=out_specs, check_vma=False)
```

```python
import functools

import jax
import jax.numpy as jnp
import numpy as np
from jax import lax
from jax.experimental import pallas as pl
from jax.experimental.pallas import tpu as pltpu
from jax.sharding import PartitionSpec as P

HEAD = 128
LENGTH = 1024
EPSILON = 1e-06
NEG_FILL = -1e30
ROPE_BASE = 500000.0
ROW_CHUNKS = 4
F32 = jnp.float32
BF16 = jnp.bfloat16


COLS = 256
LINE_FIRST = (0, 4)
Y_SLOTS = 3
B_SLOTS = 3
FEED_TICK = 3
HIDDEN_TICK = 7
BRANCH_TICK = 12
INPUT_TICK = 20
TOKEN_TICK = 25
HBM_NAMES = (
    "gdrt", "hlt", "tokens", "inner", "mixed", "gdr", "gate", "up", "branch", "cotangent",
    "query", "key", "value", "query_raw", "key_raw", "partner",
    "inverses", "seg_live", "cosine", "sine",
    "w_out", "w_gate", "w_up", "w_down", "w_query", "w_key", "w_value",
)
TILE = 512
VMEM_LIMIT = 65400 * 1024
MESH = pl.DeviceIdType.MESH

def column_sum(values):
    return jnp.sum(values, axis=0, keepdims=True)


def mean_inverse(values):
    return lax.rsqrt(jnp.mean(values * values, axis=1, keepdims=True) + EPSILON)


def tensor_peers():
    at = lax.axis_index("tensor")
    core = lax.rem(at, 2)
    return core, at + 1 - 2 * core, lax.rem(at + 2, 4)


def greet(*peers):
    barrier = pltpu.get_barrier_semaphore()
    for peer in peers:
        pl.semaphore_signal(barrier, inc=1, device_id=peer, device_id_type=MESH)
    pl.semaphore_wait(barrier, len(peers))


def forward_kernel(
    tok_hbm, cot_hbm, wq_hbm, wk_hbm, wv_hbm, wo_hbm, wg_hbm, wu_hbm, wd_hbm, cos_hbm, sin_hbm,
    seg_live, seg_row, query_gain, key_gain, attn_gain, mlp_gain,
    gate_out, up_out, inner_out, hlt_out, gdr_out, gdrt_out, branch_out, out_out,
    query_out, key_out, value_out, query_raw_out, key_raw_out, mixed_out, partner_out,
    gain_out, inverse_out, log_out,
    wg, cs, crecv, xs, xr, xr2, ag, squares, squares_in,
    w_sem, t_sem, s_sem, a_sem, r_sem, m_sem, sq_s_sem, sq_r_sem, sx_s_sem, sx_r_sem,
    cs_sem, cr_sem, xs_sem, xr_sem, as_sem, ar_sem, cs2_sem, cr2_sem, xs2_sem, xr2_sem,
    gs_sem, gr_sem, os_sem, or_sem, hs_sem, hr_sem, fs_sem, fr_sem, g_sem, h_sem, b_sem, d_sem, o_sem,
):
    core, sibling, across = tensor_peers()
    dp_at = lax.axis_index("dp")
    partner = dp_at + 1 - 2 * lax.rem(dp_at, 2)
    chunk = xs.shape[1]
    half = chunk * ROW_CHUNKS
    full = 2 * half
    both = 2 * chunk
    width, hidden = xs.shape[2], wg.shape[1]
    head_cols = wq_hbm.shape[1]
    heads = head_cols // HEAD
    tiles = hidden // TILE
    wide_tiles = width // TILE
    last = ROW_CHUNKS - 1
    nt = (((1,), (1,)), ((), ()))

    def start(copies):
        for copy in copies:
            copy.start()

    def finish(copies):
        for copy in copies:
            copy.wait()

    def own_rows(s, c):
        return pl.ds(pl.multiple_of(c * both + jnp.where(core == s, 0, chunk), chunk), chunk)

    def row_load(c, src, dst, sem):
        return pltpu.make_async_copy(src.at[own_rows(0, c)], dst.at[c % 2], sem.at[c % 2])

    wide_loads = [pltpu.make_async_copy(wg_hbm, wg, w_sem.at[0])]

    def remote(src, dst, send_sem, recv_sem, peer):
        return pltpu.make_async_remote_copy(
            src_ref=src, dst_ref=dst, send_sem=send_sem, recv_sem=recv_sem,
            device_id={"tensor": peer}, device_id_type=MESH)

    def partner_copy(c):
        return pltpu.make_async_remote_copy(
            src_ref=xr.at[c], dst_ref=partner_out.at[rows(c * chunk)], send_sem=hs_sem.at[c],
            recv_sem=hr_sem.at[c], device_id={"dp": partner}, device_id_type=MESH)

    def hand_copy(c):
        return remote(
            partner_out.at[rows(c * chunk)], partner_out.at[rows(half + c * chunk)],
            fs_sem.at[c], fr_sem.at[c], sibling)

    def core_copy(c):
        return remote(cs.at[c % 2], crecv.at[c], cs_sem.at[c], cr_sem.at[c], sibling)

    def x_copy(c):
        return remote(xs.at[c], xr.at[c], xs_sem.at[c], xr_sem.at[c], across)

    def hidden_copy(c):
        return remote(xr.at[c], ag.at[c % 2], as_sem.at[c], ar_sem.at[c], sibling)

    def core2_copy(c):
        return remote(cs.at[c % 2], crecv.at[c], cs2_sem.at[c], cr2_sem.at[c], sibling)

    def x2_copy(c):
        return remote(xs.at[c], xr2.at[c], xs2_sem.at[c], xr2_sem.at[c], across)

    def grad_copy(c):
        return remote(xr2.at[c], ag.at[c % 2], gs_sem.at[c], gr_sem.at[c], sibling)

    def out_copy(c):
        return remote(xr.at[c], crecv.at[c], os_sem.at[c], or_sem.at[c], sibling)

    def rows(first):
        return pl.ds(first, chunk)

    def side_copies(buf, dst, sem, c):
        return [
            pltpu.make_async_copy(
                buf.at[pl.ds(s * chunk, chunk)], dst.at[rows(s * half + c * chunk)], sem.at[s])
            for s in range(2)
        ]

    def turned_copies(buf, dst, sem, c):
        return [
            pltpu.make_async_copy(
                buf.at[:, pl.ds(s * chunk, chunk)], dst.at[:, rows(s * half + c * chunk)], sem.at[s])
            for s in range(2)
        ]

    def square_copy(c):
        return remote(
            squares.at[c], squares_in.at[0, c], sq_s_sem.at[c], sq_r_sem.at[c], sibling)

    def square_x_copy(c):
        return remote(
            squares.at[c], squares_in.at[1, c], sx_s_sem.at[c], sx_r_sem.at[c], across)

    def square_pass_on(c):
        square_copy(c).wait()
        squares[c] += squares_in[0, c]
        square_x_copy(c).start()

    def project(c, weights, loads, tok, tok_load, query_raw, key_raw, value, value_turned):
        at = slice(c * both, (c + 1) * both)
        lanes = lax.broadcasted_iota(jnp.int32, (both, HEAD), 1)
        tok_load(c).wait()
        if c == 0:
            loads[0].wait()
        query_raw[at, :] = jnp.dot(tok[c % 2], weights[0], preferred_element_type=F32)
        if c == 0:
            loads[1].wait()
        key_raw[at, :] = jnp.dot(tok[c % 2], weights[1], preferred_element_type=F32)
        query_square = jnp.sum(query_raw[at, :] * query_raw[at, :], axis=1, keepdims=True)
        key_square = jnp.sum(key_raw[at, :] * key_raw[at, :], axis=1, keepdims=True)
        squares[c] = jnp.where(lanes == 0, query_square, key_square)
        square_copy(c).start()
        if c == 0:
            loads[2].wait()
            start(wide_loads)
        if c == 1:
            square_pass_on(0)
        value[at, :] = jnp.dot(tok[c % 2], weights[2], preferred_element_type=F32).astype(BF16)
        value_turned[:, at] = value[at, :].T
        if c + 2 < ROW_CHUNKS:
            tok_load(c + 2).start()

    def attend(c, query_raw, key_raw, query, key, value_turned, cosine, sine, w_out, mixed, bias):
        first, keys = c * both, (c + 1) * both
        at = slice(first, keys)
        square_x_copy(c).wait()
        squares[c] += squares_in[1, c]
        inverse = lax.rsqrt(squares[c] / width + EPSILON)
        inverse_out[at, :] = inverse
        for raw, gain, lane, dst in (
            (query_raw, query_gain, 0, query), (key_raw, key_gain, 1, key)):
            gains = gain[...].astype(F32)
            for h in range(heads):
                cols = slice(h * HEAD, (h + 1) * HEAD)
                normed = raw[at, cols] * inverse[:, lane : lane + 1] * gains[h : h + 1, :]
                turned = normed * cosine[at, :] + pltpu.roll(normed, HEAD // 2, 1) * sine[at, :]
                dst[at, cols] = turned.astype(BF16)
        key_at = lax.broadcasted_iota(jnp.int32, (keys, both), 0)
        query_at = lax.broadcasted_iota(jnp.int32, (keys, both), 1) + first
        allowed = (
            (seg_live[0:keys, 0:1] == seg_row[:, at])
            & (key_at <= query_at)
            & ((seg_live[0:keys, 1:2] > 0) | (key_at == query_at)))
        bias[0:keys, :] = jnp.where(allowed, 0.0, NEG_FILL)

        def head(h, carry):
            cols = pl.ds(pl.multiple_of(h * HEAD, HEAD), HEAD)
            scores = lax.dot_general(
                key[0:keys, cols], query[at, cols], nt, preferred_element_type=F32) * HEAD ** (-0.5)
            scores = scores + bias[0:keys, :]
            top = jnp.max(scores, axis=0, keepdims=True)
            powers = jnp.exp(scores - top)
            total = jnp.sum(powers, axis=0, keepdims=True)
            prob = (powers / total).astype(BF16)
            log_out[pl.ds(h, 1), at] = top + jnp.log(total)
            turned = jnp.dot(value_turned[cols, 0:keys], prob, preferred_element_type=F32)
            mixed[c % 2, :, cols] = turned.T.astype(BF16)
            return carry
        lax.fori_loop(0, heads, head, 0)

        def mixed_rows(s):
            return pl.ds(pl.multiple_of(jnp.where(core == s, 0, chunk), chunk), chunk)
        if c + 1 < ROW_CHUNKS:
            square_pass_on(c + 1)
        if c >= 2:
            core_copy(c - 2).wait_send()
        cs[c % 2] = jnp.dot(mixed[c % 2, mixed_rows(1), :], w_out[...], preferred_element_type=F32)
        core_copy(c).start()
        xs[c] = jnp.dot(mixed[c % 2, mixed_rows(0), :], w_out[...], preferred_element_type=F32)
        start(mixed_copies(c, mixed))
        pass_on(c)

    def mixed_copies(c, mixed):
        return [
            pltpu.make_async_copy(
                mixed.at[c % 2, pl.ds(pl.multiple_of(jnp.where(core == s, 0, chunk), chunk), chunk)],
                mixed_out.at[rows(s * half + c * chunk)], m_sem.at[c % 2, s])
            for s in range(2)
        ]

    def pass_on(c):
        core_copy(c).wait_recv()
        xs[c] += crecv[c]
        x_copy(c).start()

    def attention(
        query_raw, key_raw, query, key, value, value_turned, cosine, sine, w_out, weights, tok, mixed, bias,
    ):
        def tok_load(c):
            return pltpu.make_async_copy(
                tok_hbm.at[pl.ds(c * both, both)], tok.at[c % 2], t_sem.at[c % 2])

        loads = [
            pltpu.make_async_copy(w, weights.at[i], a_sem.at[i])
            for i, w in enumerate((wq_hbm, wk_hbm, wv_hbm))
        ]
        tables = [
            pltpu.make_async_copy(src, dst, r_sem.at[i])
            for i, (src, dst) in enumerate(((cos_hbm, cosine), (sin_hbm, sine), (wo_hbm, w_out)))
        ]
        tok_load(0).start()
        start(loads)
        tok_load(1).start()
        start(tables)
        greet({"tensor": sibling}, {"tensor": across}, {"dp": partner})
        results = [
            pltpu.make_async_copy(src, dst, a_sem.at[i])
            for i, (src, dst) in enumerate((
                (value, value_out), (query_raw, query_raw_out), (key_raw, key_raw_out),
                (query, query_out), (key, key_out)))
        ]
        for c in range(ROW_CHUNKS + 1):
            if c < ROW_CHUNKS:
                project(c, weights, loads, tok, tok_load, query_raw, key_raw, value, value_turned)
            if c == 1:
                finish(tables)
            if c == last:
                start(results[:3])
            if c >= 1:
                if c >= 3:
                    finish(mixed_copies(c - 3, mixed))
                attend(
                    c - 1, query_raw, key_raw, query, key, value_turned, cosine, sine, w_out, mixed, bias)
        start(results[3:])
        for c in range(last - 1, ROW_CHUNKS):
            core_copy(c).wait_send()
            finish(mixed_copies(c, mixed))
        finish(results)

    rows_of = (full, head_cols)
    pl.run_scoped(
        attention, pltpu.VMEM(rows_of, F32), pltpu.VMEM(rows_of, F32), pltpu.VMEM(rows_of, BF16),
        pltpu.VMEM(rows_of, BF16), pltpu.VMEM(rows_of, BF16), pltpu.VMEM((head_cols, full), BF16),
        pltpu.VMEM((full, HEAD), F32), pltpu.VMEM((full, HEAD), F32), pltpu.VMEM(wo_hbm.shape, BF16),
        pltpu.VMEM((3,) + wq_hbm.shape, BF16), pltpu.VMEM((2, both, width), BF16),
        pltpu.VMEM((2, both, head_cols), BF16), pltpu.VMEM((full, both), F32))
    pl.run_scoped(
        functools.partial(
            feed_forward, core, chunk, own_rows, row_load, rows, side_copies, turned_copies,
            (x_copy, hidden_copy, core2_copy, x2_copy, grad_copy, out_copy, partner_copy, hand_copy), wide_loads, seg_live,
            (tok_hbm, cot_hbm, wu_hbm, wd_hbm, attn_gain, mlp_gain, wg),
            (gate_out, up_out, inner_out, hlt_out, gdr_out, gdrt_out, branch_out, out_out, gain_out),
            (cs, crecv, xs, xr, xr2, ag),
            (w_sem, t_sem, s_sem, g_sem, h_sem, b_sem, d_sem, o_sem)),
        pltpu.VMEM(wu_hbm.shape, BF16), pltpu.VMEM(wd_hbm.shape, BF16),
        pltpu.VMEM((both, hidden), F32), pltpu.VMEM((both, hidden), F32),
        pltpu.VMEM((both, hidden), BF16), pltpu.VMEM((both, width), BF16), pltpu.VMEM((width, both), BF16),
        pltpu.VMEM((both, width), BF16), pltpu.VMEM((2, chunk, width), BF16),
        pltpu.VMEM((2, chunk, width), BF16))


def feed_forward(
    core, chunk, own_rows, row_load, rows, side_copies, turned_copies, remote_copies, wide_loads, seg_live,
    operands, results, buffers, sems,
    wu, wd, gate_buf, up_buf, inner_buf, low_buf, hlt_buf, out_buf, tok, seed,
):
    x_copy, hidden_copy, core2_copy, x2_copy, grad_copy, out_copy, partner_copy, hand_copy = remote_copies
    tok_hbm, cot_hbm, wu_hbm, wd_hbm, attn_gain, mlp_gain, wg = operands
    gate_out, up_out, inner_out, hlt_out, gdr_out, gdrt_out, branch_out, out_out, gain_out = results
    cs, crecv, xs, xr, xr2, ag = buffers
    w_sem, t_sem, s_sem, g_sem, h_sem, b_sem, d_sem, o_sem = sems
    last = ROW_CHUNKS - 1
    tiles, wide_tiles = wg.shape[1] // TILE, wd.shape[1] // TILE
    loads = wide_loads + [
        pltpu.make_async_copy(wu_hbm, wu, w_sem.at[1]),
        pltpu.make_async_copy(wd_hbm, wd, w_sem.at[2]),
    ]
    loads[1].start()
    loads[2].start()
    for c in range(2):
        row_load(c, tok_hbm, tok, t_sem).start()
        row_load(c, cot_hbm, seed, s_sem).start()

    def hand_on(c):
        partner_copy(c).wait_recv()
        hand_copy(c).start()

    def feed(c):
        x_copy(c).wait()
        total = xs[c] + xr[c]
        xs[c] = total
        branch_copy = pltpu.make_async_copy(xs.at[c], branch_out.at[rows(c * chunk)], b_sem)
        branch_copy.start()
        row_load(c, tok_hbm, tok, t_sem).wait()
        hidden = tok[c % 2].astype(F32) + total * mean_inverse(total) * attn_gain[...]
        if c + 2 < ROW_CHUNKS:
            row_load(c + 2, tok_hbm, tok, t_sem).start()
        xr[c] = hidden
        hidden_copy(c).start()
        partner_copy(c).start()
        low_buf[0:chunk, :] = hidden.astype(BF16)
        if c >= 1:
            for copy in turned_copies(hlt_buf, hlt_out, h_sem, c - 1):
                copy.wait()
            for buf, dst, i in ((gate_buf, gate_out, 0), (up_buf, up_out, 1), (inner_buf, inner_out, 2)):
                for copy in side_copies(buf, dst, g_sem.at[i], c - 1):
                    copy.wait()
        hlt_buf[:, 0:chunk] = hidden.astype(BF16).T
        hidden_copy(c).wait_recv()
        low_buf[chunk : 2 * chunk, :] = ag[c % 2].astype(BF16)
        hlt_buf[:, chunk : 2 * chunk] = ag[c % 2].astype(BF16).T
        for copy in turned_copies(hlt_buf, hlt_out, h_sem, c):
            copy.start()
        if c == 0:
            loads[0].wait()
            loads[1].wait()

        def tile(n, carry):
            at = pl.ds(pl.multiple_of(n * TILE, TILE), TILE)
            gate = jnp.dot(low_buf[...], wg[:, at], preferred_element_type=F32)
            up = jnp.dot(low_buf[...], wu[:, at], preferred_element_type=F32)
            gate_buf[:, at] = gate
            up_buf[:, at] = up
            inner_buf[:, at] = (gate * jax.nn.sigmoid(gate) * up).astype(BF16)
            return carry
        lax.fori_loop(0, tiles, tile, 0)
        for buf, dst, i in ((gate_buf, gate_out, 0), (up_buf, up_out, 1), (inner_buf, inner_out, 2)):
            for copy in side_copies(buf, dst, g_sem.at[i], c):
                copy.start()
        if c == 0:
            loads[2].wait()
        if c >= 2:
            core2_copy(c - 2).wait_send()
        branch_copy.wait()

        def down_tile(n, carry):
            at = pl.ds(pl.multiple_of(n * TILE, TILE), TILE)
            part = jnp.dot(inner_buf[...], wd[:, at], preferred_element_type=F32)
            xs[c, :, at] = part[0:chunk]
            cs[c % 2, :, at] = part[chunk : 2 * chunk]
            return carry
        lax.fori_loop(0, wide_tiles, down_tile, 0)
        core2_copy(c).start()
        core2_copy(c).wait_recv()
        xs[c] += crecv[c]
        x2_copy(c).start()
        if c >= 1:
            hand_on(c - 1)

    def finish(c, gain_total):
        x2_copy(c).wait()
        down = xs[c] + xr2[c]
        inv = mean_inverse(down)
        row_load(c, cot_hbm, seed, s_sem).wait()
        seed_rows = seed[c % 2].astype(F32) * seg_live[own_rows(0, c), 1:2].astype(F32)
        if c + 2 < ROW_CHUNKS:
            row_load(c + 2, cot_hbm, seed, s_sem).start()
        normed = down * inv
        gain_total = gain_total + column_sum(seed_rows * normed)
        scaled = seed_rows * mlp_gain[...]
        dot = jnp.sum(scaled * down, axis=1, keepdims=True)
        grad = inv * scaled - down * (inv * inv * inv * dot / down.shape[1])
        hidden_copy(c).wait_send()
        partner_copy(c).wait_send()
        xr2[c] = grad
        grad_copy(c).start()
        xr[c] = xr[c] + normed * mlp_gain[...]
        if c == 0:
            for copy in turned_copies(hlt_buf, hlt_out, h_sem, last):
                copy.wait()
        if c >= 1:
            for copy in turned_copies(hlt_buf, gdrt_out, d_sem.at[0], c - 1):
                copy.wait()
            for copy in side_copies(low_buf, gdr_out, d_sem.at[1], c - 1):
                copy.wait()
        low_buf[0:chunk, :] = grad.astype(BF16)
        hlt_buf[:, 0:chunk] = grad.astype(BF16).T
        grad_copy(c).wait_recv()
        out_copy(c).start()
        low_buf[chunk : 2 * chunk, :] = ag[c % 2].astype(BF16)
        hlt_buf[:, chunk : 2 * chunk] = ag[c % 2].astype(BF16).T
        for copy in turned_copies(hlt_buf, gdrt_out, d_sem.at[0], c):
            copy.start()
        for copy in side_copies(low_buf, gdr_out, d_sem.at[1], c):
            copy.start()
        return gain_total

    def out_copies(c):
        return [
            pltpu.make_async_copy(
                out_buf.at[pl.ds(s * chunk, chunk)], out_out.at[own_rows(s, c)], o_sem.at[s])
            for s in range(2)
        ]

    def place(c):
        if c >= 1:
            for copy in out_copies(c - 1):
                copy.wait()
        out_buf[0:chunk, :] = xr[c].astype(BF16)
        out_copy(c).wait_recv()
        out_buf[chunk : 2 * chunk, :] = crecv[c].astype(BF16)
        for copy in out_copies(c):
            copy.start()

    for c in range(ROW_CHUNKS):
        feed(c)
    gain_total = jnp.zeros(mlp_gain.shape, F32)
    for c in range(ROW_CHUNKS):
        gain_total = finish(c, gain_total)
        if c >= 1:
            place(c - 1)
        if c == 1:
            hand_on(last)
    place(last)
    gain_out[...] = gain_total
    for buf, dst, i in ((gate_buf, gate_out, 0), (up_buf, up_out, 1), (inner_buf, inner_out, 2)):
        for copy in side_copies(buf, dst, g_sem.at[i], last):
            copy.wait()
    for copy in turned_copies(hlt_buf, gdrt_out, d_sem.at[0], last):
        copy.wait()
    for copy in side_copies(low_buf, gdr_out, d_sem.at[1], last):
        copy.wait()
    for copy in out_copies(last):
        copy.wait()
    core2_copy(last - 1).wait_send()
    core2_copy(last).wait_send()
    for c in range(ROW_CHUNKS):
        grad_copy(c).wait_send()
        out_copy(c).wait_send()
        hand_copy(c).wait()


def forward_layer(hbm, vmem_args):
    tokens, w_query, w_gate = hbm[0], hbm[2], hbm[6]
    row_count, width = tokens.shape
    hidden, head_cols = w_gate.shape[1], w_query.shape[1]
    chunk = row_count // 2 // ROW_CHUNKS
    DMA = pltpu.SemaphoreType.DMA
    vmem, any_space = pl.BlockSpec(memory_space=pltpu.VMEM), pl.BlockSpec(memory_space=pl.ANY)

    def shape(*dims, kind=F32):
        return jax.ShapeDtypeStruct(dims, kind)

    per_chunk = DMA((ROW_CHUNKS,))
    return pl.pallas_call(
        forward_kernel,
        out_shape=(
            shape(row_count, hidden),
            shape(row_count, hidden),
            shape(row_count, hidden, kind=BF16),
            shape(width, row_count, kind=BF16),
            shape(row_count, width, kind=BF16),
            shape(width, row_count, kind=BF16),
            shape(row_count // 2, width),
            shape(row_count, width, kind=BF16),
            shape(row_count, head_cols, kind=BF16),
            shape(row_count, head_cols, kind=BF16),
            shape(row_count, head_cols, kind=BF16),
            shape(row_count, head_cols),
            shape(row_count, head_cols),
            shape(row_count, head_cols, kind=BF16),
            shape(row_count, width),
            shape(1, width),
            shape(row_count, HEAD),
            shape(head_cols // HEAD, row_count),
        ),
        in_specs=[any_space] * len(hbm) + [vmem] * len(vmem_args),
        out_specs=(any_space,) * 15 + (vmem,) * 3,
        scratch_shapes=[
            pltpu.VMEM(w_gate.shape, BF16),
            pltpu.VMEM((2, chunk, width), F32),
            pltpu.VMEM((ROW_CHUNKS, chunk, width), F32),
            pltpu.VMEM((ROW_CHUNKS, chunk, width), F32),
            pltpu.VMEM((ROW_CHUNKS, chunk, width), F32),
            pltpu.VMEM((ROW_CHUNKS, chunk, width), F32),
            pltpu.VMEM((2, chunk, width), F32),
            pltpu.VMEM((ROW_CHUNKS, 2 * chunk, HEAD), F32),
            pltpu.VMEM((2, ROW_CHUNKS, 2 * chunk, HEAD), F32),
            DMA((3,)),
            DMA((2,)),
            DMA((2,)),
            DMA((5,)),
            DMA((3,)),
            DMA((2, 2)),
        ]
        + [per_chunk] * 22
        + [DMA((3, 2)), DMA((2,)), DMA, DMA((2, 2)), DMA((2,))],
        compiler_params=pltpu.CompilerParams(
            collective_id=1, has_side_effects=True, vmem_limit_bytes=VMEM_LIMIT),
    )(*hbm, *vmem_args)


def backward_kernel(
    dp_size, counts,
    gdrt_hbm, hlt_hbm, tok_hbm, inner_hbm, mixed_hbm, gdr_hbm, gate_hbm, up_hbm, branch_hbm, cot_hbm,
    query_hbm, key_hbm, value_hbm, query_raw_hbm, key_raw_hbm, partner_hbm,
    inverses_hbm, seg_live_hbm, cos_hbm, sin_hbm,
    w_out_hbm, wg_hbm, wu_hbm, wd_hbm, wq_hbm, wk_hbm, wv_hbm,
    log_totals, seg_row,
    query_gain, key_gain, attn_gain, gain_mlp_part,
    down_out, out_out, gate_out, up_out, query_out, key_out, value_out, token_out, gains_out,
    ggr_hbm, gur_hbm, gbt_hbm, gh_hbm, gqkv_hbm,
    at, bbuf, bsend, bpar, own, ysend, yrecv, fsend, frecv, zsend, zrecv, stage, stage_t, cs, crecv, xs, xr, ag, dots, dots_in,
    vec, vec_in,
    at_sem, b_sem, bs_sem, ys_sem, yr_sem, fs_sem, fr_sem, zs_sem, zr_sem, out_sem, far_sem,
    cs_sem, cr_sem, xs_sem, xr_sem, as_sem, ar_sem, cs2_sem, cr2_sem, xs2_sem, xr2_sem, as2_sem,
    ar2_sem, ds_sem, dr_sem, vs_sem, vr_sem, w_sem, pre_sem, st_sem, gh_sem, tok_sem, live_sem,
    y_credit, up_credit, down_credit,
):
    n_down, n_pairs, n_heads, n_out = counts
    first_heads = n_down + n_pairs
    first_out = first_heads + n_heads
    total = first_out + n_out
    line = dp_size // 2
    width = at.shape[1]
    block = width // dp_size
    chunk = xs.shape[1]
    half = chunk * ROW_CHUNKS
    full = 2 * half
    head_cols = query_hbm.shape[1]
    passes = total + n_pairs + len(LINE_FIRST)
    dp_at = lax.axis_index("dp")
    z, y = dp_at // 2, dp_at % 2
    partner = dp_at + 1 - 2 * y
    below, above = dp_at - 2, dp_at + 2
    has_below, has_above = z > 0, z < line - 1
    core, sibling, across = tensor_peers()
    steps = [1 << s for s in range(dp_size.bit_length() - 1)]
    vec_peers = [dp_at + bit * (1 - 2 * ((dp_at // bit) % 2)) for bit in steps]

    def at_dp(i):
        return {"dp": i}

    def at_tensor(i):
        return {"tensor": i}

    def remote(src, dst, send_sem, recv_sem, peer):
        return pltpu.make_async_remote_copy(
            src_ref=src, dst_ref=dst, send_sem=send_sem, recv_sem=recv_sem,
            device_id=peer, device_id_type=MESH)

    def y_copy(p, b):
        return remote(ysend.at[p, b], yrecv.at[p, b], ys_sem.at[p, b], yr_sem.at[p, b], at_dp(partner))

    def z_copy(p, b, slot, target):
        return remote(zsend.at[p, b], zrecv.at[p, slot], zs_sem.at[p, b], zr_sem.at[p, slot], at_dp(target))

    def final_copy(p):
        return remote(fsend.at[p], frecv.at[p], fs_sem.at[p], fr_sem.at[p], at_dp(partner))

    def is_pair(k):
        return (k >= n_down) & (k < first_heads)

    def slot_of(k):
        return lax.rem(
            (k >= n_down).astype(jnp.int32) + (k >= first_heads).astype(jnp.int32)
            + (k >= first_out).astype(jnp.int32), 2)

    def row_block(rows_at):
        return pl.ds(pl.multiple_of(rows_at * block, block), block)

    def product(k, rows_at):
        return jnp.dot(
            at[slot_of(k), row_block(rows_at), :], bbuf[lax.rem(k, B_SLOTS)],
            preferred_element_type=F32)

    def pair_product(k, rows_at):
        return product(k, rows_at) + jnp.dot(
            at[2, row_block(rows_at), :], bpar[...], preferred_element_type=F32)

    def at_load(i):
        src = (gdrt_hbm, hlt_hbm, None, gbt_hbm)[i]
        return pltpu.make_async_copy(src, at.at[i % 2], at_sem.at[i % 2])

    def b_load(k, act):
        def columns(src, at_chunk, dst, sem):
            act(pltpu.make_async_copy(
                src.at[:, pl.ds(pl.multiple_of(at_chunk * COLS, COLS), COLS)], dst, sem))
        own_dst, own_sem = bbuf.at[lax.rem(k, B_SLOTS)], b_sem.at[lax.rem(k, B_SLOTS)]

        @pl.when(k < n_down)
        def _():
            columns(inner_hbm, k, own_dst, own_sem)

        for first, src in ((n_down, ggr_hbm), (n_down + n_pairs // 2, gur_hbm)):
            @pl.when((k >= first) & (k < first + n_pairs // 2))
            def _(first=first, src=src):
                columns(src, 2 * (k - first) + y, own_dst, own_sem)
                columns(src, 2 * (k - first) + 1 - y, bsend, bs_sem)

        @pl.when((k >= first_heads) & (k < first_out))
        def _():
            columns(gqkv_hbm, k - first_heads, own_dst, own_sem)

        @pl.when((k >= first_out) & (k < total))
        def _():
            columns(mixed_hbm, k - first_out, own_dst, own_sem)

    def line_first(k):
        return functools.reduce(jnp.logical_or, [k == at_chunk for at_chunk in LINE_FIRST])

    def walk(fn):
        def body(i, carry):
            @pl.when(z <= i)
            def _():
                fn(z + line - 1 - i, True)

            @pl.when(z >= line - 1 - i)
            def _():
                fn(z - (line - 1 - i), False)
            return carry
        lax.fori_loop(0, line - 1, body, 0)

    def pair_send(k):
        p = lax.rem(k, Y_SLOTS)

        @pl.when(k >= Y_SLOTS)
        def _():
            pl.semaphore_wait(y_credit, 1)
        b_load(k, lambda copy: copy.wait())

        @pl.when(jnp.logical_not(line_first(k) | is_pair(k)))
        def _():
            def one(b, up=None):
                ysend[p, b] = product(k, 2 * b + 1 - y)
                y_copy(p, b).start()
            walk(one)
            one(z)

        @pl.when(is_pair(k))
        def _():
            def rows_out(b, carry):
                ysend[p, b] = bsend[row_block(b), :].astype(F32)
                y_copy(p, b).start()
                return carry
            lax.fori_loop(0, line, rows_out, 0)

    def line_send(q, k, source):
        p = lax.rem(q, 2)

        @pl.when(q >= 2)
        def _():
            @pl.when(has_above)
            def _():
                pl.semaphore_wait(up_credit, 1)

            @pl.when(has_below)
            def _():
                pl.semaphore_wait(down_credit, 1)

        def one(b, up):
            has_before, target = (has_below, above) if up else (has_above, below)
            zsend[p, b] = source(b)

            @pl.when(has_before)
            def _():
                z_copy(p, b, b, target).wait_recv()
                zsend[p, b] += zrecv[p, b]
            if up:
                z_copy(p, b, b, target).start()
            else:
                @pl.when(b == z - 1)
                def _():
                    z_copy(p, b, line, target).start()

                @pl.when(b != z - 1)
                def _():
                    z_copy(p, b, b, target).start()
        walk(one)

    def line_own(q, dst):
        p = lax.rem(q, 2)

        @pl.when(has_below)
        def _():
            z_copy(p, z, z, below).wait_recv()
            dst[...] += zrecv[p, z]

        @pl.when(has_above)
        def _():
            z_copy(p, z, line, below).wait_recv()
            dst[...] += zrecv[p, line]

        def drain(b, up):
            z_copy(p, b, b, below).wait_send()
        walk(drain)

        @pl.when(q < passes - 2)
        def _():
            @pl.when(has_below)
            def _():
                pl.semaphore_signal(up_credit, inc=1, device_id=at_dp(below), device_id_type=MESH)

            @pl.when(has_above)
            def _():
                pl.semaphore_signal(down_credit, inc=1, device_id=at_dp(above), device_id_type=MESH)

    def is_turned(k):
        return (k < n_down) | (k >= first_out)

    per_head = n_heads // 3
    results = (
        (0, n_down, down_out, True),
        (first_heads, per_head, query_out, False),
        (first_heads + per_head, per_head, key_out, False),
        (first_heads + 2 * per_head, per_head, value_out, False),
        (first_out, n_out, out_out, True),
    )
    pair_results = ((n_down, gate_out), (n_down + n_pairs // 2, up_out))

    def out_act(k, act):
        def place(at_chunk):
            return pl.ds(pl.multiple_of(at_chunk * COLS, COLS), COLS)

        for first, count, dst, turned in results:
            @pl.when((k >= first) & (k < first + count))
            def _(first=first, dst=dst, turned=turned):
                if turned:
                    act(pltpu.make_async_copy(stage_t, dst.at[place(k - first)], out_sem))
                else:
                    act(pltpu.make_async_copy(stage, dst.at[:, place(k - first)], out_sem))

        for first, dst in pair_results:
            @pl.when((k >= first) & (k < first + n_pairs // 2))
            def _(first=first, dst=dst):
                act(pltpu.make_async_copy(stage, dst.at[:, place(2 * (k - first) + y)], out_sem))

    def far_out(k):
        for first, dst in pair_results:
            @pl.when((k >= first) & (k < first + n_pairs // 2))
            def _(first=first, dst=dst):
                cols = pl.ds(pl.multiple_of((2 * (k - first) + 1 - y) * COLS, COLS), COLS)
                copy = pltpu.make_async_copy(frecv.at[lax.rem(k, Y_SLOTS)], dst.at[:, cols], far_sem)
                copy.start()
                copy.wait()

    def finish_chunk(k, q):
        p = lax.rem(k, Y_SLOTS)

        @pl.when(k >= 1)
        def _():
            out_act(k - 1, lambda copy: copy.wait())
        stage[...] = own[...]

        @pl.when(jnp.logical_not(is_pair(k)))
        def _():
            y_copy(p, z).wait_recv()
            stage[...] += yrecv[p, z]
        line_own(q, stage)

        @pl.when((k < n_down) | (k >= first_out))
        def _():
            stage_t[...] = stage[...].T
        out_act(k, lambda copy: copy.start())

        @pl.when(line_first(k))
        def _():
            y_copy(p, z).wait_send()

        @pl.when(jnp.logical_not(line_first(k)))
        def _():
            for b in range(line):
                y_copy(p, b).wait_send()

        @pl.when(is_pair(k))
        def _():
            final_copy(p).wait()
            far_out(k)

        @pl.when(k < total - Y_SLOTS)
        def _():
            pl.semaphore_signal(y_credit, inc=1, device_id=at_dp(partner), device_id_type=MESH)

    def pass_of(k):
        return (
            k + jnp.clip(k - n_down, 0, n_pairs)
            + sum((k > at_chunk).astype(jnp.int32) for at_chunk in LINE_FIRST))

    def prefetch(k):
        @pl.when(k + 2 < total)
        def _():
            b_load(k + 2, lambda copy: copy.start())

    def send_ahead(k):
        @pl.when(k + 2 < total)
        def _():
            pair_send(k + 2)

    def tick(k):
        p = lax.rem(k, Y_SLOTS)
        q = pass_of(k)
        is_line_first = line_first(k)
        prefetch(k)

        @pl.when(jnp.logical_not(is_line_first))
        def _():
            def mine(b):
                part = product(k, 2 * b + y)
                y_copy(p, b).wait_recv()
                return part + yrecv[p, b]
            line_send(q, k, mine)

        @pl.when(is_line_first)
        def _():
            line_send(q, k, lambda b: product(k, 2 * b + 1 - y))

        @pl.when(k >= 1)
        def _():
            finish_chunk(k - 1, q - 1)
        send_ahead(k)
        own[...] = product(k, 2 * z + y)

        @pl.when(is_line_first)
        def _():
            line_send(q + 1, k, lambda b: product(k, 2 * b + y))
            ysend[p, z] = product(k, 2 * z + 1 - y)
            line_own(q, ysend.at[p, z])
            y_copy(p, z).start()

    def pair_tick(k, work):
        p = lax.rem(k, Y_SLOTS)
        q = pass_of(k)
        prefetch(k)

        def rows_in(b, carry):
            y_copy(p, b).wait_recv()
            bpar[row_block(b), :] = yrecv[p, b].astype(BF16)
            return carry
        lax.fori_loop(0, line, rows_in, 0)
        line_send(q, k, lambda b: pair_product(k, 2 * b + 1 - y))
        finish_chunk(k - 1, q - 1)
        send_ahead(k)
        work(q)
        line_send(q + 1, k, lambda b: pair_product(k, 2 * b + y))
        own[...] = pair_product(k, 2 * z + y)
        fsend[p] = pair_product(k, 2 * z + 1 - y)
        line_own(q, fsend.at[p])
        final_copy(p).start()

    nt = (((1,), (1,)), ((), ()))

    def copies_of(sem, *pairs):
        return [pltpu.make_async_copy(src, dst, sem.at[i]) for i, (src, dst) in enumerate(pairs)]

    def start(copies):
        for copy in copies:
            copy.start()

    def finish(copies):
        for copy in copies:
            copy.wait()

    first_pair, last_pair = n_down, n_down + 2 * n_pairs

    def run_ticks(first, last, work):
        def do_work(at_half):
            for when, fn in work.items():
                low, high = when if isinstance(when, tuple) else (when, when + 1)

                @pl.when((at_half >= low) & (at_half < high))
                def _(fn=fn, low=low, high=high):
                    if isinstance(fn, list):
                        for one in fn:
                            one()
                    elif low + 1 == high:
                        fn()
                    else:
                        fn(at_half - low)

        def single(at_half, carry):
            k = jnp.where(at_half < first_pair, at_half, at_half - n_pairs)
            tick(k)
            do_work(at_half)
            return carry

        def double(m, carry):
            at_half = first_pair + 2 * m
            pair_tick(first_pair + m, lambda q: do_work(at_half))
            do_work(at_half + 1)
            return carry
        if first < first_pair:
            lax.fori_loop(first, min(last, first_pair), single, 0)
        low, high = max(first, first_pair), min(last, last_pair)
        if low < high:
            lax.fori_loop((low - first_pair) // 2, (high - first_pair) // 2, double, 0)
        if last > last_pair:
            lax.fori_loop(max(first, last_pair), last, single, 0)

    def part(fn, *args):
        return functools.partial(fn, *args)

    def side_rows(s, c):
        return pl.ds(s * half + c * chunk, chunk)

    def both_sides(hbm, buf, c, out=False):
        pairs = [(hbm.at[side_rows(s, c)], buf.at[pl.ds(s * chunk, chunk)]) for s in range(2)]
        return [(b, a) for a, b in pairs] if out else pairs

    def sequence_rows(s, c):
        return pl.ds(pl.multiple_of(2 * c * chunk + jnp.where(core == s, 0, chunk), chunk), chunk)

    def core_copy(c, again):
        ss, rs = (cs2_sem, cr2_sem) if again else (cs_sem, cr_sem)
        return remote(cs, crecv.at[c], ss.at[c], rs.at[c], at_tensor(sibling))

    def x_copy(c, again):
        ss, rs = (xs2_sem, xr2_sem) if again else (xs_sem, xr_sem)
        return remote(xs.at[c], xr.at[c], ss.at[c], rs.at[c], at_tensor(across))

    def to_sibling(c, again):
        ss, rs = (as2_sem, ar2_sem) if again else (as_sem, ar_sem)
        return remote(xr.at[c], ag.at[c % 2], ss.at[c], rs.at[c], at_tensor(sibling))

    def pass_on(c, again):
        core_copy(c, again).wait_recv()
        xs[c] += crecv[c]
        x_copy(c, again).start()
        core_copy(c, again).wait_send()

    hidden = wd_hbm.shape[0]

    def feed_phase(wd, grads, gates, ups, ggr, gur, far_rows):
        far_piece = full // ROW_CHUNKS

        def far_load(c):
            return copies_of(
                tok_sem, (partner_hbm.at[pl.ds(c * far_piece, far_piece)], far_rows))

        def far_turn(c):
            finish(far_load(c))
            at[2, :, pl.ds(c * far_piece, far_piece)] = far_rows[...].astype(BF16).T
            if c + 1 < ROW_CHUNKS:
                start(far_load(c + 1))

        def loads(c):
            return copies_of(
                pre_sem, *both_sides(gdr_hbm, grads, c), *both_sides(gate_hbm, gates, c),
                *both_sides(up_hbm, ups, c))

        def stores(c):
            return copies_of(
                st_sem, *both_sides(ggr_hbm, ggr, c, True), *both_sides(gur_hbm, gur, c, True))

        def piece(c):
            finish(loads(c))
            if c >= 1:
                finish(stores(c - 1))

            def tile(n, carry):
                cols = pl.ds(pl.multiple_of(n * TILE, TILE), TILE)
                grad = lax.dot_general(grads[...], wd[cols, :], nt, preferred_element_type=F32)
                gate = gates[:, cols]
                sig = jax.nn.sigmoid(gate)
                act = gate * sig
                ggr[:, cols] = (grad * ups[:, cols] * (sig + act * (1.0 - sig))).astype(BF16)
                gur[:, cols] = (grad * act).astype(BF16)
                return carry
            lax.fori_loop(0, hidden // TILE, tile, 0)
            start(stores(c))
            if c + 1 < ROW_CHUNKS:
                start(loads(c + 1))

        load_weight = copies_of(w_sem, (wd_hbm, wd))
        start(load_weight)
        start(loads(0))
        start(far_load(0))
        at_load(0).wait()
        pair_send(jnp.int32(0))
        pair_send(jnp.int32(1))
        finish(load_weight)
        piece(0)
        far_turn(0)
        run_ticks(0, FEED_TICK, {
            c - 1: [part(piece, c), part(far_turn, c)] for c in range(1, ROW_CHUNKS)})
        finish(stores(ROW_CHUNKS - 1))

    def hidden_phase(weights, ggr, gur):
        load_weights = copies_of(w_sem, (wg_hbm, weights.at[0]), (wu_hbm, weights.at[1]))

        def loads(c):
            return copies_of(pre_sem, *both_sides(ggr_hbm, ggr, c), *both_sides(gur_hbm, gur, c))

        def piece(c):
            if c == 0:
                finish(load_weights)
            else:
                pass_on(c - 1, False)
            finish(loads(c))

            def tile(n, carry):
                rows = pl.ds(pl.multiple_of(n * TILE, TILE), TILE)
                total_part = lax.dot_general(ggr[...], weights[0, rows, :], nt, preferred_element_type=F32)
                total_part = total_part + lax.dot_general(
                    gur[...], weights[1, rows, :], nt, preferred_element_type=F32)
                xs[c, :, rows] = total_part[0:chunk]
                cs[:, rows] = total_part[chunk : 2 * chunk]
                return carry
            lax.fori_loop(0, width // TILE, tile, 0)
            core_copy(c, False).start()
            if c + 1 < ROW_CHUNKS:
                start(loads(c + 1))

        start(load_weights)
        start(loads(0))
        run_ticks(
            FEED_TICK, HIDDEN_TICK, {FEED_TICK + c: part(piece, c) for c in range(ROW_CHUNKS)})

    def branch_phase(branch, seed, low, turned, w_out, mixed_grad, token_rows, seg_live):
        load_weight = copies_of(w_sem, (w_out_hbm, w_out))
        load_live = copies_of(live_sem, (seg_live_hbm, seg_live))
        token_piece = full // ROW_CHUNKS

        def loads(c):
            rows = pl.ds(c * chunk, chunk)
            return copies_of(
                pre_sem, (branch_hbm.at[rows], branch), (cot_hbm.at[sequence_rows(0, c)], seed))

        def stores(c):
            i = c % 2
            return copies_of(
                st_sem.at[pl.ds(4 * i, 4)],
                (turned.at[i, :, pl.ds(0, chunk)], gbt_hbm.at[:, side_rows(0, c)]),
                (turned.at[i, :, pl.ds(chunk, chunk)], gbt_hbm.at[:, side_rows(1, c)]),
                *[(
                    mixed_grad.at[i, pl.ds(s * chunk, chunk)],
                    gqkv_hbm.at[sequence_rows(s, c), pl.ds(2 * head_cols, head_cols)],
                ) for s in range(2)])

        def hidden_store(c):
            return copies_of(gh_sem, (xs.at[c], gh_hbm.at[pl.ds(c * chunk, chunk)]))

        def token_load(c):
            return copies_of(tok_sem, (tok_hbm.at[pl.ds(c * token_piece, token_piece)], token_rows))

        def first(c):
            i = c % 2
            finish(loads(c))
            if c == 0:
                finish(load_live)
            x_copy(c, False).wait()
            live = seg_live[sequence_rows(0, c), 1:2].astype(F32)
            grad_hidden = xs[c] + xr[c] + seed[...].astype(F32) * live
            xs[c] = grad_hidden
            start(hidden_store(c))
            values = branch[...]
            inv = mean_inverse(values)
            vec[1:2, :] += column_sum(grad_hidden * values * inv)
            scaled = grad_hidden * attn_gain[...]
            dot = jnp.sum(scaled * values, axis=1, keepdims=True)
            grad = inv * scaled - values * (inv * inv * inv * dot / width)
            xr[c] = grad
            to_sibling(c, False).start()
            if c >= 2:
                finish(stores(c - 2))
            low[i, 0:chunk, :] = grad.astype(BF16)
            turned[i, :, 0:chunk] = grad.astype(BF16).T
            if c + 1 < ROW_CHUNKS:
                start(loads(c + 1))

        def second(c):
            i = c % 2
            to_sibling(c, False).wait_recv()
            if c == 0:
                finish(load_weight)
            other = ag[i].astype(BF16)
            low[i, chunk : 2 * chunk, :] = other
            turned[i, :, chunk : 2 * chunk] = other.T
            mixed_grad[i] = lax.dot_general(
                low[i], w_out[...], nt, preferred_element_type=F32).astype(BF16)
            start(stores(c))
            finish(hidden_store(c))
            to_sibling(c, False).wait_send()

        def turn(c):
            finish(token_load(c))
            at[0, :, pl.ds(c * token_piece, token_piece)] = token_rows[...].T
            if c + 1 < ROW_CHUNKS:
                start(token_load(c + 1))

        start(load_weight)
        start(load_live)
        start(loads(0))
        start(token_load(0))
        work = {HIDDEN_TICK + c: [] for c in range(ROW_CHUNKS + 1)}
        work[HIDDEN_TICK].append(part(pass_on, ROW_CHUNKS - 1, False))
        for c in range(ROW_CHUNKS):
            work[HIDDEN_TICK + c].append(part(first, c))
            work[HIDDEN_TICK + c + 1].append(part(second, c))
        work[HIDDEN_TICK + 3] += [part(turn, 0)]
        work[HIDDEN_TICK + 4] += [part(turn, c) for c in range(1, ROW_CHUNKS)]
        run_ticks(HIDDEN_TICK, BRANCH_TICK, work)
        for c in range(ROW_CHUNKS - 2, ROW_CHUNKS):
            finish(stores(c))

    def attention_phase(
        query, key, value, mixed_grad, dq, dk, dv, raw, bias, inverses, seg_live, cosine, sine,
    ):
        heads = head_cols // HEAD
        q_rows = min(256, full)
        scale = HEAD ** (-0.5)
        value_cols = pl.ds(2 * head_cols, head_cols)
        loads = copies_of(
            pre_sem, (query_hbm, query), (key_hbm, key), (value_hbm, value),
            (gqkv_hbm.at[:, value_cols], mixed_grad))
        load_tables = copies_of(
            w_sem, (inverses_hbm, inverses), (seg_live_hbm, seg_live), (cos_hbm, cosine), (sin_hbm, sine))

        def masks():
            finish(load_tables)
            for i in range(full // q_rows):
                rows, keys = slice(i * q_rows, (i + 1) * q_rows), (i + 1) * q_rows
                key_at = lax.broadcasted_iota(jnp.int32, (keys, q_rows), 0)
                query_at = lax.broadcasted_iota(jnp.int32, (keys, q_rows), 1) + i * q_rows
                allowed = (
                    (seg_live[0:keys, 0:1] == seg_row[:, rows])
                    & (key_at <= query_at)
                    & ((seg_live[0:keys, 1:2] > 0) | (key_at == query_at)))
                bias[0:keys, rows] = jnp.where(allowed, 0.0, NEG_FILL).astype(BF16)
            finish(loads)

        def head(h):
            cols = pl.ds(pl.multiple_of(h * HEAD, HEAD), HEAD)
            dk[:, cols] = jnp.zeros((full, HEAD), F32)
            dv[...] = jnp.zeros((full, HEAD), F32)
            for i in range(full // q_rows):
                rows, keys = slice(i * q_rows, (i + 1) * q_rows), (i + 1) * q_rows
                q_block, grad_block = query[rows, cols], mixed_grad[rows, cols]
                key_block, value_block = key[0:keys, cols], value[0:keys, cols]
                scores = lax.dot_general(key_block, q_block, nt, preferred_element_type=F32) * scale
                prob = jnp.exp(scores + bias[0:keys, rows].astype(F32) - log_totals[pl.ds(h, 1), rows])
                grad_prob = lax.dot_general(value_block, grad_block, nt, preferred_element_type=F32)
                row_dot = jnp.sum(prob * grad_prob, axis=0, keepdims=True)
                grad_scores = (prob * (grad_prob - row_dot)).astype(BF16)
                dq[rows, cols] = lax.dot_general(
                    grad_scores, key_block, (((0,), (0,)), ((), ())), preferred_element_type=F32) * scale
                dk[0:keys, cols] += jnp.dot(grad_scores, q_block, preferred_element_type=F32) * scale
                dv[0:keys, :] += jnp.dot(prob.astype(BF16), grad_block, preferred_element_type=F32)
            mixed_grad[:, cols] = dv[...].astype(BF16)

        store_value = copies_of(st_sem, (mixed_grad, gqkv_hbm.at[:, value_cols]))
        sides = ((dq, query_raw_hbm, query_gain), (dk, key_raw_hbm, key_gain))

        def load_raw(which):
            return copies_of(pre_sem, (sides[which][1], raw))

        def back(which):
            grads, _, gain = sides[which]
            finish(load_raw(which))
            gains = gain[...].astype(F32)
            lanes = lax.broadcasted_iota(jnp.int32, (q_rows, HEAD), 1)

            def block_back(i, carry):
                rows = pl.ds(pl.multiple_of(i * q_rows, q_rows), q_rows)
                dot = jnp.zeros((q_rows, 1), F32)
                for h in range(heads):
                    cols = slice(h * HEAD, (h + 1) * HEAD)
                    grad = grads[rows, cols]
                    grad = grad * cosine[rows, :] - pltpu.roll(grad, HEAD // 2, 1) * sine[rows, :]
                    raw_rows = raw[rows, cols]
                    gain_cols = slice(which * head_cols + h * HEAD, which * head_cols + (h + 1) * HEAD)
                    vec[2:3, gain_cols] += column_sum(
                        grad * raw_rows * inverses[rows, which : which + 1])
                    scaled = grad * gains[h : h + 1, :]
                    grads[rows, cols] = scaled
                    dot = dot + jnp.sum(scaled * raw_rows, axis=1, keepdims=True)
                if which == 0:
                    dots[rows, :] = jnp.broadcast_to(dot, (q_rows, HEAD))
                else:
                    dots[rows, :] = jnp.where(lanes == 0, dots[rows, :], dot)
                return carry
            lax.fori_loop(0, full // q_rows, block_back, 0)

        def dots_copy(i):
            return remote(
                dots, dots_in.at[i], ds_sem.at[i], dr_sem.at[i], at_tensor((sibling, across)[i]))

        def dots_add(i):
            dots_copy(i).wait()
            dots[...] += dots_in[i]

        def combine(which):
            grads = sides[which][0]
            for i in range(full // q_rows):
                rows = slice(i * q_rows, (i + 1) * q_rows)
                inv_rows = inverses[rows, which : which + 1]
                dot = dots[rows, which : which + 1]
                mixed_grad[rows, :] = (
                    inv_rows * grads[rows, :]
                    - raw[rows, :] * (inv_rows * inv_rows * inv_rows * dot / width)
                ).astype(BF16)

        def store_grads(which):
            return copies_of(
                st_sem, (mixed_grad, gqkv_hbm.at[:, pl.ds(which * head_cols, head_cols)]))

        def after_heads():
            start(store_value)
            start(load_raw(0))

        def back_query():
            back(0)
            start(load_raw(1))

        def back_key():
            back(1)
            dots_copy(0).start()
            finish(store_value)

        def first_sum():
            dots_add(0)
            dots_copy(1).start()

        def second_sum():
            dots_add(1)
            combine(1)
            start(store_grads(1))
            start(load_raw(0))

        def last_part():
            finish(store_grads(1))
            finish(load_raw(0))
            combine(0)
            start(store_grads(0))

        start(loads)
        start(load_tables)
        t = BRANCH_TICK
        run_ticks(t, INPUT_TICK, {
            t: masks,
            (t, t + heads): head,
            t + heads - 1: after_heads,
            t + heads: back_query,
            t + heads + 1: back_key,
            t + heads + 2: first_sum,
            t + heads + 3: [second_sum, last_part],
        })
        finish(store_grads(0))

    def input_phase(weights, grads, grad_hidden, low):
        loads = copies_of(
            w_sem, *[(w, weights.at[i]) for i, w in enumerate((wq_hbm, wk_hbm, wv_hbm))],
            (gqkv_hbm, grads))

        def piece(c):
            if c == 0:
                finish(loads)
            else:
                pass_on(c - 1, True)
            for s in range(2):
                rows = sequence_rows(s, c)

                def tile(n, carry):
                    cols = pl.ds(pl.multiple_of(n * TILE, TILE), TILE)
                    total_part = jnp.zeros((chunk, TILE), F32)
                    for i in range(3):
                        total_part = total_part + lax.dot_general(
                            grads[rows, i * head_cols : (i + 1) * head_cols], weights[i, cols, :],
                            nt, preferred_element_type=F32)
                    if s == 0:
                        xs[c, :, cols] = total_part
                    else:
                        cs[:, cols] = total_part
                    return carry
                lax.fori_loop(0, width // TILE, tile, 0)
            core_copy(c, True).start()

        def hidden_load(c):
            return copies_of(gh_sem, (gh_hbm.at[pl.ds(c * chunk, chunk)], grad_hidden))

        def stores(c):
            return copies_of(
                st_sem, *[(low.at[s], token_out.at[sequence_rows(s, c)]) for s in range(2)])

        def first(c):
            finish(hidden_load(c))
            x_copy(c, True).wait()
            xr[c] = xs[c] + xr[c] + grad_hidden[...]
            to_sibling(c, True).start()
            if c + 1 < ROW_CHUNKS:
                start(hidden_load(c + 1))

        def second(c):
            if c >= 1:
                finish(stores(c - 1))
            low[0] = xr[c].astype(BF16)
            to_sibling(c, True).wait_recv()
            low[1] = ag[c % 2].astype(BF16)
            start(stores(c))
            to_sibling(c, True).wait_send()

        vec_peer_ids = [at_tensor(sibling)] + [at_dp(peer) for peer in vec_peers]

        def vec_copy(i):
            return remote(vec, vec_in.at[i], vs_sem.at[i], vr_sem.at[i], vec_peer_ids[i])

        def vec_step(i):
            if i >= 1:
                vec_copy(i - 1).wait()
                if i == 1:
                    vec[0:2, :] += vec_in[0, 0:2, :]
                else:
                    vec[...] += vec_in[i - 1]
            if i < len(vec_peer_ids):
                vec_copy(i).start()

        start(loads)
        start(hidden_load(0))
        halves = total + n_pairs
        work = {k: [] for k in range(INPUT_TICK, halves)}
        for c in range(ROW_CHUNKS):
            work[INPUT_TICK + c].append(part(piece, c))
            work[TOKEN_TICK + c].append(part(first, c))
            work[TOKEN_TICK + c + 1].append(part(second, c))
        work[INPUT_TICK + ROW_CHUNKS].append(part(pass_on, ROW_CHUNKS - 1, True))
        for i in range(len(vec_peer_ids) + 1):
            work[INPUT_TICK + 2 + i].append(part(vec_step, i))
        work[last_pair + 1].append(lambda: at_load(3).start())
        work[last_pair + 2].append(lambda: at_load(3).wait())
        run_ticks(INPUT_TICK, halves, {k: fns for k, fns in work.items() if fns})
        finish(stores(ROW_CHUNKS - 1))

    vec[...] = jnp.zeros(vec.shape, F32)
    vec[0:1, :] = gain_mlp_part[...]
    at_load(0).start()
    at_load(1).start()
    for k in range(2):
        b_load(jnp.int32(k), lambda copy: copy.start())
    barrier = pltpu.get_barrier_semaphore()

    def greet_one(peer):
        pl.semaphore_signal(barrier, inc=1, device_id=peer, device_id_type=MESH)

    other_z = z - 1 + 2 * lax.rem(z, 2)
    has_other = (other_z >= 0) & (other_z < line)
    for peer in vec_peers:
        greet_one(at_dp(peer))
    greet_one(at_tensor(sibling))
    greet_one(at_tensor(across))

    @pl.when(has_other)
    def _():
        greet_one(at_dp(2 * other_z + y))
    pl.semaphore_wait(barrier, len(steps) + 2 + has_other.astype(jnp.int32))

    both = 2 * chunk
    rows_of = (full, head_cols)
    pl.run_scoped(
        feed_phase, pltpu.VMEM(wd_hbm.shape, BF16), pltpu.VMEM((both, width), BF16),
        pltpu.VMEM((both, hidden), F32), pltpu.VMEM((both, hidden), F32),
        pltpu.VMEM((both, hidden), BF16), pltpu.VMEM((both, hidden), BF16),
        pltpu.VMEM((full // ROW_CHUNKS, width), F32))
    at_load(1).wait()
    pl.run_scoped(
        hidden_phase, pltpu.VMEM((2,) + wg_hbm.shape, BF16), pltpu.VMEM((both, hidden), BF16),
        pltpu.VMEM((both, hidden), BF16))
    pl.run_scoped(
        branch_phase, pltpu.VMEM((chunk, width), F32), pltpu.VMEM((chunk, width), BF16),
        pltpu.VMEM((2, both, width), BF16), pltpu.VMEM((2, width, both), BF16),
        pltpu.VMEM(w_out_hbm.shape, BF16), pltpu.VMEM((2, both, head_cols), BF16),
        pltpu.VMEM((full // ROW_CHUNKS, width), BF16), pltpu.VMEM(seg_live_hbm.shape, jnp.int32))
    pl.run_scoped(
        attention_phase, pltpu.VMEM(rows_of, BF16), pltpu.VMEM(rows_of, BF16), pltpu.VMEM(rows_of, BF16),
        pltpu.VMEM(rows_of, BF16), pltpu.VMEM(rows_of, F32), pltpu.VMEM(rows_of, F32),
        pltpu.VMEM((full, HEAD), F32), pltpu.VMEM(rows_of, F32), pltpu.VMEM((full, full), BF16),
        pltpu.VMEM((full, HEAD), F32), pltpu.VMEM(seg_live_hbm.shape, jnp.int32),
        pltpu.VMEM((full, HEAD), F32), pltpu.VMEM((full, HEAD), F32))
    pl.run_scoped(
        input_phase, pltpu.VMEM((3,) + wq_hbm.shape, BF16), pltpu.VMEM((full, 3 * head_cols), BF16),
        pltpu.VMEM((chunk, width), F32), pltpu.VMEM((2, chunk, width), BF16))
    finish_chunk(jnp.int32(total - 1), jnp.int32(passes - 1))
    out_act(jnp.int32(total - 1), lambda copy: copy.wait())
    gains_out[...] = jnp.zeros(gains_out.shape, F32)
    gains_out[0:8, :] = vec[...]
    for h in range(2 * head_cols // HEAD):
        gains_out[8 + h : 9 + h, 0:HEAD] = vec[2:3, h * HEAD : (h + 1) * HEAD]


def backward_layer(dp_size, hbm, vmem_args):
    names = dict(zip(HBM_NAMES, hbm, strict=True))
    width, row_count = names["gdrt"].shape
    hidden, head_cols = names["inner"].shape[1], names["query"].shape[1]
    line, block = dp_size // 2, width // dp_size
    chunk = row_count // 2 // ROW_CHUNKS
    counts = (hidden // COLS, hidden // COLS, 3 * head_cols // COLS, head_cols // COLS)
    DMA, REG = pltpu.SemaphoreType.DMA, pltpu.SemaphoreType.REGULAR
    vmem, any_space = pl.BlockSpec(memory_space=pltpu.VMEM), pl.BlockSpec(memory_space=pl.ANY)

    def shape(*dims, kind=F32):
        return jax.ShapeDtypeStruct(dims, kind)

    slot = (block, COLS)
    per_chunk = DMA((ROW_CHUNKS,))
    steps = dp_size.bit_length() - 1
    results = pl.pallas_call(
        functools.partial(backward_kernel, dp_size, counts),
        out_shape=(
            shape(hidden, block),
            shape(head_cols, block),
            shape(block, hidden),
            shape(block, hidden),
            shape(block, head_cols),
            shape(block, head_cols),
            shape(block, head_cols),
            shape(row_count, width, kind=BF16),
            shape(8 + 2 * head_cols // HEAD, width),
            shape(row_count, hidden, kind=BF16),
            shape(row_count, hidden, kind=BF16),
            shape(width, row_count, kind=BF16),
            shape(row_count // 2, width),
            shape(row_count, 3 * head_cols, kind=BF16),
        ),
        in_specs=[any_space] * len(hbm) + [vmem] * len(vmem_args),
        out_specs=(any_space,) * 8 + (vmem,) + (any_space,) * 5,
        scratch_shapes=[
            pltpu.VMEM((3, width, row_count), BF16),
            pltpu.VMEM((B_SLOTS, row_count, COLS), BF16),
            pltpu.VMEM((row_count, COLS), BF16),
            pltpu.VMEM((row_count, COLS), BF16),
            pltpu.VMEM(slot, F32),
            pltpu.VMEM((Y_SLOTS, line) + slot, F32),
            pltpu.VMEM((Y_SLOTS, line) + slot, F32),
            pltpu.VMEM((Y_SLOTS,) + slot, F32),
            pltpu.VMEM((Y_SLOTS,) + slot, F32),
            pltpu.VMEM((2, line) + slot, F32),
            pltpu.VMEM((2, line + 1) + slot, F32),
            pltpu.VMEM(slot, F32),
            pltpu.VMEM((COLS, block), F32),
            pltpu.VMEM((chunk, width), F32),
            pltpu.VMEM((ROW_CHUNKS, chunk, width), F32),
            pltpu.VMEM((ROW_CHUNKS, chunk, width), F32),
            pltpu.VMEM((ROW_CHUNKS, chunk, width), F32),
            pltpu.VMEM((2, chunk, width), F32),
            pltpu.VMEM((row_count, HEAD), F32),
            pltpu.VMEM((2, row_count, HEAD), F32),
            pltpu.VMEM((8, width), F32),
            pltpu.VMEM((steps + 1, 8, width), F32),
            DMA((2,)),
            DMA((B_SLOTS,)),
            DMA,
            DMA((Y_SLOTS, line)),
            DMA((Y_SLOTS, line)),
            DMA((Y_SLOTS,)),
            DMA((Y_SLOTS,)),
            DMA((2, line)),
            DMA((2, line + 1)),
            DMA,
            DMA,
        ]
        + [per_chunk] * 12
        + [DMA((2,)), DMA((2,)), DMA((steps + 1,)), DMA((steps + 1,)), DMA((4,)), DMA((6,)), DMA((8,)), DMA((1,)), DMA((1,)), DMA((1,)),
           REG, REG, REG],
        compiler_params=pltpu.CompilerParams(
            collective_id=2, has_side_effects=True, vmem_limit_bytes=VMEM_LIMIT),
    )(*hbm, *vmem_args)
    return results[:9]


def rope_tables():
    half_size = HEAD // 2
    freq_row = ROPE_BASE ** (-(np.arange(half_size, dtype=np.float64) * 2.0) / HEAD)
    angle = (np.arange(LENGTH, dtype=np.float64)[:, None] * freq_row[None, :]).astype(np.float32)
    cosine, sine = np.cos(angle), np.sin(angle)
    return np.concatenate((cosine, cosine), 1), np.concatenate((-sine, sine), 1)


def make_shards(dp_size):
    def shards(
        tokens,
        segments,
        pad_mask,
        w_query,
        w_key,
        w_value,
        w_out,
        gain_query,
        gain_key,
        gain_attn,
        w_gate,
        w_up,
        w_down,
        gain_mlp,
        cotangent,
    ):
        block = tokens.shape[1] // dp_size
        cosine, sine = (jnp.asarray(table, F32) for table in rope_tables())
        seg_live = jnp.stack((segments, pad_mask), 1)
        seg_row = segments[None, :]
        attn_gain = gain_attn.astype(F32)[None, :]
        mlp_gain = gain_mlp.astype(F32)[None, :]
        (
            gate_rows,
            up_rows,
            inner_rows,
            hidden_turned,
            grad_down_rows,
            grad_down_turned,
            branch_rows,
            output,
            query_norm,
            key_norm,
            value_rows,
            query_raw,
            key_raw,
            mixed_rows,
            partner_rows,
            gain_mlp_part,
            inverses,
            log_totals,
        ) = forward_layer(
            (
                tokens, cotangent, w_query, w_key, w_value, w_out, w_gate, w_up, w_down, cosine, sine,
            ),
            (seg_live, seg_row, gain_query, gain_key, attn_gain, mlp_gain),
        )
        (
            grad_down,
            grad_out,
            grad_gate,
            grad_up,
            grad_query,
            grad_key,
            grad_value,
            grad_tokens,
            gains,
        ) = backward_layer(
            dp_size,
            (
                grad_down_turned, hidden_turned, tokens, inner_rows, mixed_rows, grad_down_rows,
                gate_rows, up_rows, branch_rows, cotangent,
                query_norm, key_norm, value_rows, query_raw, key_raw, partner_rows,
                inverses, seg_live, cosine, sine,
                w_out, w_gate, w_up, w_down, w_query, w_key, w_value,
            ),
            (
                log_totals, seg_row, gain_query, gain_key, attn_gain, gain_mlp_part,
            ),
        )
        heads, head_block = gain_query.shape[0], HEAD // dp_size
        dp_at = lax.axis_index("dp")
        wide = lax.dynamic_slice(gains, (0, dp_at * block), (2, block))
        head_gains = lax.dynamic_slice(gains, (8, dp_at * head_block), (2 * heads, head_block))
        return (
            output,
            grad_tokens,
            grad_query,
            grad_key,
            grad_value,
            grad_out,
            head_gains[:heads],
            head_gains[heads:],
            wide[1],
            grad_gate,
            grad_up,
            grad_down,
            wide[0],
        )

    return shards


def solution(mesh):
    in_specs = (
        P("dp", None),
        P("dp"),
        P("dp"),
        P(None, "tensor"),
        P(None, "tensor"),
        P(None, "tensor"),
        P("tensor", None),
        P("tensor", None),
        P("tensor", None),
        P(),
        P(None, "tensor"),
        P(None, "tensor"),
        P("tensor", None),
        P(),
        P("dp", None),
    )
    out_specs = (
        P("dp", None),
        P("dp", None),
        P("dp", "tensor"),
        P("dp", "tensor"),
        P("dp", "tensor"),
        P("tensor", "dp"),
        P("tensor", "dp"),
        P("tensor", "dp"),
        P("dp"),
        P("dp", "tensor"),
        P("dp", "tensor"),
        P("tensor", "dp"),
        P("dp"),
    )
    shards = make_shards(mesh.shape["dp"])
    return jax.shard_map(shards, mesh=mesh, in_specs=in_specs, out_specs=out_specs, check_vma=False)
```

```python
import functools

import jax
import jax.numpy as jnp
import numpy as np
from jax import lax
from jax.experimental import pallas as pl
from jax.experimental.pallas import tpu as pltpu
from jax.sharding import PartitionSpec as P

HEAD = 128
LENGTH = 1024
EPSILON = 1e-06
NEG_FILL = -1e30
ROPE_BASE = 500000.0
ROW_CHUNKS = 4
F32 = jnp.float32
BF16 = jnp.bfloat16


COLS = 256
LINE_FIRST = (0, 4)
Y_SLOTS = 3
B_SLOTS = 3
FEED_TICK = 3
HIDDEN_TICK = 7
BRANCH_TICK = 12
INPUT_TICK = 20
TOKEN_TICK = 25
HBM_NAMES = (
    "gdrt", "hlt", "tokens", "inner", "mixed", "gdr", "gate", "up", "branch", "cotangent",
    "query", "key", "value", "query_raw", "key_raw", "partner",
    "inverses", "seg_live", "cosine", "sine",
    "w_out", "w_gate", "w_up", "w_down", "w_query", "w_key", "w_value",
)
TILE = 512
VMEM_LIMIT = 65400 * 1024
MESH = pl.DeviceIdType.MESH

def column_sum(values):
    return jnp.sum(values, axis=0, keepdims=True)


def mean_inverse(values):
    return lax.rsqrt(jnp.mean(values * values, axis=1, keepdims=True) + EPSILON)


def tensor_peers():
    at = lax.axis_index("tensor")
    core = lax.rem(at, 2)
    return core, at + 1 - 2 * core, lax.rem(at + 2, 4)


def greet(*peers):
    barrier = pltpu.get_barrier_semaphore()
    for peer in peers:
        pl.semaphore_signal(barrier, inc=1, device_id=peer, device_id_type=MESH)
    pl.semaphore_wait(barrier, len(peers))


def forward_kernel(
    tok_hbm, cot_hbm, wq_hbm, wk_hbm, wv_hbm, wo_hbm, wg_hbm, wu_hbm, wd_hbm, cos_hbm, sin_hbm,
    seg_live, seg_row, query_gain, key_gain, attn_gain, mlp_gain,
    gate_out, up_out, inner_out, hlt_out, gdr_out, gdrt_out, branch_out, out_out,
    query_out, key_out, value_out, query_raw_out, key_raw_out, mixed_out, partner_out,
    gain_out, inverse_out, log_out,
    wg, cs, crecv, xs, xr, xr2, ag, squares, squares_in,
    w_sem, t_sem, s_sem, a_sem, r_sem, m_sem, sq_s_sem, sq_r_sem, sx_s_sem, sx_r_sem,
    cs_sem, cr_sem, xs_sem, xr_sem, as_sem, ar_sem, cs2_sem, cr2_sem, xs2_sem, xr2_sem,
    gs_sem, gr_sem, os_sem, or_sem, hs_sem, hr_sem, fs_sem, fr_sem, g_sem, h_sem, b_sem, d_sem, o_sem,
):
    core, sibling, across = tensor_peers()
    dp_at = lax.axis_index("dp")
    partner = dp_at + 1 - 2 * lax.rem(dp_at, 2)
    chunk = xs.shape[1]
    half = chunk * ROW_CHUNKS
    full = 2 * half
    both = 2 * chunk
    width, hidden = xs.shape[2], wg.shape[1]
    head_cols = wq_hbm.shape[1]
    heads = head_cols // HEAD
    tiles = hidden // TILE
    wide_tiles = width // TILE
    last = ROW_CHUNKS - 1
    nt = (((1,), (1,)), ((), ()))

    def start(copies):
        for copy in copies:
            copy.start()

    def finish(copies):
        for copy in copies:
            copy.wait()

    def own_rows(s, c):
        return pl.ds(pl.multiple_of(c * both + jnp.where(core == s, 0, chunk), chunk), chunk)

    def row_load(c, src, dst, sem):
        return pltpu.make_async_copy(src.at[own_rows(0, c)], dst.at[c % 2], sem.at[c % 2])

    wide_loads = [pltpu.make_async_copy(wg_hbm, wg, w_sem.at[0])]

    def remote(src, dst, send_sem, recv_sem, peer):
        return pltpu.make_async_remote_copy(
            src_ref=src, dst_ref=dst, send_sem=send_sem, recv_sem=recv_sem,
            device_id={"tensor": peer}, device_id_type=MESH)

    def partner_copy(c):
        return pltpu.make_async_remote_copy(
            src_ref=xr.at[c], dst_ref=partner_out.at[rows(c * chunk)], send_sem=hs_sem.at[c],
            recv_sem=hr_sem.at[c], device_id={"dp": partner}, device_id_type=MESH)

    def hand_copy(c):
        return remote(
            partner_out.at[rows(c * chunk)], partner_out.at[rows(half + c * chunk)],
            fs_sem.at[c], fr_sem.at[c], sibling)

    def core_copy(c):
        return remote(cs.at[c % 2], crecv.at[c], cs_sem.at[c], cr_sem.at[c], sibling)

    def x_copy(c):
        return remote(xs.at[c], xr.at[c], xs_sem.at[c], xr_sem.at[c], across)

    def hidden_copy(c):
        return remote(xr.at[c], ag.at[c % 2], as_sem.at[c], ar_sem.at[c], sibling)

    def core2_copy(c):
        return remote(cs.at[c % 2], crecv.at[c], cs2_sem.at[c], cr2_sem.at[c], sibling)

    def x2_copy(c):
        return remote(xs.at[c], xr2.at[c], xs2_sem.at[c], xr2_sem.at[c], across)

    def grad_copy(c):
        return remote(xr2.at[c], ag.at[c % 2], gs_sem.at[c], gr_sem.at[c], sibling)

    def out_copy(c):
        return remote(xr.at[c], crecv.at[c], os_sem.at[c], or_sem.at[c], sibling)

    def rows(first):
        return pl.ds(first, chunk)

    def side_copies(buf, dst, sem, c):
        return [
            pltpu.make_async_copy(
                buf.at[pl.ds(s * chunk, chunk)], dst.at[rows(s * half + c * chunk)], sem.at[s])
            for s in range(2)
        ]

    def turned_copies(buf, dst, sem, c):
        return [
            pltpu.make_async_copy(
                buf.at[:, pl.ds(s * chunk, chunk)], dst.at[:, rows(s * half + c * chunk)], sem.at[s])
            for s in range(2)
        ]

    def square_copy(c):
        return remote(
            squares.at[c], squares_in.at[0, c], sq_s_sem.at[c], sq_r_sem.at[c], sibling)

    def square_x_copy(c):
        return remote(
            squares.at[c], squares_in.at[1, c], sx_s_sem.at[c], sx_r_sem.at[c], across)

    def square_pass_on(c):
        square_copy(c).wait()
        squares[c] += squares_in[0, c]
        square_x_copy(c).start()

    def project(c, weights, loads, tok, tok_load, query_raw, key_raw, value, value_turned):
        at = slice(c * both, (c + 1) * both)
        lanes = lax.broadcasted_iota(jnp.int32, (both, HEAD), 1)
        tok_load(c).wait()
        if c == 0:
            loads[0].wait()
        query_raw[at, :] = jnp.dot(tok[c % 2], weights[0], preferred_element_type=F32)
        if c == 0:
            loads[1].wait()
        key_raw[at, :] = jnp.dot(tok[c % 2], weights[1], preferred_element_type=F32)
        query_square = jnp.sum(query_raw[at, :] * query_raw[at, :], axis=1, keepdims=True)
        key_square = jnp.sum(key_raw[at, :] * key_raw[at, :], axis=1, keepdims=True)
        squares[c] = jnp.where(lanes == 0, query_square, key_square)
        square_copy(c).start()
        if c == 0:
            loads[2].wait()
            start(wide_loads)
        if c == 1:
            square_pass_on(0)
        value[at, :] = jnp.dot(tok[c % 2], weights[2], preferred_element_type=F32).astype(BF16)
        value_turned[:, at] = value[at, :].T
        if c + 2 < ROW_CHUNKS:
            tok_load(c + 2).start()

    def attend(c, query_raw, key_raw, query, key, value_turned, cosine, sine, w_out, mixed, bias):
        first, keys = c * both, (c + 1) * both
        at = slice(first, keys)
        square_x_copy(c).wait()
        squares[c] += squares_in[1, c]
        inverse = lax.rsqrt(squares[c] / width + EPSILON)
        inverse_out[at, :] = inverse
        for raw, gain, lane, dst in (
            (query_raw, query_gain, 0, query), (key_raw, key_gain, 1, key)):
            gains = gain[...].astype(F32)
            for h in range(heads):
                cols = slice(h * HEAD, (h + 1) * HEAD)
                normed = raw[at, cols] * inverse[:, lane : lane + 1] * gains[h : h + 1, :]
                turned = normed * cosine[at, :] + pltpu.roll(normed, HEAD // 2, 1) * sine[at, :]
                dst[at, cols] = turned.astype(BF16)
        key_at = lax.broadcasted_iota(jnp.int32, (keys, both), 0)
        query_at = lax.broadcasted_iota(jnp.int32, (keys, both), 1) + first
        allowed = (
            (seg_live[0:keys, 0:1] == seg_row[:, at])
            & (key_at <= query_at)
            & ((seg_live[0:keys, 1:2] > 0) | (key_at == query_at)))
        bias[0:keys, :] = jnp.where(allowed, 0.0, NEG_FILL)

        def head(h, carry):
            cols = pl.ds(pl.multiple_of(h * HEAD, HEAD), HEAD)
            scores = lax.dot_general(
                key[0:keys, cols], query[at, cols], nt, preferred_element_type=F32) * HEAD ** (-0.5)
            scores = scores + bias[0:keys, :]
            top = jnp.max(scores, axis=0, keepdims=True)
            powers = jnp.exp(scores - top)
            total = jnp.sum(powers, axis=0, keepdims=True)
            prob = (powers / total).astype(BF16)
            log_out[pl.ds(h, 1), at] = top + jnp.log(total)
            turned = jnp.dot(value_turned[cols, 0:keys], prob, preferred_element_type=F32)
            mixed[c % 2, :, cols] = turned.T.astype(BF16)
            return carry
        lax.fori_loop(0, heads, head, 0)

        def mixed_rows(s):
            return pl.ds(pl.multiple_of(jnp.where(core == s, 0, chunk), chunk), chunk)
        if c + 1 < ROW_CHUNKS:
            square_pass_on(c + 1)
        if c >= 2:
            core_copy(c - 2).wait_send()
        cs[c % 2] = jnp.dot(mixed[c % 2, mixed_rows(1), :], w_out[...], preferred_element_type=F32)
        core_copy(c).start()
        xs[c] = jnp.dot(mixed[c % 2, mixed_rows(0), :], w_out[...], preferred_element_type=F32)
        start(mixed_copies(c, mixed))
        pass_on(c)

    def mixed_copies(c, mixed):
        return [
            pltpu.make_async_copy(
                mixed.at[c % 2, pl.ds(pl.multiple_of(jnp.where(core == s, 0, chunk), chunk), chunk)],
                mixed_out.at[rows(s * half + c * chunk)], m_sem.at[c % 2, s])
            for s in range(2)
        ]

    def pass_on(c):
        core_copy(c).wait_recv()
        xs[c] += crecv[c]
        x_copy(c).start()

    def attention(
        query_raw, key_raw, query, key, value, value_turned, cosine, sine, w_out, weights, tok, mixed, bias,
    ):
        def tok_load(c):
            return pltpu.make_async_copy(
                tok_hbm.at[pl.ds(c * both, both)], tok.at[c % 2], t_sem.at[c % 2])

        loads = [
            pltpu.make_async_copy(w, weights.at[i], a_sem.at[i])
            for i, w in enumerate((wq_hbm, wk_hbm, wv_hbm))
        ]
        tables = [
            pltpu.make_async_copy(src, dst, r_sem.at[i])
            for i, (src, dst) in enumerate(((cos_hbm, cosine), (sin_hbm, sine), (wo_hbm, w_out)))
        ]
        tok_load(0).start()
        start(loads)
        tok_load(1).start()
        start(tables)
        greet({"tensor": sibling}, {"tensor": across}, {"dp": partner})
        results = [
            pltpu.make_async_copy(src, dst, a_sem.at[i])
            for i, (src, dst) in enumerate((
                (value, value_out), (query_raw, query_raw_out), (key_raw, key_raw_out),
                (query, query_out), (key, key_out)))
        ]
        for c in range(ROW_CHUNKS + 1):
            if c < ROW_CHUNKS:
                project(c, weights, loads, tok, tok_load, query_raw, key_raw, value, value_turned)
            if c == 1:
                finish(tables)
            if c == last:
                start(results[:3])
            if c >= 1:
                if c >= 3:
                    finish(mixed_copies(c - 3, mixed))
                attend(
                    c - 1, query_raw, key_raw, query, key, value_turned, cosine, sine, w_out, mixed, bias)
        start(results[3:])
        for c in range(last - 1, ROW_CHUNKS):
            core_copy(c).wait_send()
            finish(mixed_copies(c, mixed))
        finish(results)

    rows_of = (full, head_cols)
    pl.run_scoped(
        attention, pltpu.VMEM(rows_of, F32), pltpu.VMEM(rows_of, F32), pltpu.VMEM(rows_of, BF16),
        pltpu.VMEM(rows_of, BF16), pltpu.VMEM(rows_of, BF16), pltpu.VMEM((head_cols, full), BF16),
        pltpu.VMEM((full, HEAD), F32), pltpu.VMEM((full, HEAD), F32), pltpu.VMEM(wo_hbm.shape, BF16),
        pltpu.VMEM((3,) + wq_hbm.shape, BF16), pltpu.VMEM((2, both, width), BF16),
        pltpu.VMEM((2, both, head_cols), BF16), pltpu.VMEM((full, both), F32))
    pl.run_scoped(
        functools.partial(
            feed_forward, core, chunk, own_rows, row_load, rows, side_copies, turned_copies,
            (x_copy, hidden_copy, core2_copy, x2_copy, grad_copy, out_copy, partner_copy, hand_copy), wide_loads, seg_live,
            (tok_hbm, cot_hbm, wu_hbm, wd_hbm, attn_gain, mlp_gain, wg),
            (gate_out, up_out, inner_out, hlt_out, gdr_out, gdrt_out, branch_out, out_out, gain_out),
            (cs, crecv, xs, xr, xr2, ag),
            (w_sem, t_sem, s_sem, g_sem, h_sem, b_sem, d_sem, o_sem)),
        pltpu.VMEM(wu_hbm.shape, BF16), pltpu.VMEM(wd_hbm.shape, BF16),
        pltpu.VMEM((both, hidden), F32), pltpu.VMEM((both, hidden), F32),
        pltpu.VMEM((both, hidden), BF16), pltpu.VMEM((both, width), BF16), pltpu.VMEM((width, both), BF16),
        pltpu.VMEM((both, width), BF16), pltpu.VMEM((2, chunk, width), BF16),
        pltpu.VMEM((2, chunk, width), BF16))


def feed_forward(
    core, chunk, own_rows, row_load, rows, side_copies, turned_copies, remote_copies, wide_loads, seg_live,
    operands, results, buffers, sems,
    wu, wd, gate_buf, up_buf, inner_buf, low_buf, hlt_buf, out_buf, tok, seed,
):
    x_copy, hidden_copy, core2_copy, x2_copy, grad_copy, out_copy, partner_copy, hand_copy = remote_copies
    tok_hbm, cot_hbm, wu_hbm, wd_hbm, attn_gain, mlp_gain, wg = operands
    gate_out, up_out, inner_out, hlt_out, gdr_out, gdrt_out, branch_out, out_out, gain_out = results
    cs, crecv, xs, xr, xr2, ag = buffers
    w_sem, t_sem, s_sem, g_sem, h_sem, b_sem, d_sem, o_sem = sems
    last = ROW_CHUNKS - 1
    tiles, wide_tiles = wg.shape[1] // TILE, wd.shape[1] // TILE
    loads = wide_loads + [
        pltpu.make_async_copy(wu_hbm, wu, w_sem.at[1]),
        pltpu.make_async_copy(wd_hbm, wd, w_sem.at[2]),
    ]
    loads[1].start()
    loads[2].start()
    for c in range(2):
        row_load(c, tok_hbm, tok, t_sem).start()
        row_load(c, cot_hbm, seed, s_sem).start()

    def hand_on(c):
        partner_copy(c).wait_recv()
        hand_copy(c).start()

    def feed(c):
        x_copy(c).wait()
        total = xs[c] + xr[c]
        xs[c] = total
        branch_copy = pltpu.make_async_copy(xs.at[c], branch_out.at[rows(c * chunk)], b_sem)
        branch_copy.start()
        row_load(c, tok_hbm, tok, t_sem).wait()
        hidden = tok[c % 2].astype(F32) + total * mean_inverse(total) * attn_gain[...]
        if c + 2 < ROW_CHUNKS:
            row_load(c + 2, tok_hbm, tok, t_sem).start()
        xr[c] = hidden
        hidden_copy(c).start()
        partner_copy(c).start()
        low_buf[0:chunk, :] = hidden.astype(BF16)
        if c >= 1:
            for copy in turned_copies(hlt_buf, hlt_out, h_sem, c - 1):
                copy.wait()
            for buf, dst, i in ((gate_buf, gate_out, 0), (up_buf, up_out, 1), (inner_buf, inner_out, 2)):
                for copy in side_copies(buf, dst, g_sem.at[i], c - 1):
                    copy.wait()
        hlt_buf[:, 0:chunk] = hidden.astype(BF16).T
        hidden_copy(c).wait_recv()
        low_buf[chunk : 2 * chunk, :] = ag[c % 2].astype(BF16)
        hlt_buf[:, chunk : 2 * chunk] = ag[c % 2].astype(BF16).T
        for copy in turned_copies(hlt_buf, hlt_out, h_sem, c):
            copy.start()
        if c == 0:
            loads[0].wait()
            loads[1].wait()

        def tile(n, carry):
            at = pl.ds(pl.multiple_of(n * TILE, TILE), TILE)
            gate = jnp.dot(low_buf[...], wg[:, at], preferred_element_type=F32)
            up = jnp.dot(low_buf[...], wu[:, at], preferred_element_type=F32)
            gate_buf[:, at] = gate
            up_buf[:, at] = up
            inner_buf[:, at] = (gate * jax.nn.sigmoid(gate) * up).astype(BF16)
            return carry
        lax.fori_loop(0, tiles, tile, 0)
        for buf, dst, i in ((gate_buf, gate_out, 0), (up_buf, up_out, 1), (inner_buf, inner_out, 2)):
            for copy in side_copies(buf, dst, g_sem.at[i], c):
                copy.start()
        if c == 0:
            loads[2].wait()
        if c >= 2:
            core2_copy(c - 2).wait_send()
        branch_copy.wait()

        def down_tile(n, carry):
            at = pl.ds(pl.multiple_of(n * TILE, TILE), TILE)
            part = jnp.dot(inner_buf[...], wd[:, at], preferred_element_type=F32)
            xs[c, :, at] = part[0:chunk]
            cs[c % 2, :, at] = part[chunk : 2 * chunk]
            return carry
        lax.fori_loop(0, wide_tiles, down_tile, 0)
        core2_copy(c).start()
        core2_copy(c).wait_recv()
        xs[c] += crecv[c]
        x2_copy(c).start()
        if c >= 1:
            hand_on(c - 1)

    def finish(c, gain_total):
        x2_copy(c).wait()
        down = xs[c] + xr2[c]
        inv = mean_inverse(down)
        row_load(c, cot_hbm, seed, s_sem).wait()
        seed_rows = seed[c % 2].astype(F32) * seg_live[own_rows(0, c), 1:2].astype(F32)
        if c + 2 < ROW_CHUNKS:
            row_load(c + 2, cot_hbm, seed, s_sem).start()
        normed = down * inv
        gain_total = gain_total + column_sum(seed_rows * normed)
        scaled = seed_rows * mlp_gain[...]
        dot = jnp.sum(scaled * down, axis=1, keepdims=True)
        grad = inv * scaled - down * (inv * inv * inv * dot / down.shape[1])
        hidden_copy(c).wait_send()
        partner_copy(c).wait_send()
        xr2[c] = grad
        grad_copy(c).start()
        xr[c] = xr[c] + normed * mlp_gain[...]
        if c == 0:
            for copy in turned_copies(hlt_buf, hlt_out, h_sem, last):
                copy.wait()
        if c >= 1:
            for copy in turned_copies(hlt_buf, gdrt_out, d_sem.at[0], c - 1):
                copy.wait()
            for copy in side_copies(low_buf, gdr_out, d_sem.at[1], c - 1):
                copy.wait()
        low_buf[0:chunk, :] = grad.astype(BF16)
        hlt_buf[:, 0:chunk] = grad.astype(BF16).T
        grad_copy(c).wait_recv()
        out_copy(c).start()
        low_buf[chunk : 2 * chunk, :] = ag[c % 2].astype(BF16)
        hlt_buf[:, chunk : 2 * chunk] = ag[c % 2].astype(BF16).T
        for copy in turned_copies(hlt_buf, gdrt_out, d_sem.at[0], c):
            copy.start()
        for copy in side_copies(low_buf, gdr_out, d_sem.at[1], c):
            copy.start()
        return gain_total

    def out_copies(c):
        return [
            pltpu.make_async_copy(
                out_buf.at[pl.ds(s * chunk, chunk)], out_out.at[own_rows(s, c)], o_sem.at[s])
            for s in range(2)
        ]

    def place(c):
        if c >= 1:
            for copy in out_copies(c - 1):
                copy.wait()
        out_buf[0:chunk, :] = xr[c].astype(BF16)
        out_copy(c).wait_recv()
        out_buf[chunk : 2 * chunk, :] = crecv[c].astype(BF16)
        for copy in out_copies(c):
            copy.start()

    for c in range(ROW_CHUNKS):
        feed(c)
    gain_total = jnp.zeros(mlp_gain.shape, F32)
    for c in range(ROW_CHUNKS):
        gain_total = finish(c, gain_total)
        if c >= 1:
            place(c - 1)
        if c == 1:
            hand_on(last)
    place(last)
    gain_out[...] = gain_total
    for buf, dst, i in ((gate_buf, gate_out, 0), (up_buf, up_out, 1), (inner_buf, inner_out, 2)):
        for copy in side_copies(buf, dst, g_sem.at[i], last):
            copy.wait()
    for copy in turned_copies(hlt_buf, gdrt_out, d_sem.at[0], last):
        copy.wait()
    for copy in side_copies(low_buf, gdr_out, d_sem.at[1], last):
        copy.wait()
    for copy in out_copies(last):
        copy.wait()
    core2_copy(last - 1).wait_send()
    core2_copy(last).wait_send()
    for c in range(ROW_CHUNKS):
        grad_copy(c).wait_send()
        out_copy(c).wait_send()
        hand_copy(c).wait()


def forward_layer(hbm, vmem_args):
    tokens, w_query, w_gate = hbm[0], hbm[2], hbm[6]
    row_count, width = tokens.shape
    hidden, head_cols = w_gate.shape[1], w_query.shape[1]
    chunk = row_count // 2 // ROW_CHUNKS
    DMA = pltpu.SemaphoreType.DMA
    vmem, any_space = pl.BlockSpec(memory_space=pltpu.VMEM), pl.BlockSpec(memory_space=pl.ANY)

    def shape(*dims, kind=F32):
        return jax.ShapeDtypeStruct(dims, kind)

    per_chunk = DMA((ROW_CHUNKS,))
    return pl.pallas_call(
        forward_kernel,
        out_shape=(
            shape(row_count, hidden),
            shape(row_count, hidden),
            shape(row_count, hidden, kind=BF16),
            shape(width, row_count, kind=BF16),
            shape(row_count, width, kind=BF16),
            shape(width, row_count, kind=BF16),
            shape(row_count // 2, width),
            shape(row_count, width, kind=BF16),
            shape(row_count, head_cols, kind=BF16),
            shape(row_count, head_cols, kind=BF16),
            shape(row_count, head_cols, kind=BF16),
            shape(row_count, head_cols),
            shape(row_count, head_cols),
            shape(row_count, head_cols, kind=BF16),
            shape(row_count, width),
            shape(1, width),
            shape(row_count, HEAD),
            shape(head_cols // HEAD, row_count),
        ),
        in_specs=[any_space] * len(hbm) + [vmem] * len(vmem_args),
        out_specs=(any_space,) * 15 + (vmem,) * 3,
        scratch_shapes=[
            pltpu.VMEM(w_gate.shape, BF16),
            pltpu.VMEM((2, chunk, width), F32),
            pltpu.VMEM((ROW_CHUNKS, chunk, width), F32),
            pltpu.VMEM((ROW_CHUNKS, chunk, width), F32),
            pltpu.VMEM((ROW_CHUNKS, chunk, width), F32),
            pltpu.VMEM((ROW_CHUNKS, chunk, width), F32),
            pltpu.VMEM((2, chunk, width), F32),
            pltpu.VMEM((ROW_CHUNKS, 2 * chunk, HEAD), F32),
            pltpu.VMEM((2, ROW_CHUNKS, 2 * chunk, HEAD), F32),
            DMA((3,)),
            DMA((2,)),
            DMA((2,)),
            DMA((5,)),
            DMA((3,)),
            DMA((2, 2)),
        ]
        + [per_chunk] * 22
        + [DMA((3, 2)), DMA((2,)), DMA, DMA((2, 2)), DMA((2,))],
        compiler_params=pltpu.CompilerParams(
            collective_id=1, has_side_effects=True, vmem_limit_bytes=VMEM_LIMIT),
    )(*hbm, *vmem_args)


def backward_kernel(
    dp_size, counts,
    gdrt_hbm, hlt_hbm, tok_hbm, inner_hbm, mixed_hbm, gdr_hbm, gate_hbm, up_hbm, branch_hbm, cot_hbm,
    query_hbm, key_hbm, value_hbm, query_raw_hbm, key_raw_hbm, partner_hbm,
    inverses_hbm, seg_live_hbm, cos_hbm, sin_hbm,
    w_out_hbm, wg_hbm, wu_hbm, wd_hbm, wq_hbm, wk_hbm, wv_hbm,
    log_totals, seg_row,
    query_gain, key_gain, attn_gain, gain_mlp_part,
    down_out, out_out, gate_out, up_out, query_out, key_out, value_out, token_out, gains_out,
    ggr_hbm, gur_hbm, gbt_hbm, gh_hbm, gqkv_hbm,
    at, bbuf, bsend, bpar, own, ysend, yrecv, fsend, frecv, zsend, zrecv, stage, stage_t, cs, crecv, xs, xr, ag, dots, dots_in,
    vec, vec_in,
    at_sem, b_sem, bs_sem, ys_sem, yr_sem, fs_sem, fr_sem, zs_sem, zr_sem, out_sem, far_sem,
    cs_sem, cr_sem, xs_sem, xr_sem, as_sem, ar_sem, cs2_sem, cr2_sem, xs2_sem, xr2_sem, as2_sem,
    ar2_sem, ds_sem, dr_sem, vs_sem, vr_sem, w_sem, pre_sem, st_sem, gh_sem, tok_sem, live_sem,
    y_credit, up_credit, down_credit,
):
    n_down, n_pairs, n_heads, n_out = counts
    first_heads = n_down + n_pairs
    first_out = first_heads + n_heads
    total = first_out + n_out
    line = dp_size // 2
    width = at.shape[1]
    block = width // dp_size
    chunk = xs.shape[1]
    half = chunk * ROW_CHUNKS
    full = 2 * half
    head_cols = query_hbm.shape[1]
    passes = total + n_pairs + len(LINE_FIRST)
    dp_at = lax.axis_index("dp")
    z, y = dp_at // 2, dp_at % 2
    partner = dp_at + 1 - 2 * y
    below, above = dp_at - 2, dp_at + 2
    has_below, has_above = z > 0, z < line - 1
    core, sibling, across = tensor_peers()
    steps = [1 << s for s in range(dp_size.bit_length() - 1)]
    vec_peers = [dp_at + bit * (1 - 2 * ((dp_at // bit) % 2)) for bit in steps]

    def at_dp(i):
        return {"dp": i}

    def at_tensor(i):
        return {"tensor": i}

    def remote(src, dst, send_sem, recv_sem, peer):
        return pltpu.make_async_remote_copy(
            src_ref=src, dst_ref=dst, send_sem=send_sem, recv_sem=recv_sem,
            device_id=peer, device_id_type=MESH)

    def y_copy(p, b):
        return remote(ysend.at[p, b], yrecv.at[p, b], ys_sem.at[p, b], yr_sem.at[p, b], at_dp(partner))

    def z_copy(p, b, slot, target):
        return remote(zsend.at[p, b], zrecv.at[p, slot], zs_sem.at[p, b], zr_sem.at[p, slot], at_dp(target))

    def final_copy(p):
        return remote(fsend.at[p], frecv.at[p], fs_sem.at[p], fr_sem.at[p], at_dp(partner))

    def is_pair(k):
        return (k >= n_down) & (k < first_heads)

    def slot_of(k):
        return lax.rem(
            (k >= n_down).astype(jnp.int32) + (k >= first_heads).astype(jnp.int32)
            + (k >= first_out).astype(jnp.int32), 2)

    def row_block(rows_at):
        return pl.ds(pl.multiple_of(rows_at * block, block), block)

    def product(k, rows_at):
        return jnp.dot(
            at[slot_of(k), row_block(rows_at), :], bbuf[lax.rem(k, B_SLOTS)],
            preferred_element_type=F32)

    def pair_product(k, rows_at):
        return product(k, rows_at) + jnp.dot(
            at[2, row_block(rows_at), :], bpar[...], preferred_element_type=F32)

    def at_load(i):
        src = (gdrt_hbm, hlt_hbm, None, gbt_hbm)[i]
        return pltpu.make_async_copy(src, at.at[i % 2], at_sem.at[i % 2])

    def b_load(k, act):
        def columns(src, at_chunk, dst, sem):
            act(pltpu.make_async_copy(
                src.at[:, pl.ds(pl.multiple_of(at_chunk * COLS, COLS), COLS)], dst, sem))
        own_dst, own_sem = bbuf.at[lax.rem(k, B_SLOTS)], b_sem.at[lax.rem(k, B_SLOTS)]

        @pl.when(k < n_down)
        def _():
            columns(inner_hbm, k, own_dst, own_sem)

        for first, src in ((n_down, ggr_hbm), (n_down + n_pairs // 2, gur_hbm)):
            @pl.when((k >= first) & (k < first + n_pairs // 2))
            def _(first=first, src=src):
                columns(src, 2 * (k - first) + y, own_dst, own_sem)
                columns(src, 2 * (k - first) + 1 - y, bsend, bs_sem)

        @pl.when((k >= first_heads) & (k < first_out))
        def _():
            columns(gqkv_hbm, k - first_heads, own_dst, own_sem)

        @pl.when((k >= first_out) & (k < total))
        def _():
            columns(mixed_hbm, k - first_out, own_dst, own_sem)

    def line_first(k):
        return functools.reduce(jnp.logical_or, [k == at_chunk for at_chunk in LINE_FIRST])

    def walk(fn):
        def body(i, carry):
            @pl.when(z <= i)
            def _():
                fn(z + line - 1 - i, True)

            @pl.when(z >= line - 1 - i)
            def _():
                fn(z - (line - 1 - i), False)
            return carry
        lax.fori_loop(0, line - 1, body, 0)

    def pair_send(k):
        p = lax.rem(k, Y_SLOTS)

        @pl.when(k >= Y_SLOTS)
        def _():
            pl.semaphore_wait(y_credit, 1)
        b_load(k, lambda copy: copy.wait())

        @pl.when(jnp.logical_not(line_first(k) | is_pair(k)))
        def _():
            def one(b, up=None):
                ysend[p, b] = product(k, 2 * b + 1 - y)
                y_copy(p, b).start()
            walk(one)
            one(z)

        @pl.when(is_pair(k))
        def _():
            def rows_out(b, carry):
                ysend[p, b] = bsend[row_block(b), :].astype(F32)
                y_copy(p, b).start()
                return carry
            lax.fori_loop(0, line, rows_out, 0)

    def line_send(q, k, source):
        p = lax.rem(q, 2)

        @pl.when(q >= 2)
        def _():
            @pl.when(has_above)
            def _():
                pl.semaphore_wait(up_credit, 1)

            @pl.when(has_below)
            def _():
                pl.semaphore_wait(down_credit, 1)

        def one(b, up):
            has_before, target = (has_below, above) if up else (has_above, below)
            zsend[p, b] = source(b)

            @pl.when(has_before)
            def _():
                z_copy(p, b, b, target).wait_recv()
                zsend[p, b] += zrecv[p, b]
            if up:
                z_copy(p, b, b, target).start()
            else:
                @pl.when(b == z - 1)
                def _():
                    z_copy(p, b, line, target).start()

                @pl.when(b != z - 1)
                def _():
                    z_copy(p, b, b, target).start()
        walk(one)

    def line_own(q, dst):
        p = lax.rem(q, 2)

        @pl.when(has_below)
        def _():
            z_copy(p, z, z, below).wait_recv()
            dst[...] += zrecv[p, z]

        @pl.when(has_above)
        def _():
            z_copy(p, z, line, below).wait_recv()
            dst[...] += zrecv[p, line]

        def drain(b, up):
            z_copy(p, b, b, below).wait_send()
        walk(drain)

        @pl.when(q < passes - 2)
        def _():
            @pl.when(has_below)
            def _():
                pl.semaphore_signal(up_credit, inc=1, device_id=at_dp(below), device_id_type=MESH)

            @pl.when(has_above)
            def _():
                pl.semaphore_signal(down_credit, inc=1, device_id=at_dp(above), device_id_type=MESH)

    def is_turned(k):
        return (k < n_down) | (k >= first_out)

    per_head = n_heads // 3
    results = (
        (0, n_down, down_out, True),
        (first_heads, per_head, query_out, False),
        (first_heads + per_head, per_head, key_out, False),
        (first_heads + 2 * per_head, per_head, value_out, False),
        (first_out, n_out, out_out, True),
    )
    pair_results = ((n_down, gate_out), (n_down + n_pairs // 2, up_out))

    def out_act(k, act):
        def place(at_chunk):
            return pl.ds(pl.multiple_of(at_chunk * COLS, COLS), COLS)

        for first, count, dst, turned in results:
            @pl.when((k >= first) & (k < first + count))
            def _(first=first, dst=dst, turned=turned):
                if turned:
                    act(pltpu.make_async_copy(stage_t, dst.at[place(k - first)], out_sem))
                else:
                    act(pltpu.make_async_copy(stage, dst.at[:, place(k - first)], out_sem))

        for first, dst in pair_results:
            @pl.when((k >= first) & (k < first + n_pairs // 2))
            def _(first=first, dst=dst):
                act(pltpu.make_async_copy(stage, dst.at[:, place(2 * (k - first) + y)], out_sem))

    def far_out(k):
        for first, dst in pair_results:
            @pl.when((k >= first) & (k < first + n_pairs // 2))
            def _(first=first, dst=dst):
                cols = pl.ds(pl.multiple_of((2 * (k - first) + 1 - y) * COLS, COLS), COLS)
                copy = pltpu.make_async_copy(frecv.at[lax.rem(k, Y_SLOTS)], dst.at[:, cols], far_sem)
                copy.start()
                copy.wait()

    def finish_chunk(k, q):
        p = lax.rem(k, Y_SLOTS)

        @pl.when(k >= 1)
        def _():
            out_act(k - 1, lambda copy: copy.wait())
        stage[...] = own[...]

        @pl.when(jnp.logical_not(is_pair(k)))
        def _():
            y_copy(p, z).wait_recv()
            stage[...] += yrecv[p, z]
        line_own(q, stage)

        @pl.when((k < n_down) | (k >= first_out))
        def _():
            stage_t[...] = stage[...].T
        out_act(k, lambda copy: copy.start())

        @pl.when(line_first(k))
        def _():
            y_copy(p, z).wait_send()

        @pl.when(jnp.logical_not(line_first(k)))
        def _():
            for b in range(line):
                y_copy(p, b).wait_send()

        @pl.when(is_pair(k))
        def _():
            final_copy(p).wait()
            far_out(k)

        @pl.when(k < total - Y_SLOTS)
        def _():
            pl.semaphore_signal(y_credit, inc=1, device_id=at_dp(partner), device_id_type=MESH)

    def pass_of(k):
        return (
            k + jnp.clip(k - n_down, 0, n_pairs)
            + sum((k > at_chunk).astype(jnp.int32) for at_chunk in LINE_FIRST))

    def prefetch(k):
        @pl.when(k + 2 < total)
        def _():
            b_load(k + 2, lambda copy: copy.start())

    def send_ahead(k):
        @pl.when(k + 2 < total)
        def _():
            pair_send(k + 2)

    def tick(k):
        p = lax.rem(k, Y_SLOTS)
        q = pass_of(k)
        is_line_first = line_first(k)
        prefetch(k)

        @pl.when(jnp.logical_not(is_line_first))
        def _():
            def mine(b):
                part = product(k, 2 * b + y)
                y_copy(p, b).wait_recv()
                return part + yrecv[p, b]
            line_send(q, k, mine)

        @pl.when(is_line_first)
        def _():
            line_send(q, k, lambda b: product(k, 2 * b + 1 - y))

        @pl.when(k >= 1)
        def _():
            finish_chunk(k - 1, q - 1)
        send_ahead(k)
        own[...] = product(k, 2 * z + y)

        @pl.when(is_line_first)
        def _():
            line_send(q + 1, k, lambda b: product(k, 2 * b + y))
            ysend[p, z] = product(k, 2 * z + 1 - y)
            line_own(q, ysend.at[p, z])
            y_copy(p, z).start()

    def pair_tick(k, work):
        p = lax.rem(k, Y_SLOTS)
        q = pass_of(k)
        prefetch(k)

        def rows_in(b, carry):
            y_copy(p, b).wait_recv()
            bpar[row_block(b), :] = yrecv[p, b].astype(BF16)
            return carry
        lax.fori_loop(0, line, rows_in, 0)
        line_send(q, k, lambda b: pair_product(k, 2 * b + 1 - y))
        finish_chunk(k - 1, q - 1)
        send_ahead(k)
        work(q)
        line_send(q + 1, k, lambda b: pair_product(k, 2 * b + y))
        own[...] = pair_product(k, 2 * z + y)
        fsend[p] = pair_product(k, 2 * z + 1 - y)
        line_own(q, fsend.at[p])
        final_copy(p).start()

    nt = (((1,), (1,)), ((), ()))

    def copies_of(sem, *pairs):
        return [pltpu.make_async_copy(src, dst, sem.at[i]) for i, (src, dst) in enumerate(pairs)]

    def start(copies):
        for copy in copies:
            copy.start()

    def finish(copies):
        for copy in copies:
            copy.wait()

    first_pair, last_pair = n_down, n_down + 2 * n_pairs

    def run_ticks(first, last, work):
        def do_work(at_half):
            for when, fn in work.items():
                low, high = when if isinstance(when, tuple) else (when, when + 1)

                @pl.when((at_half >= low) & (at_half < high))
                def _(fn=fn, low=low, high=high):
                    if isinstance(fn, list):
                        for one in fn:
                            one()
                    elif low + 1 == high:
                        fn()
                    else:
                        fn(at_half - low)

        def single(at_half, carry):
            k = jnp.where(at_half < first_pair, at_half, at_half - n_pairs)
            tick(k)
            do_work(at_half)
            return carry

        def double(m, carry):
            at_half = first_pair + 2 * m
            pair_tick(first_pair + m, lambda q: do_work(at_half))
            do_work(at_half + 1)
            return carry
        if first < first_pair:
            lax.fori_loop(first, min(last, first_pair), single, 0)
        low, high = max(first, first_pair), min(last, last_pair)
        if low < high:
            lax.fori_loop((low - first_pair) // 2, (high - first_pair) // 2, double, 0)
        if last > last_pair:
            lax.fori_loop(max(first, last_pair), last, single, 0)

    def part(fn, *args):
        return functools.partial(fn, *args)

    def side_rows(s, c):
        return pl.ds(s * half + c * chunk, chunk)

    def both_sides(hbm, buf, c, out=False):
        pairs = [(hbm.at[side_rows(s, c)], buf.at[pl.ds(s * chunk, chunk)]) for s in range(2)]
        return [(b, a) for a, b in pairs] if out else pairs

    def sequence_rows(s, c):
        return pl.ds(pl.multiple_of(2 * c * chunk + jnp.where(core == s, 0, chunk), chunk), chunk)

    def core_copy(c, again):
        ss, rs = (cs2_sem, cr2_sem) if again else (cs_sem, cr_sem)
        return remote(cs, crecv.at[c], ss.at[c], rs.at[c], at_tensor(sibling))

    def x_copy(c, again):
        ss, rs = (xs2_sem, xr2_sem) if again else (xs_sem, xr_sem)
        return remote(xs.at[c], xr.at[c], ss.at[c], rs.at[c], at_tensor(across))

    def to_sibling(c, again):
        ss, rs = (as2_sem, ar2_sem) if again else (as_sem, ar_sem)
        return remote(xr.at[c], ag.at[c % 2], ss.at[c], rs.at[c], at_tensor(sibling))

    def pass_on(c, again):
        core_copy(c, again).wait_recv()
        xs[c] += crecv[c]
        x_copy(c, again).start()
        core_copy(c, again).wait_send()

    hidden = wd_hbm.shape[0]

    def feed_phase(wd, grads, gates, ups, ggr, gur, far_rows):
        far_piece = full // ROW_CHUNKS

        def far_load(c):
            return copies_of(
                tok_sem, (partner_hbm.at[pl.ds(c * far_piece, far_piece)], far_rows))

        def far_turn(c):
            finish(far_load(c))
            at[2, :, pl.ds(c * far_piece, far_piece)] = far_rows[...].astype(BF16).T
            if c + 1 < ROW_CHUNKS:
                start(far_load(c + 1))

        def loads(c):
            return copies_of(
                pre_sem, *both_sides(gdr_hbm, grads, c), *both_sides(gate_hbm, gates, c),
                *both_sides(up_hbm, ups, c))

        def stores(c):
            return copies_of(
                st_sem, *both_sides(ggr_hbm, ggr, c, True), *both_sides(gur_hbm, gur, c, True))

        def piece(c):
            finish(loads(c))
            if c == 0:
                finish(load_weight)
            if c >= 1:
                finish(stores(c - 1))

            def tile(n, carry):
                cols = pl.ds(pl.multiple_of(n * TILE, TILE), TILE)
                grad = lax.dot_general(grads[...], wd[cols, :], nt, preferred_element_type=F32)
                gate = gates[:, cols]
                sig = jax.nn.sigmoid(gate)
                act = gate * sig
                ggr[:, cols] = (grad * ups[:, cols] * (sig + act * (1.0 - sig))).astype(BF16)
                gur[:, cols] = (grad * act).astype(BF16)
                return carry
            lax.fori_loop(0, hidden // TILE, tile, 0)
            start(stores(c))
            if c + 1 < ROW_CHUNKS:
                start(loads(c + 1))

        load_weight = copies_of(w_sem, (wd_hbm, wd))
        start(load_weight)
        start(loads(0))
        start(far_load(0))
        at_load(0).wait()
        pair_send(jnp.int32(0))
        pair_send(jnp.int32(1))
        parts = [part(one, c) for c in range(ROW_CHUNKS) for one in (piece, far_turn)]
        cuts = [0, 3, 5, len(parts)]
        run_ticks(0, FEED_TICK, {k: parts[cuts[k] : cuts[k + 1]] for k in range(FEED_TICK)})
        finish(stores(ROW_CHUNKS - 1))

    def hidden_phase(weights, ggr, gur):
        load_weights = copies_of(w_sem, (wg_hbm, weights.at[0]), (wu_hbm, weights.at[1]))

        def loads(c):
            return copies_of(pre_sem, *both_sides(ggr_hbm, ggr, c), *both_sides(gur_hbm, gur, c))

        def piece(c):
            if c == 0:
                finish(load_weights)
            else:
                pass_on(c - 1, False)
            finish(loads(c))

            def tile(n, carry):
                rows = pl.ds(pl.multiple_of(n * TILE, TILE), TILE)
                total_part = lax.dot_general(ggr[...], weights[0, rows, :], nt, preferred_element_type=F32)
                total_part = total_part + lax.dot_general(
                    gur[...], weights[1, rows, :], nt, preferred_element_type=F32)
                xs[c, :, rows] = total_part[0:chunk]
                cs[:, rows] = total_part[chunk : 2 * chunk]
                return carry
            lax.fori_loop(0, width // TILE, tile, 0)
            core_copy(c, False).start()
            if c + 1 < ROW_CHUNKS:
                start(loads(c + 1))

        start(load_weights)
        start(loads(0))
        run_ticks(
            FEED_TICK, HIDDEN_TICK, {FEED_TICK + c: part(piece, c) for c in range(ROW_CHUNKS)})

    def branch_phase(branch, seed, low, turned, w_out, mixed_grad, token_rows, seg_live):
        load_weight = copies_of(w_sem, (w_out_hbm, w_out))
        load_live = copies_of(live_sem, (seg_live_hbm, seg_live))
        token_piece = full // ROW_CHUNKS

        def loads(c):
            rows = pl.ds(c * chunk, chunk)
            return copies_of(
                pre_sem, (branch_hbm.at[rows], branch), (cot_hbm.at[sequence_rows(0, c)], seed))

        def stores(c):
            i = c % 2
            return copies_of(
                st_sem.at[pl.ds(4 * i, 4)],
                (turned.at[i, :, pl.ds(0, chunk)], gbt_hbm.at[:, side_rows(0, c)]),
                (turned.at[i, :, pl.ds(chunk, chunk)], gbt_hbm.at[:, side_rows(1, c)]),
                *[(
                    mixed_grad.at[i, pl.ds(s * chunk, chunk)],
                    gqkv_hbm.at[sequence_rows(s, c), pl.ds(2 * head_cols, head_cols)],
                ) for s in range(2)])

        def hidden_store(c):
            return copies_of(gh_sem, (xs.at[c], gh_hbm.at[pl.ds(c * chunk, chunk)]))

        def token_load(c):
            return copies_of(tok_sem, (tok_hbm.at[pl.ds(c * token_piece, token_piece)], token_rows))

        def first(c):
            i = c % 2
            finish(loads(c))
            if c == 0:
                finish(load_live)
            x_copy(c, False).wait()
            live = seg_live[sequence_rows(0, c), 1:2].astype(F32)
            grad_hidden = xs[c] + xr[c] + seed[...].astype(F32) * live
            xs[c] = grad_hidden
            start(hidden_store(c))
            values = branch[...]
            inv = mean_inverse(values)
            vec[1:2, :] += column_sum(grad_hidden * values * inv)
            scaled = grad_hidden * attn_gain[...]
            dot = jnp.sum(scaled * values, axis=1, keepdims=True)
            grad = inv * scaled - values * (inv * inv * inv * dot / width)
            xr[c] = grad
            to_sibling(c, False).start()
            if c >= 2:
                finish(stores(c - 2))
            low[i, 0:chunk, :] = grad.astype(BF16)
            turned[i, :, 0:chunk] = grad.astype(BF16).T
            if c + 1 < ROW_CHUNKS:
                start(loads(c + 1))

        def second(c):
            i = c % 2
            to_sibling(c, False).wait_recv()
            if c == 0:
                finish(load_weight)
            other = ag[i].astype(BF16)
            low[i, chunk : 2 * chunk, :] = other
            turned[i, :, chunk : 2 * chunk] = other.T
            mixed_grad[i] = lax.dot_general(
                low[i], w_out[...], nt, preferred_element_type=F32).astype(BF16)
            start(stores(c))
            finish(hidden_store(c))
            to_sibling(c, False).wait_send()

        def turn(c):
            finish(token_load(c))
            at[0, :, pl.ds(c * token_piece, token_piece)] = token_rows[...].T
            if c + 1 < ROW_CHUNKS:
                start(token_load(c + 1))

        start(load_weight)
        start(load_live)
        start(loads(0))
        start(token_load(0))
        work = {HIDDEN_TICK + c: [] for c in range(ROW_CHUNKS + 1)}
        work[HIDDEN_TICK].append(part(pass_on, ROW_CHUNKS - 1, False))
        for c in range(ROW_CHUNKS):
            work[HIDDEN_TICK + c].append(part(first, c))
            work[HIDDEN_TICK + c + 1].append(part(second, c))
        work[HIDDEN_TICK + 3] += [part(turn, 0)]
        work[HIDDEN_TICK + 4] += [part(turn, c) for c in range(1, ROW_CHUNKS)]
        run_ticks(HIDDEN_TICK, BRANCH_TICK, work)
        for c in range(ROW_CHUNKS - 2, ROW_CHUNKS):
            finish(stores(c))

    def attention_phase(
        query, key, value, mixed_grad, dq, dk, dv, raw, bias, inverses, seg_live, cosine, sine,
    ):
        heads = head_cols // HEAD
        q_rows = min(256, full)
        scale = HEAD ** (-0.5)
        value_cols = pl.ds(2 * head_cols, head_cols)
        loads = copies_of(
            pre_sem, (query_hbm, query), (key_hbm, key), (value_hbm, value),
            (gqkv_hbm.at[:, value_cols], mixed_grad))
        load_tables = copies_of(
            w_sem, (inverses_hbm, inverses), (seg_live_hbm, seg_live), (cos_hbm, cosine), (sin_hbm, sine))

        def masks():
            finish(load_tables)
            for i in range(full // q_rows):
                rows, keys = slice(i * q_rows, (i + 1) * q_rows), (i + 1) * q_rows
                key_at = lax.broadcasted_iota(jnp.int32, (keys, q_rows), 0)
                query_at = lax.broadcasted_iota(jnp.int32, (keys, q_rows), 1) + i * q_rows
                allowed = (
                    (seg_live[0:keys, 0:1] == seg_row[:, rows])
                    & (key_at <= query_at)
                    & ((seg_live[0:keys, 1:2] > 0) | (key_at == query_at)))
                bias[0:keys, rows] = jnp.where(allowed, 0.0, NEG_FILL).astype(BF16)
            finish(loads)

        def head(h):
            cols = pl.ds(pl.multiple_of(h * HEAD, HEAD), HEAD)
            dk[:, cols] = jnp.zeros((full, HEAD), F32)
            dv[...] = jnp.zeros((full, HEAD), F32)
            for i in range(full // q_rows):
                rows, keys = slice(i * q_rows, (i + 1) * q_rows), (i + 1) * q_rows
                q_block, grad_block = query[rows, cols], mixed_grad[rows, cols]
                key_block, value_block = key[0:keys, cols], value[0:keys, cols]
                scores = lax.dot_general(key_block, q_block, nt, preferred_element_type=F32) * scale
                prob = jnp.exp(scores + bias[0:keys, rows].astype(F32) - log_totals[pl.ds(h, 1), rows])
                grad_prob = lax.dot_general(value_block, grad_block, nt, preferred_element_type=F32)
                row_dot = jnp.sum(prob * grad_prob, axis=0, keepdims=True)
                grad_scores = (prob * (grad_prob - row_dot)).astype(BF16)
                dq[rows, cols] = lax.dot_general(
                    grad_scores, key_block, (((0,), (0,)), ((), ())), preferred_element_type=F32) * scale
                dk[0:keys, cols] += jnp.dot(grad_scores, q_block, preferred_element_type=F32) * scale
                dv[0:keys, :] += jnp.dot(prob.astype(BF16), grad_block, preferred_element_type=F32)
            mixed_grad[:, cols] = dv[...].astype(BF16)

        store_value = copies_of(st_sem, (mixed_grad, gqkv_hbm.at[:, value_cols]))
        sides = ((dq, query_raw_hbm, query_gain), (dk, key_raw_hbm, key_gain))

        def load_raw(which):
            return copies_of(pre_sem, (sides[which][1], raw))

        def back(which):
            grads, _, gain = sides[which]
            finish(load_raw(which))
            gains = gain[...].astype(F32)
            lanes = lax.broadcasted_iota(jnp.int32, (q_rows, HEAD), 1)

            def block_back(i, carry):
                rows = pl.ds(pl.multiple_of(i * q_rows, q_rows), q_rows)
                dot = jnp.zeros((q_rows, 1), F32)
                for h in range(heads):
                    cols = slice(h * HEAD, (h + 1) * HEAD)
                    grad = grads[rows, cols]
                    grad = grad * cosine[rows, :] - pltpu.roll(grad, HEAD // 2, 1) * sine[rows, :]
                    raw_rows = raw[rows, cols]
                    gain_cols = slice(which * head_cols + h * HEAD, which * head_cols + (h + 1) * HEAD)
                    vec[2:3, gain_cols] += column_sum(
                        grad * raw_rows * inverses[rows, which : which + 1])
                    scaled = grad * gains[h : h + 1, :]
                    grads[rows, cols] = scaled
                    dot = dot + jnp.sum(scaled * raw_rows, axis=1, keepdims=True)
                if which == 0:
                    dots[rows, :] = jnp.broadcast_to(dot, (q_rows, HEAD))
                else:
                    dots[rows, :] = jnp.where(lanes == 0, dots[rows, :], dot)
                return carry
            lax.fori_loop(0, full // q_rows, block_back, 0)

        def dots_copy(i):
            return remote(
                dots, dots_in.at[i], ds_sem.at[i], dr_sem.at[i], at_tensor((sibling, across)[i]))

        def dots_add(i):
            dots_copy(i).wait()
            dots[...] += dots_in[i]

        def combine(which):
            grads = sides[which][0]
            for i in range(full // q_rows):
                rows = slice(i * q_rows, (i + 1) * q_rows)
                inv_rows = inverses[rows, which : which + 1]
                dot = dots[rows, which : which + 1]
                mixed_grad[rows, :] = (
                    inv_rows * grads[rows, :]
                    - raw[rows, :] * (inv_rows * inv_rows * inv_rows * dot / width)
                ).astype(BF16)

        def store_grads(which):
            return copies_of(
                st_sem, (mixed_grad, gqkv_hbm.at[:, pl.ds(which * head_cols, head_cols)]))

        def after_heads():
            start(store_value)
            start(load_raw(0))

        def back_query():
            back(0)
            start(load_raw(1))

        def back_key():
            back(1)
            dots_copy(0).start()
            finish(store_value)

        def first_sum():
            dots_add(0)
            dots_copy(1).start()

        def second_sum():
            dots_add(1)
            combine(1)
            start(store_grads(1))
            start(load_raw(0))

        def last_part():
            finish(store_grads(1))
            finish(load_raw(0))
            combine(0)
            start(store_grads(0))

        start(loads)
        start(load_tables)
        t = BRANCH_TICK
        run_ticks(t, INPUT_TICK, {
            t: masks,
            (t, t + heads): head,
            t + heads - 1: after_heads,
            t + heads: back_query,
            t + heads + 1: back_key,
            t + heads + 2: first_sum,
            t + heads + 3: [second_sum, last_part],
        })
        finish(store_grads(0))

    def input_phase(weights, grads, grad_hidden, low):
        loads = copies_of(
            w_sem, *[(w, weights.at[i]) for i, w in enumerate((wq_hbm, wk_hbm, wv_hbm))],
            (gqkv_hbm, grads))

        def piece(c):
            if c == 0:
                finish(loads)
            else:
                pass_on(c - 1, True)
            for s in range(2):
                rows = sequence_rows(s, c)

                def tile(n, carry):
                    cols = pl.ds(pl.multiple_of(n * TILE, TILE), TILE)
                    total_part = jnp.zeros((chunk, TILE), F32)
                    for i in range(3):
                        total_part = total_part + lax.dot_general(
                            grads[rows, i * head_cols : (i + 1) * head_cols], weights[i, cols, :],
                            nt, preferred_element_type=F32)
                    if s == 0:
                        xs[c, :, cols] = total_part
                    else:
                        cs[:, cols] = total_part
                    return carry
                lax.fori_loop(0, width // TILE, tile, 0)
            core_copy(c, True).start()

        def hidden_load(c):
            return copies_of(gh_sem, (gh_hbm.at[pl.ds(c * chunk, chunk)], grad_hidden))

        def stores(c):
            return copies_of(
                st_sem, *[(low.at[s], token_out.at[sequence_rows(s, c)]) for s in range(2)])

        def first(c):
            finish(hidden_load(c))
            x_copy(c, True).wait()
            xr[c] = xs[c] + xr[c] + grad_hidden[...]
            to_sibling(c, True).start()
            if c + 1 < ROW_CHUNKS:
                start(hidden_load(c + 1))

        def second(c):
            if c >= 1:
                finish(stores(c - 1))
            low[0] = xr[c].astype(BF16)
            to_sibling(c, True).wait_recv()
            low[1] = ag[c % 2].astype(BF16)
            start(stores(c))
            to_sibling(c, True).wait_send()

        vec_peer_ids = [at_tensor(sibling)] + [at_dp(peer) for peer in vec_peers]

        def vec_copy(i):
            return remote(vec, vec_in.at[i], vs_sem.at[i], vr_sem.at[i], vec_peer_ids[i])

        def vec_step(i):
            if i >= 1:
                vec_copy(i - 1).wait()
                if i == 1:
                    vec[0:2, :] += vec_in[0, 0:2, :]
                else:
                    vec[...] += vec_in[i - 1]
            if i < len(vec_peer_ids):
                vec_copy(i).start()

        start(loads)
        start(hidden_load(0))
        halves = total + n_pairs
        work = {k: [] for k in range(INPUT_TICK, halves)}
        for c in range(ROW_CHUNKS):
            work[INPUT_TICK + c].append(part(piece, c))
            work[TOKEN_TICK + c].append(part(first, c))
            work[TOKEN_TICK + c + 1].append(part(second, c))
        work[INPUT_TICK + ROW_CHUNKS].append(part(pass_on, ROW_CHUNKS - 1, True))
        for i in range(len(vec_peer_ids) + 1):
            work[INPUT_TICK + 2 + i].append(part(vec_step, i))
        work[last_pair + 1].append(lambda: at_load(3).start())
        work[last_pair + 2].append(lambda: at_load(3).wait())
        run_ticks(INPUT_TICK, halves, {k: fns for k, fns in work.items() if fns})
        finish(stores(ROW_CHUNKS - 1))

    vec[...] = jnp.zeros(vec.shape, F32)
    vec[0:1, :] = gain_mlp_part[...]
    at_load(0).start()
    at_load(1).start()
    for k in range(2):
        b_load(jnp.int32(k), lambda copy: copy.start())
    barrier = pltpu.get_barrier_semaphore()

    def greet_one(peer):
        pl.semaphore_signal(barrier, inc=1, device_id=peer, device_id_type=MESH)

    other_z = z - 1 + 2 * lax.rem(z, 2)
    has_other = (other_z >= 0) & (other_z < line)
    for peer in vec_peers:
        greet_one(at_dp(peer))
    greet_one(at_tensor(sibling))
    greet_one(at_tensor(across))

    @pl.when(has_other)
    def _():
        greet_one(at_dp(2 * other_z + y))
    pl.semaphore_wait(barrier, len(steps) + 2 + has_other.astype(jnp.int32))

    both = 2 * chunk
    rows_of = (full, head_cols)
    pl.run_scoped(
        feed_phase, pltpu.VMEM(wd_hbm.shape, BF16), pltpu.VMEM((both, width), BF16),
        pltpu.VMEM((both, hidden), F32), pltpu.VMEM((both, hidden), F32),
        pltpu.VMEM((both, hidden), BF16), pltpu.VMEM((both, hidden), BF16),
        pltpu.VMEM((full // ROW_CHUNKS, width), F32))
    at_load(1).wait()
    pl.run_scoped(
        hidden_phase, pltpu.VMEM((2,) + wg_hbm.shape, BF16), pltpu.VMEM((both, hidden), BF16),
        pltpu.VMEM((both, hidden), BF16))
    pl.run_scoped(
        branch_phase, pltpu.VMEM((chunk, width), F32), pltpu.VMEM((chunk, width), BF16),
        pltpu.VMEM((2, both, width), BF16), pltpu.VMEM((2, width, both), BF16),
        pltpu.VMEM(w_out_hbm.shape, BF16), pltpu.VMEM((2, both, head_cols), BF16),
        pltpu.VMEM((full // ROW_CHUNKS, width), BF16), pltpu.VMEM(seg_live_hbm.shape, jnp.int32))
    pl.run_scoped(
        attention_phase, pltpu.VMEM(rows_of, BF16), pltpu.VMEM(rows_of, BF16), pltpu.VMEM(rows_of, BF16),
        pltpu.VMEM(rows_of, BF16), pltpu.VMEM(rows_of, F32), pltpu.VMEM(rows_of, F32),
        pltpu.VMEM((full, HEAD), F32), pltpu.VMEM(rows_of, F32), pltpu.VMEM((full, full), BF16),
        pltpu.VMEM((full, HEAD), F32), pltpu.VMEM(seg_live_hbm.shape, jnp.int32),
        pltpu.VMEM((full, HEAD), F32), pltpu.VMEM((full, HEAD), F32))
    pl.run_scoped(
        input_phase, pltpu.VMEM((3,) + wq_hbm.shape, BF16), pltpu.VMEM((full, 3 * head_cols), BF16),
        pltpu.VMEM((chunk, width), F32), pltpu.VMEM((2, chunk, width), BF16))
    finish_chunk(jnp.int32(total - 1), jnp.int32(passes - 1))
    out_act(jnp.int32(total - 1), lambda copy: copy.wait())
    gains_out[...] = jnp.zeros(gains_out.shape, F32)
    gains_out[0:8, :] = vec[...]
    for h in range(2 * head_cols // HEAD):
        gains_out[8 + h : 9 + h, 0:HEAD] = vec[2:3, h * HEAD : (h + 1) * HEAD]


def backward_layer(dp_size, hbm, vmem_args):
    names = dict(zip(HBM_NAMES, hbm, strict=True))
    width, row_count = names["gdrt"].shape
    hidden, head_cols = names["inner"].shape[1], names["query"].shape[1]
    line, block = dp_size // 2, width // dp_size
    chunk = row_count // 2 // ROW_CHUNKS
    counts = (hidden // COLS, hidden // COLS, 3 * head_cols // COLS, head_cols // COLS)
    DMA, REG = pltpu.SemaphoreType.DMA, pltpu.SemaphoreType.REGULAR
    vmem, any_space = pl.BlockSpec(memory_space=pltpu.VMEM), pl.BlockSpec(memory_space=pl.ANY)

    def shape(*dims, kind=F32):
        return jax.ShapeDtypeStruct(dims, kind)

    slot = (block, COLS)
    per_chunk = DMA((ROW_CHUNKS,))
    steps = dp_size.bit_length() - 1
    results = pl.pallas_call(
        functools.partial(backward_kernel, dp_size, counts),
        out_shape=(
            shape(hidden, block),
            shape(head_cols, block),
            shape(block, hidden),
            shape(block, hidden),
            shape(block, head_cols),
            shape(block, head_cols),
            shape(block, head_cols),
            shape(row_count, width, kind=BF16),
            shape(8 + 2 * head_cols // HEAD, width),
            shape(row_count, hidden, kind=BF16),
            shape(row_count, hidden, kind=BF16),
            shape(width, row_count, kind=BF16),
            shape(row_count // 2, width),
            shape(row_count, 3 * head_cols, kind=BF16),
        ),
        in_specs=[any_space] * len(hbm) + [vmem] * len(vmem_args),
        out_specs=(any_space,) * 8 + (vmem,) + (any_space,) * 5,
        scratch_shapes=[
            pltpu.VMEM((3, width, row_count), BF16),
            pltpu.VMEM((B_SLOTS, row_count, COLS), BF16),
            pltpu.VMEM((row_count, COLS), BF16),
            pltpu.VMEM((row_count, COLS), BF16),
            pltpu.VMEM(slot, F32),
            pltpu.VMEM((Y_SLOTS, line) + slot, F32),
            pltpu.VMEM((Y_SLOTS, line) + slot, F32),
            pltpu.VMEM((Y_SLOTS,) + slot, F32),
            pltpu.VMEM((Y_SLOTS,) + slot, F32),
            pltpu.VMEM((2, line) + slot, F32),
            pltpu.VMEM((2, line + 1) + slot, F32),
            pltpu.VMEM(slot, F32),
            pltpu.VMEM((COLS, block), F32),
            pltpu.VMEM((chunk, width), F32),
            pltpu.VMEM((ROW_CHUNKS, chunk, width), F32),
            pltpu.VMEM((ROW_CHUNKS, chunk, width), F32),
            pltpu.VMEM((ROW_CHUNKS, chunk, width), F32),
            pltpu.VMEM((2, chunk, width), F32),
            pltpu.VMEM((row_count, HEAD), F32),
            pltpu.VMEM((2, row_count, HEAD), F32),
            pltpu.VMEM((8, width), F32),
            pltpu.VMEM((steps + 1, 8, width), F32),
            DMA((2,)),
            DMA((B_SLOTS,)),
            DMA,
            DMA((Y_SLOTS, line)),
            DMA((Y_SLOTS, line)),
            DMA((Y_SLOTS,)),
            DMA((Y_SLOTS,)),
            DMA((2, line)),
            DMA((2, line + 1)),
            DMA,
            DMA,
        ]
        + [per_chunk] * 12
        + [DMA((2,)), DMA((2,)), DMA((steps + 1,)), DMA((steps + 1,)), DMA((4,)), DMA((6,)), DMA((8,)), DMA((1,)), DMA((1,)), DMA((1,)),
           REG, REG, REG],
        compiler_params=pltpu.CompilerParams(
            collective_id=2, has_side_effects=True, vmem_limit_bytes=VMEM_LIMIT),
    )(*hbm, *vmem_args)
    return results[:9]


def rope_tables():
    half_size = HEAD // 2
    freq_row = ROPE_BASE ** (-(np.arange(half_size, dtype=np.float64) * 2.0) / HEAD)
    angle = (np.arange(LENGTH, dtype=np.float64)[:, None] * freq_row[None, :]).astype(np.float32)
    cosine, sine = np.cos(angle), np.sin(angle)
    return np.concatenate((cosine, cosine), 1), np.concatenate((-sine, sine), 1)


def make_shards(dp_size):
    def shards(
        tokens,
        segments,
        pad_mask,
        w_query,
        w_key,
        w_value,
        w_out,
        gain_query,
        gain_key,
        gain_attn,
        w_gate,
        w_up,
        w_down,
        gain_mlp,
        cotangent,
    ):
        block = tokens.shape[1] // dp_size
        cosine, sine = (jnp.asarray(table, F32) for table in rope_tables())
        seg_live = jnp.stack((segments, pad_mask), 1)
        seg_row = segments[None, :]
        attn_gain = gain_attn.astype(F32)[None, :]
        mlp_gain = gain_mlp.astype(F32)[None, :]
        (
            gate_rows,
            up_rows,
            inner_rows,
            hidden_turned,
            grad_down_rows,
            grad_down_turned,
            branch_rows,
            output,
            query_norm,
            key_norm,
            value_rows,
            query_raw,
            key_raw,
            mixed_rows,
            partner_rows,
            gain_mlp_part,
            inverses,
            log_totals,
        ) = forward_layer(
            (
                tokens, cotangent, w_query, w_key, w_value, w_out, w_gate, w_up, w_down, cosine, sine,
            ),
            (seg_live, seg_row, gain_query, gain_key, attn_gain, mlp_gain),
        )
        (
            grad_down,
            grad_out,
            grad_gate,
            grad_up,
            grad_query,
            grad_key,
            grad_value,
            grad_tokens,
            gains,
        ) = backward_layer(
            dp_size,
            (
                grad_down_turned, hidden_turned, tokens, inner_rows, mixed_rows, grad_down_rows,
                gate_rows, up_rows, branch_rows, cotangent,
                query_norm, key_norm, value_rows, query_raw, key_raw, partner_rows,
                inverses, seg_live, cosine, sine,
                w_out, w_gate, w_up, w_down, w_query, w_key, w_value,
            ),
            (
                log_totals, seg_row, gain_query, gain_key, attn_gain, gain_mlp_part,
            ),
        )
        heads, head_block = gain_query.shape[0], HEAD // dp_size
        dp_at = lax.axis_index("dp")
        wide = lax.dynamic_slice(gains, (0, dp_at * block), (2, block))
        head_gains = lax.dynamic_slice(gains, (8, dp_at * head_block), (2 * heads, head_block))
        return (
            output,
            grad_tokens,
            grad_query,
            grad_key,
            grad_value,
            grad_out,
            head_gains[:heads],
            head_gains[heads:],
            wide[1],
            grad_gate,
            grad_up,
            grad_down,
            wide[0],
        )

    return shards


def solution(mesh):
    in_specs = (
        P("dp", None),
        P("dp"),
        P("dp"),
        P(None, "tensor"),
        P(None, "tensor"),
        P(None, "tensor"),
        P("tensor", None),
        P("tensor", None),
        P("tensor", None),
        P(),
        P(None, "tensor"),
        P(None, "tensor"),
        P("tensor", None),
        P(),
        P("dp", None),
    )
    out_specs = (
        P("dp", None),
        P("dp", None),
        P("dp", "tensor"),
        P("dp", "tensor"),
        P("dp", "tensor"),
        P("tensor", "dp"),
        P("tensor", "dp"),
        P("tensor", "dp"),
        P("dp"),
        P("dp", "tensor"),
        P("dp", "tensor"),
        P("tensor", "dp"),
        P("dp"),
    )
    shards = make_shards(mesh.shape["dp"])
    return jax.shard_map(shards, mesh=mesh, in_specs=in_specs, out_specs=out_specs, check_vma=False)
```
